32 devices in a mesh: seq: 4 (over z), dp: 8 (over y, x, core).
Axes of the slice: x: 2, y: 2, z: 4, core: 2. Of those that a mesh axis runs over, the one named last changes fastest.
Arguments:
- layer_input: bfloat16 [8192, 1024], P(('dp', 'seq')), may hold values from -6 to 6
- out_grad: bfloat16 [8192, 1024], P(('dp', 'seq')), may hold values from -6 to 6
- lengths: int32 [8, 3], P('dp'), may hold values from 1 to 682, 1024 in all within a row
- item_owner: int32 [8192, 1], P(('dp', 'seq')), may hold values from 0 to 31; in each aligned block of 256 rows (0 to 255, 256 to 511, ...) at most 16 rows name the same one
- item_row: int32 [8192], P(('dp', 'seq')), may hold values from 0 to 511
- w_attn: bfloat16 [1024, 3072], replicated, may hold values from -0.1875 to 0.1875
- w_gate: bfloat16 [1024, 1024], replicated, may hold values from -0.1875 to 0.1875
- w_out: bfloat16 [1024, 1024], replicated, may hold values from -0.1875 to 0.1875
- emb_table: float32 [16384, 1024], P(('seq', 'dp')), may hold values from -6 to 6
- row_accum: float32 [16384], P(('seq', 'dp')), may hold values from 0.25 to 4
Outputs:
- grad_attn: float32 [1024, 3072], P('dp', 'seq')
- grad_gate: float32 [1024, 1024], P('dp', 'seq')
- grad_out: float32 [1024, 1024], P('dp', 'seq')
- new_table: float32 [16384, 1024], P(('seq', 'dp'))
- new_accum: float32 [16384], P(('seq', 'dp'))
The draws below stay inside these ranges and needn't reach their ends.
Inputs may be any that keep to these rules, and one draw needn't show every extreme that they name: Each group's 3 lengths sum to 1024; the largest is exactly 682. `item_owner`: among the 256 events of one device at most 16 name one owner, a bound that some block reaches.
All inputs are finite; a program needn't handle non-finite values.
Results may differ from the reference program's by a relative error of at most 0.0092.
Values may be sent and summed in bfloat16 or wider, within the bound.
No kernel may reach another device: no remote copies, remote signals or barrier semaphores. Data moves between devices by JAX's collectives and lax.ppermute only.
A program may use at most 128 MiB of HBM per device.

```python
import math
import jax
import jax.numpy as jnp
import numpy as np
from jax import lax

D = 1024
H = 16
DH = 64
TOK_DEV = 256
USERS = 3
ROWS_OWN = 512
PACK = 1024
MAXLEN = 682
TOKENS = 8192
CAP = 16
N_DP = 8
DEVICES = 32


def place_ends(entries, own_key, smallest, top_value):
    extent = entries.shape
    spot = [jax.random.randint(jax.random.fold_in(own_key, axis), (), 0, extent[axis]) for axis in range(len(extent))]
    entries = entries.at[tuple(spot)].set(smallest)
    longest = extent.index(max(extent))
    spot[longest] = (spot[longest] + 1) % extent[longest]
    return entries.at[tuple(spot)].set(top_value)


def block_scale(own_key, extent, cuts, low, largest):
    gain = 1.0
    for axis_at, blocks in cuts:
        heights = jax.random.uniform(jax.random.fold_in(jax.random.fold_in(own_key, 6), axis_at), (blocks,), jnp.float32, low / len(cuts), largest / len(cuts))
        gain = gain * jnp.repeat(jnp.exp(heights), extent[axis_at] // blocks).reshape((-1,) + (1,) * (len(extent) - 1 - axis_at))
    return gain


def rank_bounds(number_of, lean):
    weights = [(1 << 20) // math.isqrt(rank ** lean) + 1 for rank in range(1, number_of + 1)]
    width = 1 + sum(weights) // (1 << 30)
    return np.cumsum(np.array([max(1, weight // width) for weight in weights]))


def ranked_ids(rng, dims, number_of, slope):
    grid = rank_bounds(number_of, slope)
    pick = jax.random.randint(jax.random.fold_in(rng, 1), dims, 0, int(grid[number_of - 1]))
    grade = jnp.searchsorted(jnp.asarray(grid, jnp.int32), pick, side="right")
    return jax.random.permutation(jax.random.fold_in(rng, 2), number_of)[grade].astype(jnp.int32)


def split_up(amount, total, most, slope):
    loads = [(1 << 20) // math.isqrt(rank ** slope) + 1 for rank in range(2, amount + 1)]
    spare, given = total - most - (amount - 1), [1] * (amount - 1)
    while spare > 0:
        movable = [i for i in range(amount - 1) if given[i] < most]
        mass, remaining = sum([loads[i] for i in movable]), spare
        for i in movable:
            extra = min(most - given[i], max(1, remaining * loads[i] // mass), spare)
            given[i] = given[i] + extra
            spare = spare - extra
    return np.array([most] + given)


def ragged(own_key, amount, total, limit, skew):
    if amount == 2:
        one = jax.random.randint(own_key, (), max(1, total - limit), min(limit, total - 1) + 1)
        return jnp.stack([one, total - one])
    sizes = jnp.asarray(split_up(amount, total, limit, skew), jnp.int32)
    couples = (amount - 1) // 2
    donor, receiver = sizes[1:1 + 2 * couples:2], sizes[2:2 + 2 * couples:2]
    slack = jnp.minimum(donor - 1, limit - receiver)
    shifted = jax.random.randint(jax.random.fold_in(own_key, 1), (couples,), 0, 1 << 20) % (slack + 1)
    sizes = sizes.at[1:1 + 2 * couples:2].set(donor - shifted).at[2:2 + 2 * couples:2].set(receiver + shifted)
    return sizes[jax.random.permutation(jax.random.fold_in(own_key, 2), amount)]


def shared_out(key, own, number, rows, count, top, bound, slope):
    ranking = jax.random.permutation(key, count)
    crowded, usual = shares(count, rows * top, bound, slope, True), shares(count, rows * top, bound, slope, False)
    places = jnp.arange(count)

    def named(sizes, offset_by):
        used = int((sizes > 0).sum())
        fixed = max(1, used // 4)
        shifted = fixed + (places - fixed + offset_by * (used - fixed)) % max(1, count - fixed)
        return jnp.zeros((count,), jnp.int32).at[ranking[jnp.where(places < fixed, places, shifted)]].set(jnp.asarray(sizes, jnp.int32))

    sizes = jnp.where(number % 4 == 0, named(crowded, number // 4), named(usual, number - number // 4 - 1))
    mixed = jax.random.permutation(jax.random.fold_in(own, 3), count)
    giver, sink = mixed[0:count // 2 * 2:2], mixed[1:count // 2 * 2:2]
    margin = jnp.minimum(sizes[giver] - 1, bound - sizes[sink]) // 2
    margin = jnp.where((giver == ranking[0]) | (sink == ranking[0]) | (sizes[sink] == 0), 0, jnp.maximum(margin, 0))
    shifted = jax.random.randint(jax.random.fold_in(own, 4), (count // 2,), 0, 1 << 20) % (margin + 1)
    sizes = sizes.at[giver].add(-shifted).at[sink].add(shifted)
    members = jnp.searchsorted(jnp.cumsum(sizes), jnp.arange(rows * top), side="right").astype(jnp.int32)
    table = members.reshape(top, rows).T
    table = table[jax.random.permutation(jax.random.fold_in(own, 1), rows)]
    offset_by = jax.random.randint(jax.random.fold_in(own, 2), (rows, 1), 0, top)
    return jnp.take_along_axis(table, (jnp.arange(top)[None, :] + offset_by) % top, axis=1)


def shares(amount, total, most, slope, full):
    portions = [(1 << 20) // math.isqrt(standing ** slope) + 1 for standing in range(1, amount + 1)]
    largest = most if full else min(most, max(-(-total // amount), total * portions[0] // sum(portions)))
    least = 1 if total - largest >= amount - 1 else 0
    holding, spare = [largest] + [least] * (amount - 1), total - largest - least * (amount - 1)
    while spare > 0:
        movable = [i for i in range(1, amount) if holding[i] < largest] or [i for i in range(1, amount) if holding[i] < most]
        mass, budget = sum([portions[i] for i in movable]), spare
        for i in movable:
            more = min(most - holding[i], max(1, budget * portions[i] // mass), spare)
            holding[i] = holding[i] + more
            spare = spare - more
    return np.array(holding)


def noise(rng, shape, spread, reach, split=(), kind=jnp.bfloat16):
    entries = jax.random.normal(rng, shape, jnp.float32) * spread
    if len(split) > 0:
        entries = block_scale(rng, shape, split, -0.22, 0.18) * entries
    return jnp.clip(entries, min=-reach, max=reach).astype(kind)


def setup_inputs(seed: int = 0) -> dict:
    keys = jax.random.split(jax.random.key(seed), 11)
    layer_input = noise(keys[0], (TOKENS, D), 1.0, 6.0, ((0, 32),))
    out_grad = noise(keys[1], (TOKENS, D), 1.0, 6.0, ((0, 32),))
    lengths = jax.vmap(lambda own: ragged(own, USERS, PACK, MAXLEN, 2))(jax.random.split(keys[2], N_DP)).reshape((N_DP, USERS)).astype(jnp.int32)
    item_owner_keys = jax.random.split(jax.random.fold_in(keys[3], 1), TOKENS // TOK_DEV)
    item_owner_turns = jax.random.permutation(jax.random.fold_in(keys[3], 3), TOKENS // TOK_DEV)
    item_owner = jax.vmap(lambda own, number: shared_out(jax.random.fold_in(keys[3], 2), own, number, TOK_DEV, DEVICES, 1, CAP, 2))(item_owner_keys, item_owner_turns).reshape((TOKENS, 1))
    item_row = place_ends(ranked_ids(keys[4], (TOKENS,), ROWS_OWN, 2), jax.random.fold_in(keys[4], 3), 0, ROWS_OWN - 1).astype(jnp.int32)
    w_attn = noise(keys[5], (D, 3 * D), D ** -0.5, 0.1875)
    w_gate = noise(keys[6], (D, D), D ** -0.5, 0.1875)
    w_out = noise(keys[7], (D, D), D ** -0.5, 0.1875)
    emb_table = noise(keys[8], (DEVICES * ROWS_OWN, D), 1.0, 6.0, ((0, 32),), jnp.float32)
    row_accum = jnp.clip(jnp.exp(math.log(4.0) - 2.7725887 * jax.random.uniform(keys[9], (DEVICES * ROWS_OWN,), jnp.float32) ** block_scale(keys[9], (DEVICES * ROWS_OWN,), ((0, 32),), -0.2, 0.2)), 0.25, 4.0)
    return {"layer_input": layer_input, "out_grad": out_grad, "lengths": lengths, "item_owner": item_owner, "item_row": item_row, "w_attn": w_attn, "w_gate": w_gate, "w_out": w_out, "emb_table": emb_table, "row_accum": row_accum}


NORM_EPS = 1e-05
LEARN_RATE = 0.1

def silu_grad(pre_act):
    sigmoid = jax.nn.sigmoid(pre_act)
    return sigmoid * (1.0 + pre_act * (1.0 - sigmoid))

def segment_ids(length_row, positions):
    seg_ends = jnp.cumsum(length_row.astype(jnp.int32))
    places = jnp.arange(positions, dtype=jnp.int32)
    return lax.optimization_barrier(jnp.sum((places[:, None] >= seg_ends[None, :]).astype(jnp.int32), axis=1))

def group_backward(layer_input, out_grad, length_row, w_attn, w_gate, w_out):
    positions = layer_input.shape[0]
    scale = DH ** (-0.5)
    attn_pre = jnp.dot(layer_input, w_attn, preferred_element_type=jnp.float32)
    gate_pre = jnp.dot(layer_input, w_gate, preferred_element_type=jnp.float32)
    acts = jax.nn.silu(attn_pre).astype(jnp.bfloat16).reshape(positions, H, 3, DH)
    gate_act = jax.nn.silu(gate_pre)
    segment = segment_ids(length_row, positions)
    places = jnp.arange(positions, dtype=jnp.int32)
    allowed = (segment[:, None] == segment[None, :]) & (places[None, :] <= places[:, None])
    per_head = jnp.transpose(acts, (1, 0, 2, 3))

    def head_forward(head_item):
        scores = jnp.dot(head_item[:, 1], head_item[:, 2].T, preferred_element_type=jnp.float32) * scale
        weights = jnp.where(allowed, jax.nn.silu(scores) / MAXLEN, 0.0).astype(jnp.bfloat16)
        return jnp.dot(weights, head_item[:, 0], preferred_element_type=jnp.float32).astype(jnp.bfloat16)
    heads_out = lax.map(head_forward, per_head)
    mixed_in = jnp.transpose(heads_out, (1, 0, 2)).reshape(positions, D).astype(jnp.float32)
    centred = mixed_in - lax.optimization_barrier(jnp.mean(mixed_in, axis=1, keepdims=True))
    inv_dev = lax.rsqrt(lax.optimization_barrier(jnp.mean(centred * centred, axis=1, keepdims=True)) + NORM_EPS)
    normed = centred * inv_dev
    mixed = (normed * gate_act).astype(jnp.bfloat16)
    mixed_grad = jnp.dot(out_grad, w_out.T, preferred_element_type=jnp.float32)
    grad_out_part = jnp.dot(mixed.T, out_grad, preferred_element_type=jnp.float32)
    normed_grad = mixed_grad * gate_act
    gate_act_grad = mixed_grad * normed
    heads_grad = inv_dev * (normed_grad - lax.optimization_barrier(jnp.mean(normed_grad, axis=1, keepdims=True)) - normed * lax.optimization_barrier(jnp.mean(normed_grad * normed, axis=1, keepdims=True)))
    heads_grad = heads_grad.astype(jnp.bfloat16).reshape(positions, H, DH)

    def head_backward(head_pair):
        head_item, grad_item = head_pair
        values = head_item[:, 0]
        queries = head_item[:, 1]
        keys_head = head_item[:, 2]
        scores = jnp.dot(queries, keys_head.T, preferred_element_type=jnp.float32) * scale
        weights = jnp.where(allowed, jax.nn.silu(scores) / MAXLEN, 0.0).astype(jnp.bfloat16)
        weight_grad = jnp.dot(grad_item, values.T, preferred_element_type=jnp.float32)
        score_grad = jnp.where(allowed, weight_grad * silu_grad(scores) * (scale / MAXLEN), 0.0).astype(jnp.bfloat16)
        values_grad = jnp.dot(weights.T, grad_item, preferred_element_type=jnp.float32)
        query_grad = jnp.dot(score_grad, keys_head, preferred_element_type=jnp.float32)
        keys_grad = jnp.dot(score_grad.T, queries, preferred_element_type=jnp.float32)
        return jnp.stack([values_grad.astype(jnp.bfloat16), query_grad.astype(jnp.bfloat16), keys_grad.astype(jnp.bfloat16)], axis=1)
    acts_grad = lax.map(head_backward, (per_head, jnp.transpose(heads_grad, (1, 0, 2))))
    acts_grad = jnp.transpose(acts_grad, (1, 0, 2, 3)).reshape(positions, 3 * D)
    attn_grad = (acts_grad.astype(jnp.float32) * silu_grad(attn_pre)).astype(jnp.bfloat16)
    gate_grad = (gate_act_grad * silu_grad(gate_pre)).astype(jnp.bfloat16)
    grad_attn_part = jnp.dot(layer_input.T, attn_grad, preferred_element_type=jnp.float32)
    grad_gate_part = jnp.dot(layer_input.T, gate_grad, preferred_element_type=jnp.float32)
    input_grad = jnp.dot(attn_grad, w_attn.T, preferred_element_type=jnp.float32) + jnp.dot(gate_grad, w_gate.T, preferred_element_type=jnp.float32) + out_grad.astype(jnp.float32)
    return (grad_attn_part, grad_gate_part, grad_out_part, input_grad)

def reference(layer_input, out_grad, lengths, item_owner, item_row, w_attn, w_gate, w_out, emb_table, row_accum):
    groups = lengths.shape[0]
    inputs_grp = layer_input.reshape(groups, -1, D)
    grads_grp = out_grad.reshape(groups, -1, D)

    def step(totals, pieces):
        parts = group_backward(pieces[0], pieces[1], pieces[2], w_attn, w_gate, w_out)
        return ((totals[0] + parts[0], totals[1] + parts[1], totals[2] + parts[2]), parts[3])
    init = (jnp.zeros((D, 3 * D), jnp.float32), jnp.zeros((D, D), jnp.float32), jnp.zeros((D, D), jnp.float32))
    totals, input_grads = lax.scan(step, init, (inputs_grp, grads_grp, lengths))
    input_grads = input_grads.reshape(-1, D)
    table_rows = (item_owner[:, 0] * ROWS_OWN + item_row).astype(jnp.int32)
    table_grad = jnp.zeros(emb_table.shape, jnp.float32).at[table_rows].add(input_grads)
    new_accum = row_accum + lax.optimization_barrier(jnp.mean(table_grad * table_grad, axis=1))
    new_table = emb_table - LEARN_RATE * table_grad * lax.rsqrt(new_accum)[:, None]
    return (totals[0], totals[1], totals[2], new_table, new_accum)
```

```python
import functools

import jax
import jax.numpy as jnp
from jax import lax
from jax.experimental import pallas as pl
from jax.experimental.pallas import tpu as pltpu
from jax.sharding import PartitionSpec as P

D = 1024
H = 16
DH = 64
PAIR = 2 * DH

NORM_EPS = 1e-05
LEARN_RATE = 0.1
VMEM_LIMIT = 56 * 1024 * 1024
BF = jnp.bfloat16
F32 = jnp.float32


def dot_nn(a, b):
    return lax.dot_general(a, b, (((1,), (0,)), ((), ())), preferred_element_type=F32)


def dot_nt(a, b):
    return lax.dot_general(a, b, (((1,), (1,)), ((), ())), preferred_element_type=F32)


def history_start(lengths_ref, users, place):
    start = jnp.zeros_like(place)
    end = jnp.int32(0)
    for user in range(users - 1):
        end = end + lengths_ref[0, user]
        start = jnp.where(place >= end, end, start)
    return start


def block_needed(lengths_ref, users, i, j, blk):
    return (j + 1) * blk > history_start(lengths_ref, users, i * blk)


def forward_kernel(
    lengths_ref, x_ref, w_ref, acts_ref, dact_ref, weights_ref, slope_ref, heads_ref, q_half, *, blk, users, maxlen
):
    i = pl.program_id(1)
    positions = x_ref.shape[0]
    blocks = positions // blk

    @pl.when(i == 0)
    def _():
        def rows(r, _):
            at = pl.ds(pl.multiple_of(r * blk, blk), blk)
            pre = dot_nn(x_ref[at, :], w_ref[...])
            half = 0.5 * pre
            t = jnp.tanh(half)
            p = half * t
            acts = (half + p).astype(BF)
            acts_ref[at, :] = acts
            dact_ref[at, :] = (0.5 * (1.0 + t) * (1.0 + half - p)).astype(BF)
            q_half[at, :] = acts[:, PAIR : 2 * PAIR] * jnp.asarray(0.5 * DH**-0.5, BF)
            return 0

        lax.fori_loop(0, blocks, rows, 0)

    at_i = pl.ds(pl.multiple_of(i * blk, blk), blk)
    q_i = q_half[at_i, :]
    row = i * blk + lax.broadcasted_iota(jnp.int32, (blk, blk), 0)
    col0 = lax.broadcasted_iota(jnp.int32, (blk, blk), 1)
    start = history_start(lengths_ref, users, row)

    def column(j, acc):
        at_j = pl.ds(pl.multiple_of(j * blk, blk), blk)
        col = col0 + j * blk
        allowed = (col <= row) & (col >= start)
        outs = []
        for h in range(2):
            lanes = slice(h * DH, (h + 1) * DH)
            k_j = acts_ref[at_j, 2 * PAIR + h * DH : 2 * PAIR + (h + 1) * DH]
            v_j = acts_ref[at_j, h * DH : (h + 1) * DH]
            half = dot_nt(q_i[:, lanes], k_j)
            half = jnp.where(allowed, half, -64.0)
            t = jnp.tanh(half)
            p = half * t
            weights = (half + p).astype(BF)
            slope = ((1.0 + t) * (1.0 + half - p)).astype(BF)
            weights_ref[h, :, at_j] = weights
            slope_ref[h, :, at_j] = slope
            outs.append(acc[h] + dot_nn(weights, v_j))
        return tuple(outs)

    first = history_start(lengths_ref, users, i * blk) // blk
    zero = jnp.zeros((blk, DH), F32)
    acc = lax.fori_loop(first, i + 1, column, (zero, zero))
    heads_ref[...] = (jnp.concatenate(acc, axis=1) * (1.0 / maxlen)).astype(BF)


def forward_attention(lengths, x_full, w_pairs, blk, maxlen):
    positions = x_full.shape[0]
    pairs = w_pairs.shape[1] // (3 * PAIR)
    users = lengths.shape[1]
    blocks = positions // blk
    elements = 2 * pairs * positions * positions // 2
    return pl.pallas_call(
        functools.partial(forward_kernel, blk=blk, users=users, maxlen=maxlen),
        grid=(pairs, blocks),
        in_specs=[
            pl.BlockSpec(memory_space=pltpu.SMEM),
            pl.BlockSpec((positions, D), lambda p, i: (0, 0)),
            pl.BlockSpec((D, 3 * PAIR), lambda p, i: (0, p)),
        ],
        out_specs=[
            pl.BlockSpec((positions, 3 * PAIR), lambda p, i: (0, p)),
            pl.BlockSpec((positions, 3 * PAIR), lambda p, i: (0, p)),
            pl.BlockSpec((2, blk, positions), lambda p, i: (p, i, 0)),
            pl.BlockSpec((2, blk, positions), lambda p, i: (p, i, 0)),
            pl.BlockSpec((blk, PAIR), lambda p, i: (i, p)),
        ],
        out_shape=[
            jax.ShapeDtypeStruct((positions, pairs * 3 * PAIR), BF),
            jax.ShapeDtypeStruct((positions, pairs * 3 * PAIR), BF),
            jax.ShapeDtypeStruct((2 * pairs, positions, positions), BF),
            jax.ShapeDtypeStruct((2 * pairs, positions, positions), BF),
            jax.ShapeDtypeStruct((positions, pairs * PAIR), BF),
        ],
        scratch_shapes=[pltpu.VMEM((positions, PAIR), BF)],
        compiler_params=pltpu.CompilerParams(vmem_limit_bytes=VMEM_LIMIT),
        cost_estimate=pl.CostEstimate(
            flops=2 * positions * D * pairs * 3 * PAIR + 4 * elements * 256,
            bytes_accessed=4 * positions * D + 4 * elements,
            transcendentals=elements,
        ),
        name="attention_forward",
    )(lengths, x_full, w_pairs)


def gate_kernel(x_ref, og_ref, wg_ref, wo_ref, heads_ref, gate_ref, ng_ref, u_ref, stats_ref):
    gate_pre = dot_nn(x_ref[...], wg_ref[...])
    mixed_grad = dot_nt(og_ref[...], wo_ref[...])
    half = 0.5 * gate_pre
    t = jnp.tanh(half)
    p = half * t
    gate = half + p
    gate_ref[...] = gate
    ng = mixed_grad * gate
    ng_ref[...] = ng
    u_ref[...] = mixed_grad * (0.5 * (1.0 + t) * (1.0 + half - p))
    heads = heads_ref[...].astype(F32)
    mean = jnp.mean(heads, axis=1, keepdims=True)
    centred = heads - mean
    square = jnp.sum(centred * centred, axis=1, keepdims=True)
    total = jnp.sum(ng, axis=1, keepdims=True)
    cross = jnp.sum(ng * centred, axis=1, keepdims=True)
    lane = lax.broadcasted_iota(jnp.int32, (heads.shape[0], 128), 1)
    packed = jnp.where(lane == 0, mean, jnp.where(lane == 1, square, jnp.where(lane == 2, total, cross)))
    stats_ref[...] = jnp.transpose(packed)[:8, :]


def gate_stats(x_full, og_full, w_gate_own, w_out_own, heads, blk):
    positions = x_full.shape[0]
    cols = heads.shape[1]
    return pl.pallas_call(
        gate_kernel,
        grid=(positions // blk,),
        in_specs=[
            pl.BlockSpec((blk, D), lambda i: (i, 0)),
            pl.BlockSpec((blk, D), lambda i: (i, 0)),
            pl.BlockSpec((D, cols), lambda i: (0, 0)),
            pl.BlockSpec((cols, D), lambda i: (0, 0)),
            pl.BlockSpec((blk, cols), lambda i: (i, 0)),
        ],
        out_specs=[
            pl.BlockSpec((blk, cols), lambda i: (i, 0)),
            pl.BlockSpec((blk, cols), lambda i: (i, 0)),
            pl.BlockSpec((blk, cols), lambda i: (i, 0)),
            pl.BlockSpec((8, blk), lambda i: (0, i)),
        ],
        out_shape=[
            jax.ShapeDtypeStruct((positions, cols), F32),
            jax.ShapeDtypeStruct((positions, cols), F32),
            jax.ShapeDtypeStruct((positions, cols), F32),
            jax.ShapeDtypeStruct((8, positions), F32),
        ],
        compiler_params=pltpu.CompilerParams(vmem_limit_bytes=VMEM_LIMIT),
        cost_estimate=pl.CostEstimate(
            flops=4 * positions * D * cols, bytes_accessed=4 * positions * D, transcendentals=positions * cols
        ),
        name="gate_and_stats",
    )(x_full, og_full, w_gate_own, w_out_own, heads)


def backward_kernel(
    lengths_ref,
    stats_ref,
    heads_ref,
    gate_ref,
    ng_ref,
    u_ref,
    acts_ref,
    dact_ref,
    weights_ref,
    slope_ref,
    grad_ref,
    gate_grad_ref,
    mixed_ref,
    o_ref,
    o_t,
    q_t,
    vg_t,
    kg_t,
    qg,
    *,
    blk,
    users,
    maxlen,
    shards,
    cols,
):
    i = pl.program_id(1)
    positions = heads_ref.shape[0]
    blocks = positions // blk
    scale = DH ** (-0.5)

    @pl.when(i == 0)
    def _():
        means = [stats_ref[8 * s : 8 * s + 1, :] for s in range(shards)]
        mean = sum(means) * (1.0 / shards)
        square = jnp.zeros_like(mean)
        total = jnp.zeros_like(mean)
        cross = jnp.zeros_like(mean)
        for s in range(shards):
            shift = means[s] - mean
            part = stats_ref[8 * s + 2 : 8 * s + 3, :]
            square = square + stats_ref[8 * s + 1 : 8 * s + 2, :] + cols * shift * shift
            total = total + part
            cross = cross + stats_ref[8 * s + 3 : 8 * s + 4, :] + shift * part
        inv_dev = lax.rsqrt(square * (1.0 / D) + NORM_EPS)
        row8 = lax.broadcasted_iota(jnp.int32, (128, positions), 0)
        packed = jnp.where(
            row8 == 0,
            mean,
            jnp.where(row8 == 1, inv_dev, jnp.where(row8 == 2, total * (1.0 / D), cross * inv_dev * (1.0 / D))),
        )
        per_event = jnp.transpose(packed)
        mean_c = per_event[:, 0:1]
        inv_c = per_event[:, 1:2]
        total_c = per_event[:, 2:3]
        cross_c = per_event[:, 3:4]
        normed = (heads_ref[...].astype(F32) - mean_c) * inv_c
        mixed_ref[...] = (normed * gate_ref[...]).astype(BF)
        gate_grad_ref[...] = (u_ref[...] * normed).astype(BF)
        o = (inv_c * (ng_ref[...] - total_c - normed * cross_c)).astype(BF)
        o_ref[...] = o
        o_t[...] = jnp.transpose(o)
        q_t[...] = jnp.transpose(acts_ref[:, PAIR : 2 * PAIR])
        vg_t[...] = jnp.zeros_like(vg_t)
        kg_t[...] = jnp.zeros_like(kg_t)

    at_i = pl.ds(pl.multiple_of(i * blk, blk), blk)

    def column(j, acc):
        at_j = pl.ds(pl.multiple_of(j * blk, blk), blk)
        outs = []
        for h in range(2):
            lanes = slice(h * DH, (h + 1) * DH)
            k_j = acts_ref[at_j, 2 * PAIR + h * DH : 2 * PAIR + (h + 1) * DH]
            v_j = acts_ref[at_j, h * DH : (h + 1) * DH]
            weight_grad = dot_nt(o_ref[at_i, lanes], v_j)
            score_grad = (weight_grad * slope_ref[h, :, at_j].astype(F32)).astype(BF)
            vg_t[lanes, at_j] += dot_nn(o_t[lanes, at_i], weights_ref[h, :, at_j])
            kg_t[lanes, at_j] += dot_nn(q_t[lanes, at_i], score_grad)
            outs.append(acc[h] + dot_nn(score_grad, k_j))
        return tuple(outs)

    first = history_start(lengths_ref, users, i * blk) // blk
    zero = jnp.zeros((blk, DH), F32)
    acc = lax.fori_loop(first, i + 1, column, (zero, zero))
    qg[at_i, :] = jnp.concatenate(acc, axis=1)

    @pl.when(i == blocks - 1)
    def _():
        factor = 0.5 * scale / maxlen
        v_grad = (jnp.transpose(vg_t[...]) * (1.0 / maxlen)).astype(BF).astype(F32)
        q_grad = (qg[...] * factor).astype(BF).astype(F32)
        k_grad = (jnp.transpose(kg_t[...]) * factor).astype(BF).astype(F32)
        grad_ref[:, :PAIR] = (v_grad * dact_ref[:, :PAIR].astype(F32)).astype(BF)
        grad_ref[:, PAIR : 2 * PAIR] = (q_grad * dact_ref[:, PAIR : 2 * PAIR].astype(F32)).astype(BF)
        grad_ref[:, 2 * PAIR :] = (k_grad * dact_ref[:, 2 * PAIR :].astype(F32)).astype(BF)


def backward_attention(lengths, stats, heads, gate, ng, u, acts, dact, weights, slope, blk, maxlen, shards):
    positions, cols = heads.shape
    pairs = cols // PAIR
    users = lengths.shape[1]
    elements = 2 * pairs * positions * positions // 2
    whole = lambda p, i: (0, p)
    return pl.pallas_call(
        functools.partial(backward_kernel, blk=blk, users=users, maxlen=maxlen, shards=shards, cols=cols),
        grid=(pairs, positions // blk),
        in_specs=[
            pl.BlockSpec(memory_space=pltpu.SMEM),
            pl.BlockSpec((8 * shards, positions), lambda p, i: (0, 0)),
            pl.BlockSpec((positions, PAIR), whole),
            pl.BlockSpec((positions, PAIR), whole),
            pl.BlockSpec((positions, PAIR), whole),
            pl.BlockSpec((positions, PAIR), whole),
            pl.BlockSpec((positions, 3 * PAIR), whole),
            pl.BlockSpec((positions, 3 * PAIR), whole),
            pl.BlockSpec((2, blk, positions), lambda p, i: (p, i, 0)),
            pl.BlockSpec((2, blk, positions), lambda p, i: (p, i, 0)),
        ],
        out_specs=[
            pl.BlockSpec((positions, 3 * PAIR), whole),
            pl.BlockSpec((positions, PAIR), whole),
            pl.BlockSpec((positions, PAIR), whole),
        ],
        out_shape=[
            jax.ShapeDtypeStruct((positions, pairs * 3 * PAIR), BF),
            jax.ShapeDtypeStruct((positions, cols), BF),
            jax.ShapeDtypeStruct((positions, cols), BF),
        ],
        scratch_shapes=[
            pltpu.VMEM((positions, PAIR), BF),
            pltpu.VMEM((PAIR, positions), BF),
            pltpu.VMEM((PAIR, positions), BF),
            pltpu.VMEM((PAIR, positions), F32),
            pltpu.VMEM((PAIR, positions), F32),
            pltpu.VMEM((positions, PAIR), F32),
        ],
        compiler_params=pltpu.CompilerParams(vmem_limit_bytes=VMEM_LIMIT),
        cost_estimate=pl.CostEstimate(
            flops=8 * elements * 256, bytes_accessed=4 * elements + 20 * positions * cols, transcendentals=0
        ),
        name="attention_backward",
    )(lengths, stats, heads, gate, ng, u, acts, dact, weights, slope)


def update_kernel(ids_ref, rows_ref, table_ref, accum_ref, new_table_ref, new_accum_ref):
    i = pl.program_id(0)
    blk = table_ref.shape[0]
    slots = rows_ref.shape[0]
    row = i * blk + lax.broadcasted_iota(jnp.int32, (blk, slots), 0)
    hits = jnp.where(row == ids_ref[...], 1.0, 0.0).astype(BF)
    grad = dot_nn(hits, rows_ref[...])
    accum = accum_ref[...] + jnp.mean(grad * grad, axis=1, keepdims=True)
    new_accum_ref[...] = accum
    new_table_ref[...] = table_ref[...] - LEARN_RATE * grad * lax.rsqrt(accum)


def update_rows(got_ids, got_rows, emb_table, row_accum):
    rows_own = emb_table.shape[0]
    slots = got_rows.shape[0]
    blk = min(128, rows_own)
    new_table, new_accum = pl.pallas_call(
        update_kernel,
        grid=(rows_own // blk,),
        in_specs=[
            pl.BlockSpec((1, slots), lambda i: (0, 0)),
            pl.BlockSpec((slots, D), lambda i: (0, 0)),
            pl.BlockSpec((blk, D), lambda i: (i, 0)),
            pl.BlockSpec((blk, 1), lambda i: (i, 0)),
        ],
        out_specs=[
            pl.BlockSpec((blk, D), lambda i: (i, 0)),
            pl.BlockSpec((blk, 1), lambda i: (i, 0)),
        ],
        out_shape=[
            jax.ShapeDtypeStruct((rows_own, D), F32),
            jax.ShapeDtypeStruct((rows_own, 1), F32),
        ],
        compiler_params=pltpu.CompilerParams(vmem_limit_bytes=VMEM_LIMIT),
        cost_estimate=pl.CostEstimate(
            flops=2 * rows_own * slots * D, bytes_accessed=8 * rows_own * D + 2 * slots * D, transcendentals=rows_own
        ),
        name="update_rows",
    )(got_ids.reshape(1, slots), got_rows, emb_table, row_accum[:, None])
    return new_table, new_accum[:, 0]


def body(
    layer_input,
    out_grad,
    lengths,
    item_owner,
    item_row,
    w_attn,
    w_gate,
    w_out,
    emb_table,
    row_accum,
):
    seq_count = lax.axis_size("seq")
    dp_count = lax.axis_size("dp")
    devices = seq_count * dp_count
    seq_id = lax.axis_index("seq")
    tokens_dev = layer_input.shape[0]
    positions = tokens_dev * seq_count
    maxlen = 2 * positions // 3
    blk = min(256, positions)
    cols = D // seq_count
    pairs = cols // PAIR

    w_attn_own = lax.dynamic_slice_in_dim(w_attn, seq_id * 3 * cols, 3 * cols, 1)
    w_attn_own = w_attn_own.reshape(D, pairs, 2, 3, DH).transpose(0, 1, 3, 2, 4).reshape(D, 3 * cols)
    w_gate_own = lax.dynamic_slice_in_dim(w_gate, seq_id * cols, cols, 1)
    w_out_own = lax.dynamic_slice_in_dim(w_out, seq_id * cols, cols, 0)

    rows_own = emb_table.shape[0]
    capacity = max(2, 2 * tokens_dev // devices)
    owners = item_owner[:, 0]
    owner_hits = (owners[:, None] == jnp.arange(devices, dtype=jnp.int32)[None, :]).astype(F32)
    before = (
        jnp.arange(tokens_dev, dtype=jnp.int32)[:, None] > jnp.arange(tokens_dev, dtype=jnp.int32)[None, :]
    ).astype(F32)
    slots = jnp.sum(jnp.dot(before, owner_hits) * owner_hits, axis=1).astype(jnp.int32)
    flat_slot = owners * capacity + slots
    slot_hits = jnp.arange(devices * capacity, dtype=jnp.int32)[:, None] == flat_slot[None, :]
    send_ids = jnp.min(jnp.where(slot_hits, item_row[None, :], rows_own), axis=1).astype(jnp.int32)
    got_ids = lax.all_to_all(
        send_ids.reshape(devices, capacity), ("seq", "dp"), split_axis=0, concat_axis=0, tiled=True
    ).reshape(devices * capacity)
    slot_matrix = slot_hits.astype(BF)

    x_full = lax.all_gather(layer_input, "seq", axis=0, tiled=True)
    og_full = lax.all_gather(out_grad, "seq", axis=0, tiled=True)

    acts, dact, weights, slope, heads = forward_attention(lengths, x_full, w_attn_own, blk, maxlen)
    gate, ng, u, stats_own = gate_stats(x_full, og_full, w_gate_own, w_out_own, heads, blk)
    stats = lax.all_gather(stats_own, "seq", axis=0, tiled=True)
    attn_grad, gate_grad, mixed = backward_attention(
        lengths, stats, heads, gate, ng, u, acts, dact, weights, slope, blk, maxlen, seq_count
    )

    input_part = (dot_nt(attn_grad, w_attn_own) + dot_nt(gate_grad, w_gate_own)).astype(BF)
    got = lax.all_to_all(
        input_part.reshape(seq_count, tokens_dev, D), "seq", split_axis=0, concat_axis=0, tiled=True
    )
    input_grad = jnp.sum(got.astype(F32), axis=0) + out_grad.astype(F32)
    send_rows = jnp.dot(slot_matrix, input_grad.astype(BF), preferred_element_type=F32).astype(BF)
    got_rows = lax.all_to_all(
        send_rows.reshape(devices, capacity, D), ("seq", "dp"), split_axis=0, concat_axis=0, tiled=True
    ).reshape(devices * capacity, D)
    new_table, new_accum = update_rows(got_ids, got_rows, emb_table, row_accum)

    tn = (((0,), (0,)), ((), ()))
    attn_part = lax.dot_general(x_full, attn_grad, tn, preferred_element_type=F32).astype(BF)
    gate_part = lax.dot_general(x_full, gate_grad, tn, preferred_element_type=F32).astype(BF)
    out_part = lax.dot_general(mixed, og_full, tn, preferred_element_type=F32).astype(BF)
    share = dp_count // seq_count
    out_part = (
        out_part.reshape(share, D // dp_count, seq_count, cols).transpose(0, 2, 1, 3).reshape(D, cols)
    )
    merged = jnp.concatenate([attn_part, gate_part, out_part], axis=1)
    merged = lax.psum_scatter(merged, "dp", scatter_dimension=0, tiled=True)
    grad_attn = (
        merged[:, : 3 * cols]
        .astype(F32)
        .reshape(D // dp_count, pairs, 3, 2, DH)
        .transpose(0, 1, 3, 2, 4)
        .reshape(D // dp_count, 3 * cols)
    )
    grad_gate = merged[:, 3 * cols : 4 * cols].astype(F32)
    pairs_perm = []
    for s in range(seq_count):
        for piece in range(dp_count):
            part, target = divmod(piece, seq_count)
            pairs_perm.append((s * dp_count + piece, target * dp_count + s * share + part))
    grad_out = lax.ppermute(merged[:, 4 * cols :], ("seq", "dp"), pairs_perm).astype(F32)
    return (grad_attn, grad_gate, grad_out, new_table, new_accum)


def solution(mesh):
    placed = (
        P(("dp", "seq"), None),
        P(("dp", "seq"), None),
        P("dp", None),
        P(("dp", "seq"), None),
        P(("dp", "seq")),
        P(),
        P(),
        P(),
        P(("seq", "dp"), None),
        P(("seq", "dp")),
    )
    return jax.shard_map(
        body,
        mesh=mesh,
        in_specs=placed,
        out_specs=(
            P("dp", "seq"),
            P("dp", "seq"),
            P("dp", "seq"),
            P(("seq", "dp"), None),
            P(("seq", "dp")),
        ),
        check_vma=False,
    )
```

```python
import functools

import jax
import jax.numpy as jnp
from jax import lax
from jax.experimental import pallas as pl
from jax.experimental.pallas import tpu as pltpu
from jax.sharding import PartitionSpec as P

D = 1024
H = 16
DH = 64
PAIR = 2 * DH

NORM_EPS = 1e-05
LEARN_RATE = 0.1
VMEM_LIMIT = 56 * 1024 * 1024
BF = jnp.bfloat16
F32 = jnp.float32


def dot_nn(a, b):
    return lax.dot_general(a, b, (((1,), (0,)), ((), ())), preferred_element_type=F32)


def dot_nt(a, b):
    return lax.dot_general(a, b, (((1,), (1,)), ((), ())), preferred_element_type=F32)


def history_start(lengths_ref, users, place):
    start = jnp.zeros_like(place)
    end = jnp.int32(0)
    for user in range(users - 1):
        end = end + lengths_ref[0, user]
        start = jnp.where(place >= end, end, start)
    return start


def block_needed(lengths_ref, users, i, j, blk):
    return (j + 1) * blk > history_start(lengths_ref, users, i * blk)


def forward_kernel(*refs, blk, users, maxlen, count):
    lengths_ref, order_ref = refs[:2]
    x_refs = refs[2 : 2 + count]
    w_ref, x_out_ref, acts_ref, slopes_ref, gate_ref, weights_ref, score_slope_ref, heads_ref, q_half = refs[2 + count :]
    i = pl.program_id(1)
    block_rows = x_refs[0].shape[0]

    @pl.when((i == 0) & (pl.program_id(0) == 0))
    def _():
        for b in range(count):
            at = pl.ds(pl.multiple_of(order_ref[b] * block_rows, block_rows), block_rows)
            x_out_ref[at, :] = x_refs[b][...]

    @pl.when(i == 0)
    def _():
        for b in range(count):
            for r in range(block_rows // blk):
                at = pl.ds(pl.multiple_of(order_ref[b] * block_rows + r * blk, blk), blk)
                pre = dot_nn(x_refs[b][r * blk : (r + 1) * blk, :], w_ref[...])
                half = 0.5 * pre
                t = jnp.tanh(half)
                p = half * t
                silu = half + p
                acts = silu[:, : 3 * PAIR].astype(BF)
                acts_ref[at, :] = acts
                gate_ref[at, :] = silu[:, 3 * PAIR :]
                slopes_ref[at, :] = (0.5 * (1.0 + t) * (1.0 + half - p)).astype(BF)
                q_half[at, :] = acts[:, PAIR : 2 * PAIR] * jnp.asarray(0.5 * DH**-0.5, BF)

    at_i = pl.ds(pl.multiple_of(i * blk, blk), blk)
    q_i = q_half[at_i, :]
    row = i * blk + lax.broadcasted_iota(jnp.int32, (blk, blk), 0)
    col0 = lax.broadcasted_iota(jnp.int32, (blk, blk), 1)
    start = history_start(lengths_ref, users, row)

    def column(j, acc):
        at_j = pl.ds(pl.multiple_of(j * blk, blk), blk)
        col = col0 + j * blk
        allowed = (col <= row) & (col >= start)
        outs = []
        for h in range(2):
            lanes = slice(h * DH, (h + 1) * DH)
            k_j = acts_ref[at_j, 2 * PAIR + h * DH : 2 * PAIR + (h + 1) * DH]
            v_j = acts_ref[at_j, h * DH : (h + 1) * DH]
            half = dot_nt(q_i[:, lanes], k_j)
            half = jnp.where(allowed, half, -64.0)
            t = jnp.tanh(half)
            p = half * t
            weights = (half + p).astype(BF)
            weights_ref[h, :, at_j] = weights
            score_slope_ref[h, :, at_j] = ((1.0 + t) * (1.0 + half - p)).astype(BF)
            outs.append(acc[h] + dot_nn(weights, v_j))
        return tuple(outs)

    first = history_start(lengths_ref, users, i * blk) // blk
    zero = jnp.zeros((blk, DH), F32)
    acc = lax.fori_loop(first, i + 1, column, (zero, zero))
    heads_ref[...] = (jnp.concatenate(acc, axis=1) * (1.0 / maxlen)).astype(BF)


def forward_attention(lengths, order, x_blocks, w_own, blk, maxlen):
    count = len(x_blocks)
    block_rows = x_blocks[0].shape[0]
    positions = count * block_rows
    pairs = w_own.shape[1] // (4 * PAIR)
    users = lengths.shape[1]
    elements = pairs * positions * positions
    return pl.pallas_call(
        functools.partial(forward_kernel, blk=blk, users=users, maxlen=maxlen, count=count),
        grid=(pairs, positions // blk),
        in_specs=[pl.BlockSpec(memory_space=pltpu.SMEM), pl.BlockSpec(memory_space=pltpu.SMEM)]
        + [pl.BlockSpec((block_rows, D), lambda p, i: (0, 0))] * count
        + [pl.BlockSpec((D, 4 * PAIR), lambda p, i: (0, p))],
        out_specs=[
            pl.BlockSpec((positions, D), lambda p, i: (0, 0)),
            pl.BlockSpec((positions, 3 * PAIR), lambda p, i: (0, p)),
            pl.BlockSpec((positions, 4 * PAIR), lambda p, i: (0, p)),
            pl.BlockSpec((positions, PAIR), lambda p, i: (0, p)),
            pl.BlockSpec((2, blk, positions), lambda p, i: (p, i, 0)),
            pl.BlockSpec((2, blk, positions), lambda p, i: (p, i, 0)),
            pl.BlockSpec((blk, PAIR), lambda p, i: (i, p)),
        ],
        out_shape=[
            jax.ShapeDtypeStruct((positions, D), BF),
            jax.ShapeDtypeStruct((positions, pairs * 3 * PAIR), BF),
            jax.ShapeDtypeStruct((positions, pairs * 4 * PAIR), BF),
            jax.ShapeDtypeStruct((positions, pairs * PAIR), F32),
            jax.ShapeDtypeStruct((2 * pairs, positions, positions), BF),
            jax.ShapeDtypeStruct((2 * pairs, positions, positions), BF),
            jax.ShapeDtypeStruct((positions, pairs * PAIR), BF),
        ],
        scratch_shapes=[pltpu.VMEM((positions, PAIR), BF)],
        compiler_params=pltpu.CompilerParams(vmem_limit_bytes=VMEM_LIMIT),
        cost_estimate=pl.CostEstimate(
            flops=2 * positions * D * pairs * 4 * PAIR + 4 * elements * 256,
            bytes_accessed=4 * positions * D + 4 * elements,
            transcendentals=elements,
        ),
        name="attention_forward",
    )(lengths, order, *x_blocks, w_own)


def stats_kernel(*refs, count):
    order_ref = refs[0]
    mg_refs = refs[1 : 1 + count]
    gate_ref, heads_ref, mg_out_ref, stats_ref = refs[1 + count :]
    block_rows = mg_refs[0].shape[0]
    step = min(256, block_rows)
    for b in range(count):
        for r in range(block_rows // step):
            at = pl.ds(pl.multiple_of(order_ref[b] * block_rows + r * step, step), step)
            mg = mg_refs[b][r * step : (r + 1) * step, :]
            mg_out_ref[at, :] = mg
            ng = mg.astype(F32) * gate_ref[at, :]
            heads = heads_ref[at, :].astype(F32)
            mean = jnp.mean(heads, axis=1, keepdims=True)
            centred = heads - mean
            square = jnp.sum(centred * centred, axis=1, keepdims=True)
            total = jnp.sum(ng, axis=1, keepdims=True)
            cross = jnp.sum(ng * centred, axis=1, keepdims=True)
            lane = lax.broadcasted_iota(jnp.int32, (step, 128), 1)
            packed = jnp.where(lane == 0, mean, jnp.where(lane == 1, square, jnp.where(lane == 2, total, cross)))
            stats_ref[:, at] = jnp.transpose(packed)[:8, :]


def event_stats(order, mg_blocks, gate, heads):
    positions, cols = heads.shape
    count = len(mg_blocks)
    vmem = pl.BlockSpec(memory_space=pltpu.VMEM)
    return pl.pallas_call(
        functools.partial(stats_kernel, count=count),
        in_specs=[pl.BlockSpec(memory_space=pltpu.SMEM)] + [vmem] * (count + 2),
        out_specs=[vmem, vmem],
        out_shape=[
            jax.ShapeDtypeStruct((positions, cols), BF),
            jax.ShapeDtypeStruct((8, positions), F32),
        ],
        compiler_params=pltpu.CompilerParams(vmem_limit_bytes=VMEM_LIMIT),
        cost_estimate=pl.CostEstimate(flops=10 * positions * cols, bytes_accessed=10 * positions * cols, transcendentals=0),
        name="event_stats",
    )(order, *mg_blocks, gate, heads)


def backward_kernel(*refs, blk, users, maxlen, shards, cols):
    lengths_ref = refs[0]
    stats_refs = refs[1 : 1 + shards]
    heads_ref, gate_ref, mg_ref, acts_ref, slopes_ref, weights_ref, score_slope_ref = refs[1 + shards : 8 + shards]
    grad_ref, mixed_ref, o_ref, o_t, q_t, vg_t, kg_t, qg = refs[8 + shards :]
    i = pl.program_id(1)
    positions = heads_ref.shape[0]
    blocks = positions // blk
    scale = DH ** (-0.5)

    @pl.when(i == 0)
    def _():
        means = [ref[0:1, :] for ref in stats_refs]
        mean = sum(means) * (1.0 / shards)
        square = jnp.zeros_like(mean)
        total = jnp.zeros_like(mean)
        cross = jnp.zeros_like(mean)
        for s, ref in enumerate(stats_refs):
            shift = means[s] - mean
            part = ref[2:3, :]
            square = square + ref[1:2, :] + cols * shift * shift
            total = total + part
            cross = cross + ref[3:4, :] + shift * part
        inv_dev = lax.rsqrt(square * (1.0 / D) + NORM_EPS)
        row8 = lax.broadcasted_iota(jnp.int32, (128, positions), 0)
        packed = jnp.where(
            row8 == 0,
            mean,
            jnp.where(row8 == 1, inv_dev, jnp.where(row8 == 2, total * (1.0 / D), cross * inv_dev * (1.0 / D))),
        )
        per_event = jnp.transpose(packed)
        mean_c = per_event[:, 0:1]
        inv_c = per_event[:, 1:2]
        total_c = per_event[:, 2:3]
        cross_c = per_event[:, 3:4]
        normed = (heads_ref[...].astype(F32) - mean_c) * inv_c
        gate = gate_ref[...]
        mg = mg_ref[...].astype(F32)
        mixed_ref[...] = (normed * gate).astype(BF)
        grad_ref[:, 3 * PAIR :] = (mg * normed * slopes_ref[:, 3 * PAIR :].astype(F32)).astype(BF)
        o = (inv_c * (mg * gate - total_c - normed * cross_c)).astype(BF)
        o_ref[...] = o
        o_t[...] = jnp.transpose(o)
        q_t[...] = jnp.transpose(acts_ref[:, PAIR : 2 * PAIR])
        vg_t[...] = jnp.zeros_like(vg_t)
        kg_t[...] = jnp.zeros_like(kg_t)

    at_i = pl.ds(pl.multiple_of(i * blk, blk), blk)

    def column(j, acc):
        at_j = pl.ds(pl.multiple_of(j * blk, blk), blk)
        outs = []
        for h in range(2):
            lanes = slice(h * DH, (h + 1) * DH)
            k_j = acts_ref[at_j, 2 * PAIR + h * DH : 2 * PAIR + (h + 1) * DH]
            v_j = acts_ref[at_j, h * DH : (h + 1) * DH]
            weight_grad = dot_nt(o_ref[at_i, lanes], v_j)
            score_grad = (weight_grad * score_slope_ref[h, :, at_j].astype(F32)).astype(BF)
            vg_t[lanes, at_j] += dot_nn(o_t[lanes, at_i], weights_ref[h, :, at_j])
            kg_t[lanes, at_j] += dot_nn(q_t[lanes, at_i], score_grad)
            outs.append(acc[h] + dot_nn(score_grad, k_j))
        return tuple(outs)

    first = history_start(lengths_ref, users, i * blk) // blk
    zero = jnp.zeros((blk, DH), F32)
    acc = lax.fori_loop(first, i + 1, column, (zero, zero))
    qg[at_i, :] = jnp.concatenate(acc, axis=1)

    @pl.when(i == blocks - 1)
    def _():
        factor = 0.5 * scale / maxlen
        v_grad = (jnp.transpose(vg_t[...]) * (1.0 / maxlen)).astype(BF).astype(F32)
        q_grad = (qg[...] * factor).astype(BF).astype(F32)
        k_grad = (jnp.transpose(kg_t[...]) * factor).astype(BF).astype(F32)
        grad_ref[:, :PAIR] = (v_grad * slopes_ref[:, :PAIR].astype(F32)).astype(BF)
        grad_ref[:, PAIR : 2 * PAIR] = (q_grad * slopes_ref[:, PAIR : 2 * PAIR].astype(F32)).astype(BF)
        grad_ref[:, 2 * PAIR : 3 * PAIR] = (k_grad * slopes_ref[:, 2 * PAIR : 3 * PAIR].astype(F32)).astype(BF)


def backward_attention(lengths, stats, heads, gate, mg, acts, slopes, weights, score_slope, blk, maxlen):
    positions, cols = heads.shape
    pairs = cols // PAIR
    shards = len(stats)
    users = lengths.shape[1]
    elements = pairs * positions * positions
    whole = lambda p, i: (0, p)
    return pl.pallas_call(
        functools.partial(backward_kernel, blk=blk, users=users, maxlen=maxlen, shards=shards, cols=cols),
        grid=(pairs, positions // blk),
        in_specs=[pl.BlockSpec(memory_space=pltpu.SMEM)]
        + [pl.BlockSpec((8, positions), lambda p, i: (0, 0))] * shards
        + [
            pl.BlockSpec((positions, PAIR), whole),
            pl.BlockSpec((positions, PAIR), whole),
            pl.BlockSpec((positions, PAIR), whole),
            pl.BlockSpec((positions, 3 * PAIR), whole),
            pl.BlockSpec((positions, 4 * PAIR), whole),
            pl.BlockSpec((2, blk, positions), lambda p, i: (p, i, 0)),
            pl.BlockSpec((2, blk, positions), lambda p, i: (p, i, 0)),
        ],
        out_specs=[
            pl.BlockSpec((positions, 4 * PAIR), whole),
            pl.BlockSpec((positions, PAIR), whole),
        ],
        out_shape=[
            jax.ShapeDtypeStruct((positions, pairs * 4 * PAIR), BF),
            jax.ShapeDtypeStruct((positions, cols), BF),
        ],
        scratch_shapes=[
            pltpu.VMEM((positions, PAIR), BF),
            pltpu.VMEM((PAIR, positions), BF),
            pltpu.VMEM((PAIR, positions), BF),
            pltpu.VMEM((PAIR, positions), F32),
            pltpu.VMEM((PAIR, positions), F32),
            pltpu.VMEM((positions, PAIR), F32),
        ],
        compiler_params=pltpu.CompilerParams(vmem_limit_bytes=VMEM_LIMIT),
        cost_estimate=pl.CostEstimate(
            flops=8 * elements * 256, bytes_accessed=4 * elements + 16 * positions * cols, transcendentals=0
        ),
        name="attention_backward",
    )(lengths, *stats, heads, gate, mg, acts, slopes, weights, score_slope)


def update_kernel(ids_ref, rows_ref, table_ref, accum_ref, new_table_ref, new_accum_ref):
    i = pl.program_id(0)
    blk = table_ref.shape[0]
    slots = rows_ref.shape[0]
    row = i * blk + lax.broadcasted_iota(jnp.int32, (blk, slots), 0)
    hits = jnp.where(row == ids_ref[...], 1.0, 0.0).astype(BF)
    grad = dot_nn(hits, rows_ref[...])
    accum_rows = jnp.broadcast_to(accum_ref[...], (128, blk))
    accum = jnp.transpose(accum_rows)[:, :1] + jnp.mean(grad * grad, axis=1, keepdims=True)
    new_accum_ref[...] = jnp.transpose(jnp.broadcast_to(accum, (blk, 128)))[:1, :]
    new_table_ref[...] = table_ref[...] - LEARN_RATE * grad * lax.rsqrt(accum)


def update_rows(got_ids, got_rows, emb_table, row_accum):
    rows_own = emb_table.shape[0]
    slots = got_rows.shape[0]
    blk = min(128, rows_own)
    new_table, new_accum = pl.pallas_call(
        update_kernel,
        grid=(rows_own // blk,),
        in_specs=[
            pl.BlockSpec((1, slots), lambda i: (0, 0)),
            pl.BlockSpec((slots, D), lambda i: (0, 0)),
            pl.BlockSpec((blk, D), lambda i: (i, 0)),
            pl.BlockSpec((1, blk), lambda i: (0, i)),
        ],
        out_specs=[
            pl.BlockSpec((blk, D), lambda i: (i, 0)),
            pl.BlockSpec((1, blk), lambda i: (0, i)),
        ],
        out_shape=[
            jax.ShapeDtypeStruct((rows_own, D), F32),
            jax.ShapeDtypeStruct((1, rows_own), F32),
        ],
        compiler_params=pltpu.CompilerParams(vmem_limit_bytes=VMEM_LIMIT),
        cost_estimate=pl.CostEstimate(
            flops=2 * rows_own * slots * D, bytes_accessed=8 * rows_own * D + 2 * slots * D, transcendentals=rows_own
        ),
        name="update_rows",
    )(got_ids.reshape(1, slots), got_rows, emb_table, row_accum.reshape(1, rows_own))
    return new_table, new_accum.reshape(rows_own)


def own_weights(w_attn, w_gate, part, cols):
    pairs = cols // PAIR
    slices = jnp.concatenate(
        [
            lax.dynamic_slice_in_dim(w_attn, part * 3 * cols, 3 * cols, 1),
            lax.dynamic_slice_in_dim(w_gate, part * cols, cols, 1),
        ],
        axis=1,
    )
    place = jnp.arange(4 * cols, dtype=jnp.int32)
    pair, kind, head, entry = place // (4 * PAIR), place // PAIR % 4, place // DH % 2, place % DH
    source = jnp.where(
        kind < 3, pair * 3 * PAIR + head * 3 * DH + kind * DH + entry, 3 * cols + pair * PAIR + head * DH + entry
    )
    pick = (place[:, None] == source[None, :]).astype(BF)
    return jnp.dot(slices, pick, preferred_element_type=F32).astype(BF)


def split_columns(part, cols):
    rows = part.shape[0]
    pairs = cols // PAIR
    part = part.reshape(rows, pairs, 4, 2, DH)
    attn = part[:, :, :3].transpose(0, 1, 3, 2, 4).reshape(rows, 3 * cols)
    return attn, part[:, :, 3].reshape(rows, cols)


def row_slots(owners, rows, rows_own, devices, capacity):
    events = owners.shape[0]
    owner_hits = (owners[:, None] == jnp.arange(devices, dtype=jnp.int32)[None, :]).astype(F32)
    place = jnp.arange(events, dtype=jnp.int32)
    before = (place[:, None] > place[None, :]).astype(F32)
    slots = jnp.sum(jnp.dot(before, owner_hits) * owner_hits, axis=1).astype(jnp.int32)
    flat_slot = owners * capacity + slots
    slot_hits = jnp.arange(devices * capacity, dtype=jnp.int32)[:, None] == flat_slot[None, :]
    send_ids = jnp.min(jnp.where(slot_hits, rows[None, :], rows_own), axis=1).astype(jnp.int32)
    return slot_hits.astype(BF), send_ids


def to_owners(rows, devices, capacity):
    shape = (devices, capacity) + rows.shape[1:]
    got = lax.all_to_all(rows.reshape(shape), ("seq", "dp"), split_axis=0, concat_axis=0, tiled=True)
    return got.reshape(rows.shape)


TN = (((0,), (0,)), ((), ()))


def body_whole(
    layer_input, out_grad, lengths, item_owner, item_row, w_attn, w_gate, w_out, emb_table, row_accum
):
    seq_count = lax.axis_size("seq")
    dp_count = lax.axis_size("dp")
    devices = seq_count * dp_count
    seq_id = lax.axis_index("seq")
    tokens_dev = layer_input.shape[0]
    positions = tokens_dev * seq_count
    maxlen = 2 * positions // 3
    blk = min(256, positions)
    cols = D // seq_count
    rows_own = emb_table.shape[0]
    capacity = max(2, 2 * tokens_dev // devices)

    w_own = own_weights(w_attn, w_gate, seq_id, cols)
    w_out_own = lax.dynamic_slice_in_dim(w_out, seq_id * cols, cols, 0)
    slot_matrix, send_ids = row_slots(item_owner[:, 0], item_row, rows_own, devices, capacity)
    got_ids = to_owners(send_ids, devices, capacity)

    x_full = lax.all_gather(layer_input, "seq", axis=0, tiled=True)
    og_full = lax.all_gather(out_grad, "seq", axis=0, tiled=True)
    order = jnp.zeros((1,), jnp.int32)
    x_full, acts, slopes, gate, weights, score_slope, heads = forward_attention(
        lengths, order, [x_full], w_own, blk, maxlen
    )
    mg = dot_nt(og_full, w_out_own).astype(BF)
    mg, stats_own = event_stats(order, [mg], gate, heads)
    stats = lax.all_gather(stats_own, "seq", axis=0, tiled=False)
    grads, mixed = backward_attention(
        lengths, [stats[s] for s in range(seq_count)], heads, gate, mg, acts, slopes, weights, score_slope, blk, maxlen
    )

    input_part = dot_nt(grads, w_own).astype(BF)
    got = lax.all_to_all(
        input_part.reshape(seq_count, tokens_dev, D), "seq", split_axis=0, concat_axis=0, tiled=True
    )
    input_grad = jnp.sum(got.astype(F32), axis=0) + out_grad.astype(F32)
    send_rows = jnp.dot(slot_matrix, input_grad.astype(BF), preferred_element_type=F32).astype(BF)
    got_rows = to_owners(send_rows, devices, capacity)
    new_table, new_accum = update_rows(got_ids, got_rows, emb_table, row_accum)

    proj_part = lax.dot_general(x_full, grads, TN, preferred_element_type=F32).astype(BF)
    out_part = lax.dot_general(mixed, og_full, TN, preferred_element_type=F32).astype(BF)
    share = dp_count // seq_count
    out_part = out_part.reshape(share, D // dp_count, seq_count, cols).transpose(0, 2, 1, 3).reshape(D, cols)
    merged = jnp.concatenate([proj_part, out_part], axis=1)
    merged = lax.psum_scatter(merged, "dp", scatter_dimension=0, tiled=True)
    grad_attn, grad_gate = split_columns(merged[:, : 4 * cols].astype(F32), cols)
    steps = []
    for s in range(seq_count):
        for piece in range(dp_count):
            part, target = divmod(piece, seq_count)
            steps.append((s * dp_count + piece, target * dp_count + s * share + part))
    grad_out = lax.ppermute(merged[:, 4 * cols :], ("seq", "dp"), steps).astype(F32)
    return (grad_attn, grad_gate, grad_out, new_table, new_accum)


SEQ = 4
PLANE = 4


def send(array, target):
    steps = []
    for s in range(SEQ):
        for e in range(PLANE):
            for c in range(2):
                to = target(s, e, c)
                if to is not None:
                    steps.append((s * 2 * PLANE + 2 * e + c, to[0] * 2 * PLANE + 2 * to[1] + to[2]))
    return lax.ppermute(array, ("seq", "dp"), steps)


def home(s, c):
    return c == s // 2


def swap_far(array):
    return send(array, lambda s, e, c: None if home(s, c) else (3 - s, e, 1 - c))


def swap_near_home(array):
    return send(array, lambda s, e, c: (s ^ 1, e, c) if home(s, c) else None)


def swap_near_far(array):
    return send(array, lambda s, e, c: None if home(s, c) else (s ^ 1, e, c))


def swap_near(array):
    return send(array, lambda s, e, c: (s ^ 1, e, c))


def swap_core(array):
    return send(array, lambda s, e, c: (s, e, 1 - c))


def swap_x(array):
    return send(array, lambda s, e, c: (s, e ^ 1, c))


def swap_y(array):
    return send(array, lambda s, e, c: (s, e ^ 2, c))


def after(array, *others):
    return lax.optimization_barrier((array,) + others)[0]


def body_pairs(
    layer_input, out_grad, lengths, item_owner, item_row, w_attn, w_gate, w_out, emb_table, row_accum
):
    devices = 2 * PLANE * SEQ
    s = lax.axis_index("seq")
    d = lax.axis_index("dp")
    e, c = d // 2, d % 2
    tokens_dev = layer_input.shape[0]
    positions = tokens_dev * SEQ
    maxlen = 2 * positions // 3
    blk = min(256, positions)
    cols = D // SEQ
    rows_own = emb_table.shape[0]
    capacity = max(2, 2 * tokens_dev // devices)
    at_home = c == s // 2
    part = 2 * (s % 2) + c

    def block_of(seq, core):
        return jnp.where(core == seq // 2, seq, 3 - seq)

    mine_at, near_at = block_of(s, c), block_of(s ^ 1, c)
    core_at, diag_at = block_of(s, 1 - c), block_of(s ^ 1, 1 - c)
    order = jnp.stack([mine_at, near_at, core_at, diag_at]).astype(jnp.int32)

    x_far = swap_far(layer_input)
    x_near_home = swap_near_home(layer_input)
    x_mine = jnp.where(at_home, layer_input, x_far)
    x_near_far = swap_near_far(x_mine)
    x_core = swap_core(x_mine)
    x_near = jnp.where(at_home, x_near_home, x_near_far)
    x_diag = swap_core(x_near)

    users = lengths.shape[1]
    other_lengths = swap_core(lengths)
    lengths = jnp.where(at_home, lengths, other_lengths)
    keys = (item_owner[:, 0] * rows_own + item_row).reshape(1, tokens_dev)
    keys = jnp.where(at_home, keys, swap_far(keys)).reshape(tokens_dev)
    slot_matrix, send_ids = row_slots(keys // rows_own, keys % rows_own, rows_own, devices, capacity)
    got_ids = to_owners(send_ids, devices, capacity)
    w_own = own_weights(w_attn, w_gate, part, cols)
    mg_own = dot_nt(out_grad, w_out).astype(BF)
    mg_own = after(mg_own, x_near, got_ids)
    mg_blocks = []
    mg_order = []
    for k in range(SEQ):
        piece = lax.dynamic_slice_in_dim(mg_own, (s + k) % SEQ * cols, cols, 1)
        mg_blocks.append(send(piece, lambda s, e, c: (2 * c + (s + k) % SEQ // 2, e, (s + k) % SEQ % 2)))
        mg_order.append((part - k) % SEQ)
    mg_order = jnp.stack(mg_order).astype(jnp.int32)

    x_full, acts, slopes, gate, weights, score_slope, heads = forward_attention(
        lengths, order, [x_mine, x_near, x_core, x_diag], w_own, blk, maxlen
    )

    og_own = after(out_grad, heads)
    og_far = swap_far(og_own)
    og_near_home = swap_near_home(og_own)

    mg, stats_own = event_stats(mg_order, mg_blocks, gate, heads)
    stats = [
        stats_own,
        swap_core(stats_own),
        swap_near(stats_own),
        send(stats_own, lambda s, e, c: (s ^ 1, e, 1 - c)),
    ]
    og_mine = jnp.where(at_home, out_grad, og_far)
    og_near_far = swap_near_far(og_mine)
    og_core = swap_core(og_mine)

    grads, mixed = backward_attention(
        lengths, stats, heads, gate, mg, acts, slopes, weights, score_slope, blk, maxlen
    )
    og_near = jnp.where(at_home, og_near_home, og_near_far)
    og_diag = swap_core(og_near)

    def input_part(block):
        rows = lax.dynamic_slice_in_dim(grads, block * tokens_dev, tokens_dev, 0)
        return dot_nt(rows, w_own)

    from_diag = swap_core(input_part(diag_at).astype(BF))
    near_sum = input_part(near_at) + from_diag.astype(F32)
    from_near = swap_near(near_sum.astype(BF))
    from_core = swap_core(input_part(core_at).astype(BF))
    input_grad = input_part(mine_at) + from_core.astype(F32) + og_mine.astype(F32)
    input_grad = input_grad + from_near.astype(F32)
    send_rows = jnp.dot(slot_matrix, input_grad.astype(BF), preferred_element_type=F32).astype(BF)
    got_rows = to_owners(send_rows, devices, capacity)
    new_table, new_accum = update_rows(got_ids, got_rows, emb_table, row_accum)

    proj_part = lax.dot_general(x_full, grads, TN, preferred_element_type=F32).astype(BF)
    out_part = jnp.zeros((cols, D), F32)
    for at, og_block in ((mine_at, og_mine), (near_at, og_near), (core_at, og_core), (diag_at, og_diag)):
        rows = lax.dynamic_slice_in_dim(mixed, at * tokens_dev, tokens_dev, 0)
        out_part = out_part + lax.dot_general(rows, og_block, TN, preferred_element_type=F32)
    out_part = out_part.astype(BF).reshape(cols, SEQ, cols).transpose(1, 0, 2).reshape(D, cols)
    chip_rows = D // PLANE
    merged = jnp.concatenate([proj_part, out_part], axis=1).reshape(2, 2, chip_rows, 5 * cols)
    half = 5 * cols // 2
    y, x = e // 2, e % 2

    def halves(array, bit, axis):
        kept = lax.dynamic_index_in_dim(array, bit, axis, keepdims=False)
        sent = lax.dynamic_index_in_dim(array, 1 - bit, axis, keepdims=False)
        return kept, sent

    a_kept, a_sent = halves(merged[..., :half], x, 1)
    b_kept, b_sent = halves(merged[..., half:], y, 0)
    a = (a_kept.astype(F32) + swap_x(a_sent).astype(F32)).astype(BF)
    b = (b_kept.astype(F32) + swap_y(b_sent).astype(F32)).astype(BF)
    a_kept, a_sent = halves(a, y, 0)
    b_kept, b_sent = halves(b, x, 0)
    a = a_kept.astype(F32) + swap_y(a_sent).astype(F32)
    b = b_kept.astype(F32) + swap_x(b_sent).astype(F32)
    plane_sum = jnp.concatenate([a, b], axis=1).astype(BF).reshape(2, chip_rows // 2, 5 * cols)

    first, second = halves(plane_sum, s // 2, 0)
    proj = send(first[:, : 4 * cols], lambda s, e, c: (2 * (s % 2) + c, e, s // 2)).astype(F32)
    proj = proj + send(second[:, : 4 * cols], lambda s, e, c: (2 * (s % 2) + c, e, 1 - s // 2)).astype(F32)
    out = send(first[:, 4 * cols :], lambda s, e, c: (e, 2 * (s % 2) + c, s // 2)).astype(F32)
    out = out + send(second[:, 4 * cols :], lambda s, e, c: (e, 2 * (s % 2) + c, 1 - s // 2)).astype(F32)
    grad_attn, grad_gate = split_columns(proj, cols)
    return (grad_attn, grad_gate, out, new_table, new_accum)


def solution(mesh):
    placed = (
        P(("dp", "seq"), None),
        P(("dp", "seq"), None),
        P("dp", None),
        P(("dp", "seq"), None),
        P(("dp", "seq")),
        P(),
        P(),
        P(),
        P(("seq", "dp"), None),
        P(("seq", "dp")),
    )
    paired = mesh.shape["seq"] == SEQ and mesh.shape["dp"] == 2 * PLANE
    return jax.shard_map(
        body_pairs if paired else body_whole,
        mesh=mesh,
        in_specs=placed,
        out_specs=(
            P("dp", "seq"),
            P("dp", "seq"),
            P("dp", "seq"),
            P(("seq", "dp"), None),
            P(("seq", "dp")),
        ),
        check_vma=False,
    )
```

```python
import functools

import jax
import jax.numpy as jnp
from jax import lax
from jax.experimental import pallas as pl
from jax.experimental.pallas import tpu as pltpu
from jax.sharding import PartitionSpec as P

D = 1024
H = 16
DH = 64
PAIR = 2 * DH

NORM_EPS = 1e-05
LEARN_RATE = 0.1
VMEM_LIMIT = 56 * 1024 * 1024
BF = jnp.bfloat16
F32 = jnp.float32


def dot_nn(a, b):
    return lax.dot_general(a, b, (((1,), (0,)), ((), ())), preferred_element_type=F32)


def dot_nt(a, b):
    return lax.dot_general(a, b, (((1,), (1,)), ((), ())), preferred_element_type=F32)


def history_start(lengths_ref, users, place):
    start = jnp.zeros_like(place)
    end = jnp.int32(0)
    for user in range(users - 1):
        end = end + lengths_ref[0, user]
        start = jnp.where(place >= end, end, start)
    return start


def head_columns(kind, head):
    first = head * 3 * DH + kind * DH
    return slice(first, first + DH)


def forward_kernel(*refs, blk, users, maxlen, count):
    lengths_ref, order_ref = refs[:2]
    x_refs = refs[2 : 2 + count]
    w_ref = refs[2 + count]
    outs = refs[3 + count :]
    if count > 1:
        x_out_ref, outs = outs[0], outs[1:]
    acts_ref, slopes_ref, gate_ref, weights_ref, score_slope_ref, heads_ref = outs
    i = pl.program_id(0)
    block_rows = x_refs[0].shape[0]

    @pl.when(i == 0)
    def _():
        for b in range(count):
            for r in range(block_rows // blk):
                at = pl.ds(pl.multiple_of(order_ref[b] * block_rows + r * blk, blk), blk)
                x = x_refs[b][r * blk : (r + 1) * blk, :]
                if count > 1:
                    x_out_ref[at, :] = x
                half = 0.5 * dot_nn(x, w_ref[...])
                t = jnp.tanh(half)
                p = half * t
                silu = half + p
                acts_ref[at, :] = silu[:, : 3 * PAIR].astype(BF)
                gate_ref[at, :] = silu[:, 3 * PAIR :]
                slopes_ref[at, :] = (0.5 * (1.0 + t) * (1.0 + half - p)).astype(BF)

    at_i = pl.ds(pl.multiple_of(i * blk, blk), blk)
    q_half = [acts_ref[at_i, head_columns(1, h)] * jnp.asarray(0.5 * DH**-0.5, BF) for h in range(2)]
    row = i * blk + lax.broadcasted_iota(jnp.int32, (blk, blk), 0)
    col0 = lax.broadcasted_iota(jnp.int32, (blk, blk), 1)
    start = history_start(lengths_ref, users, row)

    def column(j, acc):
        at_j = pl.ds(pl.multiple_of(j * blk, blk), blk)
        col = col0 + j * blk
        allowed = (col <= row) & (col >= start)
        outs = []
        for h in range(2):
            half = dot_nt(q_half[h], acts_ref[at_j, head_columns(2, h)])
            half = jnp.where(allowed, half, -64.0)
            t = jnp.tanh(half)
            p = half * t
            weights = (half + p).astype(BF)
            weights_ref[h, :, at_j] = weights
            score_slope_ref[h, :, at_j] = ((1.0 + t) * (1.0 + half - p)).astype(BF)
            outs.append(acc[h] + dot_nn(weights, acts_ref[at_j, head_columns(0, h)]))
        return tuple(outs)

    first = history_start(lengths_ref, users, i * blk) // blk
    zero = jnp.zeros((blk, DH), F32)
    acc = lax.fori_loop(first, i + 1, column, (zero, zero))
    heads_ref[...] = (jnp.concatenate(acc, axis=1) * (1.0 / maxlen)).astype(BF)


def forward_pair(lengths, order, x_blocks, w_pair, blk, maxlen):
    count = len(x_blocks)
    block_rows = x_blocks[0].shape[0]
    positions = count * block_rows
    users = lengths.shape[1]
    elements = positions * positions
    whole = lambda i: (0, 0)
    out_specs = [
        pl.BlockSpec((positions, 3 * PAIR), whole),
        pl.BlockSpec((positions, 4 * PAIR), whole),
        pl.BlockSpec((positions, PAIR), whole),
        pl.BlockSpec((2, blk, positions), lambda i: (0, i, 0)),
        pl.BlockSpec((2, blk, positions), lambda i: (0, i, 0)),
        pl.BlockSpec((blk, PAIR), lambda i: (i, 0)),
    ]
    out_shape = [
        jax.ShapeDtypeStruct((positions, 3 * PAIR), BF),
        jax.ShapeDtypeStruct((positions, 4 * PAIR), BF),
        jax.ShapeDtypeStruct((positions, PAIR), F32),
        jax.ShapeDtypeStruct((2, positions, positions), BF),
        jax.ShapeDtypeStruct((2, positions, positions), BF),
        jax.ShapeDtypeStruct((positions, PAIR), BF),
    ]
    if count > 1:
        out_specs = [pl.BlockSpec((positions, D), whole)] + out_specs
        out_shape = [jax.ShapeDtypeStruct((positions, D), BF)] + out_shape
    return pl.pallas_call(
        functools.partial(forward_kernel, blk=blk, users=users, maxlen=maxlen, count=count),
        grid=(positions // blk,),
        in_specs=[pl.BlockSpec(memory_space=pltpu.SMEM), pl.BlockSpec(memory_space=pltpu.SMEM)]
        + [pl.BlockSpec((block_rows, D), whole)] * count
        + [pl.BlockSpec((D, 4 * PAIR), whole)],
        out_specs=out_specs,
        out_shape=out_shape,
        compiler_params=pltpu.CompilerParams(vmem_limit_bytes=VMEM_LIMIT),
        cost_estimate=pl.CostEstimate(
            flops=2 * positions * D * 4 * PAIR + 4 * elements * 256,
            bytes_accessed=4 * positions * D + 4 * elements,
            transcendentals=elements,
        ),
        name="attention_forward",
    )(lengths, order, *x_blocks, w_pair)


def stats_kernel(*refs, count, pairs):
    order_ref = refs[0]
    og_refs = refs[1 : 1 + count]
    w_ref = refs[1 + count]
    gate_refs = refs[2 + count : 2 + count + pairs]
    heads_refs = refs[2 + count + pairs : 2 + count + 2 * pairs]
    outs = refs[2 + count + 2 * pairs :]
    if count > 1:
        og_out_ref, outs = outs[0], outs[1:]
    mg_ref, stats_ref = outs
    block_rows = og_refs[0].shape[0]
    step = min(256, block_rows)
    cols = pairs * PAIR
    for b in range(count):
        for r in range(block_rows // step):
            at = pl.ds(pl.multiple_of(order_ref[b] * block_rows + r * step, step), step)
            og = og_refs[b][r * step : (r + 1) * step, :]
            if count > 1:
                og_out_ref[at, :] = og
            mg = dot_nt(og, w_ref[...])
            mg_ref[at, :] = mg
            ng = [mg[:, p * PAIR : (p + 1) * PAIR] * gate_refs[p][at, :] for p in range(pairs)]
            heads = [heads_refs[p][at, :].astype(F32) for p in range(pairs)]
            mean = jnp.sum(sum(heads), axis=1, keepdims=True) * (1.0 / cols)
            centred = [h - mean for h in heads]
            square = jnp.sum(sum(h * h for h in centred), axis=1, keepdims=True)
            total = jnp.sum(sum(ng), axis=1, keepdims=True)
            cross = jnp.sum(sum(n * h for n, h in zip(ng, centred)), axis=1, keepdims=True)
            lane = lax.broadcasted_iota(jnp.int32, (step, 128), 1)
            packed = jnp.where(lane == 0, mean, jnp.where(lane == 1, square, jnp.where(lane == 2, total, cross)))
            stats_ref[:, at] = jnp.transpose(packed)[:8, :]


def event_stats(order, og_blocks, w_out_own, gates, heads):
    positions = heads[0].shape[0]
    pairs = len(heads)
    cols = pairs * PAIR
    count = len(og_blocks)
    vmem = pl.BlockSpec(memory_space=pltpu.VMEM)
    out_shape = [
        jax.ShapeDtypeStruct((positions, cols), F32),
        jax.ShapeDtypeStruct((8, positions), F32),
    ]
    if count > 1:
        out_shape = [jax.ShapeDtypeStruct((positions, D), BF)] + out_shape
    return pl.pallas_call(
        functools.partial(stats_kernel, count=count, pairs=pairs),
        in_specs=[pl.BlockSpec(memory_space=pltpu.SMEM)] + [vmem] * (count + 1 + 2 * pairs),
        out_specs=[vmem] * len(out_shape),
        out_shape=out_shape,
        compiler_params=pltpu.CompilerParams(vmem_limit_bytes=VMEM_LIMIT),
        cost_estimate=pl.CostEstimate(
            flops=2 * positions * cols * D, bytes_accessed=4 * positions * D + 10 * positions * cols, transcendentals=0
        ),
        name="event_stats",
    )(order, *og_blocks, w_out_own, *gates, *heads)


def norm_kernel(*refs, shards, pairs):
    stats_refs = refs[:shards]
    mg_ref = refs[shards]
    heads_refs = refs[shards + 1 : shards + 1 + pairs]
    gate_refs = refs[shards + 1 + pairs : shards + 1 + 2 * pairs]
    slope_refs = refs[shards + 1 + 2 * pairs : shards + 1 + 3 * pairs]
    o_ref, gate_grad_ref, mixed_ref = refs[shards + 1 + 3 * pairs :]
    positions = mg_ref.shape[0]
    cols = pairs * PAIR
    means = [ref[0:1, :] for ref in stats_refs]
    mean = sum(means) * (1.0 / shards)
    square = jnp.zeros_like(mean)
    total = jnp.zeros_like(mean)
    cross = jnp.zeros_like(mean)
    for s, ref in enumerate(stats_refs):
        shift = means[s] - mean
        part = ref[2:3, :]
        square = square + ref[1:2, :] + cols * shift * shift
        total = total + part
        cross = cross + ref[3:4, :] + shift * part
    inv_dev = lax.rsqrt(square * (1.0 / D) + NORM_EPS)
    row8 = lax.broadcasted_iota(jnp.int32, (128, positions), 0)
    packed = jnp.where(
        row8 == 0,
        mean,
        jnp.where(row8 == 1, inv_dev, jnp.where(row8 == 2, total * (1.0 / D), cross * inv_dev * (1.0 / D))),
    )
    per_event = jnp.transpose(packed)
    mean_c = per_event[:, 0:1]
    inv_c = per_event[:, 1:2]
    total_c = per_event[:, 2:3]
    cross_c = per_event[:, 3:4]
    for p in range(pairs):
        lanes = slice(p * PAIR, (p + 1) * PAIR)
        normed = (heads_refs[p][...].astype(F32) - mean_c) * inv_c
        gate = gate_refs[p][...]
        mg = mg_ref[:, lanes]
        mixed_ref[:, lanes] = (normed * gate).astype(BF)
        gate_grad_ref[:, lanes] = (mg * normed * slope_refs[p][...].astype(F32)).astype(BF)
        o_ref[:, lanes] = (inv_c * (mg * gate - total_c - normed * cross_c)).astype(BF)


def norm_backward(stats, mg, heads, gates, slopes):
    positions, cols = mg.shape
    pairs = len(heads)
    shards = len(stats)
    vmem = pl.BlockSpec(memory_space=pltpu.VMEM)
    gate_slopes = pl.BlockSpec((positions, PAIR), lambda i: (0, 3))
    whole = lambda shape: pl.BlockSpec(shape, lambda i: (0, 0))
    out = jax.ShapeDtypeStruct((positions, cols), BF)
    return pl.pallas_call(
        functools.partial(norm_kernel, shards=shards, pairs=pairs),
        grid=(1,),
        in_specs=[whole((8, positions))] * shards
        + [whole((positions, cols))]
        + [whole((positions, PAIR))] * (2 * pairs)
        + [gate_slopes] * pairs,
        out_specs=[whole((positions, cols))] * 3,
        out_shape=[out, out, out],
        compiler_params=pltpu.CompilerParams(vmem_limit_bytes=VMEM_LIMIT),
        cost_estimate=pl.CostEstimate(flops=20 * positions * cols, bytes_accessed=18 * positions * cols, transcendentals=0),
        name="norm_backward",
    )(*stats, mg, *heads, *gates, *slopes)


def backward_kernel(
    lengths_ref, o_ref, acts_ref, slopes_ref, weights_ref, score_slope_ref, grad_ref, o_t, q_t, vg_t, kg_t, qg,
    *, blk, users, maxlen
):
    i = pl.program_id(0)
    blocks = o_ref.shape[0] // blk
    scale = DH ** (-0.5)

    @pl.when(i == 0)
    def _():
        o_t[...] = jnp.transpose(o_ref[...])
        queries = [acts_ref[:, head_columns(1, h)] for h in range(2)]
        q_t[...] = jnp.transpose(jnp.concatenate(queries, axis=1))
        vg_t[...] = jnp.zeros_like(vg_t)
        kg_t[...] = jnp.zeros_like(kg_t)

    at_i = pl.ds(pl.multiple_of(i * blk, blk), blk)

    def column(j, acc):
        at_j = pl.ds(pl.multiple_of(j * blk, blk), blk)
        outs = []
        for h in range(2):
            lanes = slice(h * DH, (h + 1) * DH)
            weight_grad = dot_nt(o_ref[at_i, lanes], acts_ref[at_j, head_columns(0, h)])
            score_grad = (weight_grad * score_slope_ref[h, :, at_j].astype(F32)).astype(BF)
            vg_t[lanes, at_j] += dot_nn(o_t[lanes, at_i], weights_ref[h, :, at_j])
            kg_t[lanes, at_j] += dot_nn(q_t[lanes, at_i], score_grad)
            outs.append(acc[h] + dot_nn(score_grad, acts_ref[at_j, head_columns(2, h)]))
        return tuple(outs)

    first = history_start(lengths_ref, users, i * blk) // blk
    zero = jnp.zeros((blk, DH), F32)
    acc = lax.fori_loop(first, i + 1, column, (zero, zero))
    qg[at_i, :] = jnp.concatenate(acc, axis=1)

    @pl.when(i == blocks - 1)
    def _():
        factor = 0.5 * scale / maxlen
        grads = [jnp.transpose(vg_t[...]) * (1.0 / maxlen), qg[...] * factor, jnp.transpose(kg_t[...]) * factor]
        pieces = [grads[kind][:, h * DH : (h + 1) * DH] for h in range(2) for kind in range(3)]
        for n in range(3):
            lanes = slice(n * PAIR, (n + 1) * PAIR)
            grad = jnp.concatenate(pieces[2 * n : 2 * n + 2], axis=1).astype(BF).astype(F32)
            grad_ref[:, lanes] = (grad * slopes_ref[:, lanes].astype(F32)).astype(BF)


def backward_pair(lengths, pair, o, acts, slopes, weights, score_slope, blk, maxlen):
    positions = o.shape[0]
    users = lengths.shape[1]
    elements = positions * positions
    whole = lambda i: (0, 0)
    return pl.pallas_call(
        functools.partial(backward_kernel, blk=blk, users=users, maxlen=maxlen),
        grid=(positions // blk,),
        in_specs=[
            pl.BlockSpec(memory_space=pltpu.SMEM),
            pl.BlockSpec((positions, PAIR), lambda i: (0, pair)),
            pl.BlockSpec((positions, 3 * PAIR), whole),
            pl.BlockSpec((positions, 3 * PAIR), whole),
            pl.BlockSpec((2, blk, positions), lambda i: (0, i, 0)),
            pl.BlockSpec((2, blk, positions), lambda i: (0, i, 0)),
        ],
        out_specs=pl.BlockSpec((positions, 3 * PAIR), whole),
        out_shape=jax.ShapeDtypeStruct((positions, 3 * PAIR), BF),
        scratch_shapes=[
            pltpu.VMEM((PAIR, positions), BF),
            pltpu.VMEM((PAIR, positions), BF),
            pltpu.VMEM((PAIR, positions), F32),
            pltpu.VMEM((PAIR, positions), F32),
            pltpu.VMEM((positions, PAIR), F32),
        ],
        compiler_params=pltpu.CompilerParams(vmem_limit_bytes=VMEM_LIMIT),
        cost_estimate=pl.CostEstimate(
            flops=8 * elements * 256, bytes_accessed=4 * elements + 16 * positions * PAIR, transcendentals=0
        ),
        name="attention_backward",
    )(lengths, o, acts, slopes, weights, score_slope)


def update_kernel(rows_ref, table_ref, accum_ref, new_table_ref, new_accum_ref, ids):
    i = pl.program_id(0)
    blk = table_ref.shape[0]
    slots = rows_ref.shape[0]

    @pl.when(i == 0)
    def _():
        numbers = jnp.transpose(rows_ref[:, D:].astype(F32))
        ids[...] = (numbers[0:1, :] * 256.0 + numbers[1:2, :]).astype(jnp.int32)

    row = i * blk + lax.broadcasted_iota(jnp.int32, (blk, slots), 0)
    hits = jnp.where(row == ids[...], 1.0, 0.0).astype(BF)
    grad = dot_nn(hits, rows_ref[:, :D])
    accum_rows = jnp.broadcast_to(accum_ref[...], (128, blk))
    accum = jnp.transpose(accum_rows)[:, :1] + jnp.mean(grad * grad, axis=1, keepdims=True)
    new_accum_ref[...] = jnp.transpose(jnp.broadcast_to(accum, (blk, 128)))[:1, :]
    new_table_ref[...] = table_ref[...] - LEARN_RATE * grad * lax.rsqrt(accum)


def update_rows(got_rows, emb_table, row_accum):
    rows_own = emb_table.shape[0]
    slots = got_rows.shape[0]
    blk = min(128, rows_own)
    new_table, new_accum = pl.pallas_call(
        update_kernel,
        grid=(rows_own // blk,),
        in_specs=[
            pl.BlockSpec((slots, D + 128), lambda i: (0, 0)),
            pl.BlockSpec((blk, D), lambda i: (i, 0)),
            pl.BlockSpec((1, blk), lambda i: (0, i)),
        ],
        out_specs=[
            pl.BlockSpec((blk, D), lambda i: (i, 0)),
            pl.BlockSpec((1, blk), lambda i: (0, i)),
        ],
        out_shape=[
            jax.ShapeDtypeStruct((rows_own, D), F32),
            jax.ShapeDtypeStruct((1, rows_own), F32),
        ],
        scratch_shapes=[pltpu.VMEM((1, slots), jnp.int32)],
        compiler_params=pltpu.CompilerParams(vmem_limit_bytes=VMEM_LIMIT),
        cost_estimate=pl.CostEstimate(
            flops=2 * rows_own * slots * D, bytes_accessed=8 * rows_own * D + 2 * slots * D, transcendentals=rows_own
        ),
        name="update_rows",
    )(got_rows, emb_table, row_accum.reshape(1, rows_own))
    return new_table, new_accum.reshape(rows_own)


def pair_weights(w_attn, w_gate, part, pairs):
    out = []
    for p in range(pairs):
        at = part * pairs + p
        attn = lax.dynamic_slice_in_dim(w_attn, at * 3 * PAIR, 3 * PAIR, 1)
        gate = lax.dynamic_slice_in_dim(w_gate, at * PAIR, PAIR, 1)
        out.append(jnp.concatenate([attn, gate], axis=1))
    return out


def row_slots(owners, rows, devices, capacity):
    events = owners.shape[0]
    owner_hits = (owners[:, None] == jnp.arange(devices, dtype=jnp.int32)[None, :]).astype(BF)
    place = jnp.arange(events, dtype=jnp.int32)
    before = (place[:, None] > place[None, :]).astype(BF)
    earlier = jnp.dot(before, owner_hits, preferred_element_type=F32)
    slots = jnp.sum(earlier * owner_hits.astype(F32), axis=1).astype(jnp.int32)
    flat_slot = owners * capacity + slots
    slot_hits = jnp.arange(devices * capacity, dtype=jnp.int32)[:, None] == flat_slot[None, :]
    lane = jnp.arange(128, dtype=jnp.int32)[None, :]
    numbers = jnp.where(lane == 0, rows[:, None] // 256, jnp.where(lane == 1, rows[:, None] % 256, 0))
    return slot_hits.astype(BF), numbers.astype(BF)


def rows_to_owners(slot_matrix, input_grad, numbers, devices, capacity):
    rows = jnp.concatenate([input_grad.astype(BF), numbers], axis=1)
    rows = jnp.dot(slot_matrix, rows, preferred_element_type=F32).astype(BF)
    got = lax.all_to_all(
        rows.reshape(devices, capacity, D + 128), ("seq", "dp"), split_axis=0, concat_axis=0, tiled=True
    )
    return got.reshape(devices * capacity, D + 128)


TN = (((0,), (0,)), ((), ()))


def dot_tn(a, b):
    return lax.dot_general(a, b, TN, preferred_element_type=F32)


def body_whole(
    layer_input, out_grad, lengths, item_owner, item_row, w_attn, w_gate, w_out, emb_table, row_accum
):
    seq_count = lax.axis_size("seq")
    dp_count = lax.axis_size("dp")
    devices = seq_count * dp_count
    seq_id = lax.axis_index("seq")
    tokens_dev = layer_input.shape[0]
    positions = tokens_dev * seq_count
    maxlen = 2 * positions // 3
    blk = min(256, positions)
    cols = D // seq_count
    pairs = cols // PAIR
    capacity = max(2, 2 * tokens_dev // devices)

    w_pairs = pair_weights(w_attn, w_gate, seq_id, pairs)
    w_out_own = lax.dynamic_slice_in_dim(w_out, seq_id * cols, cols, 0)
    slot_matrix, numbers = row_slots(item_owner[:, 0], item_row, devices, capacity)

    x_full = lax.all_gather(layer_input, "seq", axis=0, tiled=True)
    og_full = lax.all_gather(out_grad, "seq", axis=0, tiled=True)
    order = jnp.zeros((1,), jnp.int32)
    forward = [forward_pair(lengths, order, [x_full], w, blk, maxlen) for w in w_pairs]
    acts, slopes, gates, weights, score_slopes, heads = zip(*forward)
    mg, stats_own = event_stats(order, [og_full], w_out_own, gates, heads)
    stats = lax.all_gather(stats_own, "seq", axis=0, tiled=False)
    o, gate_grad, mixed = norm_backward([stats[s] for s in range(seq_count)], mg, heads, gates, slopes)
    grads = [
        backward_pair(lengths, p, o, acts[p], slopes[p], weights[p], score_slopes[p], blk, maxlen)
        for p in range(pairs)
    ]

    input_part = sum(dot_nt(grads[p], w_pairs[p][:, : 3 * PAIR]) for p in range(pairs))
    w_gate_own = lax.dynamic_slice_in_dim(w_gate, seq_id * cols, cols, 1)
    input_part = (input_part + dot_nt(gate_grad, w_gate_own)).astype(BF)
    got = lax.all_to_all(
        input_part.reshape(seq_count, tokens_dev, D), "seq", split_axis=0, concat_axis=0, tiled=True
    )
    input_grad = jnp.sum(got.astype(F32), axis=0) + out_grad.astype(F32)
    got_rows = rows_to_owners(slot_matrix, input_grad, numbers, devices, capacity)
    new_table, new_accum = update_rows(got_rows, emb_table, row_accum)

    out_part = dot_tn(mixed, og_full).astype(BF)
    share = dp_count // seq_count
    out_part = out_part.reshape(share, D // dp_count, seq_count, cols).transpose(0, 2, 1, 3).reshape(D, cols)
    merged = [dot_tn(x_full, g).astype(BF) for g in grads] + [dot_tn(x_full, gate_grad).astype(BF), out_part]
    merged = lax.psum_scatter(jnp.concatenate(merged, axis=1), "dp", scatter_dimension=0, tiled=True)
    steps = []
    for s in range(seq_count):
        for piece in range(dp_count):
            part, target = divmod(piece, seq_count)
            steps.append((s * dp_count + piece, target * dp_count + s * share + part))
    grad_out = lax.ppermute(merged[:, 4 * cols :], ("seq", "dp"), steps).astype(F32)
    grad_attn = merged[:, : 3 * cols].astype(F32)
    grad_gate = merged[:, 3 * cols : 4 * cols].astype(F32)
    return (grad_attn, grad_gate, grad_out, new_table, new_accum)


SEQ = 4
PLANE = 4


def send(array, target):
    steps = []
    for s in range(SEQ):
        for e in range(PLANE):
            for c in range(2):
                to = target(s, e, c)
                if to is not None:
                    steps.append((s * 2 * PLANE + 2 * e + c, to[0] * 2 * PLANE + 2 * to[1] + to[2]))
    return lax.ppermute(array, ("seq", "dp"), steps)


def home(s, c):
    return c == s // 2


def swap_far(array):
    return send(array, lambda s, e, c: None if home(s, c) else (3 - s, e, 1 - c))


def swap_near_home(array):
    return send(array, lambda s, e, c: (s ^ 1, e, c) if home(s, c) else None)


def swap_near_far(array):
    return send(array, lambda s, e, c: None if home(s, c) else (s ^ 1, e, c))


def swap_near(array):
    return send(array, lambda s, e, c: (s ^ 1, e, c))


def swap_core(array):
    return send(array, lambda s, e, c: (s, e, 1 - c))


def swap_x(array):
    return send(array, lambda s, e, c: (s, e ^ 1, c))


def swap_y(array):
    return send(array, lambda s, e, c: (s, e ^ 2, c))


def tie(*arrays):
    return lax.optimization_barrier(arrays)


def halves(array, bit, axis):
    kept = lax.dynamic_index_in_dim(array, bit, axis, keepdims=False)
    sent = lax.dynamic_index_in_dim(array, 1 - bit, axis, keepdims=False)
    return kept, sent


def plane_blocks(part):
    return part.reshape(2, 2, part.shape[0] // PLANE, part.shape[1])


def body_pairs(
    layer_input, out_grad, lengths, item_owner, item_row, w_attn, w_gate, w_out, emb_table, row_accum
):
    devices = 2 * PLANE * SEQ
    s = lax.axis_index("seq")
    d = lax.axis_index("dp")
    e, c = d // 2, d % 2
    y, x = e // 2, e % 2
    tokens_dev = layer_input.shape[0]
    positions = tokens_dev * SEQ
    maxlen = 2 * positions // 3
    blk = min(256, positions)
    cols = D // SEQ
    pairs = cols // PAIR
    rows_own = emb_table.shape[0]
    capacity = max(2, 2 * tokens_dev // devices)
    at_home = c == s // 2
    part = 2 * (s % 2) + c

    def block_of(seq, core):
        return jnp.where(core == seq // 2, seq, 3 - seq)

    mine_at, near_at = block_of(s, c), block_of(s ^ 1, c)
    core_at, diag_at = block_of(s, 1 - c), block_of(s ^ 1, 1 - c)
    order = jnp.stack([mine_at, near_at, core_at, diag_at]).astype(jnp.int32)

    x_far = swap_far(layer_input)
    x_near_home = swap_near_home(layer_input)
    users = lengths.shape[1]
    keys = (item_owner[:, 0] * rows_own + item_row).reshape(1, tokens_dev)
    small = jnp.concatenate([keys, jnp.pad(lengths, ((0, 0), (0, 128 - users)))], axis=1)
    small = jnp.where(at_home, small, swap_far(small))
    keys, lengths = small[0, :tokens_dev], small[:, tokens_dev : tokens_dev + users]
    w_pairs = pair_weights(w_attn, w_gate, part, pairs)
    x_mine = jnp.where(at_home, layer_input, x_far)
    x_near_far = swap_near_far(x_mine)
    x_core = swap_core(x_mine)
    x_near_far, keys, w_out_here = tie(x_near_far, keys, w_out)
    x_near = jnp.where(at_home, x_near_home, x_near_far)
    x_diag = swap_core(x_near)
    w_out_own = lax.dynamic_slice_in_dim(w_out_here, part * cols, cols, 0)
    w_gate_own = jnp.concatenate([w[:, 3 * PAIR :] for w in w_pairs], axis=1)
    slot_matrix, numbers = row_slots(keys // rows_own, keys % rows_own, devices, capacity)

    x_near, og_own = tie(x_near, out_grad)
    og_far = swap_far(og_own)
    og_near_home = swap_near_home(og_own)
    x_full, *first = forward_pair(lengths, order, [x_mine, x_near, x_core, x_diag], w_pairs[0], blk, maxlen)
    og_far, og_near_home, x_full = tie(og_far, og_near_home, x_full)
    og_mine = jnp.where(at_home, og_own, og_far)
    og_near_far = swap_near_far(og_mine)
    og_core = swap_core(og_mine)
    forward = [first]
    for p in range(1, pairs):
        forward.append(forward_pair(lengths, jnp.zeros((1,), jnp.int32), [x_full], w_pairs[p], blk, maxlen))
    acts, slopes, gates, weights, score_slopes, heads = (list(kind) for kind in zip(*forward))
    og_near_far, heads[-1] = tie(og_near_far, heads[-1])
    og_near = jnp.where(at_home, og_near_home, og_near_far)
    og_diag = swap_core(og_near)

    og_full, mg, stats_own = event_stats(order, [og_mine, og_near, og_core, og_diag], w_out_own, gates, heads)
    stats = [
        stats_own,
        swap_core(stats_own),
        swap_near(stats_own),
        send(stats_own, lambda s, e, c: (s ^ 1, e, 1 - c)),
    ]
    o, gate_grad, mixed = norm_backward(stats, mg, heads, gates, slopes)

    out_part = dot_tn(mixed, og_full).astype(BF).reshape(cols, SEQ, cols).transpose(1, 0, 2).reshape(D, cols)
    early = jnp.concatenate([dot_tn(x_full, gate_grad).astype(BF), out_part], axis=1)
    early_kept, early_sent = halves(plane_blocks(early), x, 1)
    early_got = swap_x(early_sent)

    grads = [
        backward_pair(lengths, p, o, acts[p], slopes[p], weights[p], score_slopes[p], blk, maxlen)
        for p in range(pairs)
    ]

    def input_part(block):
        at = block * tokens_dev
        total = dot_nt(lax.dynamic_slice_in_dim(gate_grad, at, tokens_dev, 0), w_gate_own)
        for p in range(pairs):
            rows = lax.dynamic_slice_in_dim(grads[p], at, tokens_dev, 0)
            total = total + dot_nt(rows, w_pairs[p][:, : 3 * PAIR])
        return total

    early_got, grads[-1] = tie(early_got, grads[-1])
    from_diag = swap_core(input_part(diag_at).astype(BF))
    near_sum = (input_part(near_at) + from_diag.astype(F32)).astype(BF)
    from_near = swap_near(near_sum)
    core_part = input_part(core_at).astype(BF)
    from_core = swap_core(core_part)
    input_grad = input_part(mine_at) + from_core.astype(F32) + og_mine.astype(F32)

    early_mid = (early_kept.astype(F32) + early_got.astype(F32)).astype(BF)
    early_kept, early_sent = halves(early_mid, y, 0)
    early_got = swap_y(early_sent)

    x_full, core_part = tie(x_full, core_part)
    attn = [dot_tn(x_full, g).astype(BF) for g in grads]
    a_kept, a_sent = halves(plane_blocks(attn[0]), x, 1)
    b_kept, b_sent = halves(plane_blocks(attn[1]), y, 0)
    a_got = swap_x(a_sent)
    b_got = swap_y(b_sent)

    input_grad = input_grad + from_near.astype(F32)
    got_rows = rows_to_owners(slot_matrix, input_grad, numbers, devices, capacity)

    a = (a_kept.astype(F32) + a_got.astype(F32)).astype(BF)
    b = (b_kept.astype(F32) + b_got.astype(F32)).astype(BF)
    a_kept, a_sent = halves(a, y, 0)
    b_kept, b_sent = halves(b, x, 0)
    a = a_kept.astype(F32) + swap_y(a_sent).astype(F32)
    b = b_kept.astype(F32) + swap_x(b_sent).astype(F32)
    early = early_kept.astype(F32) + early_got.astype(F32)

    def last(array, target):
        pieces = array.astype(BF).reshape(2, D // (2 * PLANE), array.shape[1])
        one, other = halves(pieces, s // 2, 0)
        one = send(one, lambda s, e, c: target(s, e, c, s // 2)).astype(F32)
        return one + send(other, lambda s, e, c: target(s, e, c, 1 - s // 2)).astype(F32)

    grad_out = last(early[:, cols:], lambda s, e, c, half: (e, 2 * (s % 2) + c, half))
    proj = jnp.concatenate([a, b, early[:, :cols]], axis=1)
    proj = last(proj, lambda s, e, c, half: (2 * (s % 2) + c, e, half))
    new_table, new_accum = update_rows(got_rows, emb_table, row_accum)
    return (proj[:, : 3 * cols], proj[:, 3 * cols :], grad_out, new_table, new_accum)


def solution(mesh):
    placed = (
        P(("dp", "seq"), None),
        P(("dp", "seq"), None),
        P("dp", None),
        P(("dp", "seq"), None),
        P(("dp", "seq")),
        P(),
        P(),
        P(),
        P(("seq", "dp"), None),
        P(("seq", "dp")),
    )
    paired = mesh.shape["seq"] == SEQ and mesh.shape["dp"] == 2 * PLANE
    return jax.shard_map(
        body_pairs if paired else body_whole,
        mesh=mesh,
        in_specs=placed,
        out_specs=(
            P("dp", "seq"),
            P("dp", "seq"),
            P("dp", "seq"),
            P(("seq", "dp"), None),
            P(("seq", "dp")),
        ),
        check_vma=False,
    )
```

```python
import functools

import jax
import jax.numpy as jnp
from jax import lax
from jax.experimental import pallas as pl
from jax.experimental.pallas import tpu as pltpu
from jax.sharding import PartitionSpec as P

D = 1024
H = 16
DH = 64
PAIR = 2 * DH

NORM_EPS = 1e-05
LEARN_RATE = 0.1
VMEM_LIMIT = 56 * 1024 * 1024
BF = jnp.bfloat16
F32 = jnp.float32


def dot_nn(a, b):
    return lax.dot_general(a, b, (((1,), (0,)), ((), ())), preferred_element_type=F32)


def dot_nt(a, b):
    return lax.dot_general(a, b, (((1,), (1,)), ((), ())), preferred_element_type=F32)


def history_start(lengths_ref, users, place):
    start = jnp.zeros_like(place)
    end = jnp.int32(0)
    for user in range(users - 1):
        end = end + lengths_ref[0, user]
        start = jnp.where(place >= end, end, start)
    return start


def head_columns(kind, head):
    first = head // 2 * 4 * PAIR + head % 2 * 3 * DH + kind * DH
    return slice(first, first + DH)


def gate_columns(pair):
    return slice(pair * 4 * PAIR + 3 * PAIR, (pair + 1) * 4 * PAIR)


def forward_kernel(*refs, blk, users, maxlen, count):
    lengths_ref, order_ref = refs[:2]
    x_refs = refs[2 : 2 + count]
    w_ref = refs[2 + count]
    outs = refs[3 + count :]
    if count > 1:
        x_out_ref, outs = outs[0], outs[1:]
    acts_ref, slopes_ref, gate_ref, weights_ref, score_slope_ref, heads_ref = outs
    i = pl.program_id(0)
    heads = weights_ref.shape[0]
    chunks = x_refs[0].shape[0] // blk

    @pl.when(i == 0)
    def _():
        for b in range(count):
            for r in range(chunks):
                at = pl.ds(pl.multiple_of(order_ref[b * chunks + r] * blk, blk), blk)
                x = x_refs[b][r * blk : (r + 1) * blk, :]
                if count > 1:
                    x_out_ref[at, :] = x
                for p in range(heads // 2):
                    lanes = slice(p * 4 * PAIR, (p + 1) * 4 * PAIR)
                    half = 0.5 * dot_nn(x, w_ref[:, lanes])
                    t = jnp.tanh(half)
                    prod = half * t
                    silu = half + prod
                    acts_ref[at, lanes] = silu.astype(BF)
                    gate_ref[at, p * PAIR : (p + 1) * PAIR] = silu[:, 3 * PAIR :]
                    slopes_ref[at, lanes] = (0.5 * (1.0 + t) * (1.0 + half - prod)).astype(BF)

    at_i = pl.ds(pl.multiple_of(i * blk, blk), blk)
    q_half = [acts_ref[at_i, head_columns(1, h)] * jnp.asarray(0.5 * DH**-0.5, BF) for h in range(heads)]
    row = i * blk + lax.broadcasted_iota(jnp.int32, (blk, blk), 0)
    col0 = lax.broadcasted_iota(jnp.int32, (blk, blk), 1)
    start = history_start(lengths_ref, users, row)

    def column(j, acc):
        at_j = pl.ds(pl.multiple_of(j * blk, blk), blk)
        col = col0 + j * blk
        allowed = (col <= row) & (col >= start)
        outs = []
        for h in range(heads):
            half = dot_nt(q_half[h], acts_ref[at_j, head_columns(2, h)])
            half = jnp.where(allowed, half, -64.0)
            t = jnp.tanh(half)
            p = half * t
            weights = (half + p).astype(BF)
            weights_ref[h, :, at_j] = weights
            score_slope_ref[h, :, at_j] = ((1.0 + t) * (1.0 + half - p)).astype(BF)
            outs.append(acc[h] + dot_nn(weights, acts_ref[at_j, head_columns(0, h)]))
        return tuple(outs)

    first = history_start(lengths_ref, users, i * blk) // blk
    zero = jnp.zeros((blk, DH), F32)
    acc = lax.fori_loop(first, i + 1, column, (zero,) * heads)
    heads_ref[...] = (jnp.concatenate(acc, axis=1) * (1.0 / maxlen)).astype(BF)


def forward_attention(lengths, order, x_blocks, w_own, blk, maxlen):
    count = len(x_blocks)
    block_rows = x_blocks[0].shape[0]
    positions = count * block_rows
    cols = w_own.shape[1] // 4
    heads = cols // DH
    users = lengths.shape[1]
    elements = heads * positions * positions // 2
    whole = lambda i: (0, 0)
    out_specs = [
        pl.BlockSpec((positions, 4 * cols), whole),
        pl.BlockSpec((positions, 4 * cols), whole),
        pl.BlockSpec((positions, cols), whole),
        pl.BlockSpec((heads, blk, positions), lambda i: (0, i, 0)),
        pl.BlockSpec((heads, blk, positions), lambda i: (0, i, 0)),
        pl.BlockSpec((blk, cols), lambda i: (i, 0)),
    ]
    out_shape = [
        jax.ShapeDtypeStruct((positions, 4 * cols), BF),
        jax.ShapeDtypeStruct((positions, 4 * cols), BF),
        jax.ShapeDtypeStruct((positions, cols), F32),
        jax.ShapeDtypeStruct((heads, positions, positions), BF),
        jax.ShapeDtypeStruct((heads, positions, positions), BF),
        jax.ShapeDtypeStruct((positions, cols), BF),
    ]
    if count > 1:
        out_specs = [pl.BlockSpec((positions, D), whole)] + out_specs
        out_shape = [jax.ShapeDtypeStruct((positions, D), BF)] + out_shape
    return pl.pallas_call(
        functools.partial(forward_kernel, blk=blk, users=users, maxlen=maxlen, count=count),
        grid=(positions // blk,),
        in_specs=[pl.BlockSpec(memory_space=pltpu.SMEM), pl.BlockSpec(memory_space=pltpu.SMEM)]
        + [pl.BlockSpec((block_rows, D), whole)] * count
        + [pl.BlockSpec((D, 4 * cols), whole)],
        out_specs=out_specs,
        out_shape=out_shape,
        compiler_params=pltpu.CompilerParams(vmem_limit_bytes=VMEM_LIMIT),
        cost_estimate=pl.CostEstimate(
            flops=8 * positions * D * cols + 4 * elements * 256,
            bytes_accessed=4 * positions * D + 4 * elements,
            transcendentals=elements,
        ),
        name="attention_forward",
    )(lengths, order, *x_blocks, w_own)


def stats_kernel(*refs, blk, count):
    order_ref = refs[0]
    og_refs = refs[1 : 1 + count]
    w_ref, gate_ref, heads_ref = refs[1 + count : 4 + count]
    outs = refs[4 + count :]
    if count > 1:
        og_out_ref, outs = outs[0], outs[1:]
    mg_ref, stats_ref = outs
    chunks = og_refs[0].shape[0] // blk
    for b in range(count):
        for r in range(chunks):
            at = pl.ds(pl.multiple_of(order_ref[b * chunks + r] * blk, blk), blk)
            og = og_refs[b][r * blk : (r + 1) * blk, :]
            if count > 1:
                og_out_ref[at, :] = og
            mg = dot_nt(og, w_ref[...])
            mg_ref[at, :] = mg
            ng = mg * gate_ref[at, :]
            heads = heads_ref[at, :].astype(F32)
            mean = jnp.mean(heads, axis=1, keepdims=True)
            centred = heads - mean
            square = jnp.sum(centred * centred, axis=1, keepdims=True)
            total = jnp.sum(ng, axis=1, keepdims=True)
            cross = jnp.sum(ng * centred, axis=1, keepdims=True)
            lane = lax.broadcasted_iota(jnp.int32, (blk, 128), 1)
            packed = jnp.where(lane == 0, mean, jnp.where(lane == 1, square, jnp.where(lane == 2, total, cross)))
            stats_ref[:, at] = jnp.transpose(packed)[:8, :]


def event_stats(order, og_blocks, w_out_own, gate, heads, blk):
    positions, cols = heads.shape
    count = len(og_blocks)
    vmem = pl.BlockSpec(memory_space=pltpu.VMEM)
    out_shape = [
        jax.ShapeDtypeStruct((positions, cols), F32),
        jax.ShapeDtypeStruct((8, positions), F32),
    ]
    if count > 1:
        out_shape = [jax.ShapeDtypeStruct((positions, D), BF)] + out_shape
    return pl.pallas_call(
        functools.partial(stats_kernel, blk=blk, count=count),
        in_specs=[pl.BlockSpec(memory_space=pltpu.SMEM)] + [vmem] * (count + 3),
        out_specs=[vmem] * len(out_shape),
        out_shape=out_shape,
        compiler_params=pltpu.CompilerParams(vmem_limit_bytes=VMEM_LIMIT),
        cost_estimate=pl.CostEstimate(
            flops=2 * positions * cols * D, bytes_accessed=4 * positions * D + 10 * positions * cols, transcendentals=0
        ),
        name="event_stats",
    )(order, *og_blocks, w_out_own, gate, heads)


def combined_stats(stats_refs, cols):
    shards = len(stats_refs)
    positions = stats_refs[0].shape[1]
    means = [ref[0:1, :] for ref in stats_refs]
    mean = sum(means) * (1.0 / shards)
    square = jnp.zeros_like(mean)
    total = jnp.zeros_like(mean)
    cross = jnp.zeros_like(mean)
    for s, ref in enumerate(stats_refs):
        shift = means[s] - mean
        part = ref[2:3, :]
        square = square + ref[1:2, :] + cols * shift * shift
        total = total + part
        cross = cross + ref[3:4, :] + shift * part
    inv_dev = lax.rsqrt(square * (1.0 / D) + NORM_EPS)
    kind = lax.broadcasted_iota(jnp.int32, (128, positions), 0)
    rest = jnp.where(kind == 2, total * (1.0 / D), cross * inv_dev * (1.0 / D))
    packed = jnp.where(kind == 0, mean, jnp.where(kind == 1, inv_dev, rest))
    per_event = jnp.transpose(packed)
    return [per_event[:, k : k + 1] for k in range(4)]


def backward_kernel(*refs, blk, users, maxlen, shards):
    lengths_ref = refs[0]
    stats_refs = refs[1 : 1 + shards]
    mg_ref, gate_ref, heads_ref, acts_ref, slopes_ref, weights_ref, score_slope_ref = refs[1 + shards : 8 + shards]
    grad_ref, mixed_ref, o_ref, o_t, q_t, vg_t, kg_t, qg = refs[8 + shards :]
    i = pl.program_id(0)
    positions, cols = o_ref.shape
    heads = cols // DH
    blocks = positions // blk
    scale = DH ** (-0.5)

    @pl.when(i == 0)
    def _():
        mean, inv_dev, total, cross = combined_stats(stats_refs, cols)
        for p in range(heads // 2):
            lanes = slice(p * PAIR, (p + 1) * PAIR)
            normed = (heads_ref[:, lanes].astype(F32) - mean) * inv_dev
            gate = gate_ref[:, lanes]
            mg = mg_ref[:, lanes]
            mixed_ref[:, lanes] = (normed * gate).astype(BF)
            gate_slope = slopes_ref[:, gate_columns(p)].astype(F32)
            grad_ref[:, gate_columns(p)] = (mg * normed * gate_slope).astype(BF)
            o_ref[:, lanes] = (inv_dev * (mg * gate - total - normed * cross)).astype(BF)
        o_t[...] = jnp.transpose(o_ref[...])
        queries = [acts_ref[:, head_columns(1, h)] for h in range(heads)]
        q_t[...] = jnp.transpose(jnp.concatenate(queries, axis=1))
        vg_t[...] = jnp.zeros_like(vg_t)
        kg_t[...] = jnp.zeros_like(kg_t)

    at_i = pl.ds(pl.multiple_of(i * blk, blk), blk)

    def column(j, acc):
        at_j = pl.ds(pl.multiple_of(j * blk, blk), blk)
        outs = []
        for h in range(heads):
            lanes = slice(h * DH, (h + 1) * DH)
            weight_grad = dot_nt(o_ref[at_i, lanes], acts_ref[at_j, head_columns(0, h)])
            score_grad = (weight_grad * score_slope_ref[h, :, at_j].astype(F32)).astype(BF)
            vg_t[lanes, at_j] += dot_nn(o_t[lanes, at_i], weights_ref[h, :, at_j])
            kg_t[lanes, at_j] += dot_nn(q_t[lanes, at_i], score_grad)
            outs.append(acc[h] + dot_nn(score_grad, acts_ref[at_j, head_columns(2, h)]))
        return tuple(outs)

    first = history_start(lengths_ref, users, i * blk) // blk
    zero = jnp.zeros((blk, DH), F32)
    acc = lax.fori_loop(first, i + 1, column, (zero,) * heads)
    qg[at_i, :] = jnp.concatenate(acc, axis=1)

    @pl.when(i == blocks - 1)
    def _():
        factor = 0.5 * scale / maxlen
        grads = [jnp.transpose(vg_t[...]) * (1.0 / maxlen), qg[...] * factor, jnp.transpose(kg_t[...]) * factor]
        pieces = [grads[kind][:, h * DH : (h + 1) * DH] for h in range(heads) for kind in range(3)]
        for n in range(3 * heads // 2):
            first_lane = n // 3 * 4 * PAIR + n % 3 * PAIR
            lanes = slice(first_lane, first_lane + PAIR)
            grad = jnp.concatenate(pieces[2 * n : 2 * n + 2], axis=1).astype(BF).astype(F32)
            grad_ref[:, lanes] = (grad * slopes_ref[:, lanes].astype(F32)).astype(BF)


def backward_attention(lengths, stats, mg, gate, head_outs, acts, slopes, weights, score_slope, blk, maxlen):
    positions, cols = mg.shape
    heads = cols // DH
    shards = len(stats)
    users = lengths.shape[1]
    elements = heads * positions * positions // 2
    whole = lambda i: (0, 0)
    return pl.pallas_call(
        functools.partial(backward_kernel, blk=blk, users=users, maxlen=maxlen, shards=shards),
        grid=(positions // blk,),
        in_specs=[pl.BlockSpec(memory_space=pltpu.SMEM)]
        + [pl.BlockSpec((8, positions), whole)] * shards
        + [
            pl.BlockSpec((positions, cols), whole),
            pl.BlockSpec((positions, cols), whole),
            pl.BlockSpec((positions, cols), whole),
            pl.BlockSpec((positions, 4 * cols), whole),
            pl.BlockSpec((positions, 4 * cols), whole),
            pl.BlockSpec((heads, blk, positions), lambda i: (0, i, 0)),
            pl.BlockSpec((heads, blk, positions), lambda i: (0, i, 0)),
        ],
        out_specs=[pl.BlockSpec((positions, 4 * cols), whole), pl.BlockSpec((positions, cols), whole)],
        out_shape=[
            jax.ShapeDtypeStruct((positions, 4 * cols), BF),
            jax.ShapeDtypeStruct((positions, cols), BF),
        ],
        scratch_shapes=[
            pltpu.VMEM((positions, cols), BF),
            pltpu.VMEM((cols, positions), BF),
            pltpu.VMEM((cols, positions), BF),
            pltpu.VMEM((cols, positions), F32),
            pltpu.VMEM((cols, positions), F32),
            pltpu.VMEM((positions, cols), F32),
        ],
        compiler_params=pltpu.CompilerParams(vmem_limit_bytes=VMEM_LIMIT),
        cost_estimate=pl.CostEstimate(
            flops=8 * elements * 256, bytes_accessed=4 * elements + 26 * positions * cols, transcendentals=0
        ),
        name="attention_backward",
    )(lengths, *stats, mg, gate, head_outs, acts, slopes, weights, score_slope)


def update_kernel(rows_ref, table_ref, accum_ref, new_table_ref, new_accum_ref, ids):
    i = pl.program_id(0)
    blk = table_ref.shape[0]
    slots = rows_ref.shape[0]

    @pl.when(i == 0)
    def _():
        numbers = jnp.transpose(rows_ref[:, D:].astype(F32))
        ids[...] = (numbers[0:1, :] * 256.0 + numbers[1:2, :]).astype(jnp.int32)

    row = i * blk + lax.broadcasted_iota(jnp.int32, (blk, slots), 0)
    hits = jnp.where(row == ids[...], 1.0, 0.0).astype(BF)
    grad = dot_nn(hits, rows_ref[:, :D])
    accum = jnp.transpose(jnp.broadcast_to(accum_ref[...], (128, blk)))[:, :1] + jnp.mean(grad * grad, axis=1, keepdims=True)
    new_accum_ref[...] = jnp.transpose(jnp.broadcast_to(accum, (blk, 128)))[:1, :]
    new_table_ref[...] = table_ref[...] - LEARN_RATE * grad * lax.rsqrt(accum)


def update_rows(got_rows, emb_table, row_accum):
    rows_own = emb_table.shape[0]
    slots = got_rows.shape[0]
    blk = min(256, rows_own)
    new_table, new_accum = pl.pallas_call(
        update_kernel,
        grid=(rows_own // blk,),
        in_specs=[
            pl.BlockSpec((slots, D + 128), lambda i: (0, 0)),
            pl.BlockSpec((blk, D), lambda i: (i, 0)),
            pl.BlockSpec((1, blk), lambda i: (0, i)),
        ],
        out_specs=[
            pl.BlockSpec((blk, D), lambda i: (i, 0)),
            pl.BlockSpec((1, blk), lambda i: (0, i)),
        ],
        out_shape=[
            jax.ShapeDtypeStruct((rows_own, D), F32),
            jax.ShapeDtypeStruct((1, rows_own), F32),
        ],
        scratch_shapes=[pltpu.VMEM((1, slots), jnp.int32)],
        compiler_params=pltpu.CompilerParams(vmem_limit_bytes=VMEM_LIMIT),
        cost_estimate=pl.CostEstimate(
            flops=2 * rows_own * slots * D, bytes_accessed=8 * rows_own * D + 2 * slots * D, transcendentals=rows_own
        ),
        name="update_rows",
    )(got_rows, emb_table, row_accum.reshape(1, rows_own))
    return new_table, new_accum.reshape(rows_own)


def own_weights(w_attn, w_gate, part, pairs):
    slices = []
    for p in range(pairs):
        at = part * pairs + p
        slices.append(lax.dynamic_slice_in_dim(w_attn, at * 3 * PAIR, 3 * PAIR, 1))
        slices.append(lax.dynamic_slice_in_dim(w_gate, at * PAIR, PAIR, 1))
    return jnp.concatenate(slices, axis=1)


def attn_and_gate(proj, pairs):
    pieces = [proj[:, p * 4 * PAIR : (p + 1) * 4 * PAIR] for p in range(pairs)]
    attn = jnp.concatenate([piece[:, : 3 * PAIR] for piece in pieces], axis=1)
    return attn, jnp.concatenate([piece[:, 3 * PAIR :] for piece in pieces], axis=1)


def row_slots(owners, rows, devices, capacity):
    events = owners.shape[0]
    owner_hits = (owners[:, None] == jnp.arange(devices, dtype=jnp.int32)[None, :]).astype(BF)
    place = jnp.arange(events, dtype=jnp.int32)
    before = (place[:, None] > place[None, :]).astype(BF)
    earlier = jnp.dot(before, owner_hits, preferred_element_type=F32)
    slots = jnp.sum(earlier * owner_hits.astype(F32), axis=1).astype(jnp.int32)
    flat_slot = owners * capacity + slots
    slot_hits = jnp.arange(devices * capacity, dtype=jnp.int32)[:, None] == flat_slot[None, :]
    lane = jnp.arange(128, dtype=jnp.int32)[None, :]
    numbers = jnp.where(lane == 0, rows[:, None] // 256, jnp.where(lane == 1, rows[:, None] % 256, 0))
    return slot_hits.astype(BF), numbers.astype(BF)


def rows_to_owners(slot_matrix, input_grad, numbers, devices, capacity):
    rows = jnp.concatenate([input_grad.astype(BF), numbers], axis=1)
    rows = jnp.dot(slot_matrix, rows, preferred_element_type=F32).astype(BF)
    got = lax.all_to_all(
        rows.reshape(devices, capacity, D + 128), ("seq", "dp"), split_axis=0, concat_axis=0, tiled=True
    )
    return got.reshape(devices * capacity, D + 128)


TN = (((0,), (0,)), ((), ()))


def dot_tn(a, b):
    return lax.dot_general(a, b, TN, preferred_element_type=F32)


def body_whole(
    layer_input, out_grad, lengths, item_owner, item_row, w_attn, w_gate, w_out, emb_table, row_accum
):
    seq_count = lax.axis_size("seq")
    dp_count = lax.axis_size("dp")
    devices = seq_count * dp_count
    seq_id = lax.axis_index("seq")
    tokens_dev = layer_input.shape[0]
    positions = tokens_dev * seq_count
    maxlen = 2 * positions // 3
    blk = min(256, positions)
    cols = D // seq_count
    pairs = cols // PAIR
    capacity = max(2, 2 * tokens_dev // devices)

    w_own = own_weights(w_attn, w_gate, seq_id, pairs)
    w_out_own = lax.dynamic_slice_in_dim(w_out, seq_id * cols, cols, 0)
    slot_matrix, numbers = row_slots(item_owner[:, 0], item_row, devices, capacity)

    x_full = lax.all_gather(layer_input, "seq", axis=0, tiled=True)
    og_full = lax.all_gather(out_grad, "seq", axis=0, tiled=True)
    order = jnp.arange(positions // blk, dtype=jnp.int32)
    acts, slopes, gate, weights, score_slope, heads = forward_attention(
        lengths, order, [x_full], w_own, blk, maxlen
    )
    mg, stats_own = event_stats(order, [og_full], w_out_own, gate, heads, blk)
    stats = lax.all_gather(stats_own, "seq", axis=0, tiled=False)
    grads, mixed = backward_attention(
        lengths, [stats[s] for s in range(seq_count)], mg, gate, heads, acts, slopes, weights, score_slope, blk, maxlen
    )

    input_part = dot_nt(grads, w_own).astype(BF)
    got = lax.all_to_all(
        input_part.reshape(seq_count, tokens_dev, D), "seq", split_axis=0, concat_axis=0, tiled=True
    )
    input_grad = jnp.sum(got.astype(F32), axis=0) + out_grad.astype(F32)
    got_rows = rows_to_owners(slot_matrix, input_grad, numbers, devices, capacity)
    new_table, new_accum = update_rows(got_rows, emb_table, row_accum)

    out_part = dot_tn(mixed, og_full).astype(BF)
    share = dp_count // seq_count
    out_part = out_part.reshape(share, D // dp_count, seq_count, cols).transpose(0, 2, 1, 3).reshape(D, cols)
    merged = jnp.concatenate([dot_tn(x_full, grads).astype(BF), out_part], axis=1)
    merged = lax.psum_scatter(merged, "dp", scatter_dimension=0, tiled=True)
    steps = []
    for s in range(seq_count):
        for piece in range(dp_count):
            part, target = divmod(piece, seq_count)
            steps.append((s * dp_count + piece, target * dp_count + s * share + part))
    grad_out = lax.ppermute(merged[:, 4 * cols :], ("seq", "dp"), steps).astype(F32)
    grad_attn, grad_gate = attn_and_gate(merged[:, : 4 * cols].astype(F32), pairs)
    return (grad_attn, grad_gate, grad_out, new_table, new_accum)


SEQ = 4
PLANE = 4


def send(array, target):
    steps = []
    for s in range(SEQ):
        for e in range(PLANE):
            for c in range(2):
                to = target(s, e, c)
                if to is not None:
                    steps.append((s * 2 * PLANE + 2 * e + c, to[0] * 2 * PLANE + 2 * to[1] + to[2]))
    return lax.ppermute(array, ("seq", "dp"), steps)


def home(s, c):
    return c == s // 2


def swap_far(array):
    return send(array, lambda s, e, c: None if home(s, c) else (3 - s, e, 1 - c))


def fetch_near(array):
    return send(array, lambda s, e, c: (s ^ 1, e, c) if home(s, c) else ((3 - s) ^ 1, e, 1 - c))


def swap_near(array):
    return send(array, lambda s, e, c: (s ^ 1, e, c))


def swap_core(array):
    return send(array, lambda s, e, c: (s, e, 1 - c))


def swap_x(array):
    return send(array, lambda s, e, c: (s, e ^ 1, c))


def swap_y(array):
    return send(array, lambda s, e, c: (s, e ^ 2, c))


def tie(*arrays):
    return lax.optimization_barrier(arrays)


def halves(array, bit, axis):
    kept = lax.dynamic_index_in_dim(array, bit, axis, keepdims=False)
    sent = lax.dynamic_index_in_dim(array, 1 - bit, axis, keepdims=False)
    return kept, sent


def body_pairs(
    layer_input, out_grad, lengths, item_owner, item_row, w_attn, w_gate, w_out, emb_table, row_accum
):
    devices = 2 * PLANE * SEQ
    s = lax.axis_index("seq")
    d = lax.axis_index("dp")
    e, c = d // 2, d % 2
    y, x = e // 2, e % 2
    tokens_dev = layer_input.shape[0]
    positions = tokens_dev * SEQ
    maxlen = 2 * positions // 3
    blk = min(256, positions)
    cols = D // SEQ
    pairs = cols // PAIR
    rows_own = emb_table.shape[0]
    capacity = max(2, 2 * tokens_dev // devices)
    at_home = c == s // 2
    part = 2 * (s % 2) + c

    def block_of(seq, core):
        return jnp.where(core == seq // 2, seq, 3 - seq)

    mine_at, near_at = block_of(s, c), block_of(s ^ 1, c)
    core_at, diag_at = block_of(s, 1 - c), block_of(s ^ 1, 1 - c)
    order = jnp.stack([mine_at, near_at, core_at, diag_at]).astype(jnp.int32)

    x_far = swap_far(layer_input)
    x_near = fetch_near(layer_input)
    users = lengths.shape[1]
    keys = (item_owner[:, 0] * rows_own + item_row).reshape(1, tokens_dev)
    small = jnp.concatenate([keys, jnp.pad(lengths, ((0, 0), (0, 128 - users)))], axis=1)
    small = jnp.where(at_home, small, swap_far(small))
    keys, lengths = small[0, :tokens_dev], small[:, tokens_dev : tokens_dev + users]
    w_own = own_weights(w_attn, w_gate, part, pairs)
    w_out_own = lax.dynamic_slice_in_dim(w_out, part * cols, cols, 0)
    slot_matrix, numbers = row_slots(keys // rows_own, keys % rows_own, devices, capacity)
    x_far, x_near, w_own, w_out_own, slot_matrix, numbers, lengths = tie(
        x_far, x_near, w_own, w_out_own, slot_matrix, numbers, lengths
    )
    x_here = jnp.concatenate([jnp.where(at_home, layer_input, x_far), x_near], axis=0)
    x_there = swap_core(x_here)
    x_here, og_own = tie(x_here, out_grad)
    og_far = swap_far(og_own)
    og_near = fetch_near(og_own)

    x_full, acts, slopes, gate, weights, score_slope, heads = forward_attention(
        lengths, order, [x_here, x_there], w_own, blk, maxlen
    )
    og_far, og_near, heads = tie(og_far, og_near, heads)
    og_mine = jnp.where(at_home, og_own, og_far)
    og_here = jnp.concatenate([og_mine, og_near], axis=0)
    og_there = swap_core(og_here)
    og_full, mg, stats_own = event_stats(order, [og_here, og_there], w_out_own, gate, heads, blk)
    stats = [
        stats_own,
        swap_core(stats_own),
        swap_near(stats_own),
        send(stats_own, lambda s, e, c: (s ^ 1, e, 1 - c)),
    ]
    grads, mixed = backward_attention(
        lengths, stats, mg, gate, heads, acts, slopes, weights, score_slope, blk, maxlen
    )

    def input_part(grads, block):
        return dot_nt(lax.dynamic_slice_in_dim(grads, block * tokens_dev, tokens_dev, 0), w_own)

    from_diag = swap_core(input_part(grads, diag_at).astype(BF))
    near_sum = (input_part(grads, near_at) + from_diag.astype(F32)).astype(BF)
    near_sum, grads = tie(near_sum, grads)
    from_near = swap_near(near_sum)
    core_part = input_part(grads, core_at).astype(BF)
    from_core = swap_core(core_part)
    input_grad = input_part(grads, mine_at) + og_mine.astype(F32)

    core_part, grads, mixed = tie(core_part, grads, mixed)
    half = 5 * cols // 2
    proj = dot_tn(x_full, grads).astype(BF).reshape(2, 2, D // PLANE, 4 * cols)
    out_part = dot_tn(mixed, og_full).astype(BF).reshape(cols, 2, 2, cols)
    a_kept, a_sent = halves(proj[..., :half], x, 1)
    b_kept, b_sent = halves(proj[..., half:], y, 0)
    out_kept, out_sent = (piece.transpose(1, 0, 2) for piece in halves(out_part, y, 1))
    b_kept = jnp.concatenate([b_kept, out_kept], axis=-1)
    b_sent = jnp.concatenate([b_sent, out_sent], axis=-1)
    a_got = swap_x(a_sent)
    b_got = swap_y(b_sent)

    input_grad = input_grad + from_core.astype(F32) + from_near.astype(F32)
    got_rows = rows_to_owners(slot_matrix, input_grad, numbers, devices, capacity)

    a = (a_kept.astype(F32) + a_got.astype(F32)).astype(BF)
    b = (b_kept.astype(F32) + b_got.astype(F32)).astype(BF)
    a_kept, a_sent = halves(a, y, 0)
    b_kept, b_sent = halves(b, x, 0)
    a = (a_kept.astype(F32) + swap_y(a_sent).astype(F32)).astype(BF)
    b = (b_kept.astype(F32) + swap_x(b_sent).astype(F32)).astype(BF)

    def last(array, target):
        pieces = array.reshape(2, D // (2 * PLANE), array.shape[1])
        one, other = halves(pieces, s // 2, 0)
        one = send(one, lambda s, e, c: target(s, e, c, s // 2)).astype(F32)
        return one + send(other, lambda s, e, c: target(s, e, c, 1 - s // 2)).astype(F32)

    proj = jnp.concatenate([a, b[:, : 4 * cols - half]], axis=1)
    proj = last(proj, lambda s, e, c, piece: (2 * (s % 2) + c, e, piece))
    grad_out = last(b[:, 4 * cols - half :], lambda s, e, c, piece: (e, 2 * (s % 2) + c, piece))
    grad_attn, grad_gate = attn_and_gate(proj, pairs)
    new_table, new_accum = update_rows(got_rows, emb_table, row_accum)
    return (grad_attn, grad_gate, grad_out, new_table, new_accum)


def solution(mesh):
    placed = (
        P(("dp", "seq"), None),
        P(("dp", "seq"), None),
        P("dp", None),
        P(("dp", "seq"), None),
        P(("dp", "seq")),
        P(),
        P(),
        P(),
        P(("seq", "dp"), None),
        P(("seq", "dp")),
    )
    paired = mesh.shape["seq"] == SEQ and mesh.shape["dp"] == 2 * PLANE
    return jax.shard_map(
        body_pairs if paired else body_whole,
        mesh=mesh,
        in_specs=placed,
        out_specs=(
            P("dp", "seq"),
            P("dp", "seq"),
            P("dp", "seq"),
            P(("seq", "dp"), None),
            P(("seq", "dp")),
        ),
        check_vma=False,
    )
```

```python
import functools

import jax
import jax.numpy as jnp
from jax import lax
from jax.experimental import pallas as pl
from jax.experimental.pallas import tpu as pltpu
from jax.sharding import PartitionSpec as P

D = 1024
H = 16
DH = 64
PAIR = 2 * DH

NORM_EPS = 1e-05
LEARN_RATE = 0.1
VMEM_LIMIT = 56 * 1024 * 1024
BF = jnp.bfloat16
F32 = jnp.float32


def dot_nn(a, b):
    return lax.dot_general(a, b, (((1,), (0,)), ((), ())), preferred_element_type=F32)


def dot_nt(a, b):
    return lax.dot_general(a, b, (((1,), (1,)), ((), ())), preferred_element_type=F32)


def history_start(lengths_ref, users, place):
    start = jnp.zeros_like(place)
    end = jnp.int32(0)
    for user in range(users - 1):
        end = end + lengths_ref[0, user]
        start = jnp.where(place >= end, end, start)
    return start


def head_columns(kind, head):
    first = head // 2 * 4 * PAIR + head % 2 * 3 * DH + kind * DH
    return slice(first, first + DH)


def gate_columns(pair):
    return slice(pair * 4 * PAIR + 3 * PAIR, (pair + 1) * 4 * PAIR)


def forward_kernel(*refs, blk, users, maxlen, count):
    lengths_ref, order_ref = refs[:2]
    x_refs = refs[2 : 2 + count]
    w_ref = refs[2 + count]
    outs = refs[3 + count :]
    if count > 1:
        x_out_ref, outs = outs[0], outs[1:]
    acts_ref, slopes_ref, gate_ref, weights_ref, score_slope_ref, heads_ref = outs
    i = pl.program_id(0)
    heads = weights_ref.shape[0]
    chunks = x_refs[0].shape[0] // blk

    @pl.when(i == 0)
    def _():
        for b in range(count):
            for r in range(chunks):
                at = pl.ds(pl.multiple_of(order_ref[b * chunks + r] * blk, blk), blk)
                x = x_refs[b][r * blk : (r + 1) * blk, :]
                if count > 1:
                    x_out_ref[at, :] = x
                for p in range(heads // 2):
                    lanes = slice(p * 4 * PAIR, (p + 1) * 4 * PAIR)
                    half = 0.5 * dot_nn(x, w_ref[:, lanes])
                    t = jnp.tanh(half)
                    prod = half * t
                    silu = half + prod
                    acts_ref[at, lanes] = silu.astype(BF)
                    gate_ref[at, p * PAIR : (p + 1) * PAIR] = silu[:, 3 * PAIR :]
                    slopes_ref[at, lanes] = (0.5 * (1.0 + t) * (1.0 + half - prod)).astype(BF)

    at_i = pl.ds(pl.multiple_of(i * blk, blk), blk)
    q_half = [acts_ref[at_i, head_columns(1, h)] * jnp.asarray(0.5 * DH**-0.5, BF) for h in range(heads)]
    row = i * blk + lax.broadcasted_iota(jnp.int32, (blk, blk), 0)
    col0 = lax.broadcasted_iota(jnp.int32, (blk, blk), 1)
    start = history_start(lengths_ref, users, row)

    def column(j, acc):
        at_j = pl.ds(pl.multiple_of(j * blk, blk), blk)
        col = col0 + j * blk
        allowed = (col <= row) & (col >= start)
        outs = []
        for h in range(heads):
            half = dot_nt(q_half[h], acts_ref[at_j, head_columns(2, h)])
            half = jnp.where(allowed, half, -64.0)
            t = jnp.tanh(half)
            p = half * t
            weights = (half + p).astype(BF)
            weights_ref[h, :, at_j] = weights
            score_slope_ref[h, :, at_j] = ((1.0 + t) * (1.0 + half - p)).astype(BF)
            outs.append(acc[h] + dot_nn(weights, acts_ref[at_j, head_columns(0, h)]))
        return tuple(outs)

    first = history_start(lengths_ref, users, i * blk) // blk
    zero = jnp.zeros((blk, DH), F32)
    acc = lax.fori_loop(first, i + 1, column, (zero,) * heads)
    heads_ref[...] = (jnp.concatenate(acc, axis=1) * (1.0 / maxlen)).astype(BF)


def forward_attention(lengths, order, x_blocks, w_own, blk, maxlen):
    count = len(x_blocks)
    block_rows = x_blocks[0].shape[0]
    positions = count * block_rows
    cols = w_own.shape[1] // 4
    heads = cols // DH
    users = lengths.shape[1]
    elements = heads * positions * positions // 2
    whole = lambda i: (0, 0)
    out_specs = [
        pl.BlockSpec((positions, 4 * cols), whole),
        pl.BlockSpec((positions, 4 * cols), whole),
        pl.BlockSpec((positions, cols), whole),
        pl.BlockSpec((heads, blk, positions), lambda i: (0, i, 0)),
        pl.BlockSpec((heads, blk, positions), lambda i: (0, i, 0)),
        pl.BlockSpec((blk, cols), lambda i: (i, 0)),
    ]
    out_shape = [
        jax.ShapeDtypeStruct((positions, 4 * cols), BF),
        jax.ShapeDtypeStruct((positions, 4 * cols), BF),
        jax.ShapeDtypeStruct((positions, cols), F32),
        jax.ShapeDtypeStruct((heads, positions, positions), BF),
        jax.ShapeDtypeStruct((heads, positions, positions), BF),
        jax.ShapeDtypeStruct((positions, cols), BF),
    ]
    if count > 1:
        out_specs = [pl.BlockSpec((positions, D), whole)] + out_specs
        out_shape = [jax.ShapeDtypeStruct((positions, D), BF)] + out_shape
    return pl.pallas_call(
        functools.partial(forward_kernel, blk=blk, users=users, maxlen=maxlen, count=count),
        grid=(positions // blk,),
        in_specs=[pl.BlockSpec(memory_space=pltpu.SMEM), pl.BlockSpec(memory_space=pltpu.SMEM)]
        + [pl.BlockSpec((block_rows, D), whole)] * count
        + [pl.BlockSpec((D, 4 * cols), whole)],
        out_specs=out_specs,
        out_shape=out_shape,
        compiler_params=pltpu.CompilerParams(vmem_limit_bytes=VMEM_LIMIT),
        cost_estimate=pl.CostEstimate(
            flops=8 * positions * D * cols + 4 * elements * 256,
            bytes_accessed=4 * positions * D + 4 * elements,
            transcendentals=elements,
        ),
        name="attention_forward",
    )(lengths, order, *x_blocks, w_own)


def stats_kernel(*refs, count):
    order_ref = refs[0]
    mg_refs = refs[1 : 1 + count]
    gate_ref, heads_ref, mg_out_ref, stats_ref = refs[1 + count :]
    rows = mg_refs[0].shape[0]
    for b in range(count):
        at = pl.ds(pl.multiple_of(order_ref[b] * rows, rows), rows)
        mg = mg_refs[b][...]
        mg_out_ref[at, :] = mg
        ng = mg.astype(F32) * gate_ref[at, :]
        heads = heads_ref[at, :].astype(F32)
        mean = jnp.mean(heads, axis=1, keepdims=True)
        centred = heads - mean
        square = jnp.sum(centred * centred, axis=1, keepdims=True)
        total = jnp.sum(ng, axis=1, keepdims=True)
        cross = jnp.sum(ng * centred, axis=1, keepdims=True)
        lane = lax.broadcasted_iota(jnp.int32, (rows, 128), 1)
        packed = jnp.where(lane == 0, mean, jnp.where(lane == 1, square, jnp.where(lane == 2, total, cross)))
        stats_ref[:, at] = jnp.transpose(packed)[:8, :]


def event_stats(order, mg_blocks, gate, heads):
    positions, cols = heads.shape
    count = len(mg_blocks)
    vmem = pl.BlockSpec(memory_space=pltpu.VMEM)
    return pl.pallas_call(
        functools.partial(stats_kernel, count=count),
        in_specs=[pl.BlockSpec(memory_space=pltpu.SMEM)] + [vmem] * (count + 2),
        out_specs=[vmem, vmem],
        out_shape=[
            jax.ShapeDtypeStruct((positions, cols), BF),
            jax.ShapeDtypeStruct((8, positions), F32),
        ],
        compiler_params=pltpu.CompilerParams(vmem_limit_bytes=VMEM_LIMIT),
        cost_estimate=pl.CostEstimate(flops=20 * positions * cols, bytes_accessed=10 * positions * cols, transcendentals=0),
        name="event_stats",
    )(order, *mg_blocks, gate, heads)


def combined_stats(stats_refs, cols):
    shards = len(stats_refs)
    positions = stats_refs[0].shape[1]
    means = [ref[0:1, :] for ref in stats_refs]
    mean = sum(means) * (1.0 / shards)
    square = jnp.zeros_like(mean)
    total = jnp.zeros_like(mean)
    cross = jnp.zeros_like(mean)
    for s, ref in enumerate(stats_refs):
        shift = means[s] - mean
        part = ref[2:3, :]
        square = square + ref[1:2, :] + cols * shift * shift
        total = total + part
        cross = cross + ref[3:4, :] + shift * part
    inv_dev = lax.rsqrt(square * (1.0 / D) + NORM_EPS)
    kind = lax.broadcasted_iota(jnp.int32, (128, positions), 0)
    rest = jnp.where(kind == 2, total * (1.0 / D), cross * inv_dev * (1.0 / D))
    packed = jnp.where(kind == 0, mean, jnp.where(kind == 1, inv_dev, rest))
    per_event = jnp.transpose(packed)
    return [per_event[:, k : k + 1] for k in range(4)]


def backward_kernel(*refs, blk, users, maxlen, shards):
    lengths_ref = refs[0]
    stats_refs = refs[1 : 1 + shards]
    mg_ref, gate_ref, heads_ref, acts_ref, slopes_ref, weights_ref, score_slope_ref = refs[1 + shards : 8 + shards]
    grad_ref, mixed_ref, o_ref, o_t, q_t, vg_t, kg_t, qg = refs[8 + shards :]
    i = pl.program_id(0)
    positions, cols = o_ref.shape
    heads = cols // DH
    blocks = positions // blk
    scale = DH ** (-0.5)

    @pl.when(i == 0)
    def _():
        mean, inv_dev, total, cross = combined_stats(stats_refs, cols)
        for p in range(heads // 2):
            lanes = slice(p * PAIR, (p + 1) * PAIR)
            normed = (heads_ref[:, lanes].astype(F32) - mean) * inv_dev
            gate = gate_ref[:, lanes]
            mg = mg_ref[:, lanes].astype(F32)
            mixed_ref[:, lanes] = (normed * gate).astype(BF)
            gate_slope = slopes_ref[:, gate_columns(p)].astype(F32)
            grad_ref[:, gate_columns(p)] = (mg * normed * gate_slope).astype(BF)
            o_ref[:, lanes] = (inv_dev * (mg * gate - total - normed * cross)).astype(BF)
        o_t[...] = jnp.transpose(o_ref[...])
        queries = [acts_ref[:, head_columns(1, h)] for h in range(heads)]
        q_t[...] = jnp.transpose(jnp.concatenate(queries, axis=1))
        vg_t[...] = jnp.zeros_like(vg_t)
        kg_t[...] = jnp.zeros_like(kg_t)

    at_i = pl.ds(pl.multiple_of(i * blk, blk), blk)

    def column(j, acc):
        at_j = pl.ds(pl.multiple_of(j * blk, blk), blk)
        outs = []
        for h in range(heads):
            lanes = slice(h * DH, (h + 1) * DH)
            weight_grad = dot_nt(o_ref[at_i, lanes], acts_ref[at_j, head_columns(0, h)])
            score_grad = (weight_grad * score_slope_ref[h, :, at_j].astype(F32)).astype(BF)
            vg_t[lanes, at_j] += dot_nn(o_t[lanes, at_i], weights_ref[h, :, at_j])
            kg_t[lanes, at_j] += dot_nn(q_t[lanes, at_i], score_grad)
            outs.append(acc[h] + dot_nn(score_grad, acts_ref[at_j, head_columns(2, h)]))
        return tuple(outs)

    first = history_start(lengths_ref, users, i * blk) // blk
    zero = jnp.zeros((blk, DH), F32)
    acc = lax.fori_loop(first, i + 1, column, (zero,) * heads)
    qg[at_i, :] = jnp.concatenate(acc, axis=1)

    @pl.when(i == blocks - 1)
    def _():
        factor = 0.5 * scale / maxlen
        grads = [jnp.transpose(vg_t[...]) * (1.0 / maxlen), qg[...] * factor, jnp.transpose(kg_t[...]) * factor]
        pieces = [grads[kind][:, h * DH : (h + 1) * DH] for h in range(heads) for kind in range(3)]
        for n in range(3 * heads // 2):
            first_lane = n // 3 * 4 * PAIR + n % 3 * PAIR
            lanes = slice(first_lane, first_lane + PAIR)
            grad = jnp.concatenate(pieces[2 * n : 2 * n + 2], axis=1).astype(BF).astype(F32)
            grad_ref[:, lanes] = (grad * slopes_ref[:, lanes].astype(F32)).astype(BF)


def backward_attention(lengths, stats, mg, gate, head_outs, acts, slopes, weights, score_slope, blk, maxlen):
    positions, cols = mg.shape
    heads = cols // DH
    shards = len(stats)
    users = lengths.shape[1]
    elements = heads * positions * positions // 2
    whole = lambda i: (0, 0)
    return pl.pallas_call(
        functools.partial(backward_kernel, blk=blk, users=users, maxlen=maxlen, shards=shards),
        grid=(positions // blk,),
        in_specs=[pl.BlockSpec(memory_space=pltpu.SMEM)]
        + [pl.BlockSpec((8, positions), whole)] * shards
        + [
            pl.BlockSpec((positions, cols), whole),
            pl.BlockSpec((positions, cols), whole),
            pl.BlockSpec((positions, cols), whole),
            pl.BlockSpec((positions, 4 * cols), whole),
            pl.BlockSpec((positions, 4 * cols), whole),
            pl.BlockSpec((heads, blk, positions), lambda i: (0, i, 0)),
            pl.BlockSpec((heads, blk, positions), lambda i: (0, i, 0)),
        ],
        out_specs=[pl.BlockSpec((positions, 4 * cols), whole), pl.BlockSpec((positions, cols), whole)],
        out_shape=[
            jax.ShapeDtypeStruct((positions, 4 * cols), BF),
            jax.ShapeDtypeStruct((positions, cols), BF),
        ],
        scratch_shapes=[
            pltpu.VMEM((positions, cols), BF),
            pltpu.VMEM((cols, positions), BF),
            pltpu.VMEM((cols, positions), BF),
            pltpu.VMEM((cols, positions), F32),
            pltpu.VMEM((cols, positions), F32),
            pltpu.VMEM((positions, cols), F32),
        ],
        compiler_params=pltpu.CompilerParams(vmem_limit_bytes=VMEM_LIMIT),
        cost_estimate=pl.CostEstimate(
            flops=8 * elements * 256, bytes_accessed=4 * elements + 26 * positions * cols, transcendentals=0
        ),
        name="attention_backward",
    )(lengths, *stats, mg, gate, head_outs, acts, slopes, weights, score_slope)


def update_kernel(ids_ref, rows_ref, table_ref, accum_ref, new_table_ref, new_accum_ref):
    i = pl.program_id(0)
    blk = table_ref.shape[0]
    slots = rows_ref.shape[0]
    row = i * blk + lax.broadcasted_iota(jnp.int32, (blk, slots), 0)
    hits = jnp.where(row == ids_ref[...], 1.0, 0.0).astype(BF)
    grad = dot_nn(hits, rows_ref[...])
    accum = jnp.transpose(jnp.broadcast_to(accum_ref[...], (128, blk)))[:, :1] + jnp.mean(grad * grad, axis=1, keepdims=True)
    new_accum_ref[...] = jnp.transpose(jnp.broadcast_to(accum, (blk, 128)))[:1, :]
    new_table_ref[...] = table_ref[...] - LEARN_RATE * grad * lax.rsqrt(accum)


def update_rows(got_ids, got_rows, emb_table, row_accum):
    rows_own = emb_table.shape[0]
    slots = got_rows.shape[0]
    blk = min(256, rows_own)
    new_table, new_accum = pl.pallas_call(
        update_kernel,
        grid=(rows_own // blk,),
        in_specs=[
            pl.BlockSpec((1, slots), lambda i: (0, 0)),
            pl.BlockSpec((slots, D), lambda i: (0, 0)),
            pl.BlockSpec((blk, D), lambda i: (i, 0)),
            pl.BlockSpec((1, blk), lambda i: (0, i)),
        ],
        out_specs=[
            pl.BlockSpec((blk, D), lambda i: (i, 0)),
            pl.BlockSpec((1, blk), lambda i: (0, i)),
        ],
        out_shape=[
            jax.ShapeDtypeStruct((rows_own, D), F32),
            jax.ShapeDtypeStruct((1, rows_own), F32),
        ],
        compiler_params=pltpu.CompilerParams(vmem_limit_bytes=VMEM_LIMIT),
        cost_estimate=pl.CostEstimate(
            flops=2 * rows_own * slots * D, bytes_accessed=8 * rows_own * D + 2 * slots * D, transcendentals=rows_own
        ),
        name="update_rows",
    )(got_ids.reshape(1, slots), got_rows, emb_table, row_accum.reshape(1, rows_own))
    return new_table, new_accum.reshape(rows_own)


def own_weights(w_attn, w_gate, part, pairs):
    slices = []
    for p in range(pairs):
        at = part * pairs + p
        slices.append(lax.dynamic_slice_in_dim(w_attn, at * 3 * PAIR, 3 * PAIR, 1))
        slices.append(lax.dynamic_slice_in_dim(w_gate, at * PAIR, PAIR, 1))
    return jnp.concatenate(slices, axis=1)


def attn_and_gate(proj, pairs):
    pieces = [proj[:, p * 4 * PAIR : (p + 1) * 4 * PAIR] for p in range(pairs)]
    attn = jnp.concatenate([piece[:, : 3 * PAIR] for piece in pieces], axis=1)
    return attn, jnp.concatenate([piece[:, 3 * PAIR :] for piece in pieces], axis=1)


def row_slots(owners, devices, capacity):
    events = owners.shape[0]
    owner_hits = (owners[:, None] == jnp.arange(devices, dtype=jnp.int32)[None, :]).astype(BF)
    place = jnp.arange(events, dtype=jnp.int32)
    before = (place[:, None] > place[None, :]).astype(BF)
    earlier = jnp.dot(before, owner_hits, preferred_element_type=F32)
    return owners * capacity + jnp.sum(earlier * owner_hits.astype(F32), axis=1).astype(jnp.int32)


def slot_table(flat_slot, slots):
    return jnp.arange(slots, dtype=jnp.int32)[:, None] == flat_slot[None, :]


def to_owners(rows, devices, capacity):
    shape = (devices, capacity) + rows.shape[1:]
    got = lax.all_to_all(rows.reshape(shape), ("seq", "dp"), split_axis=0, concat_axis=0, tiled=True)
    return got.reshape(rows.shape)


def ids_to_owners(flat_slot, item_row, rows_own, devices, capacity):
    filled = slot_table(flat_slot, devices * capacity)
    ids = jnp.min(jnp.where(filled, item_row[None, :], rows_own), axis=1).astype(jnp.int32)
    return to_owners(ids, devices, capacity)


def rows_by_slot(flat_slot, input_grad, slots):
    filled = slot_table(flat_slot, slots).astype(BF)
    return jnp.dot(filled, input_grad.astype(BF), preferred_element_type=F32).astype(BF)


TN = (((0,), (0,)), ((), ()))


def dot_tn(a, b):
    return lax.dot_general(a, b, TN, preferred_element_type=F32)


def body_whole(
    layer_input, out_grad, lengths, item_owner, item_row, w_attn, w_gate, w_out, emb_table, row_accum
):
    seq_count = lax.axis_size("seq")
    dp_count = lax.axis_size("dp")
    devices = seq_count * dp_count
    seq_id = lax.axis_index("seq")
    tokens_dev = layer_input.shape[0]
    positions = tokens_dev * seq_count
    maxlen = 2 * positions // 3
    blk = min(256, positions)
    cols = D // seq_count
    pairs = cols // PAIR
    capacity = max(2, 2 * tokens_dev // devices)

    w_own = own_weights(w_attn, w_gate, seq_id, pairs)
    w_out_own = lax.dynamic_slice_in_dim(w_out, seq_id * cols, cols, 0)
    flat_slot = row_slots(item_owner[:, 0], devices, capacity)
    got_ids = ids_to_owners(flat_slot, item_row, emb_table.shape[0], devices, capacity)

    x_full = lax.all_gather(layer_input, "seq", axis=0, tiled=True)
    og_full = lax.all_gather(out_grad, "seq", axis=0, tiled=True)
    order = jnp.arange(positions // blk, dtype=jnp.int32)
    acts, slopes, gate, weights, score_slope, heads = forward_attention(
        lengths, order, [x_full], w_own, blk, maxlen
    )
    mg = dot_nt(og_full, w_out_own).astype(BF)
    mg, stats_own = event_stats(jnp.zeros((1,), jnp.int32), [mg], gate, heads)
    stats = lax.all_gather(stats_own, "seq", axis=0, tiled=False)
    grads, mixed = backward_attention(
        lengths, [stats[s] for s in range(seq_count)], mg, gate, heads, acts, slopes, weights, score_slope, blk, maxlen
    )

    input_part = dot_nt(grads, w_own).astype(BF)
    got = lax.all_to_all(
        input_part.reshape(seq_count, tokens_dev, D), "seq", split_axis=0, concat_axis=0, tiled=True
    )
    input_grad = jnp.sum(got.astype(F32), axis=0) + out_grad.astype(F32)
    got_rows = to_owners(rows_by_slot(flat_slot, input_grad, devices * capacity), devices, capacity)
    new_table, new_accum = update_rows(got_ids, got_rows, emb_table, row_accum)

    out_part = dot_tn(mixed, og_full).astype(BF)
    share = dp_count // seq_count
    out_part = out_part.reshape(share, D // dp_count, seq_count, cols).transpose(0, 2, 1, 3).reshape(D, cols)
    merged = jnp.concatenate([dot_tn(x_full, grads).astype(BF), out_part], axis=1)
    merged = lax.psum_scatter(merged, "dp", scatter_dimension=0, tiled=True)
    steps = []
    for s in range(seq_count):
        for piece in range(dp_count):
            part, target = divmod(piece, seq_count)
            steps.append((s * dp_count + piece, target * dp_count + s * share + part))
    grad_out = lax.ppermute(merged[:, 4 * cols :], ("seq", "dp"), steps).astype(F32)
    grad_attn, grad_gate = attn_and_gate(merged[:, : 4 * cols].astype(F32), pairs)
    return (grad_attn, grad_gate, grad_out, new_table, new_accum)


SEQ = 4
PLANE = 4


def send(array, target):
    steps = []
    for s in range(SEQ):
        for e in range(PLANE):
            for c in range(2):
                to = target(s, e, c)
                if to is not None:
                    steps.append((s * 2 * PLANE + 2 * e + c, to[0] * 2 * PLANE + 2 * to[1] + to[2]))
    return lax.ppermute(array, ("seq", "dp"), steps)


def home(s, c):
    return c == s // 2


def swap_far(array):
    return send(array, lambda s, e, c: None if home(s, c) else (3 - s, e, 1 - c))


def fetch_near(array):
    return send(array, lambda s, e, c: (s ^ 1, e, c) if home(s, c) else ((3 - s) ^ 1, e, 1 - c))


def swap_near(array):
    return send(array, lambda s, e, c: (s ^ 1, e, c))


def swap_core(array):
    return send(array, lambda s, e, c: (s, e, 1 - c))


def swap_x(array):
    return send(array, lambda s, e, c: (s, e ^ 1, c))


def swap_y(array):
    return send(array, lambda s, e, c: (s, e ^ 2, c))


def tie(*arrays):
    return lax.optimization_barrier(arrays)


def halves(array, bit, axis):
    kept = lax.dynamic_index_in_dim(array, bit, axis, keepdims=False)
    sent = lax.dynamic_index_in_dim(array, 1 - bit, axis, keepdims=False)
    return kept, sent


def body_pairs(
    layer_input, out_grad, lengths, item_owner, item_row, w_attn, w_gate, w_out, emb_table, row_accum
):
    devices = 2 * PLANE * SEQ
    s = lax.axis_index("seq")
    d = lax.axis_index("dp")
    e, c = d // 2, d % 2
    y, x = e // 2, e % 2
    tokens_dev = layer_input.shape[0]
    positions = tokens_dev * SEQ
    maxlen = 2 * positions // 3
    blk = min(256, positions)
    cols = D // SEQ
    pairs = cols // PAIR
    rows_own = emb_table.shape[0]
    capacity = max(2, 2 * tokens_dev // devices)
    at_home = c == s // 2
    part = 2 * (s % 2) + c

    def block_of(seq, core):
        return jnp.where(core == seq // 2, seq, 3 - seq)

    mine_at, near_at = block_of(s, c), block_of(s ^ 1, c)
    core_at, diag_at = block_of(s, 1 - c), block_of(s ^ 1, 1 - c)
    order = jnp.stack([mine_at, near_at, core_at, diag_at]).astype(jnp.int32)

    x_far = swap_far(layer_input)
    x_near = fetch_near(layer_input)
    users = lengths.shape[1]
    flat_slot = row_slots(item_owner[:, 0], devices, capacity)
    small = jnp.concatenate([flat_slot[None, :], jnp.pad(lengths, ((0, 0), (0, 128 - users)))], axis=1)
    small = jnp.where(at_home, small, swap_far(small))
    lengths = small[:, tokens_dev : tokens_dev + users]
    got_ids = ids_to_owners(flat_slot, item_row, rows_own, devices, capacity)
    w_own = own_weights(w_attn, w_gate, part, pairs)
    mg_own = dot_nt(out_grad, w_out).astype(BF)
    mg_sent = [lax.dynamic_slice_in_dim(mg_own, (s + k) % SEQ * cols, cols, 1) for k in range(SEQ)]
    x_far, x_near, w_own, lengths, got_ids, *mg_sent = tie(x_far, x_near, w_own, lengths, got_ids, *mg_sent)
    x_here = jnp.concatenate([jnp.where(at_home, layer_input, x_far), x_near], axis=0)
    x_there = swap_core(x_here)
    x_here, *mg_sent = tie(x_here, *mg_sent)
    mg_blocks = []
    for k, piece in enumerate(mg_sent):
        mg_blocks.append(send(piece, lambda s, e, c: (2 * c + (s + k) % SEQ // 2, e, (s + k) % SEQ % 2)))
    mg_order = jnp.stack([(part - k) % SEQ for k in range(SEQ)]).astype(jnp.int32)

    x_full, acts, slopes, gate, weights, score_slope, heads = forward_attention(
        lengths, order, [x_here, x_there], w_own, blk, maxlen
    )
    heads, *mg_blocks = tie(heads, *mg_blocks)
    mg, stats_own = event_stats(mg_order, mg_blocks, gate, heads)
    stats = [
        stats_own,
        swap_core(stats_own),
        swap_near(stats_own),
        send(stats_own, lambda s, e, c: (s ^ 1, e, 1 - c)),
    ]
    *stats, og_own = tie(*stats, out_grad)
    og_far = swap_far(og_own)
    og_near = fetch_near(og_own)
    grads, mixed = backward_attention(
        lengths, stats, mg, gate, heads, acts, slopes, weights, score_slope, blk, maxlen
    )

    def input_part(grads, block, columns=slice(None)):
        return dot_nt(lax.dynamic_slice_in_dim(grads, block * tokens_dev, tokens_dev, 0), w_own[columns])

    og_far, og_near, grads = tie(og_far, og_near, grads)
    from_diag, near_sums, from_near = [], [], []
    column_halves = (slice(0, D // 2), slice(D // 2, D))
    for columns in column_halves:
        from_diag.append(swap_core(input_part(grads, diag_at, columns).astype(BF)))
    for columns, got in zip(column_halves, from_diag):
        near_sums.append((input_part(grads, near_at, columns) + got.astype(F32)).astype(BF))
        from_near.append(swap_near(near_sums[-1]))
    *near_sums, grads, og_far, og_near = tie(*near_sums, grads, og_far, og_near)
    core_part = input_part(grads, core_at).astype(BF)
    from_core = swap_core(core_part)
    og_mine = jnp.where(at_home, out_grad, og_far)
    input_grad = input_part(grads, mine_at) + og_mine.astype(F32)

    core_part, grads, mixed = tie(core_part, grads, mixed)
    half = 5 * cols // 2
    rest = 4 * cols - half
    proj = dot_tn(x_full, grads).astype(BF).reshape(2, 2, D // PLANE, 4 * cols)
    a_kept, a_sent = halves(proj[..., :half], x, 1)
    b_kept, b_sent = halves(proj[..., half:], y, 0)
    a_got = swap_x(a_sent)
    og_here = jnp.concatenate([og_mine, og_near], axis=0)
    og_there = swap_core(og_here)
    a_sent, mixed = tie(a_sent, mixed)
    mixed_rows = [lax.dynamic_slice_in_dim(mixed, at * tokens_dev, tokens_dev, 0) for at in (mine_at, near_at, core_at, diag_at)]
    out_part = dot_tn(jnp.concatenate(mixed_rows[:2], axis=0), og_here)
    out_part = (out_part + dot_tn(jnp.concatenate(mixed_rows[2:], axis=0), og_there)).astype(BF)

    def picked(bit, low, high):
        return jnp.where(bit == 0, low, high)

    def b_message(rows, out):
        return jnp.concatenate([rows[0], rows[1], out], axis=1)

    low, high = out_part[:, : D // 2], out_part[:, D // 2 :]
    b_kept = b_message(b_kept, picked(y, low, high))
    b_sent = b_message(b_sent, picked(y, high, low))
    b_got = swap_y(b_sent)

    input_grad = input_grad + from_core.astype(F32) + jnp.concatenate(from_near, axis=1).astype(F32)
    got_rows = to_owners(rows_by_slot(small[0, :tokens_dev], input_grad, devices * capacity), devices, capacity)

    a = (a_kept.astype(F32) + a_got.astype(F32)).astype(BF)
    a_kept, a_sent = halves(a, y, 0)
    a_got = swap_y(a_sent)
    b = (b_kept.astype(F32) + b_got.astype(F32)).astype(BF)
    b0 = jnp.concatenate([b[:, :rest], b[:, 2 * rest : 2 * rest + cols]], axis=1)
    b1 = jnp.concatenate([b[:, rest : 2 * rest], b[:, 2 * rest + cols :]], axis=1)
    b_got = swap_x(picked(x, b1, b0))
    a = (a_kept.astype(F32) + a_got.astype(F32)).astype(BF)
    b = (picked(x, b0, b1).astype(F32) + b_got.astype(F32)).astype(BF)

    def last(array, target):
        pieces = array.reshape(2, D // (2 * PLANE), array.shape[1])
        one, other = halves(pieces, s // 2, 0)
        one = send(one, lambda s, e, c: target(s, e, c, s // 2))
        return one, send(other, lambda s, e, c: target(s, e, c, 1 - s // 2))

    proj = last(jnp.concatenate([a, b[:, :rest]], axis=1), lambda s, e, c, piece: (2 * (s % 2) + c, e, piece))
    out = last(b[:, rest:], lambda s, e, c, piece: (e, 2 * (s % 2) + c, piece))
    ids = got_ids.reshape(SEQ, PLANE, 2, capacity)
    at_seq = jnp.arange(SEQ, dtype=jnp.int32)[:, None, None, None]
    at_core = jnp.arange(2, dtype=jnp.int32)[None, None, :, None]
    ids = jnp.where(at_core == at_seq // 2, ids, ids[::-1, :, ::-1])
    new_table, new_accum = update_rows(ids, got_rows, emb_table, row_accum)
    *proj, new_accum = tie(*proj, new_accum)
    grad_attn, grad_gate = attn_and_gate(proj[0].astype(F32) + proj[1].astype(F32), pairs)
    return (grad_attn, grad_gate, out[0].astype(F32) + out[1].astype(F32), new_table, new_accum)


def solution(mesh):
    placed = (
        P(("dp", "seq"), None),
        P(("dp", "seq"), None),
        P("dp", None),
        P(("dp", "seq"), None),
        P(("dp", "seq")),
        P(),
        P(),
        P(),
        P(("seq", "dp"), None),
        P(("seq", "dp")),
    )
    paired = mesh.shape["seq"] == SEQ and mesh.shape["dp"] == 2 * PLANE
    return jax.shard_map(
        body_pairs if paired else body_whole,
        mesh=mesh,
        in_specs=placed,
        out_specs=(
            P("dp", "seq"),
            P("dp", "seq"),
            P("dp", "seq"),
            P(("seq", "dp"), None),
            P(("seq", "dp")),
        ),
        check_vma=False,
    )
```

```python
import functools

import jax
import jax.numpy as jnp
from jax import lax
from jax.experimental import pallas as pl
from jax.experimental.pallas import tpu as pltpu
from jax.sharding import PartitionSpec as P

D = 1024
H = 16
DH = 64
PAIR = 2 * DH

NORM_EPS = 1e-05
LEARN_RATE = 0.1
VMEM_LIMIT = 56 * 1024 * 1024
BF = jnp.bfloat16
F32 = jnp.float32


def dot_nn(a, b):
    return lax.dot_general(a, b, (((1,), (0,)), ((), ())), preferred_element_type=F32)


def dot_nt(a, b):
    return lax.dot_general(a, b, (((1,), (1,)), ((), ())), preferred_element_type=F32)


def history_start(lengths_ref, users, place):
    start = jnp.zeros_like(place)
    end = jnp.int32(0)
    for user in range(users - 1):
        end = end + lengths_ref[0, user]
        start = jnp.where(place >= end, end, start)
    return start


def head_columns(kind, head):
    first = head // 2 * 4 * PAIR + head % 2 * 3 * DH + kind * DH
    return slice(first, first + DH)


def gate_columns(pair):
    return slice(pair * 4 * PAIR + 3 * PAIR, (pair + 1) * 4 * PAIR)


def forward_kernel(*refs, blk, users, maxlen, count):
    lengths_ref, order_ref = refs[:2]
    x_refs = refs[2 : 2 + count]
    w_ref = refs[2 + count]
    outs = refs[3 + count :]
    if count > 1:
        x_out_ref, outs = outs[0], outs[1:]
    acts_ref, slopes_ref, gate_ref, weights_ref, score_slope_ref, heads_ref = outs
    i = pl.program_id(0)
    heads = weights_ref.shape[0]
    chunks = x_refs[0].shape[0] // blk

    @pl.when(i == 0)
    def _():
        for b in range(count):
            for r in range(chunks):
                at = pl.ds(pl.multiple_of(order_ref[b * chunks + r] * blk, blk), blk)
                x = x_refs[b][r * blk : (r + 1) * blk, :]
                if count > 1:
                    x_out_ref[at, :] = x
                for p in range(heads // 2):
                    lanes = slice(p * 4 * PAIR, (p + 1) * 4 * PAIR)
                    half = 0.5 * dot_nn(x, w_ref[:, lanes])
                    t = jnp.tanh(half)
                    prod = half * t
                    silu = half + prod
                    acts_ref[at, lanes] = silu.astype(BF)
                    gate_ref[at, p * PAIR : (p + 1) * PAIR] = silu[:, 3 * PAIR :]
                    slopes_ref[at, lanes] = (0.5 * (1.0 + t) * (1.0 + half - prod)).astype(BF)

    at_i = pl.ds(pl.multiple_of(i * blk, blk), blk)
    q_half = [acts_ref[at_i, head_columns(1, h)] * jnp.asarray(0.5 * DH**-0.5, BF) for h in range(heads)]
    row = i * blk + lax.broadcasted_iota(jnp.int32, (blk, blk), 0)
    col0 = lax.broadcasted_iota(jnp.int32, (blk, blk), 1)
    start = history_start(lengths_ref, users, row)

    def column(j, acc):
        at_j = pl.ds(pl.multiple_of(j * blk, blk), blk)
        col = col0 + j * blk
        allowed = (col <= row) & (col >= start)
        outs = []
        for h in range(heads):
            half = dot_nt(q_half[h], acts_ref[at_j, head_columns(2, h)])
            half = jnp.where(allowed, half, -64.0)
            t = jnp.tanh(half)
            p = half * t
            weights = (half + p).astype(BF)
            weights_ref[h, :, at_j] = weights
            score_slope_ref[h, :, at_j] = ((1.0 + t) * (1.0 + half - p)).astype(BF)
            outs.append(acc[h] + dot_nn(weights, acts_ref[at_j, head_columns(0, h)]))
        return tuple(outs)

    first = history_start(lengths_ref, users, i * blk) // blk
    zero = jnp.zeros((blk, DH), F32)
    acc = lax.fori_loop(first, i + 1, column, (zero,) * heads)
    heads_ref[...] = (jnp.concatenate(acc, axis=1) * (1.0 / maxlen)).astype(BF)


def forward_attention(lengths, order, x_blocks, w_own, blk, maxlen):
    count = len(x_blocks)
    block_rows = x_blocks[0].shape[0]
    positions = count * block_rows
    cols = w_own.shape[1] // 4
    heads = cols // DH
    users = lengths.shape[1]
    elements = heads * positions * positions // 2
    whole = lambda i: (0, 0)
    out_specs = [
        pl.BlockSpec((positions, 4 * cols), whole),
        pl.BlockSpec((positions, 4 * cols), whole),
        pl.BlockSpec((positions, cols), whole),
        pl.BlockSpec((heads, blk, positions), lambda i: (0, i, 0)),
        pl.BlockSpec((heads, blk, positions), lambda i: (0, i, 0)),
        pl.BlockSpec((blk, cols), lambda i: (i, 0)),
    ]
    out_shape = [
        jax.ShapeDtypeStruct((positions, 4 * cols), BF),
        jax.ShapeDtypeStruct((positions, 4 * cols), BF),
        jax.ShapeDtypeStruct((positions, cols), F32),
        jax.ShapeDtypeStruct((heads, positions, positions), BF),
        jax.ShapeDtypeStruct((heads, positions, positions), BF),
        jax.ShapeDtypeStruct((positions, cols), BF),
    ]
    if count > 1:
        out_specs = [pl.BlockSpec((positions, D), whole)] + out_specs
        out_shape = [jax.ShapeDtypeStruct((positions, D), BF)] + out_shape
    return pl.pallas_call(
        functools.partial(forward_kernel, blk=blk, users=users, maxlen=maxlen, count=count),
        grid=(positions // blk,),
        in_specs=[pl.BlockSpec(memory_space=pltpu.SMEM), pl.BlockSpec(memory_space=pltpu.SMEM)]
        + [pl.BlockSpec((block_rows, D), whole)] * count
        + [pl.BlockSpec((D, 4 * cols), whole)],
        out_specs=out_specs,
        out_shape=out_shape,
        compiler_params=pltpu.CompilerParams(vmem_limit_bytes=VMEM_LIMIT),
        cost_estimate=pl.CostEstimate(
            flops=8 * positions * D * cols + 4 * elements * 256,
            bytes_accessed=4 * positions * D + 4 * elements,
            transcendentals=elements,
        ),
        name="attention_forward",
    )(lengths, order, *x_blocks, w_own)


def stats_kernel(*refs, count):
    order_ref = refs[0]
    mg_refs = refs[1 : 1 + count]
    gate_ref, heads_ref, mg_out_ref, stats_ref = refs[1 + count :]
    blocks = order_ref.shape[0]
    rows = gate_ref.shape[0] // blocks
    chunks = blocks // count
    for b in range(blocks):
        at = pl.ds(pl.multiple_of(order_ref[b] * rows, rows), rows)
        mg = mg_refs[b // chunks][b % chunks * rows : (b % chunks + 1) * rows, :]
        mg_out_ref[at, :] = mg
        ng = mg.astype(F32) * gate_ref[at, :]
        heads = heads_ref[at, :].astype(F32)
        mean = jnp.mean(heads, axis=1, keepdims=True)
        centred = heads - mean
        square = jnp.sum(centred * centred, axis=1, keepdims=True)
        total = jnp.sum(ng, axis=1, keepdims=True)
        cross = jnp.sum(ng * centred, axis=1, keepdims=True)
        lane = lax.broadcasted_iota(jnp.int32, (rows, 128), 1)
        packed = jnp.where(lane == 0, mean, jnp.where(lane == 1, square, jnp.where(lane == 2, total, cross)))
        stats_ref[:, at] = jnp.transpose(packed)[:8, :]


def event_stats(order, mg_blocks, gate, heads):
    positions, cols = heads.shape
    count = len(mg_blocks)
    vmem = pl.BlockSpec(memory_space=pltpu.VMEM)
    return pl.pallas_call(
        functools.partial(stats_kernel, count=count),
        in_specs=[pl.BlockSpec(memory_space=pltpu.SMEM)] + [vmem] * (count + 2),
        out_specs=[vmem, vmem],
        out_shape=[
            jax.ShapeDtypeStruct((positions, cols), BF),
            jax.ShapeDtypeStruct((8, positions), F32),
        ],
        compiler_params=pltpu.CompilerParams(vmem_limit_bytes=VMEM_LIMIT),
        cost_estimate=pl.CostEstimate(flops=20 * positions * cols, bytes_accessed=10 * positions * cols, transcendentals=0),
        name="event_stats",
    )(order, *mg_blocks, gate, heads)


def combined_stats(stats_refs, cols):
    shards = len(stats_refs)
    positions = stats_refs[0].shape[1]
    means = [ref[0:1, :] for ref in stats_refs]
    mean = sum(means) * (1.0 / shards)
    square = jnp.zeros_like(mean)
    total = jnp.zeros_like(mean)
    cross = jnp.zeros_like(mean)
    for s, ref in enumerate(stats_refs):
        shift = means[s] - mean
        part = ref[2:3, :]
        square = square + ref[1:2, :] + cols * shift * shift
        total = total + part
        cross = cross + ref[3:4, :] + shift * part
    inv_dev = lax.rsqrt(square * (1.0 / D) + NORM_EPS)
    kind = lax.broadcasted_iota(jnp.int32, (128, positions), 0)
    rest = jnp.where(kind == 2, total * (1.0 / D), cross * inv_dev * (1.0 / D))
    packed = jnp.where(kind == 0, mean, jnp.where(kind == 1, inv_dev, rest))
    per_event = jnp.transpose(packed)
    return [per_event[:, k : k + 1] for k in range(4)]


def backward_kernel(*refs, blk, users, maxlen, shards):
    lengths_ref = refs[0]
    stats_refs = refs[1 : 1 + shards]
    mg_ref, gate_ref, heads_ref, acts_ref, slopes_ref, weights_ref, score_slope_ref = refs[1 + shards : 8 + shards]
    grad_ref, mixed_ref, o_ref, o_t, q_t, vg_t, kg_t, qg = refs[8 + shards :]
    i = pl.program_id(0)
    positions, cols = o_ref.shape
    heads = cols // DH
    blocks = positions // blk
    scale = DH ** (-0.5)

    @pl.when(i == 0)
    def _():
        mean, inv_dev, total, cross = combined_stats(stats_refs, cols)
        for p in range(heads // 2):
            lanes = slice(p * PAIR, (p + 1) * PAIR)
            normed = (heads_ref[:, lanes].astype(F32) - mean) * inv_dev
            gate = gate_ref[:, lanes]
            mg = mg_ref[:, lanes].astype(F32)
            mixed_ref[:, lanes] = (normed * gate).astype(BF)
            gate_slope = slopes_ref[:, gate_columns(p)].astype(F32)
            grad_ref[:, gate_columns(p)] = (mg * normed * gate_slope).astype(BF)
            o_ref[:, lanes] = (inv_dev * (mg * gate - total - normed * cross)).astype(BF)
        o_t[...] = jnp.transpose(o_ref[...])
        queries = [acts_ref[:, head_columns(1, h)] for h in range(heads)]
        q_t[...] = jnp.transpose(jnp.concatenate(queries, axis=1))
        vg_t[...] = jnp.zeros_like(vg_t)
        kg_t[...] = jnp.zeros_like(kg_t)

    at_i = pl.ds(pl.multiple_of(i * blk, blk), blk)

    def column(j, acc):
        at_j = pl.ds(pl.multiple_of(j * blk, blk), blk)
        outs = []
        for h in range(heads):
            lanes = slice(h * DH, (h + 1) * DH)
            weight_grad = dot_nt(o_ref[at_i, lanes], acts_ref[at_j, head_columns(0, h)])
            score_grad = (weight_grad * score_slope_ref[h, :, at_j].astype(F32)).astype(BF)
            vg_t[lanes, at_j] += dot_nn(o_t[lanes, at_i], weights_ref[h, :, at_j])
            kg_t[lanes, at_j] += dot_nn(q_t[lanes, at_i], score_grad)
            outs.append(acc[h] + dot_nn(score_grad, acts_ref[at_j, head_columns(2, h)]))
        return tuple(outs)

    first = history_start(lengths_ref, users, i * blk) // blk
    zero = jnp.zeros((blk, DH), F32)
    acc = lax.fori_loop(first, i + 1, column, (zero,) * heads)
    qg[at_i, :] = jnp.concatenate(acc, axis=1)

    @pl.when(i == blocks - 1)
    def _():
        factor = 0.5 * scale / maxlen
        grads = [jnp.transpose(vg_t[...]) * (1.0 / maxlen), qg[...] * factor, jnp.transpose(kg_t[...]) * factor]
        pieces = [grads[kind][:, h * DH : (h + 1) * DH] for h in range(heads) for kind in range(3)]
        for n in range(3 * heads // 2):
            first_lane = n // 3 * 4 * PAIR + n % 3 * PAIR
            lanes = slice(first_lane, first_lane + PAIR)
            grad = jnp.concatenate(pieces[2 * n : 2 * n + 2], axis=1).astype(BF).astype(F32)
            grad_ref[:, lanes] = (grad * slopes_ref[:, lanes].astype(F32)).astype(BF)


def backward_attention(lengths, stats, mg, gate, head_outs, acts, slopes, weights, score_slope, blk, maxlen):
    positions, cols = mg.shape
    heads = cols // DH
    shards = len(stats)
    users = lengths.shape[1]
    elements = heads * positions * positions // 2
    whole = lambda i: (0, 0)
    return pl.pallas_call(
        functools.partial(backward_kernel, blk=blk, users=users, maxlen=maxlen, shards=shards),
        grid=(positions // blk,),
        in_specs=[pl.BlockSpec(memory_space=pltpu.SMEM)]
        + [pl.BlockSpec((8, positions), whole)] * shards
        + [
            pl.BlockSpec((positions, cols), whole),
            pl.BlockSpec((positions, cols), whole),
            pl.BlockSpec((positions, cols), whole),
            pl.BlockSpec((positions, 4 * cols), whole),
            pl.BlockSpec((positions, 4 * cols), whole),
            pl.BlockSpec((heads, blk, positions), lambda i: (0, i, 0)),
            pl.BlockSpec((heads, blk, positions), lambda i: (0, i, 0)),
        ],
        out_specs=[pl.BlockSpec((positions, 4 * cols), whole), pl.BlockSpec((positions, cols), whole)],
        out_shape=[
            jax.ShapeDtypeStruct((positions, 4 * cols), BF),
            jax.ShapeDtypeStruct((positions, cols), BF),
        ],
        scratch_shapes=[
            pltpu.VMEM((positions, cols), BF),
            pltpu.VMEM((cols, positions), BF),
            pltpu.VMEM((cols, positions), BF),
            pltpu.VMEM((cols, positions), F32),
            pltpu.VMEM((cols, positions), F32),
            pltpu.VMEM((positions, cols), F32),
        ],
        compiler_params=pltpu.CompilerParams(vmem_limit_bytes=VMEM_LIMIT),
        cost_estimate=pl.CostEstimate(
            flops=8 * elements * 256, bytes_accessed=4 * elements + 26 * positions * cols, transcendentals=0
        ),
        name="attention_backward",
    )(lengths, *stats, mg, gate, head_outs, acts, slopes, weights, score_slope)


def update_kernel(rows_ref, table_ref, accum_ref, new_table_ref, new_accum_ref, ids):
    i = pl.program_id(0)
    blk = table_ref.shape[0]
    slots = rows_ref.shape[0]

    @pl.when(i == 0)
    def _():
        numbers = jnp.transpose(rows_ref[:, D:].astype(F32))
        ids[...] = (numbers[0:1, :] * 256.0 + numbers[1:2, :]).astype(jnp.int32)

    row = i * blk + lax.broadcasted_iota(jnp.int32, (blk, slots), 0)
    hits = jnp.where(row == ids[...], 1.0, 0.0).astype(BF)
    grad = dot_nn(hits, rows_ref[:, :D])
    accum = jnp.transpose(jnp.broadcast_to(accum_ref[...], (128, blk)))[:, :1] + jnp.mean(grad * grad, axis=1, keepdims=True)
    new_accum_ref[...] = jnp.transpose(jnp.broadcast_to(accum, (blk, 128)))[:1, :]
    new_table_ref[...] = table_ref[...] - LEARN_RATE * grad * lax.rsqrt(accum)


def update_rows(got_rows, emb_table, row_accum):
    rows_own = emb_table.shape[0]
    slots = got_rows.shape[0]
    blk = min(256, rows_own)
    new_table, new_accum = pl.pallas_call(
        update_kernel,
        grid=(rows_own // blk,),
        in_specs=[
            pl.BlockSpec((slots, D + 128), lambda i: (0, 0)),
            pl.BlockSpec((blk, D), lambda i: (i, 0)),
            pl.BlockSpec((1, blk), lambda i: (0, i)),
        ],
        out_specs=[
            pl.BlockSpec((blk, D), lambda i: (i, 0)),
            pl.BlockSpec((1, blk), lambda i: (0, i)),
        ],
        out_shape=[
            jax.ShapeDtypeStruct((rows_own, D), F32),
            jax.ShapeDtypeStruct((1, rows_own), F32),
        ],
        scratch_shapes=[pltpu.VMEM((1, slots), jnp.int32)],
        compiler_params=pltpu.CompilerParams(vmem_limit_bytes=VMEM_LIMIT),
        cost_estimate=pl.CostEstimate(
            flops=2 * rows_own * slots * D, bytes_accessed=8 * rows_own * D + 2 * slots * D, transcendentals=rows_own
        ),
        name="update_rows",
    )(got_rows, emb_table, row_accum.reshape(1, rows_own))
    return new_table, new_accum.reshape(rows_own)


def own_weights(w_attn, w_gate, part, pairs):
    slices = []
    for p in range(pairs):
        at = part * pairs + p
        slices.append(lax.dynamic_slice_in_dim(w_attn, at * 3 * PAIR, 3 * PAIR, 1))
        slices.append(lax.dynamic_slice_in_dim(w_gate, at * PAIR, PAIR, 1))
    return jnp.concatenate(slices, axis=1)


def attn_and_gate(proj, pairs):
    pieces = [proj[:, p * 4 * PAIR : (p + 1) * 4 * PAIR] for p in range(pairs)]
    attn = jnp.concatenate([piece[:, : 3 * PAIR] for piece in pieces], axis=1)
    return attn, jnp.concatenate([piece[:, 3 * PAIR :] for piece in pieces], axis=1)


def row_slots(owners, rows, devices, capacity):
    events = owners.shape[0]
    owner_hits = (owners[:, None] == jnp.arange(devices, dtype=jnp.int32)[None, :]).astype(BF)
    place = jnp.arange(events, dtype=jnp.int32)
    before = (place[:, None] > place[None, :]).astype(BF)
    earlier = jnp.dot(before, owner_hits, preferred_element_type=F32)
    slots = jnp.sum(earlier * owner_hits.astype(F32), axis=1).astype(jnp.int32)
    flat_slot = owners * capacity + slots
    slot_hits = jnp.arange(devices * capacity, dtype=jnp.int32)[:, None] == flat_slot[None, :]
    lane = jnp.arange(128, dtype=jnp.int32)[None, :]
    numbers = jnp.where(lane == 0, rows[:, None] // 256, jnp.where(lane == 1, rows[:, None] % 256, 0))
    return slot_hits.astype(BF), numbers.astype(BF)


def rows_by_slot(slot_matrix, input_grad, numbers):
    rows = jnp.concatenate([input_grad.astype(BF), numbers], axis=1)
    return jnp.dot(slot_matrix, rows, preferred_element_type=F32).astype(BF)


def to_owners(rows, devices, capacity):
    shape = (devices, capacity) + rows.shape[1:]
    got = lax.all_to_all(rows.reshape(shape), ("seq", "dp"), split_axis=0, concat_axis=0, tiled=True)
    return got.reshape(rows.shape)


TN = (((0,), (0,)), ((), ()))


def dot_tn(a, b):
    return lax.dot_general(a, b, TN, preferred_element_type=F32)


def body_whole(
    layer_input, out_grad, lengths, item_owner, item_row, w_attn, w_gate, w_out, emb_table, row_accum
):
    seq_count = lax.axis_size("seq")
    dp_count = lax.axis_size("dp")
    devices = seq_count * dp_count
    seq_id = lax.axis_index("seq")
    tokens_dev = layer_input.shape[0]
    positions = tokens_dev * seq_count
    maxlen = 2 * positions // 3
    blk = min(256, positions)
    cols = D // seq_count
    pairs = cols // PAIR
    capacity = max(2, 2 * tokens_dev // devices)

    w_own = own_weights(w_attn, w_gate, seq_id, pairs)
    w_out_own = lax.dynamic_slice_in_dim(w_out, seq_id * cols, cols, 0)
    slot_matrix, numbers = row_slots(item_owner[:, 0], item_row, devices, capacity)

    x_full = lax.all_gather(layer_input, "seq", axis=0, tiled=True)
    og_full = lax.all_gather(out_grad, "seq", axis=0, tiled=True)
    order = jnp.arange(positions // blk, dtype=jnp.int32)
    acts, slopes, gate, weights, score_slope, heads = forward_attention(
        lengths, order, [x_full], w_own, blk, maxlen
    )
    mg = dot_nt(og_full, w_out_own).astype(BF)
    mg, stats_own = event_stats(jnp.zeros((1,), jnp.int32), [mg], gate, heads)
    stats = lax.all_gather(stats_own, "seq", axis=0, tiled=False)
    grads, mixed = backward_attention(
        lengths, [stats[s] for s in range(seq_count)], mg, gate, heads, acts, slopes, weights, score_slope, blk, maxlen
    )

    input_part = dot_nt(grads, w_own).astype(BF)
    got = lax.all_to_all(
        input_part.reshape(seq_count, tokens_dev, D), "seq", split_axis=0, concat_axis=0, tiled=True
    )
    input_grad = jnp.sum(got.astype(F32), axis=0) + out_grad.astype(F32)
    got_rows = to_owners(rows_by_slot(slot_matrix, input_grad, numbers), devices, capacity)
    new_table, new_accum = update_rows(got_rows, emb_table, row_accum)

    out_part = dot_tn(mixed, og_full).astype(BF)
    share = dp_count // seq_count
    out_part = out_part.reshape(share, D // dp_count, seq_count, cols).transpose(0, 2, 1, 3).reshape(D, cols)
    merged = jnp.concatenate([dot_tn(x_full, grads).astype(BF), out_part], axis=1)
    merged = lax.psum_scatter(merged, "dp", scatter_dimension=0, tiled=True)
    steps = []
    for s in range(seq_count):
        for piece in range(dp_count):
            part, target = divmod(piece, seq_count)
            steps.append((s * dp_count + piece, target * dp_count + s * share + part))
    grad_out = lax.ppermute(merged[:, 4 * cols :], ("seq", "dp"), steps).astype(F32)
    grad_attn, grad_gate = attn_and_gate(merged[:, : 4 * cols].astype(F32), pairs)
    return (grad_attn, grad_gate, grad_out, new_table, new_accum)


SEQ = 4
PLANE = 4


def send(array, target):
    steps = []
    for s in range(SEQ):
        for e in range(PLANE):
            for c in range(2):
                to = target(s, e, c)
                if to is not None:
                    steps.append((s * 2 * PLANE + 2 * e + c, to[0] * 2 * PLANE + 2 * to[1] + to[2]))
    return lax.ppermute(array, ("seq", "dp"), steps)


def home(s, c):
    return c == s // 2


def swap_far(array):
    return send(array, lambda s, e, c: None if home(s, c) else (3 - s, e, 1 - c))


def swap_near_home(array):
    return send(array, lambda s, e, c: (s ^ 1, e, c) if home(s, c) else None)


def swap_near_far(array):
    return send(array, lambda s, e, c: None if home(s, c) else (s ^ 1, e, c))


def fetch_near(array):
    return send(array, lambda s, e, c: (s ^ 1, e, c) if home(s, c) else ((3 - s) ^ 1, e, 1 - c))


def swap_near(array):
    return send(array, lambda s, e, c: (s ^ 1, e, c))


def swap_core(array):
    return send(array, lambda s, e, c: (s, e, 1 - c))


def swap_x(array):
    return send(array, lambda s, e, c: (s, e ^ 1, c))


def swap_y(array):
    return send(array, lambda s, e, c: (s, e ^ 2, c))


def tie(*arrays):
    return lax.optimization_barrier(arrays)


def halves(array, bit, axis):
    kept = lax.dynamic_index_in_dim(array, bit, axis, keepdims=False)
    sent = lax.dynamic_index_in_dim(array, 1 - bit, axis, keepdims=False)
    return kept, sent


def body_pairs(
    layer_input, out_grad, lengths, item_owner, item_row, w_attn, w_gate, w_out, emb_table, row_accum
):
    devices = 2 * PLANE * SEQ
    s = lax.axis_index("seq")
    d = lax.axis_index("dp")
    e, c = d // 2, d % 2
    y, x = e // 2, e % 2
    tokens_dev = layer_input.shape[0]
    positions = tokens_dev * SEQ
    maxlen = 2 * positions // 3
    blk = min(256, positions)
    cols = D // SEQ
    pairs = cols // PAIR
    rows_own = emb_table.shape[0]
    capacity = max(2, 2 * tokens_dev // devices)
    at_home = c == s // 2
    part = 2 * (s % 2) + c

    def block_of(seq, core):
        return jnp.where(core == seq // 2, seq, 3 - seq)

    mine_at, near_at = block_of(s, c), block_of(s ^ 1, c)
    core_at, diag_at = block_of(s, 1 - c), block_of(s ^ 1, 1 - c)
    order = jnp.stack([mine_at, near_at, core_at, diag_at]).astype(jnp.int32)

    x_far = swap_far(layer_input)
    x_near = fetch_near(layer_input)
    users = lengths.shape[1]
    keys = (item_owner[:, 0] * rows_own + item_row).reshape(1, tokens_dev)
    small = jnp.concatenate([keys, jnp.pad(lengths, ((0, 0), (0, 128 - users)))], axis=1)
    small = jnp.where(at_home, small, swap_far(small))
    keys, lengths = small[0, :tokens_dev], small[:, tokens_dev : tokens_dev + users]
    w_own = own_weights(w_attn, w_gate, part, pairs)
    slot_matrix, numbers = row_slots(keys // rows_own, keys % rows_own, devices, capacity)
    mg_own = dot_nt(out_grad, w_out).astype(BF)
    x_far, x_near, w_own, slot_matrix, numbers, lengths, mg_own = tie(
        x_far, x_near, w_own, slot_matrix, numbers, lengths, mg_own
    )
    x_here = jnp.concatenate([jnp.where(at_home, layer_input, x_far), x_near], axis=0)
    x_there = swap_core(x_here)

    x_here, mg_own = tie(x_here, mg_own)
    mg_even, mg_odd = mg_own[:, : D // 2], mg_own[:, D // 2 :]
    even = s % 2 == 0
    mg_kept, mg_sent = jnp.where(even, mg_even, mg_odd), jnp.where(even, mg_odd, mg_even)
    mg_first = send(mg_sent, lambda s, e, c: (s ^ 1, e, c) if home(s, c) else (3 - s, e, 1 - c))
    mg_second = send(mg_kept, lambda s, e, c: None if home(s, c) else ((3 - s) ^ 1, e, 1 - c))

    x_full, acts, slopes, gate, weights, score_slope, heads = forward_attention(
        lengths, order, [x_here, x_there], w_own, blk, maxlen
    )
    heads, mg_first, mg_second = tie(heads, mg_first, mg_second)
    mg_mine = jnp.where(at_home, mg_kept, mg_first)
    mg_near = jnp.where(at_home, mg_first, mg_second)
    mg_both = jnp.concatenate([mg_mine, mg_near], axis=0)
    mg_here = jnp.where(c == 0, mg_both[:, :cols], mg_both[:, cols:])
    mg_there = swap_core(jnp.where(c == 0, mg_both[:, cols:], mg_both[:, :cols]))
    mg, stats_own = event_stats(order, [mg_here, mg_there], gate, heads)
    stats = [
        stats_own,
        swap_core(stats_own),
        swap_near(stats_own),
        send(stats_own, lambda s, e, c: (s ^ 1, e, 1 - c)),
    ]
    *stats, og_own = tie(*stats, out_grad)
    og_far = swap_far(og_own)
    og_near_home = swap_near_home(og_own)
    grads, mixed = backward_attention(
        lengths, stats, mg, gate, heads, acts, slopes, weights, score_slope, blk, maxlen
    )

    grads, og_far, og_near_home = tie(grads, og_far, og_near_home)

    def input_part(grads, block):
        return dot_nt(lax.dynamic_slice_in_dim(grads, block * tokens_dev, tokens_dev, 0), w_own)

    diag_part = input_part(grads, diag_at).astype(BF)
    from_diag = swap_core(diag_part)
    diag_part, grads = tie(diag_part, grads)
    near_part = input_part(grads, near_at)
    near_part, from_diag = tie(near_part, from_diag)
    near_sum = (near_part + from_diag.astype(F32)).astype(BF)
    from_near = swap_near(near_sum)
    near_sum, grads = tie(near_sum, grads)
    half = 2 * cols
    proj = dot_tn(x_full, grads).astype(BF).reshape(2, 2, D // PLANE, 4 * cols)
    a_kept, a_sent = halves(proj[..., :half], x, 1)
    b_kept, b_sent = halves(proj[..., half:], y, 0)
    a_sent, b_sent, grads = tie(a_sent, b_sent, grads)
    a_got = swap_x(a_sent)
    b_got = swap_y(b_sent)
    core_part = input_part(grads, core_at).astype(BF)
    from_core = swap_core(core_part)
    mine_part = input_part(grads, mine_at)
    og_mine = jnp.where(at_home, out_grad, og_far)
    input_grad = mine_part + from_core.astype(F32) + from_near.astype(F32) + og_mine.astype(F32)
    rows = rows_by_slot(slot_matrix, input_grad, numbers)
    rows, a_got, b_got, og_mine, og_near_home, mixed = tie(rows, a_got, b_got, og_mine, og_near_home, mixed)
    got_rows = to_owners(rows, devices, capacity)
    a = (a_kept.astype(F32) + a_got.astype(F32)).astype(BF)
    a_kept, a_sent = halves(a, y, 0)
    b = (b_kept.astype(F32) + b_got.astype(F32)).astype(BF)
    b_kept, b_sent = halves(b, x, 0)
    a_sent, b_sent, og_mine = tie(a_sent, b_sent, og_mine)
    a_got = swap_y(a_sent)
    b_got = swap_x(b_sent)
    og_near = jnp.where(at_home, og_near_home, swap_near_far(og_mine))

    def picked(bit, low, high):
        return jnp.where(bit == 0, low, high)

    og_here = jnp.concatenate([og_mine, og_near], axis=0)
    og_there = swap_core(og_here)
    mixed_rows = [lax.dynamic_slice_in_dim(mixed, at * tokens_dev, tokens_dev, 0) for at in (mine_at, near_at, core_at, diag_at)]
    out_part = dot_tn(jnp.concatenate(mixed_rows[:2], axis=0), og_here)
    out_part = (out_part + dot_tn(jnp.concatenate(mixed_rows[2:], axis=0), og_there)).astype(BF)
    low, high = out_part[:, : D // 2], out_part[:, D // 2 :]
    out = picked(y, low, high).astype(F32) + swap_y(picked(y, high, low)).astype(F32)
    out = out.astype(BF)

    a = (a_kept.astype(F32) + a_got.astype(F32)).astype(BF)
    b = (b_kept.astype(F32) + b_got.astype(F32)).astype(BF)

    def last(array, target):
        pieces = array.reshape(2, D // (2 * PLANE), array.shape[1])
        one, other = halves(pieces, s // 2, 0)
        one = send(one, lambda s, e, c: target(s, e, c, s // 2))
        return one, send(other, lambda s, e, c: target(s, e, c, 1 - s // 2))

    proj = jnp.concatenate([a, b], axis=1)
    low, high = out[:, :cols], out[:, cols:]
    out = picked(x, low, high).astype(F32) + swap_x(picked(x, high, low)).astype(F32)
    proj, out, row_accum = tie(proj, out.astype(BF), row_accum)
    proj = last(proj, lambda s, e, c, piece: (2 * (s % 2) + c, e, piece))
    out = last(out, lambda s, e, c, piece: (e, 2 * (s % 2) + c, piece))
    new_table, new_accum = update_rows(got_rows, emb_table, row_accum)
    *proj, new_accum = tie(*proj, new_accum)
    grad_attn, grad_gate = attn_and_gate(proj[0].astype(F32) + proj[1].astype(F32), pairs)
    return (grad_attn, grad_gate, out[0].astype(F32) + out[1].astype(F32), new_table, new_accum)


def solution(mesh):
    placed = (
        P(("dp", "seq"), None),
        P(("dp", "seq"), None),
        P("dp", None),
        P(("dp", "seq"), None),
        P(("dp", "seq")),
        P(),
        P(),
        P(),
        P(("seq", "dp"), None),
        P(("seq", "dp")),
    )
    paired = mesh.shape["seq"] == SEQ and mesh.shape["dp"] == 2 * PLANE
    return jax.shard_map(
        body_pairs if paired else body_whole,
        mesh=mesh,
        in_specs=placed,
        out_specs=(
            P("dp", "seq"),
            P("dp", "seq"),
            P("dp", "seq"),
            P(("seq", "dp"), None),
            P(("seq", "dp")),
        ),
        check_vma=False,
    )
```

```python
import functools

import jax
import jax.numpy as jnp
from jax import lax
from jax.experimental import pallas as pl
from jax.experimental.pallas import tpu as pltpu
from jax.sharding import PartitionSpec as P

D = 1024
H = 16
DH = 64
PAIR = 2 * DH

NORM_EPS = 1e-05
LEARN_RATE = 0.1
VMEM_LIMIT = 56 * 1024 * 1024
BF = jnp.bfloat16
F32 = jnp.float32


def dot_nn(a, b):
    return lax.dot_general(a, b, (((1,), (0,)), ((), ())), preferred_element_type=F32)


def dot_nt(a, b):
    return lax.dot_general(a, b, (((1,), (1,)), ((), ())), preferred_element_type=F32)


def history_start(lengths_ref, users, place):
    start = jnp.zeros_like(place)
    end = jnp.int32(0)
    for user in range(users - 1):
        end = end + lengths_ref[0, user]
        start = jnp.where(place >= end, end, start)
    return start


def head_columns(kind, head):
    first = head * 3 * DH + kind * DH
    return slice(first, first + DH)


def forward_kernel(*refs, blk, users, maxlen, count):
    lengths_ref, order_ref = refs[:2]
    x_refs = refs[2 : 2 + count]
    w_ref = refs[2 + count]
    outs = refs[3 + count :]
    if count > 1:
        x_out_ref, outs = outs[0], outs[1:]
    acts_ref, slopes_ref, gate_ref, weights_ref, score_slope_ref, heads_ref = outs
    i = pl.program_id(0)
    heads = weights_ref.shape[0]
    attn = 3 * heads * DH
    chunks = x_refs[0].shape[0] // blk

    @pl.when(i == 0)
    def _():
        for b in range(count):
            for r in range(chunks):
                at = pl.ds(pl.multiple_of(order_ref[b * chunks + r] * blk, blk), blk)
                x = x_refs[b][r * blk : (r + 1) * blk, :]
                if count > 1:
                    x_out_ref[at, :] = x
                for lane in range(0, w_ref.shape[1], 512):
                    lanes = slice(lane, lane + 512)
                    half = 0.5 * dot_nn(x, w_ref[:, lanes])
                    t = jnp.tanh(half)
                    prod = half * t
                    silu = half + prod
                    acts_ref[at, lanes] = silu.astype(BF)
                    slopes_ref[at, lanes] = (0.5 * (1.0 + t) * (1.0 + half - prod)).astype(BF)
                    skip = max(0, attn - lane)
                    if skip < 512:
                        gate_ref[at, lane + skip - attn : lane + 512 - attn] = silu[:, skip:]

    at_i = pl.ds(pl.multiple_of(i * blk, blk), blk)
    q_half = [acts_ref[at_i, head_columns(1, h)] * jnp.asarray(0.5 * DH**-0.5, BF) for h in range(heads)]
    row = i * blk + lax.broadcasted_iota(jnp.int32, (blk, blk), 0)
    col0 = lax.broadcasted_iota(jnp.int32, (blk, blk), 1)
    start = history_start(lengths_ref, users, row)

    def column(j, acc):
        at_j = pl.ds(pl.multiple_of(j * blk, blk), blk)
        col = col0 + j * blk
        allowed = (col <= row) & (col >= start)
        outs = []
        for h in range(heads):
            half = dot_nt(q_half[h], acts_ref[at_j, head_columns(2, h)])
            half = jnp.where(allowed, half, -64.0)
            t = jnp.tanh(half)
            p = half * t
            weights = (half + p).astype(BF)
            weights_ref[h, :, at_j] = weights
            score_slope_ref[h, :, at_j] = ((1.0 + t) * (1.0 + half - p)).astype(BF)
            outs.append(acc[h] + dot_nn(weights, acts_ref[at_j, head_columns(0, h)]))
        return tuple(outs)

    first = history_start(lengths_ref, users, i * blk) // blk
    zero = jnp.zeros((blk, DH), F32)
    acc = lax.fori_loop(first, i + 1, column, (zero,) * heads)
    heads_ref[...] = (jnp.concatenate(acc, axis=1) * (1.0 / maxlen)).astype(BF)


def forward_attention(lengths, order, x_blocks, w_own, blk, maxlen):
    count = len(x_blocks)
    block_rows = x_blocks[0].shape[0]
    positions = count * block_rows
    cols = w_own.shape[1] // 4
    heads = cols // DH
    users = lengths.shape[1]
    elements = heads * positions * positions // 2
    whole = lambda i: (0, 0)
    out_specs = [
        pl.BlockSpec((positions, 4 * cols), whole),
        pl.BlockSpec((positions, 4 * cols), whole),
        pl.BlockSpec((positions, cols), whole),
        pl.BlockSpec((heads, blk, positions), lambda i: (0, i, 0)),
        pl.BlockSpec((heads, blk, positions), lambda i: (0, i, 0)),
        pl.BlockSpec((blk, cols), lambda i: (i, 0)),
    ]
    out_shape = [
        jax.ShapeDtypeStruct((positions, 4 * cols), BF),
        jax.ShapeDtypeStruct((positions, 4 * cols), BF),
        jax.ShapeDtypeStruct((positions, cols), F32),
        jax.ShapeDtypeStruct((heads, positions, positions), BF),
        jax.ShapeDtypeStruct((heads, positions, positions), BF),
        jax.ShapeDtypeStruct((positions, cols), BF),
    ]
    if count > 1:
        out_specs = [pl.BlockSpec((positions, D), whole)] + out_specs
        out_shape = [jax.ShapeDtypeStruct((positions, D), BF)] + out_shape
    return pl.pallas_call(
        functools.partial(forward_kernel, blk=blk, users=users, maxlen=maxlen, count=count),
        grid=(positions // blk,),
        in_specs=[pl.BlockSpec(memory_space=pltpu.SMEM), pl.BlockSpec(memory_space=pltpu.SMEM)]
        + [pl.BlockSpec((block_rows, D), whole)] * count
        + [pl.BlockSpec((D, 4 * cols), whole)],
        out_specs=out_specs,
        out_shape=out_shape,
        compiler_params=pltpu.CompilerParams(vmem_limit_bytes=VMEM_LIMIT),
        cost_estimate=pl.CostEstimate(
            flops=8 * positions * D * cols + 4 * elements * 256,
            bytes_accessed=4 * positions * D + 4 * elements,
            transcendentals=elements,
        ),
        name="attention_forward",
    )(lengths, order, *x_blocks, w_own)


def stats_kernel(*refs, blk, count):
    order_ref = refs[0]
    og_refs = refs[1 : 1 + count]
    w_ref, gate_ref, heads_ref = refs[1 + count : 4 + count]
    outs = refs[4 + count :]
    if count > 1:
        og_out_ref, outs = outs[0], outs[1:]
    mg_ref, stats_ref = outs
    chunks = og_refs[0].shape[0] // blk
    for b in range(count):
        for r in range(chunks):
            at = pl.ds(pl.multiple_of(order_ref[b * chunks + r] * blk, blk), blk)
            og = og_refs[b][r * blk : (r + 1) * blk, :]
            if count > 1:
                og_out_ref[at, :] = og
            mg = dot_nt(og, w_ref[...])
            mg_ref[at, :] = mg
            ng = mg * gate_ref[at, :]
            heads = heads_ref[at, :].astype(F32)
            mean = jnp.mean(heads, axis=1, keepdims=True)
            centred = heads - mean
            square = jnp.sum(centred * centred, axis=1, keepdims=True)
            total = jnp.sum(ng, axis=1, keepdims=True)
            cross = jnp.sum(ng * centred, axis=1, keepdims=True)
            lane = lax.broadcasted_iota(jnp.int32, (blk, 128), 1)
            packed = jnp.where(lane == 0, mean, jnp.where(lane == 1, square, jnp.where(lane == 2, total, cross)))
            stats_ref[:, at] = jnp.transpose(packed)[:8, :]


def event_stats(order, og_blocks, w_out_own, gate, heads, blk):
    positions, cols = heads.shape
    count = len(og_blocks)
    vmem = pl.BlockSpec(memory_space=pltpu.VMEM)
    out_shape = [
        jax.ShapeDtypeStruct((positions, cols), F32),
        jax.ShapeDtypeStruct((8, positions), F32),
    ]
    if count > 1:
        out_shape = [jax.ShapeDtypeStruct((positions, D), BF)] + out_shape
    return pl.pallas_call(
        functools.partial(stats_kernel, blk=blk, count=count),
        in_specs=[pl.BlockSpec(memory_space=pltpu.SMEM)] + [vmem] * (count + 3),
        out_specs=[vmem] * len(out_shape),
        out_shape=out_shape,
        compiler_params=pltpu.CompilerParams(vmem_limit_bytes=VMEM_LIMIT),
        cost_estimate=pl.CostEstimate(
            flops=2 * positions * cols * D, bytes_accessed=4 * positions * D + 10 * positions * cols, transcendentals=0
        ),
        name="event_stats",
    )(order, *og_blocks, w_out_own, gate, heads)


def combined_stats(stats_refs, cols):
    shards = len(stats_refs)
    positions = stats_refs[0].shape[1]
    means = [ref[0:1, :] for ref in stats_refs]
    mean = sum(means) * (1.0 / shards)
    square = jnp.zeros_like(mean)
    total = jnp.zeros_like(mean)
    cross = jnp.zeros_like(mean)
    for s, ref in enumerate(stats_refs):
        shift = means[s] - mean
        part = ref[2:3, :]
        square = square + ref[1:2, :] + cols * shift * shift
        total = total + part
        cross = cross + ref[3:4, :] + shift * part
    inv_dev = lax.rsqrt(square * (1.0 / D) + NORM_EPS)
    kind = lax.broadcasted_iota(jnp.int32, (128, positions), 0)
    rest = jnp.where(kind == 2, total * (1.0 / D), cross * inv_dev * (1.0 / D))
    packed = jnp.where(kind == 0, mean, jnp.where(kind == 1, inv_dev, rest))
    per_event = jnp.transpose(packed)
    return [per_event[:, k : k + 1] for k in range(4)]


def backward_kernel(*refs, blk, users, maxlen, shards):
    lengths_ref = refs[0]
    stats_refs = refs[1 : 1 + shards]
    mg_ref, gate_ref, heads_ref, acts_ref, slopes_ref, weights_ref, score_slope_ref = refs[1 + shards : 8 + shards]
    grad_ref, mixed_ref, o_ref, o_t, q_t, vg_t, kg_t, qg = refs[8 + shards :]
    i = pl.program_id(0)
    positions, cols = o_ref.shape
    heads = cols // DH
    blocks = positions // blk
    scale = DH ** (-0.5)

    @pl.when(i == 0)
    def _():
        mean, inv_dev, total, cross = combined_stats(stats_refs, cols)
        for p in range(heads // 2):
            lanes = slice(p * PAIR, (p + 1) * PAIR)
            normed = (heads_ref[:, lanes].astype(F32) - mean) * inv_dev
            gate = gate_ref[:, lanes]
            mg = mg_ref[:, lanes]
            mixed_ref[:, lanes] = (normed * gate).astype(BF)
            gate_lanes = slice(3 * cols + p * PAIR, 3 * cols + (p + 1) * PAIR)
            gate_slope = slopes_ref[:, gate_lanes].astype(F32)
            grad_ref[:, gate_lanes] = (mg * normed * gate_slope).astype(BF)
            o_ref[:, lanes] = (inv_dev * (mg * gate - total - normed * cross)).astype(BF)
        o_t[...] = jnp.transpose(o_ref[...])
        queries = [acts_ref[:, head_columns(1, h)] for h in range(heads)]
        q_t[...] = jnp.transpose(jnp.concatenate(queries, axis=1))
        vg_t[...] = jnp.zeros_like(vg_t)
        kg_t[...] = jnp.zeros_like(kg_t)

    at_i = pl.ds(pl.multiple_of(i * blk, blk), blk)

    def column(j, acc):
        at_j = pl.ds(pl.multiple_of(j * blk, blk), blk)
        outs = []
        for h in range(heads):
            lanes = slice(h * DH, (h + 1) * DH)
            weight_grad = dot_nt(o_ref[at_i, lanes], acts_ref[at_j, head_columns(0, h)])
            score_grad = (weight_grad * score_slope_ref[h, :, at_j].astype(F32)).astype(BF)
            vg_t[lanes, at_j] += dot_nn(o_t[lanes, at_i], weights_ref[h, :, at_j])
            kg_t[lanes, at_j] += dot_nn(q_t[lanes, at_i], score_grad)
            outs.append(acc[h] + dot_nn(score_grad, acts_ref[at_j, head_columns(2, h)]))
        return tuple(outs)

    first = history_start(lengths_ref, users, i * blk) // blk
    zero = jnp.zeros((blk, DH), F32)
    acc = lax.fori_loop(first, i + 1, column, (zero,) * heads)
    qg[at_i, :] = jnp.concatenate(acc, axis=1)

    @pl.when(i == blocks - 1)
    def _():
        factor = 0.5 * scale / maxlen
        grads = [jnp.transpose(vg_t[...]) * (1.0 / maxlen), qg[...] * factor, jnp.transpose(kg_t[...]) * factor]
        pieces = [grads[kind][:, h * DH : (h + 1) * DH] for h in range(heads) for kind in range(3)]
        for n in range(3 * heads // 2):
            lanes = slice(n * PAIR, (n + 1) * PAIR)
            grad = jnp.concatenate(pieces[2 * n : 2 * n + 2], axis=1).astype(BF).astype(F32)
            grad_ref[:, lanes] = (grad * slopes_ref[:, lanes].astype(F32)).astype(BF)


def backward_attention(lengths, stats, mg, gate, head_outs, acts, slopes, weights, score_slope, blk, maxlen):
    positions, cols = mg.shape
    heads = cols // DH
    shards = len(stats)
    users = lengths.shape[1]
    elements = heads * positions * positions // 2
    whole = lambda i: (0, 0)
    return pl.pallas_call(
        functools.partial(backward_kernel, blk=blk, users=users, maxlen=maxlen, shards=shards),
        grid=(positions // blk,),
        in_specs=[pl.BlockSpec(memory_space=pltpu.SMEM)]
        + [pl.BlockSpec((8, positions), whole)] * shards
        + [
            pl.BlockSpec((positions, cols), whole),
            pl.BlockSpec((positions, cols), whole),
            pl.BlockSpec((positions, cols), whole),
            pl.BlockSpec((positions, 4 * cols), whole),
            pl.BlockSpec((positions, 4 * cols), whole),
            pl.BlockSpec((heads, blk, positions), lambda i: (0, i, 0)),
            pl.BlockSpec((heads, blk, positions), lambda i: (0, i, 0)),
        ],
        out_specs=[pl.BlockSpec((positions, 4 * cols), whole), pl.BlockSpec((positions, cols), whole)],
        out_shape=[
            jax.ShapeDtypeStruct((positions, 4 * cols), BF),
            jax.ShapeDtypeStruct((positions, cols), BF),
        ],
        scratch_shapes=[
            pltpu.VMEM((positions, cols), BF),
            pltpu.VMEM((cols, positions), BF),
            pltpu.VMEM((cols, positions), BF),
            pltpu.VMEM((cols, positions), F32),
            pltpu.VMEM((cols, positions), F32),
            pltpu.VMEM((positions, cols), F32),
        ],
        compiler_params=pltpu.CompilerParams(vmem_limit_bytes=VMEM_LIMIT),
        cost_estimate=pl.CostEstimate(
            flops=8 * elements * 256, bytes_accessed=4 * elements + 26 * positions * cols, transcendentals=0
        ),
        name="attention_backward",
    )(lengths, *stats, mg, gate, head_outs, acts, slopes, weights, score_slope)


def update_kernel(rows_ref, table_ref, accum_ref, new_table_ref, new_accum_ref, ids):
    i = pl.program_id(0)
    blk = table_ref.shape[0]
    slots = rows_ref.shape[0]

    @pl.when(i == 0)
    def _():
        numbers = jnp.transpose(rows_ref[:, D:].astype(F32))
        ids[...] = (numbers[0:1, :] * 256.0 + numbers[1:2, :]).astype(jnp.int32)

    row = i * blk + lax.broadcasted_iota(jnp.int32, (blk, slots), 0)
    hits = jnp.where(row == ids[...], 1.0, 0.0).astype(BF)
    grad = dot_nn(hits, rows_ref[:, :D])
    accum = jnp.transpose(jnp.broadcast_to(accum_ref[...], (128, blk)))[:, :1] + jnp.mean(grad * grad, axis=1, keepdims=True)
    new_accum_ref[...] = jnp.transpose(jnp.broadcast_to(accum, (blk, 128)))[:1, :]
    new_table_ref[...] = table_ref[...] - LEARN_RATE * grad * lax.rsqrt(accum)


def update_rows(got_rows, emb_table, row_accum):
    rows_own = emb_table.shape[0]
    slots = got_rows.shape[0]
    blk = min(256, rows_own)
    new_table, new_accum = pl.pallas_call(
        update_kernel,
        grid=(rows_own // blk,),
        in_specs=[
            pl.BlockSpec((slots, D + 128), lambda i: (0, 0)),
            pl.BlockSpec((blk, D), lambda i: (i, 0)),
            pl.BlockSpec((1, blk), lambda i: (0, i)),
        ],
        out_specs=[
            pl.BlockSpec((blk, D), lambda i: (i, 0)),
            pl.BlockSpec((1, blk), lambda i: (0, i)),
        ],
        out_shape=[
            jax.ShapeDtypeStruct((rows_own, D), F32),
            jax.ShapeDtypeStruct((1, rows_own), F32),
        ],
        scratch_shapes=[pltpu.VMEM((1, slots), jnp.int32)],
        compiler_params=pltpu.CompilerParams(vmem_limit_bytes=VMEM_LIMIT),
        cost_estimate=pl.CostEstimate(
            flops=2 * rows_own * slots * D, bytes_accessed=8 * rows_own * D + 2 * slots * D, transcendentals=rows_own
        ),
        name="update_rows",
    )(got_rows, emb_table, row_accum.reshape(1, rows_own))
    return new_table, new_accum.reshape(rows_own)


def own_weights(w_attn, w_gate, part, cols):
    attn = lax.dynamic_slice_in_dim(w_attn, part * 3 * cols, 3 * cols, 1)
    gate = lax.dynamic_slice_in_dim(w_gate, part * cols, cols, 1)
    return jnp.concatenate([attn, gate], axis=1)


def row_slots(owners, rows, devices, capacity):
    events = owners.shape[0]
    owner_hits = (owners[:, None] == jnp.arange(devices, dtype=jnp.int32)[None, :]).astype(BF)
    place = jnp.arange(events, dtype=jnp.int32)
    before = (place[:, None] > place[None, :]).astype(BF)
    earlier = jnp.dot(before, owner_hits, preferred_element_type=F32)
    slots = jnp.sum(earlier * owner_hits.astype(F32), axis=1).astype(jnp.int32)
    flat_slot = owners * capacity + slots
    slot_hits = jnp.arange(devices * capacity, dtype=jnp.int32)[:, None] == flat_slot[None, :]
    lane = jnp.arange(128, dtype=jnp.int32)[None, :]
    numbers = jnp.where(lane == 0, rows[:, None] // 256, jnp.where(lane == 1, rows[:, None] % 256, 0))
    return slot_hits.astype(BF), numbers.astype(BF)


def to_owners(rows, devices, capacity):
    shape = (devices, capacity) + rows.shape[1:]
    got = lax.all_to_all(rows.reshape(shape), ("seq", "dp"), split_axis=0, concat_axis=0, tiled=True)
    return got.reshape(rows.shape)


TN = (((0,), (0,)), ((), ()))


def dot_tn(a, b):
    return lax.dot_general(a, b, TN, preferred_element_type=F32)


def body_whole(
    layer_input, out_grad, lengths, item_owner, item_row, w_attn, w_gate, w_out, emb_table, row_accum
):
    seq_count = lax.axis_size("seq")
    dp_count = lax.axis_size("dp")
    devices = seq_count * dp_count
    seq_id = lax.axis_index("seq")
    tokens_dev = layer_input.shape[0]
    positions = tokens_dev * seq_count
    maxlen = 2 * positions // 3
    blk = min(256, positions)
    cols = D // seq_count
    capacity = max(2, 2 * tokens_dev // devices)

    w_own = own_weights(w_attn, w_gate, seq_id, cols)
    w_out_own = lax.dynamic_slice_in_dim(w_out, seq_id * cols, cols, 0)
    slot_matrix, numbers = row_slots(item_owner[:, 0], item_row, devices, capacity)

    x_full = lax.all_gather(layer_input, "seq", axis=0, tiled=True)
    og_full = lax.all_gather(out_grad, "seq", axis=0, tiled=True)
    order = jnp.arange(positions // blk, dtype=jnp.int32)
    acts, slopes, gate, weights, score_slope, heads = forward_attention(
        lengths, order, [x_full], w_own, blk, maxlen
    )
    mg, stats_own = event_stats(order, [og_full], w_out_own, gate, heads, blk)
    stats = lax.all_gather(stats_own, "seq", axis=0, tiled=False)
    grads, mixed = backward_attention(
        lengths, [stats[s] for s in range(seq_count)], mg, gate, heads, acts, slopes, weights, score_slope, blk, maxlen
    )

    input_part = dot_nt(grads, w_own).astype(BF)
    got = lax.all_to_all(
        input_part.reshape(seq_count, tokens_dev, D), "seq", split_axis=0, concat_axis=0, tiled=True
    )
    input_grad = jnp.sum(got.astype(F32), axis=0) + out_grad.astype(F32)
    rows = jnp.concatenate([input_grad.astype(BF), numbers], axis=1)
    rows = jnp.dot(slot_matrix, rows, preferred_element_type=F32).astype(BF)
    got_rows = to_owners(rows, devices, capacity)
    new_table, new_accum = update_rows(got_rows, emb_table, row_accum)

    out_part = dot_tn(mixed, og_full).astype(BF)
    share = dp_count // seq_count
    out_part = out_part.reshape(share, D // dp_count, seq_count, cols).transpose(0, 2, 1, 3).reshape(D, cols)
    merged = jnp.concatenate([dot_tn(x_full, grads).astype(BF), out_part], axis=1)
    merged = lax.psum_scatter(merged, "dp", scatter_dimension=0, tiled=True)
    steps = []
    for s in range(seq_count):
        for piece in range(dp_count):
            part, target = divmod(piece, seq_count)
            steps.append((s * dp_count + piece, target * dp_count + s * share + part))
    grad_out = lax.ppermute(merged[:, 4 * cols :], ("seq", "dp"), steps).astype(F32)
    grad_attn = merged[:, : 3 * cols].astype(F32)
    grad_gate = merged[:, 3 * cols : 4 * cols].astype(F32)
    return (grad_attn, grad_gate, grad_out, new_table, new_accum)


SMEM = pl.BlockSpec(memory_space=pltpu.SMEM)
VMEM = pl.BlockSpec(memory_space=pltpu.VMEM)


def small_call(kernel, name, in_specs, out_shape):
    return pl.pallas_call(
        kernel,
        in_specs=in_specs,
        out_specs=[VMEM] * len(out_shape),
        out_shape=out_shape,
        compiler_params=pltpu.CompilerParams(vmem_limit_bytes=VMEM_LIMIT),
        cost_estimate=pl.CostEstimate(flops=0, bytes_accessed=0, transcendentals=0),
        name=name,
    )


def input_parts(grads, w_own, rows, blocks, dtype):
    def kernel(at_ref, g_ref, w_ref, o_ref):
        o_ref[...] = dot_nt(g_ref[...], w_ref[...]).astype(o_ref.dtype)

    cols = grads.shape[1]
    return pl.pallas_call(
        kernel,
        grid_spec=pltpu.PrefetchScalarGridSpec(
            num_scalar_prefetch=1,
            grid=(len(blocks),),
            in_specs=[
                pl.BlockSpec((rows, cols), lambda i, at: (at[i], 0)),
                pl.BlockSpec((D, cols), lambda i, at: (0, 0)),
            ],
            out_specs=pl.BlockSpec((rows, D), lambda i, at: (i, 0)),
        ),
        out_shape=jax.ShapeDtypeStruct((len(blocks) * rows, D), dtype),
        compiler_params=pltpu.CompilerParams(vmem_limit_bytes=VMEM_LIMIT),
        cost_estimate=pl.CostEstimate(flops=0, bytes_accessed=0, transcendentals=0),
        name="input_parts",
    )(jnp.stack(blocks).astype(jnp.int32), grads, w_own)


def pack_kernel(mine_ref, core_ref, near_ref, og_ref, slots_ref, numbers_ref, rows_ref):
    events = mine_ref.shape[0]
    total = mine_ref[...] + core_ref[events:, :].astype(F32) + near_ref[...].astype(F32) + og_ref[...].astype(F32)
    rows_ref[:, :D] = dot_nn(slots_ref[...], total.astype(BF)).astype(BF)
    rows_ref[:, D:] = dot_nn(slots_ref[...], numbers_ref[...]).astype(BF)


def weight_kernel(yx_ref, x_ref, grads_ref, mixed_ref, og_ref, a_kept, a_sent, b_kept, b_sent):
    chip = pl.program_id(0)
    chip_y, chip_x = chip // 2, chip % 2
    cut = a_kept.shape[2]
    proj = dot_tn(x_ref[...], grads_ref[...]).astype(BF)
    out = dot_tn(mixed_ref[...], og_ref[...]).astype(BF)
    rest = proj.shape[1] - cut

    def store_b(ref):
        ref[chip_x, :, :rest] = proj[:, cut:]
        ref[chip_x, :, rest:] = out

    @pl.when(chip_x == yx_ref[1])
    def _():
        a_kept[chip_y] = proj[:, :cut]

    @pl.when(chip_x != yx_ref[1])
    def _():
        a_sent[chip_y] = proj[:, :cut]

    @pl.when(chip_y == yx_ref[0])
    def _():
        store_b(b_kept)

    @pl.when(chip_y != yx_ref[0])
    def _():
        store_b(b_sent)


def weight_parts(yx, x_full, grads, mixed, og_full):
    positions, cols = mixed.shape
    rows = D // PLANE
    whole = lambda e: (0, 0)
    out = jax.ShapeDtypeStruct((2, rows, 5 * cols // 2), BF)
    return pl.pallas_call(
        weight_kernel,
        grid=(PLANE,),
        in_specs=[
            SMEM,
            pl.BlockSpec((positions, rows), lambda e: (0, e)),
            pl.BlockSpec((positions, 4 * cols), whole),
            pl.BlockSpec((positions, cols), whole),
            pl.BlockSpec((positions, D // PLANE), lambda e: (0, e)),
        ],
        out_specs=[pl.BlockSpec(out.shape, lambda e: (0, 0, 0))] * 4,
        out_shape=[out] * 4,
        compiler_params=pltpu.CompilerParams(vmem_limit_bytes=VMEM_LIMIT),
        cost_estimate=pl.CostEstimate(flops=0, bytes_accessed=0, transcendentals=0),
        name="weight_parts",
    )(yx, x_full, grads, mixed, og_full)


def merge_kernel(bit_ref, kept_ref, got_ref, next_kept, next_sent):
    bit = bit_ref[0]
    next_kept[...] = (kept_ref[bit].astype(F32) + got_ref[bit].astype(F32)).astype(BF)
    next_sent[...] = (kept_ref[1 - bit].astype(F32) + got_ref[1 - bit].astype(F32)).astype(BF)


def merge_halves(bit, kept, got):
    out = jax.ShapeDtypeStruct(kept.shape[1:], BF)
    return small_call(merge_kernel, "merge_halves", [SMEM, VMEM, VMEM], [out, out])(bit, kept, got)


def last_kernel(bit_ref, a_kept, a_got, b_kept, b_got, proj_one, proj_other, out_one, out_other):
    rows, cut = proj_one.shape[0], a_kept.shape[1]
    rest = proj_one.shape[1] - cut
    for flip, proj_ref, out_ref in ((0, proj_one, out_one), (1, proj_other, out_other)):
        half = bit_ref[0] + flip - 2 * flip * bit_ref[0]
        at = pl.ds(pl.multiple_of(half * rows, rows), rows)
        proj_ref[:, :cut] = (a_kept[at, :].astype(F32) + a_got[at, :].astype(F32)).astype(BF)
        b = (b_kept[at, :].astype(F32) + b_got[at, :].astype(F32)).astype(BF)
        proj_ref[:, cut:] = b[:, :rest]
        out_ref[...] = b[:, rest:]


def last_pieces(bit, a_kept, a_got, b_kept, b_got, cols):
    rows = a_kept.shape[0] // 2
    proj = jax.ShapeDtypeStruct((rows, 4 * cols), BF)
    out = jax.ShapeDtypeStruct((rows, cols), BF)
    return small_call(last_kernel, "last_pieces", [SMEM] + [VMEM] * 4, [proj, proj, out, out])(
        bit, a_kept, a_got, b_kept, b_got
    )


SEQ = 4
PLANE = 4


def send(array, target):
    steps = []
    for s in range(SEQ):
        for e in range(PLANE):
            for c in range(2):
                to = target(s, e, c)
                if to is not None:
                    steps.append((s * 2 * PLANE + 2 * e + c, to[0] * 2 * PLANE + 2 * to[1] + to[2]))
    return lax.ppermute(array, ("seq", "dp"), steps)


def home(s, c):
    return c == s // 2


def swap_far(array):
    return send(array, lambda s, e, c: None if home(s, c) else (3 - s, e, 1 - c))


def fetch_near(array):
    return send(array, lambda s, e, c: (s ^ 1, e, c) if home(s, c) else ((3 - s) ^ 1, e, 1 - c))


def swap_near(array):
    return send(array, lambda s, e, c: (s ^ 1, e, c))


def swap_core(array):
    return send(array, lambda s, e, c: (s, e, 1 - c))


def swap_x(array):
    return send(array, lambda s, e, c: (s, e ^ 1, c))


def swap_y(array):
    return send(array, lambda s, e, c: (s, e ^ 2, c))


def tie(*arrays):
    return lax.optimization_barrier(arrays)


def body_pairs(
    layer_input, out_grad, lengths, item_owner, item_row, w_attn, w_gate, w_out, emb_table, row_accum
):
    devices = 2 * PLANE * SEQ
    s = lax.axis_index("seq")
    d = lax.axis_index("dp")
    e, c = d // 2, d % 2
    y, x = e // 2, e % 2
    tokens_dev = layer_input.shape[0]
    positions = tokens_dev * SEQ
    maxlen = 2 * positions // 3
    blk = min(256, positions)
    cols = D // SEQ
    rows_own = emb_table.shape[0]
    capacity = max(2, 2 * tokens_dev // devices)
    at_home = c == s // 2
    part = 2 * (s % 2) + c

    def block_of(seq, core):
        return jnp.where(core == seq // 2, seq, 3 - seq)

    mine_at, near_at = block_of(s, c), block_of(s ^ 1, c)
    core_at, diag_at = block_of(s, 1 - c), block_of(s ^ 1, 1 - c)
    order = jnp.stack([mine_at, near_at, core_at, diag_at]).astype(jnp.int32)

    x_far = swap_far(layer_input)
    x_near = fetch_near(layer_input)
    users = lengths.shape[1]
    keys = (item_owner[:, 0] * rows_own + item_row).reshape(1, tokens_dev)
    small = jnp.concatenate([keys, jnp.pad(lengths, ((0, 0), (0, 128 - users)))], axis=1)
    small = jnp.where(at_home, small, swap_far(small))
    keys, lengths = small[0, :tokens_dev], small[:, tokens_dev : tokens_dev + users]
    w_own = own_weights(w_attn, w_gate, part, cols)
    w_out_own = lax.dynamic_slice_in_dim(w_out, part * cols, cols, 0)
    slot_matrix, numbers = row_slots(keys // rows_own, keys % rows_own, devices, capacity)
    x_far, x_near, w_own, w_out_own, slot_matrix, numbers, lengths = tie(
        x_far, x_near, w_own, w_out_own, slot_matrix, numbers, lengths
    )
    x_here = jnp.concatenate([jnp.where(at_home, layer_input, x_far), x_near], axis=0)
    x_there = swap_core(x_here)
    x_here, og_own = tie(x_here, out_grad)
    og_far = swap_far(og_own)
    og_near = fetch_near(og_own)

    x_full, acts, slopes, gate, weights, score_slope, heads = forward_attention(
        lengths, order, [x_here, x_there], w_own, blk, maxlen
    )
    og_far, og_near, heads = tie(og_far, og_near, heads)
    og_mine = jnp.where(at_home, og_own, og_far)
    og_here = jnp.concatenate([og_mine, og_near], axis=0)
    og_there = swap_core(og_here)
    og_full, mg, stats_own = event_stats(order, [og_here, og_there], w_out_own, gate, heads, blk)
    stats = [
        stats_own,
        swap_core(stats_own),
        swap_near(stats_own),
        send(stats_own, lambda s, e, c: (s ^ 1, e, 1 - c)),
    ]
    grads, mixed = backward_attention(
        lengths, stats, mg, gate, heads, acts, slopes, weights, score_slope, blk, maxlen
    )

    core_parts = input_parts(grads, w_own, tokens_dev, [diag_at, core_at], BF)
    from_core = swap_core(core_parts)
    core_parts, grads = tie(core_parts, grads)
    near_part = input_parts(grads, w_own, tokens_dev, [near_at], F32)
    near_part, from_core = tie(near_part, from_core)
    near_sum = (near_part + from_core[:tokens_dev].astype(F32)).astype(BF)
    from_near = swap_near(near_sum)

    near_sum, grads, mixed = tie(near_sum, grads, mixed)
    yx = jnp.stack([y, x]).astype(jnp.int32)
    a_kept, a_sent, b_kept, b_sent = weight_parts(yx, x_full, grads, mixed, og_full)
    a_sent, b_sent, grads = tie(a_sent, b_sent, grads)
    a_got = swap_x(a_sent)
    b_got = swap_y(b_sent)

    mine_part = input_parts(grads, w_own, tokens_dev, [mine_at], F32)
    out_rows = jax.ShapeDtypeStruct((devices * capacity, D + 128), BF)
    (rows,) = small_call(pack_kernel, "pack_rows", [VMEM] * 6, [out_rows])(
        mine_part, from_core, from_near, og_mine, slot_matrix, numbers
    )
    rows, a_kept, b_kept = tie(rows, a_kept, b_kept)
    got_rows = to_owners(rows, devices, capacity)

    a_kept, a_sent = merge_halves(yx[:1], a_kept, a_got)
    a_got = swap_y(a_sent)
    b_kept, b_sent = merge_halves(yx[1:], b_kept, b_got)
    b_got = swap_x(b_sent)

    pieces = last_pieces((s // 2).reshape(1).astype(jnp.int32), a_kept, a_got, b_kept, b_got, cols)
    *pieces, row_accum = tie(*pieces, row_accum)
    proj = [
        send(pieces[0], lambda s, e, c: (2 * (s % 2) + c, e, s // 2)),
        send(pieces[1], lambda s, e, c: (2 * (s % 2) + c, e, 1 - s // 2)),
    ]
    out = [
        send(pieces[2], lambda s, e, c: (e, 2 * (s % 2) + c, s // 2)),
        send(pieces[3], lambda s, e, c: (e, 2 * (s % 2) + c, 1 - s // 2)),
    ]
    new_table, new_accum = update_rows(got_rows, emb_table, row_accum)
    *proj, new_accum = tie(*proj, new_accum)
    attn = proj[0][:, : 3 * cols].astype(F32) + proj[1][:, : 3 * cols].astype(F32)
    gate = proj[0][:, 3 * cols :].astype(F32) + proj[1][:, 3 * cols :].astype(F32)
    return (attn, gate, out[0].astype(F32) + out[1].astype(F32), new_table, new_accum)


def solution(mesh):
    placed = (
        P(("dp", "seq"), None),
        P(("dp", "seq"), None),
        P("dp", None),
        P(("dp", "seq"), None),
        P(("dp", "seq")),
        P(),
        P(),
        P(),
        P(("seq", "dp"), None),
        P(("seq", "dp")),
    )
    paired = mesh.shape["seq"] == SEQ and mesh.shape["dp"] == 2 * PLANE
    return jax.shard_map(
        body_pairs if paired else body_whole,
        mesh=mesh,
        in_specs=placed,
        out_specs=(
            P("dp", "seq"),
            P("dp", "seq"),
            P("dp", "seq"),
            P(("seq", "dp"), None),
            P(("seq", "dp")),
        ),
        check_vma=False,
    )
```

```python
import functools

import jax
import jax.numpy as jnp
from jax import lax
from jax.experimental import pallas as pl
from jax.experimental.pallas import tpu as pltpu
from jax.sharding import PartitionSpec as P

D = 1024
H = 16
DH = 64
PAIR = 2 * DH

NORM_EPS = 1e-05
LEARN_RATE = 0.1
VMEM_LIMIT = 56 * 1024 * 1024
BF = jnp.bfloat16
F32 = jnp.float32


def dot_nn(a, b):
    return lax.dot_general(a, b, (((1,), (0,)), ((), ())), preferred_element_type=F32)


def dot_nt(a, b):
    return lax.dot_general(a, b, (((1,), (1,)), ((), ())), preferred_element_type=F32)


def history_start(lengths_ref, users, place):
    start = jnp.zeros_like(place)
    end = jnp.int32(0)
    for user in range(users - 1):
        end = end + lengths_ref[0, user]
        start = jnp.where(place >= end, end, start)
    return start


def head_columns(kind, head):
    first = head * 3 * DH + kind * DH
    return slice(first, first + DH)


def split_pairs(acts_ref, split_ref, kind, block, blk):
    at = pl.ds(pl.multiple_of(block * blk, blk), blk)
    zero = jnp.zeros((blk, DH), BF)
    for p in range(split_ref.shape[0]):
        one, two = (acts_ref[at, head_columns(kind, 2 * p + h)] for h in range(2))
        below = pl.multiple_of(block * 2 * blk + blk, blk)
        split_ref[p, pl.ds(pl.multiple_of(block * 2 * blk, blk), blk), :] = jnp.concatenate([one, zero], axis=1)
        split_ref[p, pl.ds(below, blk), :] = jnp.concatenate([zero, two], axis=1)


def forward_kernel(*refs, blk, users, maxlen, count):
    lengths_ref, order_ref = refs[:2]
    x_refs = refs[2 : 2 + count]
    w_ref = refs[2 + count]
    outs = refs[3 + count :]
    if count > 1:
        x_out_ref, outs = outs[0], outs[1:]
    acts_ref, slopes_ref, gate_ref, weights_ref, score_slope_ref, heads_ref, k_t, v_split = outs
    i = pl.program_id(0)
    heads = weights_ref.shape[0]
    attn = 3 * heads * DH
    chunks = x_refs[0].shape[0] // blk

    @pl.when(i == 0)
    def _():
        for b in range(count):
            for r in range(chunks):
                at = pl.ds(pl.multiple_of(order_ref[b * chunks + r] * blk, blk), blk)
                x = x_refs[b][r * blk : (r + 1) * blk, :]
                if count > 1:
                    x_out_ref[at, :] = x
                for lane in range(0, w_ref.shape[1], 512):
                    lanes = slice(lane, lane + 512)
                    half = 0.5 * dot_nn(x, w_ref[:, lanes])
                    t = jnp.tanh(half)
                    prod = half * t
                    silu = half + prod
                    acts_ref[at, lanes] = silu.astype(BF)
                    slopes_ref[at, lanes] = (0.5 * (1.0 + t) * (1.0 + half - prod)).astype(BF)
                    skip = max(0, attn - lane)
                    if skip < 512:
                        gate_ref[at, lane + skip - attn : lane + 512 - attn] = silu[:, skip:]
                for h in range(heads):
                    k_t[h * DH : (h + 1) * DH, at] = jnp.transpose(acts_ref[at, head_columns(2, h)])
                split_pairs(acts_ref, v_split, 0, order_ref[b * chunks + r], blk)

    at_i = pl.ds(pl.multiple_of(i * blk, blk), blk)
    q_half = [acts_ref[at_i, head_columns(1, h)] * jnp.asarray(0.5 * DH**-0.5, BF) for h in range(heads)]
    row = i * blk + lax.broadcasted_iota(jnp.int32, (blk, blk), 0)
    col0 = lax.broadcasted_iota(jnp.int32, (blk, blk), 1)
    start = history_start(lengths_ref, users, row)

    def column(j, acc):
        at_j = pl.ds(pl.multiple_of(j * blk, blk), blk)
        both_j = pl.ds(pl.multiple_of(j * 2 * blk, 2 * blk), 2 * blk)
        col = col0 + j * blk
        allowed = (col <= row) & (col >= start)
        per_head = []
        for h in range(heads):
            half = dot_nn(q_half[h], k_t[h * DH : (h + 1) * DH, at_j])
            half = jnp.where(allowed, half, -64.0)
            t = jnp.tanh(half)
            p = half * t
            weights = (half + p).astype(BF)
            weights_ref[h, :, at_j] = weights
            score_slope_ref[h, :, at_j] = ((1.0 + t) * (1.0 + half - p)).astype(BF)
            per_head.append(weights)
        return tuple(
            acc[p] + dot_nn(jnp.concatenate(per_head[2 * p : 2 * p + 2], axis=1), v_split[p, both_j, :])
            for p in range(heads // 2)
        )

    first = history_start(lengths_ref, users, i * blk) // blk
    zero = jnp.zeros((blk, PAIR), F32)
    acc = lax.fori_loop(first, i + 1, column, (zero,) * (heads // 2))
    heads_ref[...] = (jnp.concatenate(acc, axis=1) * (1.0 / maxlen)).astype(BF)


def forward_attention(lengths, order, x_blocks, w_own, blk, maxlen):
    count = len(x_blocks)
    block_rows = x_blocks[0].shape[0]
    positions = count * block_rows
    cols = w_own.shape[1] // 4
    heads = cols // DH
    users = lengths.shape[1]
    elements = heads * positions * positions // 2
    whole = lambda i: (0, 0)
    out_specs = [
        pl.BlockSpec((positions, 4 * cols), whole),
        pl.BlockSpec((positions, 4 * cols), whole),
        pl.BlockSpec((positions, cols), whole),
        pl.BlockSpec((heads, blk, positions), lambda i: (0, i, 0)),
        pl.BlockSpec((heads, blk, positions), lambda i: (0, i, 0)),
        pl.BlockSpec((blk, cols), lambda i: (i, 0)),
    ]
    out_shape = [
        jax.ShapeDtypeStruct((positions, 4 * cols), BF),
        jax.ShapeDtypeStruct((positions, 4 * cols), BF),
        jax.ShapeDtypeStruct((positions, cols), F32),
        jax.ShapeDtypeStruct((heads, positions, positions), BF),
        jax.ShapeDtypeStruct((heads, positions, positions), BF),
        jax.ShapeDtypeStruct((positions, cols), BF),
    ]
    if count > 1:
        out_specs = [pl.BlockSpec((positions, D), whole)] + out_specs
        out_shape = [jax.ShapeDtypeStruct((positions, D), BF)] + out_shape
    return pl.pallas_call(
        functools.partial(forward_kernel, blk=blk, users=users, maxlen=maxlen, count=count),
        grid=(positions // blk,),
        in_specs=[pl.BlockSpec(memory_space=pltpu.SMEM), pl.BlockSpec(memory_space=pltpu.SMEM)]
        + [pl.BlockSpec((block_rows, D), whole)] * count
        + [pl.BlockSpec((D, 4 * cols), whole)],
        out_specs=out_specs,
        out_shape=out_shape,
        scratch_shapes=[pltpu.VMEM((cols, positions), BF), pltpu.VMEM((cols // PAIR, 2 * positions, PAIR), BF)],
        compiler_params=pltpu.CompilerParams(vmem_limit_bytes=VMEM_LIMIT),
        cost_estimate=pl.CostEstimate(
            flops=8 * positions * D * cols + 4 * elements * 256,
            bytes_accessed=4 * positions * D + 4 * elements,
            transcendentals=elements,
        ),
        name="attention_forward",
    )(lengths, order, *x_blocks, w_own)


def stats_kernel(*refs, blk, count):
    order_ref = refs[0]
    og_refs = refs[1 : 1 + count]
    w_ref, gate_ref, heads_ref = refs[1 + count : 4 + count]
    outs = refs[4 + count :]
    if count > 1:
        og_out_ref, outs = outs[0], outs[1:]
    mg_ref, stats_ref = outs
    chunks = og_refs[0].shape[0] // blk
    for b in range(count):
        for r in range(chunks):
            at = pl.ds(pl.multiple_of(order_ref[b * chunks + r] * blk, blk), blk)
            og = og_refs[b][r * blk : (r + 1) * blk, :]
            if count > 1:
                og_out_ref[at, :] = og
            mg = dot_nt(og, w_ref[...])
            mg_ref[at, :] = mg
            ng = mg * gate_ref[at, :]
            heads = heads_ref[at, :].astype(F32)
            mean = jnp.mean(heads, axis=1, keepdims=True)
            centred = heads - mean
            square = jnp.sum(centred * centred, axis=1, keepdims=True)
            total = jnp.sum(ng, axis=1, keepdims=True)
            cross = jnp.sum(ng * centred, axis=1, keepdims=True)
            lane = lax.broadcasted_iota(jnp.int32, (blk, 128), 1)
            packed = jnp.where(lane == 0, mean, jnp.where(lane == 1, square, jnp.where(lane == 2, total, cross)))
            stats_ref[:, at] = jnp.transpose(packed)[:8, :]


def event_stats(order, og_blocks, w_out_own, gate, heads, blk):
    positions, cols = heads.shape
    count = len(og_blocks)
    vmem = pl.BlockSpec(memory_space=pltpu.VMEM)
    out_shape = [
        jax.ShapeDtypeStruct((positions, cols), F32),
        jax.ShapeDtypeStruct((8, positions), F32),
    ]
    if count > 1:
        out_shape = [jax.ShapeDtypeStruct((positions, D), BF)] + out_shape
    return pl.pallas_call(
        functools.partial(stats_kernel, blk=blk, count=count),
        in_specs=[pl.BlockSpec(memory_space=pltpu.SMEM)] + [vmem] * (count + 3),
        out_specs=[vmem] * len(out_shape),
        out_shape=out_shape,
        compiler_params=pltpu.CompilerParams(vmem_limit_bytes=VMEM_LIMIT),
        cost_estimate=pl.CostEstimate(
            flops=2 * positions * cols * D, bytes_accessed=4 * positions * D + 10 * positions * cols, transcendentals=0
        ),
        name="event_stats",
    )(order, *og_blocks, w_out_own, gate, heads)


def combined_stats(stats_refs, cols):
    shards = len(stats_refs)
    positions = stats_refs[0].shape[1]
    means = [ref[0:1, :] for ref in stats_refs]
    mean = sum(means) * (1.0 / shards)
    square = jnp.zeros_like(mean)
    total = jnp.zeros_like(mean)
    cross = jnp.zeros_like(mean)
    for s, ref in enumerate(stats_refs):
        shift = means[s] - mean
        part = ref[2:3, :]
        square = square + ref[1:2, :] + cols * shift * shift
        total = total + part
        cross = cross + ref[3:4, :] + shift * part
    inv_dev = lax.rsqrt(square * (1.0 / D) + NORM_EPS)
    kind = lax.broadcasted_iota(jnp.int32, (128, positions), 0)
    rest = jnp.where(kind == 2, total * (1.0 / D), cross * inv_dev * (1.0 / D))
    packed = jnp.where(kind == 0, mean, jnp.where(kind == 1, inv_dev, rest))
    per_event = jnp.transpose(packed)
    return [per_event[:, k : k + 1] for k in range(4)]


def backward_kernel(*refs, blk, users, maxlen, shards):
    lengths_ref = refs[0]
    stats_refs = refs[1 : 1 + shards]
    mg_ref, gate_ref, heads_ref, acts_ref, slopes_ref, weights_ref, score_slope_ref = refs[1 + shards : 8 + shards]
    grad_ref, mixed_ref, o_ref, o_t, q_t, v_t, k_split, vg_t, kg_t, qg = refs[8 + shards :]
    i = pl.program_id(0)
    positions, cols = o_ref.shape
    heads = cols // DH
    blocks = positions // blk
    scale = DH ** (-0.5)

    @pl.when(i == 0)
    def _():
        mean, inv_dev, total, cross = combined_stats(stats_refs, cols)
        for p in range(heads // 2):
            lanes = slice(p * PAIR, (p + 1) * PAIR)
            normed = (heads_ref[:, lanes].astype(F32) - mean) * inv_dev
            gate = gate_ref[:, lanes]
            mg = mg_ref[:, lanes]
            mixed_ref[:, lanes] = (normed * gate).astype(BF)
            gate_lanes = slice(3 * cols + p * PAIR, 3 * cols + (p + 1) * PAIR)
            gate_slope = slopes_ref[:, gate_lanes].astype(F32)
            grad_ref[:, gate_lanes] = (mg * normed * gate_slope).astype(BF)
            o_ref[:, lanes] = (inv_dev * (mg * gate - total - normed * cross)).astype(BF)
        o_t[...] = jnp.transpose(o_ref[...])
        for scratch, kind in ((v_t, 0), (q_t, 1)):
            scratch[...] = jnp.transpose(jnp.concatenate([acts_ref[:, head_columns(kind, h)] for h in range(heads)], axis=1))
        for block in range(blocks):
            split_pairs(acts_ref, k_split, 2, block, blk)
        vg_t[...] = jnp.zeros_like(vg_t)
        kg_t[...] = jnp.zeros_like(kg_t)

    at_i = pl.ds(pl.multiple_of(i * blk, blk), blk)
    o_i = [o_ref[at_i, h * DH : (h + 1) * DH] for h in range(heads)]

    def column(j, acc):
        at_j = pl.ds(pl.multiple_of(j * blk, blk), blk)
        both_j = pl.ds(pl.multiple_of(j * 2 * blk, 2 * blk), 2 * blk)
        per_head = []
        for h in range(heads):
            lanes = slice(h * DH, (h + 1) * DH)
            weight_grad = dot_nn(o_i[h], v_t[lanes, at_j])
            score_grad = (weight_grad * score_slope_ref[h, :, at_j].astype(F32)).astype(BF)
            vg_t[lanes, at_j] += dot_nn(o_t[lanes, at_i], weights_ref[h, :, at_j])
            kg_t[lanes, at_j] += dot_nn(q_t[lanes, at_i], score_grad)
            per_head.append(score_grad)
        return tuple(
            acc[p] + dot_nn(jnp.concatenate(per_head[2 * p : 2 * p + 2], axis=1), k_split[p, both_j, :])
            for p in range(heads // 2)
        )

    first = history_start(lengths_ref, users, i * blk) // blk
    zero = jnp.zeros((blk, PAIR), F32)
    acc = lax.fori_loop(first, i + 1, column, (zero,) * (heads // 2))
    qg[at_i, :] = jnp.concatenate(acc, axis=1)

    @pl.when(i == blocks - 1)
    def _():
        factor = 0.5 * scale / maxlen
        grads = [jnp.transpose(vg_t[...]) * (1.0 / maxlen), qg[...] * factor, jnp.transpose(kg_t[...]) * factor]
        pieces = [grads[kind][:, h * DH : (h + 1) * DH] for h in range(heads) for kind in range(3)]
        for n in range(3 * heads // 2):
            lanes = slice(n * PAIR, (n + 1) * PAIR)
            grad = jnp.concatenate(pieces[2 * n : 2 * n + 2], axis=1).astype(BF).astype(F32)
            grad_ref[:, lanes] = (grad * slopes_ref[:, lanes].astype(F32)).astype(BF)


def backward_attention(lengths, stats, mg, gate, head_outs, acts, slopes, weights, score_slope, blk, maxlen):
    positions, cols = mg.shape
    heads = cols // DH
    shards = len(stats)
    users = lengths.shape[1]
    elements = heads * positions * positions // 2
    whole = lambda i: (0, 0)
    return pl.pallas_call(
        functools.partial(backward_kernel, blk=blk, users=users, maxlen=maxlen, shards=shards),
        grid=(positions // blk,),
        in_specs=[pl.BlockSpec(memory_space=pltpu.SMEM)]
        + [pl.BlockSpec((8, positions), whole)] * shards
        + [
            pl.BlockSpec((positions, cols), whole),
            pl.BlockSpec((positions, cols), whole),
            pl.BlockSpec((positions, cols), whole),
            pl.BlockSpec((positions, 4 * cols), whole),
            pl.BlockSpec((positions, 4 * cols), whole),
            pl.BlockSpec((heads, blk, positions), lambda i: (0, i, 0)),
            pl.BlockSpec((heads, blk, positions), lambda i: (0, i, 0)),
        ],
        out_specs=[pl.BlockSpec((positions, 4 * cols), whole), pl.BlockSpec((positions, cols), whole)],
        out_shape=[
            jax.ShapeDtypeStruct((positions, 4 * cols), BF),
            jax.ShapeDtypeStruct((positions, cols), BF),
        ],
        scratch_shapes=[
            pltpu.VMEM((positions, cols), BF),
            pltpu.VMEM((cols, positions), BF),
            pltpu.VMEM((cols, positions), BF),
            pltpu.VMEM((cols, positions), BF),
            pltpu.VMEM((cols // PAIR, 2 * positions, PAIR), BF),
            pltpu.VMEM((cols, positions), F32),
            pltpu.VMEM((cols, positions), F32),
            pltpu.VMEM((positions, cols), F32),
        ],
        compiler_params=pltpu.CompilerParams(vmem_limit_bytes=VMEM_LIMIT),
        cost_estimate=pl.CostEstimate(
            flops=8 * elements * 256, bytes_accessed=4 * elements + 26 * positions * cols, transcendentals=0
        ),
        name="attention_backward",
    )(lengths, *stats, mg, gate, head_outs, acts, slopes, weights, score_slope)


def update_kernel(rows_ref, table_ref, accum_ref, new_table_ref, new_accum_ref, ids):
    i = pl.program_id(0)
    blk = table_ref.shape[0]
    slots = rows_ref.shape[0]

    @pl.when(i == 0)
    def _():
        numbers = jnp.transpose(rows_ref[:, D:].astype(F32))
        ids[...] = (numbers[0:1, :] * 256.0 + numbers[1:2, :]).astype(jnp.int32)

    row = i * blk + lax.broadcasted_iota(jnp.int32, (blk, slots), 0)
    hits = jnp.where(row == ids[...], 1.0, 0.0).astype(BF)
    grad = dot_nn(hits, rows_ref[:, :D])
    accum = jnp.transpose(jnp.broadcast_to(accum_ref[...], (128, blk)))[:, :1] + jnp.mean(grad * grad, axis=1, keepdims=True)
    new_accum_ref[...] = jnp.transpose(jnp.broadcast_to(accum, (blk, 128)))[:1, :]
    new_table_ref[...] = table_ref[...] - LEARN_RATE * grad * lax.rsqrt(accum)


def update_rows(got_rows, emb_table, row_accum):
    rows_own = emb_table.shape[0]
    slots = got_rows.shape[0]
    blk = min(256, rows_own)
    new_table, new_accum = pl.pallas_call(
        update_kernel,
        grid=(rows_own // blk,),
        in_specs=[
            pl.BlockSpec((slots, D + 128), lambda i: (0, 0)),
            pl.BlockSpec((blk, D), lambda i: (i, 0)),
            pl.BlockSpec((1, blk), lambda i: (0, i)),
        ],
        out_specs=[
            pl.BlockSpec((blk, D), lambda i: (i, 0)),
            pl.BlockSpec((1, blk), lambda i: (0, i)),
        ],
        out_shape=[
            jax.ShapeDtypeStruct((rows_own, D), F32),
            jax.ShapeDtypeStruct((1, rows_own), F32),
        ],
        scratch_shapes=[pltpu.VMEM((1, slots), jnp.int32)],
        compiler_params=pltpu.CompilerParams(vmem_limit_bytes=VMEM_LIMIT),
        cost_estimate=pl.CostEstimate(
            flops=2 * rows_own * slots * D, bytes_accessed=8 * rows_own * D + 2 * slots * D, transcendentals=rows_own
        ),
        name="update_rows",
    )(got_rows, emb_table, row_accum.reshape(1, rows_own))
    return new_table, new_accum.reshape(rows_own)


def own_weights(w_attn, w_gate, part, cols):
    attn = lax.dynamic_slice_in_dim(w_attn, part * 3 * cols, 3 * cols, 1)
    gate = lax.dynamic_slice_in_dim(w_gate, part * cols, cols, 1)
    return jnp.concatenate([attn, gate], axis=1)


def row_slots(owners, rows, devices, capacity):
    events = owners.shape[0]
    owner_hits = (owners[:, None] == jnp.arange(devices, dtype=jnp.int32)[None, :]).astype(BF)
    place = jnp.arange(events, dtype=jnp.int32)
    before = (place[:, None] > place[None, :]).astype(BF)
    earlier = jnp.dot(before, owner_hits, preferred_element_type=F32)
    slots = jnp.sum(earlier * owner_hits.astype(F32), axis=1).astype(jnp.int32)
    flat_slot = owners * capacity + slots
    slot_hits = jnp.arange(devices * capacity, dtype=jnp.int32)[:, None] == flat_slot[None, :]
    lane = jnp.arange(128, dtype=jnp.int32)[None, :]
    numbers = jnp.where(lane == 0, rows[:, None] // 256, jnp.where(lane == 1, rows[:, None] % 256, 0))
    return slot_hits.astype(BF), numbers.astype(BF)


def to_owners(rows, devices, capacity):
    shape = (devices, capacity) + rows.shape[1:]
    got = lax.all_to_all(rows.reshape(shape), ("seq", "dp"), split_axis=0, concat_axis=0, tiled=True)
    return got.reshape(rows.shape)


TN = (((0,), (0,)), ((), ()))


def dot_tn(a, b):
    return lax.dot_general(a, b, TN, preferred_element_type=F32)


def body_whole(
    layer_input, out_grad, lengths, item_owner, item_row, w_attn, w_gate, w_out, emb_table, row_accum
):
    seq_count = lax.axis_size("seq")
    dp_count = lax.axis_size("dp")
    devices = seq_count * dp_count
    seq_id = lax.axis_index("seq")
    tokens_dev = layer_input.shape[0]
    positions = tokens_dev * seq_count
    maxlen = 2 * positions // 3
    blk = min(256, positions)
    cols = D // seq_count
    capacity = max(2, 2 * tokens_dev // devices)

    w_own = own_weights(w_attn, w_gate, seq_id, cols)
    w_out_own = lax.dynamic_slice_in_dim(w_out, seq_id * cols, cols, 0)
    slot_matrix, numbers = row_slots(item_owner[:, 0], item_row, devices, capacity)

    x_full = lax.all_gather(layer_input, "seq", axis=0, tiled=True)
    og_full = lax.all_gather(out_grad, "seq", axis=0, tiled=True)
    order = jnp.arange(positions // blk, dtype=jnp.int32)
    acts, slopes, gate, weights, score_slope, heads = forward_attention(
        lengths, order, [x_full], w_own, blk, maxlen
    )
    mg, stats_own = event_stats(order, [og_full], w_out_own, gate, heads, blk)
    stats = lax.all_gather(stats_own, "seq", axis=0, tiled=False)
    grads, mixed = backward_attention(
        lengths, [stats[s] for s in range(seq_count)], mg, gate, heads, acts, slopes, weights, score_slope, blk, maxlen
    )

    input_part = dot_nt(grads, w_own).astype(BF)
    got = lax.all_to_all(
        input_part.reshape(seq_count, tokens_dev, D), "seq", split_axis=0, concat_axis=0, tiled=True
    )
    input_grad = jnp.sum(got.astype(F32), axis=0) + out_grad.astype(F32)
    rows = jnp.concatenate([input_grad.astype(BF), numbers], axis=1)
    rows = jnp.dot(slot_matrix, rows, preferred_element_type=F32).astype(BF)
    got_rows = to_owners(rows, devices, capacity)
    new_table, new_accum = update_rows(got_rows, emb_table, row_accum)

    out_part = dot_tn(mixed, og_full).astype(BF)
    share = dp_count // seq_count
    out_part = out_part.reshape(share, D // dp_count, seq_count, cols).transpose(0, 2, 1, 3).reshape(D, cols)
    merged = jnp.concatenate([dot_tn(x_full, grads).astype(BF), out_part], axis=1)
    merged = lax.psum_scatter(merged, "dp", scatter_dimension=0, tiled=True)
    steps = []
    for s in range(seq_count):
        for piece in range(dp_count):
            part, target = divmod(piece, seq_count)
            steps.append((s * dp_count + piece, target * dp_count + s * share + part))
    grad_out = lax.ppermute(merged[:, 4 * cols :], ("seq", "dp"), steps).astype(F32)
    grad_attn = merged[:, : 3 * cols].astype(F32)
    grad_gate = merged[:, 3 * cols : 4 * cols].astype(F32)
    return (grad_attn, grad_gate, grad_out, new_table, new_accum)


SMEM = pl.BlockSpec(memory_space=pltpu.SMEM)
VMEM = pl.BlockSpec(memory_space=pltpu.VMEM)


def small_call(kernel, name, in_specs, out_shape, cost=0):
    return pl.pallas_call(
        kernel,
        in_specs=in_specs,
        out_specs=[VMEM] * len(out_shape),
        out_shape=out_shape,
        compiler_params=pltpu.CompilerParams(vmem_limit_bytes=VMEM_LIMIT),
        cost_estimate=pl.CostEstimate(flops=0, bytes_accessed=cost, transcendentals=0),
        name=name,
    )


def pack_kernel(mine_ref, core_ref, near_ref, og_ref, slots_ref, numbers_ref, rows_ref):
    total = mine_ref[...] + core_ref[...].astype(F32) + near_ref[...].astype(F32) + og_ref[...].astype(F32)
    rows_ref[:, :D] = dot_nn(slots_ref[...], total.astype(BF)).astype(BF)
    rows_ref[:, D:] = dot_nn(slots_ref[...], numbers_ref[...]).astype(BF)


def tail_kernel(
    at_ref, x_ref, grads_ref, mixed_ref, og_ref, w_ref, a_kept, a_sent, b_kept, b_sent, mine_ref
):
    chip = pl.program_id(0)
    chip_y, chip_x = chip // 2, chip % 2
    events = mine_ref.shape[0]

    @pl.when(chip == 0)
    def _():
        block = grads_ref[pl.ds(pl.multiple_of(at_ref[2] * events, events), events), :]
        mine_ref[...] = dot_nt(block, w_ref[...])

    cut = a_kept.shape[2]
    proj = dot_tn(x_ref[...], grads_ref[...]).astype(BF)
    out = dot_tn(mixed_ref[...], og_ref[...]).astype(BF)
    rest = proj.shape[1] - cut

    def store_b(ref):
        ref[chip_x, :, :rest] = proj[:, cut:]
        ref[chip_x, :, rest:] = out

    @pl.when(chip_x == at_ref[1])
    def _():
        a_kept[chip_y] = proj[:, :cut]

    @pl.when(chip_x != at_ref[1])
    def _():
        a_sent[chip_y] = proj[:, :cut]

    @pl.when(chip_y == at_ref[0])
    def _():
        store_b(b_kept)

    @pl.when(chip_y != at_ref[0])
    def _():
        store_b(b_sent)


def tail_products(at, x_full, grads, mixed, og_full, w_own, events):
    positions, cols = mixed.shape
    rows = D // PLANE
    whole = lambda e: (0, 0)
    half = jax.ShapeDtypeStruct((2, rows, 5 * cols // 2), BF)
    return pl.pallas_call(
        tail_kernel,
        grid=(PLANE,),
        in_specs=[
            SMEM,
            pl.BlockSpec((positions, rows), lambda e: (0, e)),
            pl.BlockSpec((positions, 4 * cols), whole),
            pl.BlockSpec((positions, cols), whole),
            pl.BlockSpec((positions, rows), lambda e: (0, e)),
            pl.BlockSpec((D, 4 * cols), whole),
        ],
        out_specs=[pl.BlockSpec(half.shape, lambda e: (0, 0, 0))] * 4 + [pl.BlockSpec((events, D), whole)],
        out_shape=[half] * 4 + [jax.ShapeDtypeStruct((events, D), F32)],
        compiler_params=pltpu.CompilerParams(vmem_limit_bytes=VMEM_LIMIT),
        cost_estimate=pl.CostEstimate(flops=0, bytes_accessed=40_000_000, transcendentals=0),
        name="tail_products",
    )(at, x_full, grads, mixed, og_full, w_own)


def merge_kernel(bit_ref, kept_ref, got_ref, next_kept, next_sent):
    bit = bit_ref[0]
    next_kept[...] = (kept_ref[bit].astype(F32) + got_ref[bit].astype(F32)).astype(BF)
    next_sent[...] = (kept_ref[1 - bit].astype(F32) + got_ref[1 - bit].astype(F32)).astype(BF)


def merge_halves(bit, kept, got):
    out = jax.ShapeDtypeStruct(kept.shape[1:], BF)
    return small_call(merge_kernel, "merge_halves", [SMEM, VMEM, VMEM], [out, out])(bit, kept, got)


def last_kernel(bit_ref, a_kept, a_got, b_kept, b_got, proj_one, proj_other, out_one, out_other):
    rows, cut = proj_one.shape[0], a_kept.shape[1]
    rest = proj_one.shape[1] - cut
    for flip, proj_ref, out_ref in ((0, proj_one, out_one), (1, proj_other, out_other)):
        half = bit_ref[0] + flip - 2 * flip * bit_ref[0]
        at = pl.ds(pl.multiple_of(half * rows, rows), rows)
        proj_ref[:, :cut] = (a_kept[at, :].astype(F32) + a_got[at, :].astype(F32)).astype(BF)
        b = (b_kept[at, :].astype(F32) + b_got[at, :].astype(F32)).astype(BF)
        proj_ref[:, cut:] = b[:, :rest]
        out_ref[...] = b[:, rest:]


def last_pieces(bit, a_kept, a_got, b_kept, b_got, cols):
    rows = a_kept.shape[0] // 2
    proj = jax.ShapeDtypeStruct((rows, 4 * cols), BF)
    out = jax.ShapeDtypeStruct((rows, cols), BF)
    return small_call(last_kernel, "last_pieces", [SMEM] + [VMEM] * 4, [proj, proj, out, out])(
        bit, a_kept, a_got, b_kept, b_got
    )


SEQ = 4
PLANE = 4


def send(array, target):
    steps = []
    for s in range(SEQ):
        for e in range(PLANE):
            for c in range(2):
                to = target(s, e, c)
                if to is not None:
                    steps.append((s * 2 * PLANE + 2 * e + c, to[0] * 2 * PLANE + 2 * to[1] + to[2]))
    return lax.ppermute(array, ("seq", "dp"), steps)


def home(s, c):
    return c == s // 2


def swap_far(array):
    return send(array, lambda s, e, c: None if home(s, c) else (3 - s, e, 1 - c))


def fetch_near(array):
    return send(array, lambda s, e, c: (s ^ 1, e, c) if home(s, c) else ((3 - s) ^ 1, e, 1 - c))


def swap_near(array):
    return send(array, lambda s, e, c: (s ^ 1, e, c))


def swap_core(array):
    return send(array, lambda s, e, c: (s, e, 1 - c))


def swap_x(array):
    return send(array, lambda s, e, c: (s, e ^ 1, c))


def swap_y(array):
    return send(array, lambda s, e, c: (s, e ^ 2, c))


def tie(*arrays):
    return lax.optimization_barrier(arrays)


def body_pairs(
    layer_input, out_grad, lengths, item_owner, item_row, w_attn, w_gate, w_out, emb_table, row_accum
):
    devices = 2 * PLANE * SEQ
    s = lax.axis_index("seq")
    d = lax.axis_index("dp")
    e, c = d // 2, d % 2
    y, x = e // 2, e % 2
    tokens_dev = layer_input.shape[0]
    positions = tokens_dev * SEQ
    maxlen = 2 * positions // 3
    blk = min(256, positions)
    cols = D // SEQ
    rows_own = emb_table.shape[0]
    capacity = max(2, 2 * tokens_dev // devices)
    at_home = c == s // 2
    part = 2 * (s % 2) + c

    def block_of(seq, core):
        return jnp.where(core == seq // 2, seq, 3 - seq)

    mine_at, near_at = block_of(s, c), block_of(s ^ 1, c)
    core_at, diag_at = block_of(s, 1 - c), block_of(s ^ 1, 1 - c)
    order = jnp.stack([mine_at, near_at, core_at, diag_at]).astype(jnp.int32)

    x_far = swap_far(layer_input)
    x_near = fetch_near(layer_input)
    users = lengths.shape[1]
    keys = (item_owner[:, 0] * rows_own + item_row).reshape(1, tokens_dev)
    small = jnp.concatenate([keys, jnp.pad(lengths, ((0, 0), (0, 128 - users)))], axis=1)
    small = jnp.where(at_home, small, swap_far(small))
    keys, lengths = small[0, :tokens_dev], small[:, tokens_dev : tokens_dev + users]
    w_own = own_weights(w_attn, w_gate, part, cols)
    w_out_own = lax.dynamic_slice_in_dim(w_out, part * cols, cols, 0)
    slot_matrix, numbers = row_slots(keys // rows_own, keys % rows_own, devices, capacity)
    x_far, x_near, w_own, w_out_own, slot_matrix, numbers, lengths = tie(
        x_far, x_near, w_own, w_out_own, slot_matrix, numbers, lengths
    )
    x_here = jnp.concatenate([jnp.where(at_home, layer_input, x_far), x_near], axis=0)
    x_there = swap_core(x_here)
    x_here, og_own = tie(x_here, out_grad)
    og_far = swap_far(og_own)
    og_near = fetch_near(og_own)

    x_full, acts, slopes, gate, weights, score_slope, heads = forward_attention(
        lengths, order, [x_here, x_there], w_own, blk, maxlen
    )
    og_far, og_near, heads = tie(og_far, og_near, heads)
    og_mine = jnp.where(at_home, og_own, og_far)
    og_here = jnp.concatenate([og_mine, og_near], axis=0)
    og_there = swap_core(og_here)
    og_full, mg, stats_own = event_stats(order, [og_here, og_there], w_out_own, gate, heads, blk)
    stats = [
        stats_own,
        swap_core(stats_own),
        swap_near(stats_own),
        send(stats_own, lambda s, e, c: (s ^ 1, e, 1 - c)),
    ]
    grads, mixed = backward_attention(
        lengths, stats, mg, gate, heads, acts, slopes, weights, score_slope, blk, maxlen
    )

    def input_part(grads, block):
        return dot_nt(lax.dynamic_slice_in_dim(grads, block * tokens_dev, tokens_dev, 0), w_own)

    diag_part = input_part(grads, diag_at).astype(BF)
    from_diag = swap_core(diag_part)
    diag_part, grads = tie(diag_part, grads)
    core_part = input_part(grads, core_at).astype(BF)
    from_core = swap_core(core_part)
    core_part, grads = tie(core_part, grads)
    near_part = input_part(grads, near_at)
    near_part, from_diag, from_core = tie(near_part, from_diag, from_core)
    near_sum = (near_part + from_diag.astype(F32)).astype(BF)
    from_near = swap_near(near_sum)

    near_sum, grads, mixed = tie(near_sum, grads, mixed)
    at = jnp.stack([y, x, mine_at]).astype(jnp.int32)
    a_kept, a_sent, b_kept, b_sent, mine_part = tail_products(
        at, x_full, grads, mixed, og_full, w_own, tokens_dev
    )
    a_got = swap_x(a_sent)
    b_got = swap_y(b_sent)

    out_rows = jax.ShapeDtypeStruct((devices * capacity, D + 128), BF)
    (rows,) = small_call(pack_kernel, "pack_rows", [VMEM] * 6, [out_rows], 40_000_000)(
        mine_part, from_core, from_near, og_mine, slot_matrix, numbers
    )
    rows, a_got, b_got = tie(rows, a_got, b_got)
    got_rows = to_owners(rows, devices, capacity)

    a_kept, a_sent = merge_halves(at[:1], a_kept, a_got)
    a_got = swap_y(a_sent)
    b_kept, b_sent = merge_halves(at[1:2], b_kept, b_got)
    b_got = swap_x(b_sent)

    pieces = last_pieces((s // 2).reshape(1).astype(jnp.int32), a_kept, a_got, b_kept, b_got, cols)
    *pieces, row_accum = tie(*pieces, row_accum)
    proj = [
        send(pieces[0], lambda s, e, c: (2 * (s % 2) + c, e, s // 2)),
        send(pieces[1], lambda s, e, c: (2 * (s % 2) + c, e, 1 - s // 2)),
    ]
    out = [
        send(pieces[2], lambda s, e, c: (e, 2 * (s % 2) + c, s // 2)),
        send(pieces[3], lambda s, e, c: (e, 2 * (s % 2) + c, 1 - s // 2)),
    ]
    new_table, new_accum = update_rows(got_rows, emb_table, row_accum)
    *proj, new_accum = tie(*proj, new_accum)
    attn = proj[0][:, : 3 * cols].astype(F32) + proj[1][:, : 3 * cols].astype(F32)
    gate = proj[0][:, 3 * cols :].astype(F32) + proj[1][:, 3 * cols :].astype(F32)
    return (attn, gate, out[0].astype(F32) + out[1].astype(F32), new_table, new_accum)


def solution(mesh):
    placed = (
        P(("dp", "seq"), None),
        P(("dp", "seq"), None),
        P("dp", None),
        P(("dp", "seq"), None),
        P(("dp", "seq")),
        P(),
        P(),
        P(),
        P(("seq", "dp"), None),
        P(("seq", "dp")),
    )
    paired = mesh.shape["seq"] == SEQ and mesh.shape["dp"] == 2 * PLANE
    return jax.shard_map(
        body_pairs if paired else body_whole,
        mesh=mesh,
        in_specs=placed,
        out_specs=(
            P("dp", "seq"),
            P("dp", "seq"),
            P("dp", "seq"),
            P(("seq", "dp"), None),
            P(("seq", "dp")),
        ),
        check_vma=False,
    )
```

```python
import functools

import jax
import jax.numpy as jnp
from jax import lax
from jax.experimental import pallas as pl
from jax.experimental.pallas import tpu as pltpu
from jax.sharding import PartitionSpec as P

D = 1024
H = 16
DH = 64
PAIR = 2 * DH

NORM_EPS = 1e-05
LEARN_RATE = 0.1
VMEM_LIMIT = 56 * 1024 * 1024
BF = jnp.bfloat16
F32 = jnp.float32


def dot_nn(a, b):
    return lax.dot_general(a, b, (((1,), (0,)), ((), ())), preferred_element_type=F32)


def dot_nt(a, b):
    return lax.dot_general(a, b, (((1,), (1,)), ((), ())), preferred_element_type=F32)


def history_start(lengths_ref, users, place):
    start = jnp.zeros_like(place)
    end = jnp.int32(0)
    for user in range(users - 1):
        end = end + lengths_ref[0, user]
        start = jnp.where(place >= end, end, start)
    return start


def head_columns(kind, head):
    first = head * 3 * DH + kind * DH
    return slice(first, first + DH)


def split_pairs(acts_ref, split_ref, kind, block, blk):
    at = pl.ds(pl.multiple_of(block * blk, blk), blk)
    zero = jnp.zeros((blk, DH), BF)
    for p in range(split_ref.shape[0]):
        one, two = (acts_ref[at, head_columns(kind, 2 * p + h)] for h in range(2))
        below = pl.multiple_of(block * 2 * blk + blk, blk)
        split_ref[p, pl.ds(pl.multiple_of(block * 2 * blk, blk), blk), :] = jnp.concatenate([one, zero], axis=1)
        split_ref[p, pl.ds(below, blk), :] = jnp.concatenate([zero, two], axis=1)


def forward_kernel(*refs, blk, users, maxlen, count):
    lengths_ref, order_ref = refs[:2]
    x_refs = refs[2 : 2 + count]
    w_ref = refs[2 + count]
    outs = refs[3 + count :]
    if count > 1:
        x_out_ref, outs = outs[0], outs[1:]
    acts_ref, slopes_ref, gate_ref, weights_ref, score_slope_ref, heads_ref, k_t, v_split = outs
    i = pl.program_id(0)
    heads = weights_ref.shape[0]
    attn = 3 * heads * DH
    chunks = x_refs[0].shape[0] // blk

    @pl.when(i == 0)
    def _():
        for b in range(count):
            for r in range(chunks):
                at = pl.ds(pl.multiple_of(order_ref[b * chunks + r] * blk, blk), blk)
                x = x_refs[b][r * blk : (r + 1) * blk, :]
                if count > 1:
                    x_out_ref[at, :] = x
                for lane in range(0, w_ref.shape[1], 512):
                    lanes = slice(lane, lane + 512)
                    half = 0.5 * dot_nn(x, w_ref[:, lanes])
                    t = jnp.tanh(half)
                    prod = half * t
                    silu = half + prod
                    acts_ref[at, lanes] = silu.astype(BF)
                    slopes_ref[at, lanes] = (0.5 * (1.0 + t) * (1.0 + half - prod)).astype(BF)
                    skip = max(0, attn - lane)
                    if skip < 512:
                        gate_ref[at, lane + skip - attn : lane + 512 - attn] = silu[:, skip:]
                for h in range(heads):
                    k_t[h * DH : (h + 1) * DH, at] = jnp.transpose(acts_ref[at, head_columns(2, h)])
                split_pairs(acts_ref, v_split, 0, order_ref[b * chunks + r], blk)

    at_i = pl.ds(pl.multiple_of(i * blk, blk), blk)
    q_half = [acts_ref[at_i, head_columns(1, h)] * jnp.asarray(0.5 * DH**-0.5, BF) for h in range(heads)]
    row = i * blk + lax.broadcasted_iota(jnp.int32, (blk, blk), 0)
    col0 = lax.broadcasted_iota(jnp.int32, (blk, blk), 1)
    start = history_start(lengths_ref, users, row)

    def column(j, acc):
        at_j = pl.ds(pl.multiple_of(j * blk, blk), blk)
        both_j = pl.ds(pl.multiple_of(j * 2 * blk, 2 * blk), 2 * blk)
        col = col0 + j * blk
        allowed = (col <= row) & (col >= start)
        per_head = []
        for h in range(heads):
            half = dot_nn(q_half[h], k_t[h * DH : (h + 1) * DH, at_j])
            half = jnp.where(allowed, half, -64.0)
            t = jnp.tanh(half)
            p = half * t
            weights = (half + p).astype(BF)
            weights_ref[h, :, at_j] = weights
            score_slope_ref[h, :, at_j] = ((1.0 + t) * (1.0 + half - p)).astype(BF)
            per_head.append(weights)
        return tuple(
            acc[p] + dot_nn(jnp.concatenate(per_head[2 * p : 2 * p + 2], axis=1), v_split[p, both_j, :])
            for p in range(heads // 2)
        )

    first = history_start(lengths_ref, users, i * blk) // blk
    zero = jnp.zeros((blk, PAIR), F32)
    acc = lax.fori_loop(first, i + 1, column, (zero,) * (heads // 2))
    heads_ref[...] = (jnp.concatenate(acc, axis=1) * (1.0 / maxlen)).astype(BF)


def forward_attention(lengths, order, x_blocks, w_own, blk, maxlen):
    count = len(x_blocks)
    block_rows = x_blocks[0].shape[0]
    positions = count * block_rows
    cols = w_own.shape[1] // 4
    heads = cols // DH
    users = lengths.shape[1]
    elements = heads * positions * positions // 2
    whole = lambda i: (0, 0)
    out_specs = [
        pl.BlockSpec((positions, 4 * cols), whole),
        pl.BlockSpec((positions, 4 * cols), whole),
        pl.BlockSpec((positions, cols), whole),
        pl.BlockSpec((heads, blk, positions), lambda i: (0, i, 0)),
        pl.BlockSpec((heads, blk, positions), lambda i: (0, i, 0)),
        pl.BlockSpec((blk, cols), lambda i: (i, 0)),
    ]
    out_shape = [
        jax.ShapeDtypeStruct((positions, 4 * cols), BF),
        jax.ShapeDtypeStruct((positions, 4 * cols), BF),
        jax.ShapeDtypeStruct((positions, cols), F32),
        jax.ShapeDtypeStruct((heads, positions, positions), BF),
        jax.ShapeDtypeStruct((heads, positions, positions), BF),
        jax.ShapeDtypeStruct((positions, cols), BF),
    ]
    if count > 1:
        out_specs = [pl.BlockSpec((positions, D), whole)] + out_specs
        out_shape = [jax.ShapeDtypeStruct((positions, D), BF)] + out_shape
    return pl.pallas_call(
        functools.partial(forward_kernel, blk=blk, users=users, maxlen=maxlen, count=count),
        grid=(positions // blk,),
        in_specs=[pl.BlockSpec(memory_space=pltpu.SMEM), pl.BlockSpec(memory_space=pltpu.SMEM)]
        + [pl.BlockSpec((block_rows, D), whole)] * count
        + [pl.BlockSpec((D, 4 * cols), whole)],
        out_specs=out_specs,
        out_shape=out_shape,
        scratch_shapes=[pltpu.VMEM((cols, positions), BF), pltpu.VMEM((cols // PAIR, 2 * positions, PAIR), BF)],
        compiler_params=pltpu.CompilerParams(vmem_limit_bytes=VMEM_LIMIT),
        cost_estimate=pl.CostEstimate(
            flops=8 * positions * D * cols + 4 * elements * 256,
            bytes_accessed=4 * positions * D + 4 * elements,
            transcendentals=elements,
        ),
        name="attention_forward",
    )(lengths, order, *x_blocks, w_own)


def stats_kernel(*refs, blk, count):
    order_ref = refs[0]
    og_refs = refs[1 : 1 + count]
    w_ref, gate_ref, heads_ref = refs[1 + count : 4 + count]
    outs = refs[4 + count :]
    if count > 1:
        og_out_ref, outs = outs[0], outs[1:]
    mg_ref, stats_ref = outs
    chunks = og_refs[0].shape[0] // blk
    for b in range(count):
        for r in range(chunks):
            at = pl.ds(pl.multiple_of(order_ref[b * chunks + r] * blk, blk), blk)
            og = og_refs[b][r * blk : (r + 1) * blk, :]
            if count > 1:
                og_out_ref[at, :] = og
            mg = dot_nt(og, w_ref[...])
            mg_ref[at, :] = mg
            ng = mg * gate_ref[at, :]
            heads = heads_ref[at, :].astype(F32)
            mean = jnp.mean(heads, axis=1, keepdims=True)
            centred = heads - mean
            square = jnp.sum(centred * centred, axis=1, keepdims=True)
            total = jnp.sum(ng, axis=1, keepdims=True)
            cross = jnp.sum(ng * centred, axis=1, keepdims=True)
            lane = lax.broadcasted_iota(jnp.int32, (blk, 128), 1)
            packed = jnp.where(lane == 0, mean, jnp.where(lane == 1, square, jnp.where(lane == 2, total, cross)))
            stats_ref[:, at] = jnp.transpose(packed)[:8, :]


def event_stats(order, og_blocks, w_out_own, gate, heads, blk):
    positions, cols = heads.shape
    count = len(og_blocks)
    vmem = pl.BlockSpec(memory_space=pltpu.VMEM)
    out_shape = [
        jax.ShapeDtypeStruct((positions, cols), F32),
        jax.ShapeDtypeStruct((8, positions), F32),
    ]
    if count > 1:
        out_shape = [jax.ShapeDtypeStruct((positions, D), BF)] + out_shape
    return pl.pallas_call(
        functools.partial(stats_kernel, blk=blk, count=count),
        in_specs=[pl.BlockSpec(memory_space=pltpu.SMEM)] + [vmem] * (count + 3),
        out_specs=[vmem] * len(out_shape),
        out_shape=out_shape,
        compiler_params=pltpu.CompilerParams(vmem_limit_bytes=VMEM_LIMIT),
        cost_estimate=pl.CostEstimate(
            flops=2 * positions * cols * D, bytes_accessed=4 * positions * D + 10 * positions * cols, transcendentals=0
        ),
        name="event_stats",
    )(order, *og_blocks, w_out_own, gate, heads)


def combined_stats(stats_refs, cols):
    shards = len(stats_refs)
    positions = stats_refs[0].shape[1]
    means = [ref[0:1, :] for ref in stats_refs]
    mean = sum(means) * (1.0 / shards)
    square = jnp.zeros_like(mean)
    total = jnp.zeros_like(mean)
    cross = jnp.zeros_like(mean)
    for s, ref in enumerate(stats_refs):
        shift = means[s] - mean
        part = ref[2:3, :]
        square = square + ref[1:2, :] + cols * shift * shift
        total = total + part
        cross = cross + ref[3:4, :] + shift * part
    inv_dev = lax.rsqrt(square * (1.0 / D) + NORM_EPS)
    kind = lax.broadcasted_iota(jnp.int32, (128, positions), 0)
    rest = jnp.where(kind == 2, total * (1.0 / D), cross * inv_dev * (1.0 / D))
    packed = jnp.where(kind == 0, mean, jnp.where(kind == 1, inv_dev, rest))
    per_event = jnp.transpose(packed)
    return [per_event[:, k : k + 1] for k in range(4)]


def backward_kernel(*refs, blk, users, maxlen, shards):
    lengths_ref = refs[0]
    stats_refs = refs[1 : 1 + shards]
    mg_ref, gate_ref, heads_ref, acts_ref, slopes_ref, weights_ref, score_slope_ref = refs[1 + shards : 8 + shards]
    grad_ref, mixed_ref, o_ref, o_t, q_t, v_t, k_split, vg_t, kg_t, qg = refs[8 + shards :]
    i = pl.program_id(0)
    positions, cols = o_ref.shape
    heads = cols // DH
    blocks = positions // blk
    scale = DH ** (-0.5)

    @pl.when(i == 0)
    def _():
        mean, inv_dev, total, cross = combined_stats(stats_refs, cols)
        for p in range(heads // 2):
            lanes = slice(p * PAIR, (p + 1) * PAIR)
            normed = (heads_ref[:, lanes].astype(F32) - mean) * inv_dev
            gate = gate_ref[:, lanes]
            mg = mg_ref[:, lanes]
            mixed_ref[:, lanes] = (normed * gate).astype(BF)
            gate_lanes = slice(3 * cols + p * PAIR, 3 * cols + (p + 1) * PAIR)
            gate_slope = slopes_ref[:, gate_lanes].astype(F32)
            grad_ref[:, gate_lanes] = (mg * normed * gate_slope).astype(BF)
            o_ref[:, lanes] = (inv_dev * (mg * gate - total - normed * cross)).astype(BF)
        o_t[...] = jnp.transpose(o_ref[...])
        for scratch, kind in ((v_t, 0), (q_t, 1)):
            scratch[...] = jnp.transpose(jnp.concatenate([acts_ref[:, head_columns(kind, h)] for h in range(heads)], axis=1))
        for block in range(blocks):
            split_pairs(acts_ref, k_split, 2, block, blk)
        vg_t[...] = jnp.zeros_like(vg_t)
        kg_t[...] = jnp.zeros_like(kg_t)

    at_i = pl.ds(pl.multiple_of(i * blk, blk), blk)
    o_i = [o_ref[at_i, h * DH : (h + 1) * DH] for h in range(heads)]

    def column(j, acc):
        at_j = pl.ds(pl.multiple_of(j * blk, blk), blk)
        both_j = pl.ds(pl.multiple_of(j * 2 * blk, 2 * blk), 2 * blk)
        per_head = []
        for h in range(heads):
            lanes = slice(h * DH, (h + 1) * DH)
            weight_grad = dot_nn(o_i[h], v_t[lanes, at_j])
            score_grad = (weight_grad * score_slope_ref[h, :, at_j].astype(F32)).astype(BF)
            vg_t[lanes, at_j] += dot_nn(o_t[lanes, at_i], weights_ref[h, :, at_j])
            kg_t[lanes, at_j] += dot_nn(q_t[lanes, at_i], score_grad)
            per_head.append(score_grad)
        return tuple(
            acc[p] + dot_nn(jnp.concatenate(per_head[2 * p : 2 * p + 2], axis=1), k_split[p, both_j, :])
            for p in range(heads // 2)
        )

    first = history_start(lengths_ref, users, i * blk) // blk
    zero = jnp.zeros((blk, PAIR), F32)
    acc = lax.fori_loop(first, i + 1, column, (zero,) * (heads // 2))
    qg[at_i, :] = jnp.concatenate(acc, axis=1)

    @pl.when(i == blocks - 1)
    def _():
        factor = 0.5 * scale / maxlen
        grads = [jnp.transpose(vg_t[...]) * (1.0 / maxlen), qg[...] * factor, jnp.transpose(kg_t[...]) * factor]
        pieces = [grads[kind][:, h * DH : (h + 1) * DH] for h in range(heads) for kind in range(3)]
        for n in range(3 * heads // 2):
            lanes = slice(n * PAIR, (n + 1) * PAIR)
            grad = jnp.concatenate(pieces[2 * n : 2 * n + 2], axis=1).astype(BF).astype(F32)
            grad_ref[:, lanes] = (grad * slopes_ref[:, lanes].astype(F32)).astype(BF)


def backward_attention(lengths, stats, mg, gate, head_outs, acts, slopes, weights, score_slope, blk, maxlen):
    positions, cols = mg.shape
    heads = cols // DH
    shards = len(stats)
    users = lengths.shape[1]
    elements = heads * positions * positions // 2
    whole = lambda i: (0, 0)
    return pl.pallas_call(
        functools.partial(backward_kernel, blk=blk, users=users, maxlen=maxlen, shards=shards),
        grid=(positions // blk,),
        in_specs=[pl.BlockSpec(memory_space=pltpu.SMEM)]
        + [pl.BlockSpec((8, positions), whole)] * shards
        + [
            pl.BlockSpec((positions, cols), whole),
            pl.BlockSpec((positions, cols), whole),
            pl.BlockSpec((positions, cols), whole),
            pl.BlockSpec((positions, 4 * cols), whole),
            pl.BlockSpec((positions, 4 * cols), whole),
            pl.BlockSpec((heads, blk, positions), lambda i: (0, i, 0)),
            pl.BlockSpec((heads, blk, positions), lambda i: (0, i, 0)),
        ],
        out_specs=[pl.BlockSpec((positions, 4 * cols), whole), pl.BlockSpec((positions, cols), whole)],
        out_shape=[
            jax.ShapeDtypeStruct((positions, 4 * cols), BF),
            jax.ShapeDtypeStruct((positions, cols), BF),
        ],
        scratch_shapes=[
            pltpu.VMEM((positions, cols), BF),
            pltpu.VMEM((cols, positions), BF),
            pltpu.VMEM((cols, positions), BF),
            pltpu.VMEM((cols, positions), BF),
            pltpu.VMEM((cols // PAIR, 2 * positions, PAIR), BF),
            pltpu.VMEM((cols, positions), F32),
            pltpu.VMEM((cols, positions), F32),
            pltpu.VMEM((positions, cols), F32),
        ],
        compiler_params=pltpu.CompilerParams(vmem_limit_bytes=VMEM_LIMIT),
        cost_estimate=pl.CostEstimate(
            flops=8 * elements * 256, bytes_accessed=4 * elements + 26 * positions * cols, transcendentals=0
        ),
        name="attention_backward",
    )(lengths, *stats, mg, gate, head_outs, acts, slopes, weights, score_slope)


def update_kernel(rows_ref, table_ref, accum_ref, new_table_ref, new_accum_ref, ids):
    i = pl.program_id(0)
    blk = table_ref.shape[0]
    slots = rows_ref.shape[0]

    @pl.when(i == 0)
    def _():
        numbers = jnp.transpose(rows_ref[:, D:].astype(F32))
        ids[...] = (numbers[0:1, :] * 256.0 + numbers[1:2, :]).astype(jnp.int32)

    row = i * blk + lax.broadcasted_iota(jnp.int32, (blk, slots), 0)
    hits = jnp.where(row == ids[...], 1.0, 0.0).astype(BF)
    grad = dot_nn(hits, rows_ref[:, :D])
    accum = jnp.transpose(jnp.broadcast_to(accum_ref[...], (128, blk)))[:, :1] + jnp.mean(grad * grad, axis=1, keepdims=True)
    new_accum_ref[...] = jnp.transpose(jnp.broadcast_to(accum, (blk, 128)))[:1, :]
    new_table_ref[...] = table_ref[...] - LEARN_RATE * grad * lax.rsqrt(accum)


def update_rows(got_rows, emb_table, row_accum):
    rows_own = emb_table.shape[0]
    slots = got_rows.shape[0]
    blk = min(256, rows_own)
    new_table, new_accum = pl.pallas_call(
        update_kernel,
        grid=(rows_own // blk,),
        in_specs=[
            pl.BlockSpec((slots, D + 128), lambda i: (0, 0)),
            pl.BlockSpec((blk, D), lambda i: (i, 0)),
            pl.BlockSpec((1, blk), lambda i: (0, i)),
        ],
        out_specs=[
            pl.BlockSpec((blk, D), lambda i: (i, 0)),
            pl.BlockSpec((1, blk), lambda i: (0, i)),
        ],
        out_shape=[
            jax.ShapeDtypeStruct((rows_own, D), F32),
            jax.ShapeDtypeStruct((1, rows_own), F32),
        ],
        scratch_shapes=[pltpu.VMEM((1, slots), jnp.int32)],
        compiler_params=pltpu.CompilerParams(vmem_limit_bytes=VMEM_LIMIT),
        cost_estimate=pl.CostEstimate(
            flops=2 * rows_own * slots * D, bytes_accessed=8 * rows_own * D + 2 * slots * D, transcendentals=rows_own
        ),
        name="update_rows",
    )(got_rows, emb_table, row_accum.reshape(1, rows_own))
    return new_table, new_accum.reshape(rows_own)


def own_weights(w_attn, w_gate, part, cols):
    attn = lax.dynamic_slice_in_dim(w_attn, part * 3 * cols, 3 * cols, 1)
    gate = lax.dynamic_slice_in_dim(w_gate, part * cols, cols, 1)
    return jnp.concatenate([attn, gate], axis=1)


def row_slots(owners, rows, devices, capacity):
    events = owners.shape[0]
    owner_hits = (owners[:, None] == jnp.arange(devices, dtype=jnp.int32)[None, :]).astype(BF)
    place = jnp.arange(events, dtype=jnp.int32)
    before = (place[:, None] > place[None, :]).astype(BF)
    earlier = jnp.dot(before, owner_hits, preferred_element_type=F32)
    slots = jnp.sum(earlier * owner_hits.astype(F32), axis=1).astype(jnp.int32)
    flat_slot = owners * capacity + slots
    slot_hits = jnp.arange(devices * capacity, dtype=jnp.int32)[:, None] == flat_slot[None, :]
    lane = jnp.arange(128, dtype=jnp.int32)[None, :]
    numbers = jnp.where(lane == 0, rows[:, None] // 256, jnp.where(lane == 1, rows[:, None] % 256, 0))
    return slot_hits.astype(BF), numbers.astype(BF)


def to_owners(rows, devices, capacity):
    shape = (devices, capacity) + rows.shape[1:]
    got = lax.all_to_all(rows.reshape(shape), ("seq", "dp"), split_axis=0, concat_axis=0, tiled=True)
    return got.reshape(rows.shape)


TN = (((0,), (0,)), ((), ()))


def dot_tn(a, b):
    return lax.dot_general(a, b, TN, preferred_element_type=F32)


def body_whole(
    layer_input, out_grad, lengths, item_owner, item_row, w_attn, w_gate, w_out, emb_table, row_accum
):
    seq_count = lax.axis_size("seq")
    dp_count = lax.axis_size("dp")
    devices = seq_count * dp_count
    seq_id = lax.axis_index("seq")
    tokens_dev = layer_input.shape[0]
    positions = tokens_dev * seq_count
    maxlen = 2 * positions // 3
    blk = min(256, positions)
    cols = D // seq_count
    capacity = max(2, 2 * tokens_dev // devices)

    w_own = own_weights(w_attn, w_gate, seq_id, cols)
    w_out_own = lax.dynamic_slice_in_dim(w_out, seq_id * cols, cols, 0)
    slot_matrix, numbers = row_slots(item_owner[:, 0], item_row, devices, capacity)

    x_full = lax.all_gather(layer_input, "seq", axis=0, tiled=True)
    og_full = lax.all_gather(out_grad, "seq", axis=0, tiled=True)
    order = jnp.arange(positions // blk, dtype=jnp.int32)
    acts, slopes, gate, weights, score_slope, heads = forward_attention(
        lengths, order, [x_full], w_own, blk, maxlen
    )
    mg, stats_own = event_stats(order, [og_full], w_out_own, gate, heads, blk)
    stats = lax.all_gather(stats_own, "seq", axis=0, tiled=False)
    grads, mixed = backward_attention(
        lengths, [stats[s] for s in range(seq_count)], mg, gate, heads, acts, slopes, weights, score_slope, blk, maxlen
    )

    input_part = dot_nt(grads, w_own).astype(BF)
    got = lax.all_to_all(
        input_part.reshape(seq_count, tokens_dev, D), "seq", split_axis=0, concat_axis=0, tiled=True
    )
    input_grad = jnp.sum(got.astype(F32), axis=0) + out_grad.astype(F32)
    rows = jnp.concatenate([input_grad.astype(BF), numbers], axis=1)
    rows = jnp.dot(slot_matrix, rows, preferred_element_type=F32).astype(BF)
    got_rows = to_owners(rows, devices, capacity)
    new_table, new_accum = update_rows(got_rows, emb_table, row_accum)

    out_part = dot_tn(mixed, og_full).astype(BF)
    share = dp_count // seq_count
    out_part = out_part.reshape(share, D // dp_count, seq_count, cols).transpose(0, 2, 1, 3).reshape(D, cols)
    merged = jnp.concatenate([dot_tn(x_full, grads).astype(BF), out_part], axis=1)
    merged = lax.psum_scatter(merged, "dp", scatter_dimension=0, tiled=True)
    steps = []
    for s in range(seq_count):
        for piece in range(dp_count):
            part, target = divmod(piece, seq_count)
            steps.append((s * dp_count + piece, target * dp_count + s * share + part))
    grad_out = lax.ppermute(merged[:, 4 * cols :], ("seq", "dp"), steps).astype(F32)
    grad_attn = merged[:, : 3 * cols].astype(F32)
    grad_gate = merged[:, 3 * cols : 4 * cols].astype(F32)
    return (grad_attn, grad_gate, grad_out, new_table, new_accum)


SEQ = 4
PLANE = 4


def send(array, target):
    steps = []
    for s in range(SEQ):
        for e in range(PLANE):
            for c in range(2):
                to = target(s, e, c)
                if to is not None:
                    steps.append((s * 2 * PLANE + 2 * e + c, to[0] * 2 * PLANE + 2 * to[1] + to[2]))
    return lax.ppermute(array, ("seq", "dp"), steps)


def home(s, c):
    return c == s // 2


def swap_far(array):
    return send(array, lambda s, e, c: None if home(s, c) else (3 - s, e, 1 - c))


def fetch_near(array):
    return send(array, lambda s, e, c: (s ^ 1, e, c) if home(s, c) else ((3 - s) ^ 1, e, 1 - c))


def swap_near(array):
    return send(array, lambda s, e, c: (s ^ 1, e, c))


def swap_core(array):
    return send(array, lambda s, e, c: (s, e, 1 - c))


def swap_x(array):
    return send(array, lambda s, e, c: (s, e ^ 1, c))


def swap_y(array):
    return send(array, lambda s, e, c: (s, e ^ 2, c))


def tie(*arrays):
    return lax.optimization_barrier(arrays)


def halves(array, bit, axis):
    kept = lax.dynamic_index_in_dim(array, bit, axis, keepdims=False)
    sent = lax.dynamic_index_in_dim(array, 1 - bit, axis, keepdims=False)
    return kept, sent


def body_pairs(
    layer_input, out_grad, lengths, item_owner, item_row, w_attn, w_gate, w_out, emb_table, row_accum
):
    devices = 2 * PLANE * SEQ
    s = lax.axis_index("seq")
    d = lax.axis_index("dp")
    e, c = d // 2, d % 2
    y, x = e // 2, e % 2
    tokens_dev = layer_input.shape[0]
    positions = tokens_dev * SEQ
    maxlen = 2 * positions // 3
    blk = min(256, positions)
    cols = D // SEQ
    rows_own = emb_table.shape[0]
    capacity = max(2, 2 * tokens_dev // devices)
    at_home = c == s // 2
    part = 2 * (s % 2) + c

    def block_of(seq, core):
        return jnp.where(core == seq // 2, seq, 3 - seq)

    mine_at, near_at = block_of(s, c), block_of(s ^ 1, c)
    core_at, diag_at = block_of(s, 1 - c), block_of(s ^ 1, 1 - c)
    order = jnp.stack([mine_at, near_at, core_at, diag_at]).astype(jnp.int32)

    x_far = swap_far(layer_input)
    x_near = fetch_near(layer_input)
    users = lengths.shape[1]
    keys = (item_owner[:, 0] * rows_own + item_row).reshape(1, tokens_dev)
    small = jnp.concatenate([keys, jnp.pad(lengths, ((0, 0), (0, 128 - users)))], axis=1)
    small = jnp.where(at_home, small, swap_far(small))
    keys, lengths = small[0, :tokens_dev], small[:, tokens_dev : tokens_dev + users]
    w_own = own_weights(w_attn, w_gate, part, cols)
    w_out_own = lax.dynamic_slice_in_dim(w_out, part * cols, cols, 0)
    slot_matrix, numbers = row_slots(keys // rows_own, keys % rows_own, devices, capacity)
    x_far, x_near, w_own, w_out_own, slot_matrix, numbers, lengths = tie(
        x_far, x_near, w_own, w_out_own, slot_matrix, numbers, lengths
    )
    x_here = jnp.concatenate([jnp.where(at_home, layer_input, x_far), x_near], axis=0)
    x_there = swap_core(x_here)
    x_here, og_own = tie(x_here, out_grad)
    og_far = swap_far(og_own)
    og_near = fetch_near(og_own)

    x_full, acts, slopes, gate, weights, score_slope, heads = forward_attention(
        lengths, order, [x_here, x_there], w_own, blk, maxlen
    )
    og_far, og_near, heads = tie(og_far, og_near, heads)
    og_mine = jnp.where(at_home, og_own, og_far)
    og_here = jnp.concatenate([og_mine, og_near], axis=0)
    og_there = swap_core(og_here)
    og_full, mg, stats_own = event_stats(order, [og_here, og_there], w_out_own, gate, heads, blk)
    stats = [
        stats_own,
        swap_core(stats_own),
        swap_near(stats_own),
        send(stats_own, lambda s, e, c: (s ^ 1, e, 1 - c)),
    ]
    grads, mixed = backward_attention(
        lengths, stats, mg, gate, heads, acts, slopes, weights, score_slope, blk, maxlen
    )

    def input_part(grads, block):
        return dot_nt(lax.dynamic_slice_in_dim(grads, block * tokens_dev, tokens_dev, 0), w_own)

    from_diag = swap_core(input_part(grads, diag_at).astype(BF))
    near_sum = (input_part(grads, near_at) + from_diag.astype(F32)).astype(BF)
    near_sum, grads = tie(near_sum, grads)
    from_near = swap_near(near_sum)
    core_part = input_part(grads, core_at).astype(BF)
    from_core = swap_core(core_part)
    input_grad = input_part(grads, mine_at) + og_mine.astype(F32)

    core_part, grads, mixed = tie(core_part, grads, mixed)
    half = 5 * cols // 2
    proj = dot_tn(x_full, grads).astype(BF).reshape(2, 2, D // PLANE, 4 * cols)
    out_part = dot_tn(mixed, og_full).astype(BF).reshape(cols, 2, 2, cols)
    a_kept, a_sent = halves(proj[..., :half], x, 1)
    b_kept, b_sent = halves(proj[..., half:], y, 0)
    out_kept, out_sent = (piece.transpose(1, 0, 2) for piece in halves(out_part, y, 1))
    b_kept = jnp.concatenate([b_kept, out_kept], axis=-1)
    b_sent = jnp.concatenate([b_sent, out_sent], axis=-1)
    a_got = swap_x(a_sent)
    b_got = swap_y(b_sent)

    input_grad = input_grad + from_core.astype(F32) + from_near.astype(F32)
    rows = jnp.concatenate([input_grad.astype(BF), numbers], axis=1)
    rows = jnp.dot(slot_matrix, rows, preferred_element_type=F32).astype(BF)
    got_rows = to_owners(rows, devices, capacity)

    a = (a_kept.astype(F32) + a_got.astype(F32)).astype(BF)
    b = (b_kept.astype(F32) + b_got.astype(F32)).astype(BF)
    a_kept, a_sent = halves(a, y, 0)
    b_kept, b_sent = halves(b, x, 0)
    a = (a_kept.astype(F32) + swap_y(a_sent).astype(F32)).astype(BF)
    b = (b_kept.astype(F32) + swap_x(b_sent).astype(F32)).astype(BF)

    def last(array, target):
        pieces = array.reshape(2, D // (2 * PLANE), array.shape[1])
        one, other = halves(pieces, s // 2, 0)
        one = send(one, lambda s, e, c: target(s, e, c, s // 2))
        return one, send(other, lambda s, e, c: target(s, e, c, 1 - s // 2))

    proj = jnp.concatenate([a, b[:, : 4 * cols - half]], axis=1)
    proj = last(proj, lambda s, e, c, piece: (2 * (s % 2) + c, e, piece))
    out = last(b[:, 4 * cols - half :], lambda s, e, c, piece: (e, 2 * (s % 2) + c, piece))
    new_table, new_accum = update_rows(got_rows, emb_table, row_accum)
    *proj, new_accum = tie(*proj, new_accum)
    attn = proj[0][:, : 3 * cols].astype(F32) + proj[1][:, : 3 * cols].astype(F32)
    gate = proj[0][:, 3 * cols :].astype(F32) + proj[1][:, 3 * cols :].astype(F32)
    return (attn, gate, out[0].astype(F32) + out[1].astype(F32), new_table, new_accum)


def solution(mesh):
    placed = (
        P(("dp", "seq"), None),
        P(("dp", "seq"), None),
        P("dp", None),
        P(("dp", "seq"), None),
        P(("dp", "seq")),
        P(),
        P(),
        P(),
        P(("seq", "dp"), None),
        P(("seq", "dp")),
    )
    paired = mesh.shape["seq"] == SEQ and mesh.shape["dp"] == 2 * PLANE
    return jax.shard_map(
        body_pairs if paired else body_whole,
        mesh=mesh,
        in_specs=placed,
        out_specs=(
            P("dp", "seq"),
            P("dp", "seq"),
            P("dp", "seq"),
            P(("seq", "dp"), None),
            P(("seq", "dp")),
        ),
        check_vma=False,
    )
```

```python
import functools

import jax
import jax.numpy as jnp
from jax import lax
from jax.experimental import pallas as pl
from jax.experimental.pallas import tpu as pltpu
from jax.sharding import PartitionSpec as P

D = 1024
H = 16
DH = 64
PAIR = 2 * DH

NORM_EPS = 1e-05
LEARN_RATE = 0.1
VMEM_LIMIT = 56 * 1024 * 1024
BF = jnp.bfloat16
F32 = jnp.float32


def dot_nn(a, b):
    return lax.dot_general(a, b, (((1,), (0,)), ((), ())), preferred_element_type=F32)


def dot_nt(a, b):
    return lax.dot_general(a, b, (((1,), (1,)), ((), ())), preferred_element_type=F32)


def history_start(lengths_ref, users, place):
    start = jnp.zeros_like(place)
    end = jnp.int32(0)
    for user in range(users - 1):
        end = end + lengths_ref[0, user]
        start = jnp.where(place >= end, end, start)
    return start


def head_columns(kind, head):
    first = head * 3 * DH + kind * DH
    return slice(first, first + DH)


def split_pairs(acts_ref, split_ref, kind, block, blk):
    at = pl.ds(pl.multiple_of(block * blk, blk), blk)
    zero = jnp.zeros((blk, DH), BF)
    for p in range(split_ref.shape[0]):
        one, two = (acts_ref[at, head_columns(kind, 2 * p + h)] for h in range(2))
        below = pl.multiple_of(block * 2 * blk + blk, blk)
        split_ref[p, pl.ds(pl.multiple_of(block * 2 * blk, blk), blk), :] = jnp.concatenate([one, zero], axis=1)
        split_ref[p, pl.ds(below, blk), :] = jnp.concatenate([zero, two], axis=1)


def forward_kernel(*refs, blk, users, maxlen, count):
    lengths_ref, order_ref = refs[:2]
    x_refs = refs[2 : 2 + count]
    w_ref = refs[2 + count]
    outs = refs[3 + count :]
    if count > 1:
        x_out_ref, outs = outs[0], outs[1:]
    acts_ref, slopes_ref, gate_ref, weights_ref, score_slope_ref, heads_ref, k_t, v_split = outs
    i = pl.program_id(0)
    heads = weights_ref.shape[0]
    attn = 3 * heads * DH
    chunks = x_refs[0].shape[0] // blk

    @pl.when(i == 0)
    def _():
        for b in range(count):
            for r in range(chunks):
                at = pl.ds(pl.multiple_of(order_ref[b * chunks + r] * blk, blk), blk)
                x = x_refs[b][r * blk : (r + 1) * blk, :]
                if count > 1:
                    x_out_ref[at, :] = x
                for lane in range(0, w_ref.shape[1], 512):
                    lanes = slice(lane, lane + 512)
                    half = 0.5 * dot_nn(x, w_ref[:, lanes])
                    t = jnp.tanh(half)
                    prod = half * t
                    silu = half + prod
                    acts_ref[at, lanes] = silu.astype(BF)
                    slopes_ref[at, lanes] = (0.5 * (1.0 + t) * (1.0 + half - prod)).astype(BF)
                    skip = max(0, attn - lane)
                    if skip < 512:
                        gate_ref[at, lane + skip - attn : lane + 512 - attn] = silu[:, skip:]
                for h in range(heads):
                    k_t[h * DH : (h + 1) * DH, at] = jnp.transpose(acts_ref[at, head_columns(2, h)])
                split_pairs(acts_ref, v_split, 0, order_ref[b * chunks + r], blk)

    at_i = pl.ds(pl.multiple_of(i * blk, blk), blk)
    q_half = [acts_ref[at_i, head_columns(1, h)] * jnp.asarray(0.5 * DH**-0.5, BF) for h in range(heads)]
    row = i * blk + lax.broadcasted_iota(jnp.int32, (blk, blk), 0)
    col0 = lax.broadcasted_iota(jnp.int32, (blk, blk), 1)
    start = history_start(lengths_ref, users, row)

    def column(j, acc):
        at_j = pl.ds(pl.multiple_of(j * blk, blk), blk)
        both_j = pl.ds(pl.multiple_of(j * 2 * blk, 2 * blk), 2 * blk)
        col = col0 + j * blk
        allowed = (col <= row) & (col >= start)
        per_head = []
        for h in range(heads):
            half = dot_nn(q_half[h], k_t[h * DH : (h + 1) * DH, at_j])
            half = jnp.where(allowed, half, -64.0)
            t = jnp.tanh(half)
            p = half * t
            weights = (half + p).astype(BF)
            weights_ref[h, :, at_j] = weights
            score_slope_ref[h, :, at_j] = ((1.0 + t) * (1.0 + half - p)).astype(BF)
            per_head.append(weights)
        return tuple(
            acc[p] + dot_nn(jnp.concatenate(per_head[2 * p : 2 * p + 2], axis=1), v_split[p, both_j, :])
            for p in range(heads // 2)
        )

    first = history_start(lengths_ref, users, i * blk) // blk
    zero = jnp.zeros((blk, PAIR), F32)
    acc = lax.fori_loop(first, i + 1, column, (zero,) * (heads // 2))
    heads_ref[...] = (jnp.concatenate(acc, axis=1) * (1.0 / maxlen)).astype(BF)


def forward_attention(lengths, order, x_blocks, w_own, blk, maxlen):
    count = len(x_blocks)
    block_rows = x_blocks[0].shape[0]
    positions = count * block_rows
    cols = w_own.shape[1] // 4
    heads = cols // DH
    users = lengths.shape[1]
    elements = heads * positions * positions // 2
    whole = lambda i: (0, 0)
    out_specs = [
        pl.BlockSpec((positions, 4 * cols), whole),
        pl.BlockSpec((positions, 4 * cols), whole),
        pl.BlockSpec((positions, cols), whole),
        pl.BlockSpec((heads, blk, positions), lambda i: (0, i, 0)),
        pl.BlockSpec((heads, blk, positions), lambda i: (0, i, 0)),
        pl.BlockSpec((blk, cols), lambda i: (i, 0)),
    ]
    out_shape = [
        jax.ShapeDtypeStruct((positions, 4 * cols), BF),
        jax.ShapeDtypeStruct((positions, 4 * cols), BF),
        jax.ShapeDtypeStruct((positions, cols), F32),
        jax.ShapeDtypeStruct((heads, positions, positions), BF),
        jax.ShapeDtypeStruct((heads, positions, positions), BF),
        jax.ShapeDtypeStruct((positions, cols), BF),
    ]
    if count > 1:
        out_specs = [pl.BlockSpec((positions, D), whole)] + out_specs
        out_shape = [jax.ShapeDtypeStruct((positions, D), BF)] + out_shape
    return pl.pallas_call(
        functools.partial(forward_kernel, blk=blk, users=users, maxlen=maxlen, count=count),
        grid=(positions // blk,),
        in_specs=[pl.BlockSpec(memory_space=pltpu.SMEM), pl.BlockSpec(memory_space=pltpu.SMEM)]
        + [pl.BlockSpec((block_rows, D), whole)] * count
        + [pl.BlockSpec((D, 4 * cols), whole)],
        out_specs=out_specs,
        out_shape=out_shape,
        scratch_shapes=[pltpu.VMEM((cols, positions), BF), pltpu.VMEM((cols // PAIR, 2 * positions, PAIR), BF)],
        compiler_params=pltpu.CompilerParams(vmem_limit_bytes=VMEM_LIMIT),
        cost_estimate=pl.CostEstimate(
            flops=8 * positions * D * cols + 4 * elements * 256,
            bytes_accessed=4 * positions * D + 4 * elements,
            transcendentals=elements,
        ),
        name="attention_forward",
    )(lengths, order, *x_blocks, w_own)


def stats_kernel(*refs, blk, count):
    order_ref = refs[0]
    og_refs = refs[1 : 1 + count]
    w_ref, gate_ref, heads_ref = refs[1 + count : 4 + count]
    outs = refs[4 + count :]
    if count > 1:
        og_out_ref, outs = outs[0], outs[1:]
    mg_ref, stats_ref = outs
    chunks = og_refs[0].shape[0] // blk
    for b in range(count):
        for r in range(chunks):
            at = pl.ds(pl.multiple_of(order_ref[b * chunks + r] * blk, blk), blk)
            og = og_refs[b][r * blk : (r + 1) * blk, :]
            if count > 1:
                og_out_ref[at, :] = og
            mg = dot_nt(og, w_ref[...])
            mg_ref[at, :] = mg
            ng = mg * gate_ref[at, :]
            heads = heads_ref[at, :].astype(F32)
            mean = jnp.mean(heads, axis=1, keepdims=True)
            centred = heads - mean
            square = jnp.sum(centred * centred, axis=1, keepdims=True)
            total = jnp.sum(ng, axis=1, keepdims=True)
            cross = jnp.sum(ng * centred, axis=1, keepdims=True)
            lane = lax.broadcasted_iota(jnp.int32, (blk, 128), 1)
            packed = jnp.where(lane == 0, mean, jnp.where(lane == 1, square, jnp.where(lane == 2, total, cross)))
            stats_ref[:, at] = jnp.transpose(packed)[:8, :]


def event_stats(order, og_blocks, w_out_own, gate, heads, blk):
    positions, cols = heads.shape
    count = len(og_blocks)
    vmem = pl.BlockSpec(memory_space=pltpu.VMEM)
    out_shape = [
        jax.ShapeDtypeStruct((positions, cols), F32),
        jax.ShapeDtypeStruct((8, positions), F32),
    ]
    if count > 1:
        out_shape = [jax.ShapeDtypeStruct((positions, D), BF)] + out_shape
    return pl.pallas_call(
        functools.partial(stats_kernel, blk=blk, count=count),
        in_specs=[pl.BlockSpec(memory_space=pltpu.SMEM)] + [vmem] * (count + 3),
        out_specs=[vmem] * len(out_shape),
        out_shape=out_shape,
        compiler_params=pltpu.CompilerParams(vmem_limit_bytes=VMEM_LIMIT),
        cost_estimate=pl.CostEstimate(
            flops=2 * positions * cols * D, bytes_accessed=4 * positions * D + 10 * positions * cols, transcendentals=0
        ),
        name="event_stats",
    )(order, *og_blocks, w_out_own, gate, heads)


def combined_stats(stats_refs, cols):
    shards = len(stats_refs)
    positions = stats_refs[0].shape[1]
    means = [ref[0:1, :] for ref in stats_refs]
    mean = sum(means) * (1.0 / shards)
    square = jnp.zeros_like(mean)
    total = jnp.zeros_like(mean)
    cross = jnp.zeros_like(mean)
    for s, ref in enumerate(stats_refs):
        shift = means[s] - mean
        part = ref[2:3, :]
        square = square + ref[1:2, :] + cols * shift * shift
        total = total + part
        cross = cross + ref[3:4, :] + shift * part
    inv_dev = lax.rsqrt(square * (1.0 / D) + NORM_EPS)
    kind = lax.broadcasted_iota(jnp.int32, (128, positions), 0)
    rest = jnp.where(kind == 2, total * (1.0 / D), cross * inv_dev * (1.0 / D))
    packed = jnp.where(kind == 0, mean, jnp.where(kind == 1, inv_dev, rest))
    per_event = jnp.transpose(packed)
    return [per_event[:, k : k + 1] for k in range(4)]


def backward_kernel(*refs, blk, users, maxlen, shards):
    lengths_ref = refs[0]
    stats_refs = refs[1 : 1 + shards]
    mg_ref, gate_ref, heads_ref, acts_ref, slopes_ref, weights_ref, score_slope_ref = refs[1 + shards : 8 + shards]
    grad_ref, mixed_ref, o_ref, o_t, q_t, v_t, k_split, vg_t, kg_t, qg = refs[8 + shards :]
    i = pl.program_id(0)
    positions, cols = o_ref.shape
    heads = cols // DH
    blocks = positions // blk
    scale = DH ** (-0.5)

    @pl.when(i == 0)
    def _():
        mean, inv_dev, total, cross = combined_stats(stats_refs, cols)
        for p in range(heads // 2):
            lanes = slice(p * PAIR, (p + 1) * PAIR)
            normed = (heads_ref[:, lanes].astype(F32) - mean) * inv_dev
            gate = gate_ref[:, lanes]
            mg = mg_ref[:, lanes]
            mixed_ref[:, lanes] = (normed * gate).astype(BF)
            gate_lanes = slice(3 * cols + p * PAIR, 3 * cols + (p + 1) * PAIR)
            gate_slope = slopes_ref[:, gate_lanes].astype(F32)
            grad_ref[:, gate_lanes] = (mg * normed * gate_slope).astype(BF)
            o_ref[:, lanes] = (inv_dev * (mg * gate - total - normed * cross)).astype(BF)
        o_t[...] = jnp.transpose(o_ref[...])
        for scratch, kind in ((v_t, 0), (q_t, 1)):
            scratch[...] = jnp.transpose(jnp.concatenate([acts_ref[:, head_columns(kind, h)] for h in range(heads)], axis=1))
        for block in range(blocks):
            split_pairs(acts_ref, k_split, 2, block, blk)
        vg_t[...] = jnp.zeros_like(vg_t)
        kg_t[...] = jnp.zeros_like(kg_t)

    at_i = pl.ds(pl.multiple_of(i * blk, blk), blk)
    o_i = [o_ref[at_i, h * DH : (h + 1) * DH] for h in range(heads)]

    def column(j, acc):
        at_j = pl.ds(pl.multiple_of(j * blk, blk), blk)
        both_j = pl.ds(pl.multiple_of(j * 2 * blk, 2 * blk), 2 * blk)
        per_head = []
        for h in range(heads):
            lanes = slice(h * DH, (h + 1) * DH)
            weight_grad = dot_nn(o_i[h], v_t[lanes, at_j])
            score_grad = (weight_grad * score_slope_ref[h, :, at_j].astype(F32)).astype(BF)
            vg_t[lanes, at_j] += dot_nn(o_t[lanes, at_i], weights_ref[h, :, at_j])
            kg_t[lanes, at_j] += dot_nn(q_t[lanes, at_i], score_grad)
            per_head.append(score_grad)
        return tuple(
            acc[p] + dot_nn(jnp.concatenate(per_head[2 * p : 2 * p + 2], axis=1), k_split[p, both_j, :])
            for p in range(heads // 2)
        )

    first = history_start(lengths_ref, users, i * blk) // blk
    zero = jnp.zeros((blk, PAIR), F32)
    acc = lax.fori_loop(first, i + 1, column, (zero,) * (heads // 2))
    qg[at_i, :] = jnp.concatenate(acc, axis=1)

    @pl.when(i == blocks - 1)
    def _():
        factor = 0.5 * scale / maxlen
        grads = [jnp.transpose(vg_t[...]) * (1.0 / maxlen), qg[...] * factor, jnp.transpose(kg_t[...]) * factor]
        pieces = [grads[kind][:, h * DH : (h + 1) * DH] for h in range(heads) for kind in range(3)]
        for n in range(3 * heads // 2):
            lanes = slice(n * PAIR, (n + 1) * PAIR)
            grad = jnp.concatenate(pieces[2 * n : 2 * n + 2], axis=1).astype(BF).astype(F32)
            grad_ref[:, lanes] = (grad * slopes_ref[:, lanes].astype(F32)).astype(BF)


def backward_attention(lengths, stats, mg, gate, head_outs, acts, slopes, weights, score_slope, blk, maxlen):
    positions, cols = mg.shape
    heads = cols // DH
    shards = len(stats)
    users = lengths.shape[1]
    elements = heads * positions * positions // 2
    whole = lambda i: (0, 0)
    return pl.pallas_call(
        functools.partial(backward_kernel, blk=blk, users=users, maxlen=maxlen, shards=shards),
        grid=(positions // blk,),
        in_specs=[pl.BlockSpec(memory_space=pltpu.SMEM)]
        + [pl.BlockSpec((8, positions), whole)] * shards
        + [
            pl.BlockSpec((positions, cols), whole),
            pl.BlockSpec((positions, cols), whole),
            pl.BlockSpec((positions, cols), whole),
            pl.BlockSpec((positions, 4 * cols), whole),
            pl.BlockSpec((positions, 4 * cols), whole),
            pl.BlockSpec((heads, blk, positions), lambda i: (0, i, 0)),
            pl.BlockSpec((heads, blk, positions), lambda i: (0, i, 0)),
        ],
        out_specs=[pl.BlockSpec((positions, 4 * cols), whole), pl.BlockSpec((positions, cols), whole)],
        out_shape=[
            jax.ShapeDtypeStruct((positions, 4 * cols), BF),
            jax.ShapeDtypeStruct((positions, cols), BF),
        ],
        scratch_shapes=[
            pltpu.VMEM((positions, cols), BF),
            pltpu.VMEM((cols, positions), BF),
            pltpu.VMEM((cols, positions), BF),
            pltpu.VMEM((cols, positions), BF),
            pltpu.VMEM((cols // PAIR, 2 * positions, PAIR), BF),
            pltpu.VMEM((cols, positions), F32),
            pltpu.VMEM((cols, positions), F32),
            pltpu.VMEM((positions, cols), F32),
        ],
        compiler_params=pltpu.CompilerParams(vmem_limit_bytes=VMEM_LIMIT),
        cost_estimate=pl.CostEstimate(
            flops=8 * elements * 256, bytes_accessed=4 * elements + 26 * positions * cols, transcendentals=0
        ),
        name="attention_backward",
    )(lengths, *stats, mg, gate, head_outs, acts, slopes, weights, score_slope)


def update_kernel(rows_ref, table_ref, accum_ref, new_table_ref, new_accum_ref, ids):
    i = pl.program_id(0)
    blk = table_ref.shape[0]
    slots = rows_ref.shape[0]

    @pl.when(i == 0)
    def _():
        numbers = jnp.transpose(rows_ref[:, D:].astype(F32))
        ids[...] = (numbers[0:1, :] * 256.0 + numbers[1:2, :]).astype(jnp.int32)

    row = i * blk + lax.broadcasted_iota(jnp.int32, (blk, slots), 0)
    hits = jnp.where(row == ids[...], 1.0, 0.0).astype(BF)
    grad = dot_nn(hits, rows_ref[:, :D])
    accum = jnp.transpose(jnp.broadcast_to(accum_ref[...], (128, blk)))[:, :1] + jnp.mean(grad * grad, axis=1, keepdims=True)
    new_accum_ref[...] = jnp.transpose(jnp.broadcast_to(accum, (blk, 128)))[:1, :]
    new_table_ref[...] = table_ref[...] - LEARN_RATE * grad * lax.rsqrt(accum)


def update_rows(got_rows, emb_table, row_accum):
    rows_own = emb_table.shape[0]
    slots = got_rows.shape[0]
    blk = min(256, rows_own)
    new_table, new_accum = pl.pallas_call(
        update_kernel,
        grid=(rows_own // blk,),
        in_specs=[
            pl.BlockSpec((slots, D + 128), lambda i: (0, 0)),
            pl.BlockSpec((blk, D), lambda i: (i, 0)),
            pl.BlockSpec((1, blk), lambda i: (0, i)),
        ],
        out_specs=[
            pl.BlockSpec((blk, D), lambda i: (i, 0)),
            pl.BlockSpec((1, blk), lambda i: (0, i)),
        ],
        out_shape=[
            jax.ShapeDtypeStruct((rows_own, D), F32),
            jax.ShapeDtypeStruct((1, rows_own), F32),
        ],
        scratch_shapes=[pltpu.VMEM((1, slots), jnp.int32)],
        compiler_params=pltpu.CompilerParams(vmem_limit_bytes=VMEM_LIMIT),
        cost_estimate=pl.CostEstimate(
            flops=2 * rows_own * slots * D, bytes_accessed=8 * rows_own * D + 2 * slots * D, transcendentals=rows_own
        ),
        name="update_rows",
    )(got_rows, emb_table, row_accum.reshape(1, rows_own))
    return new_table, new_accum.reshape(rows_own)


def own_weights(w_attn, w_gate, part, cols):
    attn = lax.dynamic_slice_in_dim(w_attn, part * 3 * cols, 3 * cols, 1)
    gate = lax.dynamic_slice_in_dim(w_gate, part * cols, cols, 1)
    return jnp.concatenate([attn, gate], axis=1)


def row_slots(owners, rows, devices, capacity):
    events = owners.shape[0]
    owner_hits = (owners[:, None] == jnp.arange(devices, dtype=jnp.int32)[None, :]).astype(BF)
    place = jnp.arange(events, dtype=jnp.int32)
    before = (place[:, None] > place[None, :]).astype(BF)
    earlier = jnp.dot(before, owner_hits, preferred_element_type=F32)
    slots = jnp.sum(earlier * owner_hits.astype(F32), axis=1).astype(jnp.int32)
    flat_slot = owners * capacity + slots
    slot_hits = jnp.arange(devices * capacity, dtype=jnp.int32)[:, None] == flat_slot[None, :]
    lane = jnp.arange(128, dtype=jnp.int32)[None, :]
    numbers = jnp.where(lane == 0, rows[:, None] // 256, jnp.where(lane == 1, rows[:, None] % 256, 0))
    return slot_hits.astype(BF), numbers.astype(BF)


def to_owners(rows, devices, capacity):
    shape = (devices, capacity) + rows.shape[1:]
    got = lax.all_to_all(rows.reshape(shape), ("seq", "dp"), split_axis=0, concat_axis=0, tiled=True)
    return got.reshape(rows.shape)


TN = (((0,), (0,)), ((), ()))


def dot_tn(a, b):
    return lax.dot_general(a, b, TN, preferred_element_type=F32)


def body_whole(
    layer_input, out_grad, lengths, item_owner, item_row, w_attn, w_gate, w_out, emb_table, row_accum
):
    seq_count = lax.axis_size("seq")
    dp_count = lax.axis_size("dp")
    devices = seq_count * dp_count
    seq_id = lax.axis_index("seq")
    tokens_dev = layer_input.shape[0]
    positions = tokens_dev * seq_count
    maxlen = 2 * positions // 3
    blk = min(256, positions)
    cols = D // seq_count
    capacity = max(2, 2 * tokens_dev // devices)

    w_own = own_weights(w_attn, w_gate, seq_id, cols)
    w_out_own = lax.dynamic_slice_in_dim(w_out, seq_id * cols, cols, 0)
    slot_matrix, numbers = row_slots(item_owner[:, 0], item_row, devices, capacity)

    x_full = lax.all_gather(layer_input, "seq", axis=0, tiled=True)
    og_full = lax.all_gather(out_grad, "seq", axis=0, tiled=True)
    order = jnp.arange(positions // blk, dtype=jnp.int32)
    acts, slopes, gate, weights, score_slope, heads = forward_attention(
        lengths, order, [x_full], w_own, blk, maxlen
    )
    mg, stats_own = event_stats(order, [og_full], w_out_own, gate, heads, blk)
    stats = lax.all_gather(stats_own, "seq", axis=0, tiled=False)
    grads, mixed = backward_attention(
        lengths, [stats[s] for s in range(seq_count)], mg, gate, heads, acts, slopes, weights, score_slope, blk, maxlen
    )

    input_part = dot_nt(grads, w_own).astype(BF)
    got = lax.all_to_all(
        input_part.reshape(seq_count, tokens_dev, D), "seq", split_axis=0, concat_axis=0, tiled=True
    )
    input_grad = jnp.sum(got.astype(F32), axis=0) + out_grad.astype(F32)
    rows = jnp.concatenate([input_grad.astype(BF), numbers], axis=1)
    rows = jnp.dot(slot_matrix, rows, preferred_element_type=F32).astype(BF)
    got_rows = to_owners(rows, devices, capacity)
    new_table, new_accum = update_rows(got_rows, emb_table, row_accum)

    out_part = dot_tn(mixed, og_full).astype(BF)
    share = dp_count // seq_count
    out_part = out_part.reshape(share, D // dp_count, seq_count, cols).transpose(0, 2, 1, 3).reshape(D, cols)
    merged = jnp.concatenate([dot_tn(x_full, grads).astype(BF), out_part], axis=1)
    merged = lax.psum_scatter(merged, "dp", scatter_dimension=0, tiled=True)
    steps = []
    for s in range(seq_count):
        for piece in range(dp_count):
            part, target = divmod(piece, seq_count)
            steps.append((s * dp_count + piece, target * dp_count + s * share + part))
    grad_out = lax.ppermute(merged[:, 4 * cols :], ("seq", "dp"), steps).astype(F32)
    grad_attn = merged[:, : 3 * cols].astype(F32)
    grad_gate = merged[:, 3 * cols : 4 * cols].astype(F32)
    return (grad_attn, grad_gate, grad_out, new_table, new_accum)


SEQ = 4
PLANE = 4


def send(array, target):
    steps = []
    for s in range(SEQ):
        for e in range(PLANE):
            for c in range(2):
                to = target(s, e, c)
                if to is not None:
                    steps.append((s * 2 * PLANE + 2 * e + c, to[0] * 2 * PLANE + 2 * to[1] + to[2]))
    return lax.ppermute(array, ("seq", "dp"), steps)


def home(s, c):
    return c == s // 2


def swap_far(array):
    return send(array, lambda s, e, c: None if home(s, c) else (3 - s, e, 1 - c))


def fetch_near(array):
    return send(array, lambda s, e, c: (s ^ 1, e, c) if home(s, c) else ((3 - s) ^ 1, e, 1 - c))


def swap_near(array):
    return send(array, lambda s, e, c: (s ^ 1, e, c))


def swap_core(array):
    return send(array, lambda s, e, c: (s, e, 1 - c))


def swap_x(array):
    return send(array, lambda s, e, c: (s, e ^ 1, c))


def swap_y(array):
    return send(array, lambda s, e, c: (s, e ^ 2, c))


def tie(*arrays):
    return lax.optimization_barrier(arrays)


def sums_kernel(proj_one, proj_two, out_one, out_two, attn_ref, gate_ref, out_ref):
    cut = attn_ref.shape[1]
    attn_ref[...] = proj_one[:, :cut].astype(F32) + proj_two[:, :cut].astype(F32)
    gate_ref[...] = proj_one[:, cut:].astype(F32) + proj_two[:, cut:].astype(F32)
    out_ref[...] = out_one[...].astype(F32) + out_two[...].astype(F32)


def last_sums(proj, out):
    rows, cols = out[0].shape
    widths = (proj[0].shape[1] - cols, cols, cols)
    return pl.pallas_call(
        sums_kernel,
        in_specs=[pl.BlockSpec(memory_space=pltpu.VMEM)] * 4,
        out_specs=[pl.BlockSpec(memory_space=pltpu.VMEM)] * 3,
        out_shape=[jax.ShapeDtypeStruct((rows, width), F32) for width in widths],
        compiler_params=pltpu.CompilerParams(vmem_limit_bytes=VMEM_LIMIT),
        cost_estimate=pl.CostEstimate(flops=0, bytes_accessed=12 * rows * cols * 5, transcendentals=0),
        name="last_sums",
    )(*proj, *out)


def halves(array, bit, axis):
    kept = lax.dynamic_index_in_dim(array, bit, axis, keepdims=False)
    sent = lax.dynamic_index_in_dim(array, 1 - bit, axis, keepdims=False)
    return kept, sent


def body_pairs(
    layer_input, out_grad, lengths, item_owner, item_row, w_attn, w_gate, w_out, emb_table, row_accum
):
    devices = 2 * PLANE * SEQ
    s = lax.axis_index("seq")
    d = lax.axis_index("dp")
    e, c = d // 2, d % 2
    y, x = e // 2, e % 2
    tokens_dev = layer_input.shape[0]
    positions = tokens_dev * SEQ
    maxlen = 2 * positions // 3
    blk = min(256, positions)
    cols = D // SEQ
    rows_own = emb_table.shape[0]
    capacity = max(2, 2 * tokens_dev // devices)
    at_home = c == s // 2
    part = 2 * (s % 2) + c

    def block_of(seq, core):
        return jnp.where(core == seq // 2, seq, 3 - seq)

    mine_at, near_at = block_of(s, c), block_of(s ^ 1, c)
    core_at, diag_at = block_of(s, 1 - c), block_of(s ^ 1, 1 - c)
    order = jnp.stack([mine_at, near_at, core_at, diag_at]).astype(jnp.int32)

    x_far = swap_far(layer_input)
    x_near = fetch_near(layer_input)
    users = lengths.shape[1]
    keys = (item_owner[:, 0] * rows_own + item_row).reshape(1, tokens_dev)
    small = jnp.concatenate([keys, jnp.pad(lengths, ((0, 0), (0, 128 - users)))], axis=1)
    small = jnp.where(at_home, small, swap_far(small))
    keys, lengths = small[0, :tokens_dev], small[:, tokens_dev : tokens_dev + users]
    w_own = own_weights(w_attn, w_gate, part, cols)
    w_out_own = lax.dynamic_slice_in_dim(w_out, part * cols, cols, 0)
    slot_matrix, numbers = row_slots(keys // rows_own, keys % rows_own, devices, capacity)
    x_far, x_near, w_own, w_out_own, slot_matrix, numbers, lengths = tie(
        x_far, x_near, w_own, w_out_own, slot_matrix, numbers, lengths
    )
    x_here = jnp.concatenate([jnp.where(at_home, layer_input, x_far), x_near], axis=0)
    x_there = swap_core(x_here)
    x_here, og_own = tie(x_here, out_grad)
    og_near = fetch_near(og_own)
    og_far = swap_far(og_own)

    x_full, acts, slopes, gate, weights, score_slope, heads = forward_attention(
        lengths, order, [x_here, x_there], w_own, blk, maxlen
    )
    og_far, og_near, heads = tie(og_far, og_near, heads)
    og_mine = jnp.where(at_home, og_own, og_far)
    og_here = jnp.concatenate([og_mine, og_near], axis=0)
    og_there = swap_core(og_here)
    og_full, mg, stats_own = event_stats(order, [og_here, og_there], w_out_own, gate, heads, blk)
    stats = [
        stats_own,
        swap_core(stats_own),
        swap_near(stats_own),
        send(stats_own, lambda s, e, c: (s ^ 1, e, 1 - c)),
    ]
    grads, mixed = backward_attention(
        lengths, stats, mg, gate, heads, acts, slopes, weights, score_slope, blk, maxlen
    )

    def input_part(grads, block):
        return dot_nt(lax.dynamic_slice_in_dim(grads, block * tokens_dev, tokens_dev, 0), w_own)

    from_diag = swap_core(input_part(grads, diag_at).astype(BF))
    near_sum = (input_part(grads, near_at) + from_diag.astype(F32)).astype(BF)
    near_sum, grads = tie(near_sum, grads)
    from_near = swap_near(near_sum)
    core_part = input_part(grads, core_at).astype(BF)
    from_core = swap_core(core_part)
    input_grad = input_part(grads, mine_at) + og_mine.astype(F32)

    core_part, grads, mixed = tie(core_part, grads, mixed)
    half = 5 * cols // 2
    proj = dot_tn(x_full, grads).astype(BF).reshape(2, 2, D // PLANE, 4 * cols)
    out_part = dot_tn(mixed, og_full).astype(BF).reshape(cols, 2, 2, cols)
    a_kept, a_sent = halves(proj[..., :half], x, 1)
    b_kept, b_sent = halves(proj[..., half:], y, 0)
    out_kept, out_sent = (piece.transpose(1, 0, 2) for piece in halves(out_part, y, 1))
    b_kept = jnp.concatenate([b_kept, out_kept], axis=-1)
    b_sent = jnp.concatenate([b_sent, out_sent], axis=-1)
    a_got = swap_x(a_sent)
    b_got = swap_y(b_sent)

    input_grad = input_grad + from_core.astype(F32) + from_near.astype(F32)
    rows = jnp.concatenate([input_grad.astype(BF), numbers], axis=1)
    rows = jnp.dot(slot_matrix, rows, preferred_element_type=F32).astype(BF)
    rows, a_got, b_got = tie(rows, a_got, b_got)
    got_rows = to_owners(rows, devices, capacity)

    a = (a_kept.astype(F32) + a_got.astype(F32)).astype(BF)
    b = (b_kept.astype(F32) + b_got.astype(F32)).astype(BF)
    a_kept, a_sent = halves(a, y, 0)
    b_kept, b_sent = halves(b, x, 0)
    a = (a_kept.astype(F32) + swap_y(a_sent).astype(F32)).astype(BF)
    b = (b_kept.astype(F32) + swap_x(b_sent).astype(F32)).astype(BF)

    def last(array, target):
        pieces = array.reshape(2, D // (2 * PLANE), array.shape[1])
        one, other = halves(pieces, s // 2, 0)
        one = send(one, lambda s, e, c: target(s, e, c, s // 2))
        return one, send(other, lambda s, e, c: target(s, e, c, 1 - s // 2))

    proj = jnp.concatenate([a, b[:, : 4 * cols - half]], axis=1)
    proj = last(proj, lambda s, e, c, piece: (2 * (s % 2) + c, e, piece))
    out = last(b[:, 4 * cols - half :], lambda s, e, c, piece: (e, 2 * (s % 2) + c, piece))
    new_table, new_accum = update_rows(got_rows, emb_table, row_accum)
    *proj, new_accum = tie(*proj, new_accum)
    attn, gate, grad_out = last_sums(proj, out)
    return (attn, gate, grad_out, new_table, new_accum)


def solution(mesh):
    placed = (
        P(("dp", "seq"), None),
        P(("dp", "seq"), None),
        P("dp", None),
        P(("dp", "seq"), None),
        P(("dp", "seq")),
        P(),
        P(),
        P(),
        P(("seq", "dp"), None),
        P(("seq", "dp")),
    )
    paired = mesh.shape["seq"] == SEQ and mesh.shape["dp"] == 2 * PLANE
    return jax.shard_map(
        body_pairs if paired else body_whole,
        mesh=mesh,
        in_specs=placed,
        out_specs=(
            P("dp", "seq"),
            P("dp", "seq"),
            P("dp", "seq"),
            P(("seq", "dp"), None),
            P(("seq", "dp")),
        ),
        check_vma=False,
    )
```

```python
import functools

import jax
import jax.numpy as jnp
from jax import lax
from jax.experimental import pallas as pl
from jax.experimental.pallas import tpu as pltpu
from jax.sharding import PartitionSpec as P

D = 1024
H = 16
DH = 64
PAIR = 2 * DH

NORM_EPS = 1e-05
LEARN_RATE = 0.1
VMEM_LIMIT = 56 * 1024 * 1024
BF = jnp.bfloat16
F32 = jnp.float32


def dot_nn(a, b):
    return lax.dot_general(a, b, (((1,), (0,)), ((), ())), preferred_element_type=F32)


def dot_nt(a, b):
    return lax.dot_general(a, b, (((1,), (1,)), ((), ())), preferred_element_type=F32)


def history_start(lengths_ref, users, place):
    start = jnp.zeros_like(place)
    end = jnp.int32(0)
    for user in range(users - 1):
        end = end + lengths_ref[0, user]
        start = jnp.where(place >= end, end, start)
    return start


def head_columns(kind, head):
    first = head * 3 * DH + kind * DH
    return slice(first, first + DH)


def split_pairs(acts_ref, split_ref, kind, block, blk):
    at = pl.ds(pl.multiple_of(block * blk, blk), blk)
    zero = jnp.zeros((blk, DH), BF)
    for p in range(split_ref.shape[0]):
        one, two = (acts_ref[at, head_columns(kind, 2 * p + h)] for h in range(2))
        below = pl.multiple_of(block * 2 * blk + blk, blk)
        split_ref[p, pl.ds(pl.multiple_of(block * 2 * blk, blk), blk), :] = jnp.concatenate([one, zero], axis=1)
        split_ref[p, pl.ds(below, blk), :] = jnp.concatenate([zero, two], axis=1)


def forward_kernel(*refs, blk, users, maxlen, count):
    lengths_ref, order_ref = refs[:2]
    x_refs = refs[2 : 2 + count]
    w_ref = refs[2 + count]
    outs = refs[3 + count :]
    if count > 1:
        x_out_ref, outs = outs[0], outs[1:]
    acts_ref, slopes_ref, gate_ref, weights_ref, score_slope_ref, heads_ref, k_t, v_split = outs
    i = pl.program_id(0)
    heads = weights_ref.shape[0]
    attn = 3 * heads * DH
    chunks = x_refs[0].shape[0] // blk

    @pl.when(i == 0)
    def _():
        for b in range(count):
            for r in range(chunks):
                at = pl.ds(pl.multiple_of(order_ref[b * chunks + r] * blk, blk), blk)
                x = x_refs[b][r * blk : (r + 1) * blk, :]
                if count > 1:
                    x_out_ref[at, :] = x
                for lane in range(0, w_ref.shape[1], 512):
                    lanes = slice(lane, lane + 512)
                    half = 0.5 * dot_nn(x, w_ref[:, lanes])
                    t = jnp.tanh(half)
                    prod = half * t
                    silu = half + prod
                    acts_ref[at, lanes] = silu.astype(BF)
                    slopes_ref[at, lanes] = (0.5 * (1.0 + t) * (1.0 + half - prod)).astype(BF)
                    skip = max(0, attn - lane)
                    if skip < 512:
                        gate_ref[at, lane + skip - attn : lane + 512 - attn] = silu[:, skip:]
                for h in range(heads):
                    k_t[h * DH : (h + 1) * DH, at] = jnp.transpose(acts_ref[at, head_columns(2, h)])
                split_pairs(acts_ref, v_split, 0, order_ref[b * chunks + r], blk)

    at_i = pl.ds(pl.multiple_of(i * blk, blk), blk)
    q_half = [acts_ref[at_i, head_columns(1, h)] * jnp.asarray(0.5 * DH**-0.5, BF) for h in range(heads)]
    row = i * blk + lax.broadcasted_iota(jnp.int32, (blk, blk), 0)
    col0 = lax.broadcasted_iota(jnp.int32, (blk, blk), 1)
    start = history_start(lengths_ref, users, row)

    def column(j, acc):
        at_j = pl.ds(pl.multiple_of(j * blk, blk), blk)
        both_j = pl.ds(pl.multiple_of(j * 2 * blk, 2 * blk), 2 * blk)
        col = col0 + j * blk
        allowed = (col <= row) & (col >= start)
        per_head = []
        for h in range(heads):
            half = dot_nn(q_half[h], k_t[h * DH : (h + 1) * DH, at_j])
            half = jnp.where(allowed, half, -64.0)
            t = jnp.tanh(half)
            p = half * t
            weights = (half + p).astype(BF)
            weights_ref[h, :, at_j] = weights
            score_slope_ref[h, :, at_j] = ((1.0 + t) * (1.0 + half - p)).astype(BF)
            per_head.append(weights)
        return tuple(
            acc[p] + dot_nn(jnp.concatenate(per_head[2 * p : 2 * p + 2], axis=1), v_split[p, both_j, :])
            for p in range(heads // 2)
        )

    first = history_start(lengths_ref, users, i * blk) // blk
    zero = jnp.zeros((blk, PAIR), F32)
    acc = lax.fori_loop(first, i + 1, column, (zero,) * (heads // 2))
    heads_ref[...] = (jnp.concatenate(acc, axis=1) * (1.0 / maxlen)).astype(BF)


def forward_attention(lengths, order, x_blocks, w_own, blk, maxlen):
    count = len(x_blocks)
    block_rows = x_blocks[0].shape[0]
    positions = count * block_rows
    cols = w_own.shape[1] // 4
    heads = cols // DH
    users = lengths.shape[1]
    elements = heads * positions * positions // 2
    whole = lambda i: (0, 0)
    out_specs = [
        pl.BlockSpec((positions, 4 * cols), whole),
        pl.BlockSpec((positions, 4 * cols), whole),
        pl.BlockSpec((positions, cols), whole),
        pl.BlockSpec((heads, blk, positions), lambda i: (0, i, 0)),
        pl.BlockSpec((heads, blk, positions), lambda i: (0, i, 0)),
        pl.BlockSpec((blk, cols), lambda i: (i, 0)),
    ]
    out_shape = [
        jax.ShapeDtypeStruct((positions, 4 * cols), BF),
        jax.ShapeDtypeStruct((positions, 4 * cols), BF),
        jax.ShapeDtypeStruct((positions, cols), F32),
        jax.ShapeDtypeStruct((heads, positions, positions), BF),
        jax.ShapeDtypeStruct((heads, positions, positions), BF),
        jax.ShapeDtypeStruct((positions, cols), BF),
    ]
    if count > 1:
        out_specs = [pl.BlockSpec((positions, D), whole)] + out_specs
        out_shape = [jax.ShapeDtypeStruct((positions, D), BF)] + out_shape
    return pl.pallas_call(
        functools.partial(forward_kernel, blk=blk, users=users, maxlen=maxlen, count=count),
        grid=(positions // blk,),
        in_specs=[pl.BlockSpec(memory_space=pltpu.SMEM), pl.BlockSpec(memory_space=pltpu.SMEM)]
        + [pl.BlockSpec((block_rows, D), whole)] * count
        + [pl.BlockSpec((D, 4 * cols), whole)],
        out_specs=out_specs,
        out_shape=out_shape,
        scratch_shapes=[pltpu.VMEM((cols, positions), BF), pltpu.VMEM((cols // PAIR, 2 * positions, PAIR), BF)],
        compiler_params=pltpu.CompilerParams(vmem_limit_bytes=VMEM_LIMIT),
        cost_estimate=pl.CostEstimate(
            flops=8 * positions * D * cols + 4 * elements * 256,
            bytes_accessed=4 * positions * D + 4 * elements,
            transcendentals=elements,
        ),
        name="attention_forward",
    )(lengths, order, *x_blocks, w_own)


def stats_kernel(*refs, blk, count):
    order_ref = refs[0]
    og_refs = refs[1 : 1 + count]
    w_ref, gate_ref, heads_ref = refs[1 + count : 4 + count]
    outs = refs[4 + count :]
    if count > 1:
        og_out_ref, outs = outs[0], outs[1:]
    mg_ref, stats_ref = outs
    chunks = og_refs[0].shape[0] // blk
    for b in range(count):
        for r in range(chunks):
            at = pl.ds(pl.multiple_of(order_ref[b * chunks + r] * blk, blk), blk)
            og = og_refs[b][r * blk : (r + 1) * blk, :]
            if count > 1:
                og_out_ref[at, :] = og
            mg = dot_nt(og, w_ref[...])
            mg_ref[at, :] = mg
            ng = mg * gate_ref[at, :]
            heads = heads_ref[at, :].astype(F32)
            mean = jnp.mean(heads, axis=1, keepdims=True)
            centred = heads - mean
            square = jnp.sum(centred * centred, axis=1, keepdims=True)
            total = jnp.sum(ng, axis=1, keepdims=True)
            cross = jnp.sum(ng * centred, axis=1, keepdims=True)
            lane = lax.broadcasted_iota(jnp.int32, (blk, 128), 1)
            packed = jnp.where(lane == 0, mean, jnp.where(lane == 1, square, jnp.where(lane == 2, total, cross)))
            stats_ref[:, at] = jnp.transpose(packed)[:8, :]


def event_stats(order, og_blocks, w_out_own, gate, heads, blk):
    positions, cols = heads.shape
    count = len(og_blocks)
    vmem = pl.BlockSpec(memory_space=pltpu.VMEM)
    out_shape = [
        jax.ShapeDtypeStruct((positions, cols), F32),
        jax.ShapeDtypeStruct((8, positions), F32),
    ]
    if count > 1:
        out_shape = [jax.ShapeDtypeStruct((positions, D), BF)] + out_shape
    return pl.pallas_call(
        functools.partial(stats_kernel, blk=blk, count=count),
        in_specs=[pl.BlockSpec(memory_space=pltpu.SMEM)] + [vmem] * (count + 3),
        out_specs=[vmem] * len(out_shape),
        out_shape=out_shape,
        compiler_params=pltpu.CompilerParams(vmem_limit_bytes=VMEM_LIMIT),
        cost_estimate=pl.CostEstimate(
            flops=2 * positions * cols * D, bytes_accessed=4 * positions * D + 10 * positions * cols, transcendentals=0
        ),
        name="event_stats",
    )(order, *og_blocks, w_out_own, gate, heads)


def combined_stats(stats_refs, cols):
    shards = len(stats_refs)
    positions = stats_refs[0].shape[1]
    means = [ref[0:1, :] for ref in stats_refs]
    mean = sum(means) * (1.0 / shards)
    square = jnp.zeros_like(mean)
    total = jnp.zeros_like(mean)
    cross = jnp.zeros_like(mean)
    for s, ref in enumerate(stats_refs):
        shift = means[s] - mean
        part = ref[2:3, :]
        square = square + ref[1:2, :] + cols * shift * shift
        total = total + part
        cross = cross + ref[3:4, :] + shift * part
    inv_dev = lax.rsqrt(square * (1.0 / D) + NORM_EPS)
    kind = lax.broadcasted_iota(jnp.int32, (128, positions), 0)
    rest = jnp.where(kind == 2, total * (1.0 / D), cross * inv_dev * (1.0 / D))
    packed = jnp.where(kind == 0, mean, jnp.where(kind == 1, inv_dev, rest))
    per_event = jnp.transpose(packed)
    return [per_event[:, k : k + 1] for k in range(4)]


def backward_kernel(*refs, blk, users, maxlen, shards):
    lengths_ref = refs[0]
    stats_refs = refs[1 : 1 + shards]
    mg_ref, gate_ref, heads_ref, acts_ref, slopes_ref, weights_ref, score_slope_ref = refs[1 + shards : 8 + shards]
    grad_ref, mixed_ref, o_ref, o_t, q_t, v_t, k_split, vg_t, kg_t, qg = refs[8 + shards :]
    i = pl.program_id(0)
    positions, cols = o_ref.shape
    heads = cols // DH
    blocks = positions // blk
    scale = DH ** (-0.5)

    @pl.when(i == 0)
    def _():
        mean, inv_dev, total, cross = combined_stats(stats_refs, cols)
        for p in range(heads // 2):
            lanes = slice(p * PAIR, (p + 1) * PAIR)
            normed = (heads_ref[:, lanes].astype(F32) - mean) * inv_dev
            gate = gate_ref[:, lanes]
            mg = mg_ref[:, lanes]
            mixed_ref[:, lanes] = (normed * gate).astype(BF)
            gate_lanes = slice(3 * cols + p * PAIR, 3 * cols + (p + 1) * PAIR)
            gate_slope = slopes_ref[:, gate_lanes].astype(F32)
            grad_ref[:, gate_lanes] = (mg * normed * gate_slope).astype(BF)
            o_ref[:, lanes] = (inv_dev * (mg * gate - total - normed * cross)).astype(BF)
        o_t[...] = jnp.transpose(o_ref[...])
        for scratch, kind in ((v_t, 0), (q_t, 1)):
            scratch[...] = jnp.transpose(jnp.concatenate([acts_ref[:, head_columns(kind, h)] for h in range(heads)], axis=1))
        for block in range(blocks):
            split_pairs(acts_ref, k_split, 2, block, blk)
        vg_t[...] = jnp.zeros_like(vg_t)
        kg_t[...] = jnp.zeros_like(kg_t)

    at_i = pl.ds(pl.multiple_of(i * blk, blk), blk)
    o_i = [o_ref[at_i, h * DH : (h + 1) * DH] for h in range(heads)]

    def column(j, acc):
        at_j = pl.ds(pl.multiple_of(j * blk, blk), blk)
        both_j = pl.ds(pl.multiple_of(j * 2 * blk, 2 * blk), 2 * blk)
        per_head = []
        for h in range(heads):
            lanes = slice(h * DH, (h + 1) * DH)
            weight_grad = dot_nn(o_i[h], v_t[lanes, at_j])
            score_grad = (weight_grad * score_slope_ref[h, :, at_j].astype(F32)).astype(BF)
            vg_t[lanes, at_j] += dot_nn(o_t[lanes, at_i], weights_ref[h, :, at_j])
            kg_t[lanes, at_j] += dot_nn(q_t[lanes, at_i], score_grad)
            per_head.append(score_grad)
        return tuple(
            acc[p] + dot_nn(jnp.concatenate(per_head[2 * p : 2 * p + 2], axis=1), k_split[p, both_j, :])
            for p in range(heads // 2)
        )

    first = history_start(lengths_ref, users, i * blk) // blk
    zero = jnp.zeros((blk, PAIR), F32)
    acc = lax.fori_loop(first, i + 1, column, (zero,) * (heads // 2))
    qg[at_i, :] = jnp.concatenate(acc, axis=1)

    @pl.when(i == blocks - 1)
    def _():
        factor = 0.5 * scale / maxlen
        grads = [jnp.transpose(vg_t[...]) * (1.0 / maxlen), qg[...] * factor, jnp.transpose(kg_t[...]) * factor]
        pieces = [grads[kind][:, h * DH : (h + 1) * DH] for h in range(heads) for kind in range(3)]
        for n in range(3 * heads // 2):
            lanes = slice(n * PAIR, (n + 1) * PAIR)
            grad = jnp.concatenate(pieces[2 * n : 2 * n + 2], axis=1).astype(BF).astype(F32)
            grad_ref[:, lanes] = (grad * slopes_ref[:, lanes].astype(F32)).astype(BF)


def backward_attention(lengths, stats, mg, gate, head_outs, acts, slopes, weights, score_slope, blk, maxlen):
    positions, cols = mg.shape
    heads = cols // DH
    shards = len(stats)
    users = lengths.shape[1]
    elements = heads * positions * positions // 2
    whole = lambda i: (0, 0)
    return pl.pallas_call(
        functools.partial(backward_kernel, blk=blk, users=users, maxlen=maxlen, shards=shards),
        grid=(positions // blk,),
        in_specs=[pl.BlockSpec(memory_space=pltpu.SMEM)]
        + [pl.BlockSpec((8, positions), whole)] * shards
        + [
            pl.BlockSpec((positions, cols), whole),
            pl.BlockSpec((positions, cols), whole),
            pl.BlockSpec((positions, cols), whole),
            pl.BlockSpec((positions, 4 * cols), whole),
            pl.BlockSpec((positions, 4 * cols), whole),
            pl.BlockSpec((heads, blk, positions), lambda i: (0, i, 0)),
            pl.BlockSpec((heads, blk, positions), lambda i: (0, i, 0)),
        ],
        out_specs=[pl.BlockSpec((positions, 4 * cols), whole), pl.BlockSpec((positions, cols), whole)],
        out_shape=[
            jax.ShapeDtypeStruct((positions, 4 * cols), BF),
            jax.ShapeDtypeStruct((positions, cols), BF),
        ],
        scratch_shapes=[
            pltpu.VMEM((positions, cols), BF),
            pltpu.VMEM((cols, positions), BF),
            pltpu.VMEM((cols, positions), BF),
            pltpu.VMEM((cols, positions), BF),
            pltpu.VMEM((cols // PAIR, 2 * positions, PAIR), BF),
            pltpu.VMEM((cols, positions), F32),
            pltpu.VMEM((cols, positions), F32),
            pltpu.VMEM((positions, cols), F32),
        ],
        compiler_params=pltpu.CompilerParams(vmem_limit_bytes=VMEM_LIMIT),
        cost_estimate=pl.CostEstimate(
            flops=8 * elements * 256, bytes_accessed=4 * elements + 26 * positions * cols, transcendentals=0
        ),
        name="attention_backward",
    )(lengths, *stats, mg, gate, head_outs, acts, slopes, weights, score_slope)


def update_kernel(rows_ref, table_ref, accum_ref, new_table_ref, new_accum_ref, ids):
    i = pl.program_id(0)
    blk = table_ref.shape[0]
    slots = rows_ref.shape[0]

    @pl.when(i == 0)
    def _():
        numbers = jnp.transpose(rows_ref[:, D:].astype(F32))
        ids[...] = (numbers[0:1, :] * 256.0 + numbers[1:2, :]).astype(jnp.int32)

    row = i * blk + lax.broadcasted_iota(jnp.int32, (blk, slots), 0)
    hits = jnp.where(row == ids[...], 1.0, 0.0).astype(BF)
    grad = dot_nn(hits, rows_ref[:, :D])
    accum = jnp.transpose(jnp.broadcast_to(accum_ref[...], (128, blk)))[:, :1] + jnp.mean(grad * grad, axis=1, keepdims=True)
    new_accum_ref[...] = jnp.transpose(jnp.broadcast_to(accum, (blk, 128)))[:1, :]
    new_table_ref[...] = table_ref[...] - LEARN_RATE * grad * lax.rsqrt(accum)


def update_rows(got_rows, emb_table, row_accum):
    rows_own = emb_table.shape[0]
    slots = got_rows.shape[0]
    blk = min(256, rows_own)
    new_table, new_accum = pl.pallas_call(
        update_kernel,
        grid=(rows_own // blk,),
        in_specs=[
            pl.BlockSpec((slots, D + 128), lambda i: (0, 0)),
            pl.BlockSpec((blk, D), lambda i: (i, 0)),
            pl.BlockSpec((1, blk), lambda i: (0, i)),
        ],
        out_specs=[
            pl.BlockSpec((blk, D), lambda i: (i, 0)),
            pl.BlockSpec((1, blk), lambda i: (0, i)),
        ],
        out_shape=[
            jax.ShapeDtypeStruct((rows_own, D), F32),
            jax.ShapeDtypeStruct((1, rows_own), F32),
        ],
        scratch_shapes=[pltpu.VMEM((1, slots), jnp.int32)],
        compiler_params=pltpu.CompilerParams(vmem_limit_bytes=VMEM_LIMIT),
        cost_estimate=pl.CostEstimate(
            flops=2 * rows_own * slots * D, bytes_accessed=8 * rows_own * D + 2 * slots * D, transcendentals=rows_own
        ),
        name="update_rows",
    )(got_rows, emb_table, row_accum.reshape(1, rows_own))
    return new_table, new_accum.reshape(rows_own)


def own_weights(w_attn, w_gate, part, cols):
    attn = lax.dynamic_slice_in_dim(w_attn, part * 3 * cols, 3 * cols, 1)
    gate = lax.dynamic_slice_in_dim(w_gate, part * cols, cols, 1)
    return jnp.concatenate([attn, gate], axis=1)


def row_slots(owners, rows, devices, capacity):
    events = owners.shape[0]
    owner_hits = (owners[:, None] == jnp.arange(devices, dtype=jnp.int32)[None, :]).astype(BF)
    place = jnp.arange(events, dtype=jnp.int32)
    before = (place[:, None] > place[None, :]).astype(BF)
    earlier = jnp.dot(before, owner_hits, preferred_element_type=F32)
    slots = jnp.sum(earlier * owner_hits.astype(F32), axis=1).astype(jnp.int32)
    flat_slot = owners * capacity + slots
    slot_hits = jnp.arange(devices * capacity, dtype=jnp.int32)[:, None] == flat_slot[None, :]
    lane = jnp.arange(128, dtype=jnp.int32)[None, :]
    numbers = jnp.where(lane == 0, rows[:, None] // 256, jnp.where(lane == 1, rows[:, None] % 256, 0))
    return slot_hits.astype(BF), numbers.astype(BF)


def to_owners(rows, devices, capacity):
    shape = (devices, capacity) + rows.shape[1:]
    got = lax.all_to_all(rows.reshape(shape), ("seq", "dp"), split_axis=0, concat_axis=0, tiled=True)
    return got.reshape(rows.shape)


TN = (((0,), (0,)), ((), ()))


def dot_tn(a, b):
    return lax.dot_general(a, b, TN, preferred_element_type=F32)


def body_whole(
    layer_input, out_grad, lengths, item_owner, item_row, w_attn, w_gate, w_out, emb_table, row_accum
):
    seq_count = lax.axis_size("seq")
    dp_count = lax.axis_size("dp")
    devices = seq_count * dp_count
    seq_id = lax.axis_index("seq")
    tokens_dev = layer_input.shape[0]
    positions = tokens_dev * seq_count
    maxlen = 2 * positions // 3
    blk = min(256, positions)
    cols = D // seq_count
    capacity = max(2, 2 * tokens_dev // devices)

    w_own = own_weights(w_attn, w_gate, seq_id, cols)
    w_out_own = lax.dynamic_slice_in_dim(w_out, seq_id * cols, cols, 0)
    slot_matrix, numbers = row_slots(item_owner[:, 0], item_row, devices, capacity)

    x_full = lax.all_gather(layer_input, "seq", axis=0, tiled=True)
    og_full = lax.all_gather(out_grad, "seq", axis=0, tiled=True)
    order = jnp.arange(positions // blk, dtype=jnp.int32)
    acts, slopes, gate, weights, score_slope, heads = forward_attention(
        lengths, order, [x_full], w_own, blk, maxlen
    )
    mg, stats_own = event_stats(order, [og_full], w_out_own, gate, heads, blk)
    stats = lax.all_gather(stats_own, "seq", axis=0, tiled=False)
    grads, mixed = backward_attention(
        lengths, [stats[s] for s in range(seq_count)], mg, gate, heads, acts, slopes, weights, score_slope, blk, maxlen
    )

    input_part = dot_nt(grads, w_own).astype(BF)
    got = lax.all_to_all(
        input_part.reshape(seq_count, tokens_dev, D), "seq", split_axis=0, concat_axis=0, tiled=True
    )
    input_grad = jnp.sum(got.astype(F32), axis=0) + out_grad.astype(F32)
    rows = jnp.concatenate([input_grad.astype(BF), numbers], axis=1)
    rows = jnp.dot(slot_matrix, rows, preferred_element_type=F32).astype(BF)
    got_rows = to_owners(rows, devices, capacity)
    new_table, new_accum = update_rows(got_rows, emb_table, row_accum)

    out_part = dot_tn(mixed, og_full).astype(BF)
    share = dp_count // seq_count
    out_part = out_part.reshape(share, D // dp_count, seq_count, cols).transpose(0, 2, 1, 3).reshape(D, cols)
    merged = jnp.concatenate([dot_tn(x_full, grads).astype(BF), out_part], axis=1)
    merged = lax.psum_scatter(merged, "dp", scatter_dimension=0, tiled=True)
    steps = []
    for s in range(seq_count):
        for piece in range(dp_count):
            part, target = divmod(piece, seq_count)
            steps.append((s * dp_count + piece, target * dp_count + s * share + part))
    grad_out = lax.ppermute(merged[:, 4 * cols :], ("seq", "dp"), steps).astype(F32)
    grad_attn = merged[:, : 3 * cols].astype(F32)
    grad_gate = merged[:, 3 * cols : 4 * cols].astype(F32)
    return (grad_attn, grad_gate, grad_out, new_table, new_accum)


SEQ = 4
PLANE = 4


def send(array, target):
    steps = []
    for s in range(SEQ):
        for e in range(PLANE):
            for c in range(2):
                to = target(s, e, c)
                if to is not None:
                    steps.append((s * 2 * PLANE + 2 * e + c, to[0] * 2 * PLANE + 2 * to[1] + to[2]))
    return lax.ppermute(array, ("seq", "dp"), steps)


def home(s, c):
    return c == s // 2


def swap_far(array):
    return send(array, lambda s, e, c: None if home(s, c) else (3 - s, e, 1 - c))


def fetch_near(array):
    return send(array, lambda s, e, c: (s ^ 1, e, c) if home(s, c) else ((3 - s) ^ 1, e, 1 - c))


def swap_near(array):
    return send(array, lambda s, e, c: (s ^ 1, e, c))


def swap_core(array):
    return send(array, lambda s, e, c: (s, e, 1 - c))


def swap_x(array):
    return send(array, lambda s, e, c: (s, e ^ 1, c))


def swap_y(array):
    return send(array, lambda s, e, c: (s, e ^ 2, c))


def tie(*arrays):
    return lax.optimization_barrier(arrays)


def last_kernel(
    rows_ref, table_ref, accum_ref, proj_one, proj_two, out_one, out_two,
    attn_ref, gate_ref, out_ref, new_table_ref, new_accum_ref, ids,
):
    @pl.when(pl.program_id(0) == 0)
    def _():
        cut = attn_ref.shape[1]
        attn_ref[...] = proj_one[:, :cut].astype(F32) + proj_two[:, :cut].astype(F32)
        gate_ref[...] = proj_one[:, cut:].astype(F32) + proj_two[:, cut:].astype(F32)
        out_ref[...] = out_one[...].astype(F32) + out_two[...].astype(F32)

    update_kernel(rows_ref, table_ref, accum_ref, new_table_ref, new_accum_ref, ids)


def update_and_sum(got_rows, emb_table, row_accum, proj, out):
    rows_own = emb_table.shape[0]
    slots = got_rows.shape[0]
    blk = min(256, rows_own)
    rows, cols = out[0].shape
    whole = lambda array: pl.BlockSpec(array.shape, lambda i: (0, 0))
    sums = [jax.ShapeDtypeStruct((rows, width), F32) for width in (proj[0].shape[1] - cols, cols, cols)]
    update_specs = [pl.BlockSpec((blk, D), lambda i: (i, 0)), pl.BlockSpec((1, blk), lambda i: (0, i))]
    attn, gate, grad_out, new_table, new_accum = pl.pallas_call(
        last_kernel,
        grid=(rows_own // blk,),
        in_specs=[whole(got_rows)] + update_specs + [whole(array) for array in (*proj, *out)],
        out_specs=[whole(array) for array in sums] + update_specs,
        out_shape=sums
        + [jax.ShapeDtypeStruct((rows_own, D), F32), jax.ShapeDtypeStruct((1, rows_own), F32)],
        scratch_shapes=[pltpu.VMEM((1, slots), jnp.int32)],
        compiler_params=pltpu.CompilerParams(vmem_limit_bytes=VMEM_LIMIT),
        cost_estimate=pl.CostEstimate(
            flops=2 * rows_own * slots * D, bytes_accessed=8 * rows_own * D + 2 * slots * D, transcendentals=rows_own
        ),
        name="update_and_sum",
    )(got_rows, emb_table, row_accum.reshape(1, rows_own), *proj, *out)
    return attn, gate, grad_out, new_table, new_accum.reshape(rows_own)


def halves(array, bit, axis):
    kept = lax.dynamic_index_in_dim(array, bit, axis, keepdims=False)
    sent = lax.dynamic_index_in_dim(array, 1 - bit, axis, keepdims=False)
    return kept, sent


def body_pairs(
    layer_input, out_grad, lengths, item_owner, item_row, w_attn, w_gate, w_out, emb_table, row_accum
):
    devices = 2 * PLANE * SEQ
    s = lax.axis_index("seq")
    d = lax.axis_index("dp")
    e, c = d // 2, d % 2
    y, x = e // 2, e % 2
    tokens_dev = layer_input.shape[0]
    positions = tokens_dev * SEQ
    maxlen = 2 * positions // 3
    blk = min(256, positions)
    cols = D // SEQ
    rows_own = emb_table.shape[0]
    capacity = max(2, 2 * tokens_dev // devices)
    at_home = c == s // 2
    part = 2 * (s % 2) + c

    def block_of(seq, core):
        return jnp.where(core == seq // 2, seq, 3 - seq)

    mine_at, near_at = block_of(s, c), block_of(s ^ 1, c)
    core_at, diag_at = block_of(s, 1 - c), block_of(s ^ 1, 1 - c)
    order = jnp.stack([mine_at, near_at, core_at, diag_at]).astype(jnp.int32)

    x_far = swap_far(layer_input)
    x_near = fetch_near(layer_input)
    users = lengths.shape[1]
    keys = (item_owner[:, 0] * rows_own + item_row).reshape(1, tokens_dev)
    small = jnp.concatenate([keys, jnp.pad(lengths, ((0, 0), (0, 128 - users)))], axis=1)
    small = jnp.where(at_home, small, swap_far(small))
    keys, lengths = small[0, :tokens_dev], small[:, tokens_dev : tokens_dev + users]
    w_own = own_weights(w_attn, w_gate, part, cols)
    w_out_own = lax.dynamic_slice_in_dim(w_out, part * cols, cols, 0)
    slot_matrix, numbers = row_slots(keys // rows_own, keys % rows_own, devices, capacity)
    x_far, x_near, w_own, w_out_own, slot_matrix, numbers, lengths = tie(
        x_far, x_near, w_own, w_out_own, slot_matrix, numbers, lengths
    )
    x_here = jnp.concatenate([jnp.where(at_home, layer_input, x_far), x_near], axis=0)
    x_there = swap_core(x_here)
    x_here, og_own = tie(x_here, out_grad)
    og_near = fetch_near(og_own)
    og_far = swap_far(og_own)

    x_full, acts, slopes, gate, weights, score_slope, heads = forward_attention(
        lengths, order, [x_here, x_there], w_own, blk, maxlen
    )
    og_far, og_near, heads = tie(og_far, og_near, heads)
    og_mine = jnp.where(at_home, og_own, og_far)
    og_here = jnp.concatenate([og_mine, og_near], axis=0)
    og_there = swap_core(og_here)
    og_full, mg, stats_own = event_stats(order, [og_here, og_there], w_out_own, gate, heads, blk)
    stats = [
        stats_own,
        swap_core(stats_own),
        swap_near(stats_own),
        send(stats_own, lambda s, e, c: (s ^ 1, e, 1 - c)),
    ]
    grads, mixed = backward_attention(
        lengths, stats, mg, gate, heads, acts, slopes, weights, score_slope, blk, maxlen
    )

    def input_part(grads, block):
        return dot_nt(lax.dynamic_slice_in_dim(grads, block * tokens_dev, tokens_dev, 0), w_own)

    from_diag = swap_core(input_part(grads, diag_at).astype(BF))
    near_sum = (input_part(grads, near_at) + from_diag.astype(F32)).astype(BF)
    near_sum, grads = tie(near_sum, grads)
    from_near = swap_near(near_sum)
    core_part = input_part(grads, core_at).astype(BF)
    from_core = swap_core(core_part)
    input_grad = input_part(grads, mine_at) + og_mine.astype(F32)

    core_part, grads, mixed = tie(core_part, grads, mixed)
    half = 5 * cols // 2
    proj = dot_tn(x_full, grads).astype(BF).reshape(2, 2, D // PLANE, 4 * cols)
    out_part = dot_tn(mixed, og_full).astype(BF).reshape(cols, 2, 2, cols)
    a_kept, a_sent = halves(proj[..., :half], x, 1)
    b_kept, b_sent = halves(proj[..., half:], y, 0)
    out_kept, out_sent = (piece.transpose(1, 0, 2) for piece in halves(out_part, y, 1))
    b_kept = jnp.concatenate([b_kept, out_kept], axis=-1)
    b_sent = jnp.concatenate([b_sent, out_sent], axis=-1)
    a_got = swap_x(a_sent)
    b_got = swap_y(b_sent)

    input_grad = input_grad + from_core.astype(F32) + from_near.astype(F32)
    rows = jnp.concatenate([input_grad.astype(BF), numbers], axis=1)
    rows = jnp.dot(slot_matrix, rows, preferred_element_type=F32).astype(BF)
    got_rows = to_owners(rows, devices, capacity)

    a = (a_kept.astype(F32) + a_got.astype(F32)).astype(BF)
    b = (b_kept.astype(F32) + b_got.astype(F32)).astype(BF)
    a_kept, a_sent = halves(a, y, 0)
    b_kept, b_sent = halves(b, x, 0)
    a = (a_kept.astype(F32) + swap_y(a_sent).astype(F32)).astype(BF)
    b = (b_kept.astype(F32) + swap_x(b_sent).astype(F32)).astype(BF)

    def last(array, target):
        pieces = array.reshape(2, D // (2 * PLANE), array.shape[1])
        one, other = halves(pieces, s // 2, 0)
        one = send(one, lambda s, e, c: target(s, e, c, s // 2))
        return one, send(other, lambda s, e, c: target(s, e, c, 1 - s // 2))

    proj = jnp.concatenate([a, b[:, : 4 * cols - half]], axis=1)
    proj = last(proj, lambda s, e, c, piece: (2 * (s % 2) + c, e, piece))
    out = last(b[:, 4 * cols - half :], lambda s, e, c, piece: (e, 2 * (s % 2) + c, piece))
    return update_and_sum(got_rows, emb_table, row_accum, proj, out)


def solution(mesh):
    placed = (
        P(("dp", "seq"), None),
        P(("dp", "seq"), None),
        P("dp", None),
        P(("dp", "seq"), None),
        P(("dp", "seq")),
        P(),
        P(),
        P(),
        P(("seq", "dp"), None),
        P(("seq", "dp")),
    )
    paired = mesh.shape["seq"] == SEQ and mesh.shape["dp"] == 2 * PLANE
    return jax.shard_map(
        body_pairs if paired else body_whole,
        mesh=mesh,
        in_specs=placed,
        out_specs=(
            P("dp", "seq"),
            P("dp", "seq"),
            P("dp", "seq"),
            P(("seq", "dp"), None),
            P(("seq", "dp")),
        ),
        check_vma=False,
    )
```

```python
import functools

import jax
import jax.numpy as jnp
from jax import lax
from jax.experimental import pallas as pl
from jax.experimental.pallas import tpu as pltpu
from jax.sharding import PartitionSpec as P

D = 1024
H = 16
DH = 64
PAIR = 2 * DH

NORM_EPS = 1e-05
LEARN_RATE = 0.1
VMEM_LIMIT = 56 * 1024 * 1024
BF = jnp.bfloat16
F32 = jnp.float32


def dot_nn(a, b):
    return lax.dot_general(a, b, (((1,), (0,)), ((), ())), preferred_element_type=F32)


def dot_nt(a, b):
    return lax.dot_general(a, b, (((1,), (1,)), ((), ())), preferred_element_type=F32)


def history_start(lengths_ref, users, place):
    start = jnp.zeros_like(place)
    end = jnp.int32(0)
    for user in range(users - 1):
        end = end + lengths_ref[0, user]
        start = jnp.where(place >= end, end, start)
    return start


def head_columns(kind, head):
    first = head * 3 * DH + kind * DH
    return slice(first, first + DH)


def split_pairs(acts_ref, split_ref, kind, block, blk):
    at = pl.ds(pl.multiple_of(block * blk, blk), blk)
    zero = jnp.zeros((blk, DH), BF)
    for p in range(split_ref.shape[0]):
        one, two = (acts_ref[at, head_columns(kind, 2 * p + h)] for h in range(2))
        below = pl.multiple_of(block * 2 * blk + blk, blk)
        split_ref[p, pl.ds(pl.multiple_of(block * 2 * blk, blk), blk), :] = jnp.concatenate([one, zero], axis=1)
        split_ref[p, pl.ds(below, blk), :] = jnp.concatenate([zero, two], axis=1)


def forward_kernel(*refs, blk, users, maxlen, count):
    lengths_ref, order_ref = refs[:2]
    x_refs = refs[2 : 2 + count]
    w_ref = refs[2 + count]
    outs = refs[3 + count :]
    if count > 1:
        x_out_ref, outs = outs[0], outs[1:]
    acts_ref, slopes_ref, gate_ref, weights_ref, score_slope_ref, heads_ref, k_t, v_split = outs
    i = pl.program_id(0)
    heads = weights_ref.shape[0]
    attn = 3 * heads * DH
    chunks = x_refs[0].shape[0] // blk

    @pl.when(i == 0)
    def _():
        for b in range(count):
            for r in range(chunks):
                at = pl.ds(pl.multiple_of(order_ref[b * chunks + r] * blk, blk), blk)
                x = x_refs[b][r * blk : (r + 1) * blk, :]
                if count > 1:
                    x_out_ref[at, :] = x
                for lane in range(0, w_ref.shape[1], 512):
                    lanes = slice(lane, lane + 512)
                    half = 0.5 * dot_nn(x, w_ref[:, lanes])
                    t = jnp.tanh(half)
                    prod = half * t
                    silu = half + prod
                    acts_ref[at, lanes] = silu.astype(BF)
                    slopes_ref[at, lanes] = (0.5 * (1.0 + t) * (1.0 + half - prod)).astype(BF)
                    skip = max(0, attn - lane)
                    if skip < 512:
                        gate_ref[at, lane + skip - attn : lane + 512 - attn] = silu[:, skip:]
                for h in range(heads):
                    k_t[h * DH : (h + 1) * DH, at] = jnp.transpose(acts_ref[at, head_columns(2, h)])
                split_pairs(acts_ref, v_split, 0, order_ref[b * chunks + r], blk)

    at_i = pl.ds(pl.multiple_of(i * blk, blk), blk)
    q_half = [acts_ref[at_i, head_columns(1, h)] * jnp.asarray(0.5 * DH**-0.5, BF) for h in range(heads)]
    row = i * blk + lax.broadcasted_iota(jnp.int32, (blk, blk), 0)
    col0 = lax.broadcasted_iota(jnp.int32, (blk, blk), 1)
    start = history_start(lengths_ref, users, row)

    def column(j, acc):
        at_j = pl.ds(pl.multiple_of(j * blk, blk), blk)
        both_j = pl.ds(pl.multiple_of(j * 2 * blk, 2 * blk), 2 * blk)
        col = col0 + j * blk
        allowed = (col <= row) & (col >= start)
        per_head = []
        for h in range(heads):
            half = dot_nn(q_half[h], k_t[h * DH : (h + 1) * DH, at_j])
            half = jnp.where(allowed, half, -64.0)
            t = jnp.tanh(half)
            p = half * t
            weights = (half + p).astype(BF)
            weights_ref[h, :, at_j] = weights
            score_slope_ref[h, :, at_j] = ((1.0 + t) * (1.0 + half - p)).astype(BF)
            per_head.append(weights)
        return tuple(
            acc[p] + dot_nn(jnp.concatenate(per_head[2 * p : 2 * p + 2], axis=1), v_split[p, both_j, :])
            for p in range(heads // 2)
        )

    first = history_start(lengths_ref, users, i * blk) // blk
    zero = jnp.zeros((blk, PAIR), F32)
    acc = lax.fori_loop(first, i + 1, column, (zero,) * (heads // 2))
    heads_ref[...] = (jnp.concatenate(acc, axis=1) * (1.0 / maxlen)).astype(BF)


def forward_attention(lengths, order, x_blocks, w_own, blk, maxlen):
    count = len(x_blocks)
    block_rows = x_blocks[0].shape[0]
    positions = count * block_rows
    cols = w_own.shape[1] // 4
    heads = cols // DH
    users = lengths.shape[1]
    elements = heads * positions * positions // 2
    whole = lambda i: (0, 0)
    out_specs = [
        pl.BlockSpec((positions, 4 * cols), whole),
        pl.BlockSpec((positions, 4 * cols), whole),
        pl.BlockSpec((positions, cols), whole),
        pl.BlockSpec((heads, blk, positions), lambda i: (0, i, 0)),
        pl.BlockSpec((heads, blk, positions), lambda i: (0, i, 0)),
        pl.BlockSpec((blk, cols), lambda i: (i, 0)),
    ]
    out_shape = [
        jax.ShapeDtypeStruct((positions, 4 * cols), BF),
        jax.ShapeDtypeStruct((positions, 4 * cols), BF),
        jax.ShapeDtypeStruct((positions, cols), F32),
        jax.ShapeDtypeStruct((heads, positions, positions), BF),
        jax.ShapeDtypeStruct((heads, positions, positions), BF),
        jax.ShapeDtypeStruct((positions, cols), BF),
    ]
    if count > 1:
        out_specs = [pl.BlockSpec((positions, D), whole)] + out_specs
        out_shape = [jax.ShapeDtypeStruct((positions, D), BF)] + out_shape
    return pl.pallas_call(
        functools.partial(forward_kernel, blk=blk, users=users, maxlen=maxlen, count=count),
        grid=(positions // blk,),
        in_specs=[pl.BlockSpec(memory_space=pltpu.SMEM), pl.BlockSpec(memory_space=pltpu.SMEM)]
        + [pl.BlockSpec((block_rows, D), whole)] * count
        + [pl.BlockSpec((D, 4 * cols), whole)],
        out_specs=out_specs,
        out_shape=out_shape,
        scratch_shapes=[pltpu.VMEM((cols, positions), BF), pltpu.VMEM((cols // PAIR, 2 * positions, PAIR), BF)],
        compiler_params=pltpu.CompilerParams(vmem_limit_bytes=VMEM_LIMIT),
        cost_estimate=pl.CostEstimate(
            flops=8 * positions * D * cols + 4 * elements * 256,
            bytes_accessed=4 * positions * D + 4 * elements,
            transcendentals=elements,
        ),
        name="attention_forward",
    )(lengths, order, *x_blocks, w_own)


def stats_kernel(*refs, blk, count):
    order_ref = refs[0]
    og_refs = refs[1 : 1 + count]
    w_ref, gate_ref, heads_ref = refs[1 + count : 4 + count]
    outs = refs[4 + count :]
    if count > 1:
        og_out_ref, outs = outs[0], outs[1:]
    mg_ref, stats_ref = outs
    chunks = og_refs[0].shape[0] // blk
    for b in range(count):
        for r in range(chunks):
            at = pl.ds(pl.multiple_of(order_ref[b * chunks + r] * blk, blk), blk)
            og = og_refs[b][r * blk : (r + 1) * blk, :]
            if count > 1:
                og_out_ref[at, :] = og
            mg = dot_nt(og, w_ref[...])
            mg_ref[at, :] = mg
            ng = mg * gate_ref[at, :]
            heads = heads_ref[at, :].astype(F32)
            mean = jnp.mean(heads, axis=1, keepdims=True)
            centred = heads - mean
            square = jnp.sum(centred * centred, axis=1, keepdims=True)
            total = jnp.sum(ng, axis=1, keepdims=True)
            cross = jnp.sum(ng * centred, axis=1, keepdims=True)
            lane = lax.broadcasted_iota(jnp.int32, (blk, 128), 1)
            packed = jnp.where(lane == 0, mean, jnp.where(lane == 1, square, jnp.where(lane == 2, total, cross)))
            stats_ref[:, at] = jnp.transpose(packed)[:8, :]


def event_stats(order, og_blocks, w_out_own, gate, heads, blk):
    positions, cols = heads.shape
    count = len(og_blocks)
    vmem = pl.BlockSpec(memory_space=pltpu.VMEM)
    out_shape = [
        jax.ShapeDtypeStruct((positions, cols), F32),
        jax.ShapeDtypeStruct((8, positions), F32),
    ]
    if count > 1:
        out_shape = [jax.ShapeDtypeStruct((positions, D), BF)] + out_shape
    return pl.pallas_call(
        functools.partial(stats_kernel, blk=blk, count=count),
        in_specs=[pl.BlockSpec(memory_space=pltpu.SMEM)] + [vmem] * (count + 3),
        out_specs=[vmem] * len(out_shape),
        out_shape=out_shape,
        compiler_params=pltpu.CompilerParams(vmem_limit_bytes=VMEM_LIMIT),
        cost_estimate=pl.CostEstimate(
            flops=2 * positions * cols * D, bytes_accessed=4 * positions * D + 10 * positions * cols, transcendentals=0
        ),
        name="event_stats",
    )(order, *og_blocks, w_out_own, gate, heads)


def combined_stats(stats_refs, cols):
    shards = len(stats_refs)
    positions = stats_refs[0].shape[1]
    means = [ref[0:1, :] for ref in stats_refs]
    mean = sum(means) * (1.0 / shards)
    square = jnp.zeros_like(mean)
    total = jnp.zeros_like(mean)
    cross = jnp.zeros_like(mean)
    for s, ref in enumerate(stats_refs):
        shift = means[s] - mean
        part = ref[2:3, :]
        square = square + ref[1:2, :] + cols * shift * shift
        total = total + part
        cross = cross + ref[3:4, :] + shift * part
    inv_dev = lax.rsqrt(square * (1.0 / D) + NORM_EPS)
    kind = lax.broadcasted_iota(jnp.int32, (128, positions), 0)
    rest = jnp.where(kind == 2, total * (1.0 / D), cross * inv_dev * (1.0 / D))
    packed = jnp.where(kind == 0, mean, jnp.where(kind == 1, inv_dev, rest))
    per_event = jnp.transpose(packed)
    return [per_event[:, k : k + 1] for k in range(4)]


def backward_kernel(*refs, blk, users, maxlen, shards):
    lengths_ref = refs[0]
    stats_refs = refs[1 : 1 + shards]
    mg_ref, gate_ref, heads_ref, acts_ref, slopes_ref, weights_ref, score_slope_ref = refs[1 + shards : 8 + shards]
    grad_ref, mixed_ref, o_ref, o_t, q_t, v_t, k_split, vg_t, kg_t, qg = refs[8 + shards :]
    i = pl.program_id(0)
    positions, cols = o_ref.shape
    heads = cols // DH
    blocks = positions // blk
    scale = DH ** (-0.5)

    @pl.when(i == 0)
    def _():
        mean, inv_dev, total, cross = combined_stats(stats_refs, cols)
        for p in range(heads // 2):
            lanes = slice(p * PAIR, (p + 1) * PAIR)
            normed = (heads_ref[:, lanes].astype(F32) - mean) * inv_dev
            gate = gate_ref[:, lanes]
            mg = mg_ref[:, lanes]
            mixed_ref[:, lanes] = (normed * gate).astype(BF)
            gate_lanes = slice(3 * cols + p * PAIR, 3 * cols + (p + 1) * PAIR)
            gate_slope = slopes_ref[:, gate_lanes].astype(F32)
            grad_ref[:, gate_lanes] = (mg * normed * gate_slope).astype(BF)
            o_ref[:, lanes] = (inv_dev * (mg * gate - total - normed * cross)).astype(BF)
        o_t[...] = jnp.transpose(o_ref[...])
        for scratch, kind in ((v_t, 0), (q_t, 1)):
            scratch[...] = jnp.transpose(jnp.concatenate([acts_ref[:, head_columns(kind, h)] for h in range(heads)], axis=1))
        for block in range(blocks):
            split_pairs(acts_ref, k_split, 2, block, blk)
        vg_t[...] = jnp.zeros_like(vg_t)
        kg_t[...] = jnp.zeros_like(kg_t)

    at_i = pl.ds(pl.multiple_of(i * blk, blk), blk)
    o_i = [o_ref[at_i, h * DH : (h + 1) * DH] for h in range(heads)]

    def column(j, acc):
        at_j = pl.ds(pl.multiple_of(j * blk, blk), blk)
        both_j = pl.ds(pl.multiple_of(j * 2 * blk, 2 * blk), 2 * blk)
        per_head = []
        for h in range(heads):
            lanes = slice(h * DH, (h + 1) * DH)
            weight_grad = dot_nn(o_i[h], v_t[lanes, at_j])
            score_grad = (weight_grad * score_slope_ref[h, :, at_j].astype(F32)).astype(BF)
            vg_t[lanes, at_j] += dot_nn(o_t[lanes, at_i], weights_ref[h, :, at_j])
            kg_t[lanes, at_j] += dot_nn(q_t[lanes, at_i], score_grad)
            per_head.append(score_grad)
        return tuple(
            acc[p] + dot_nn(jnp.concatenate(per_head[2 * p : 2 * p + 2], axis=1), k_split[p, both_j, :])
            for p in range(heads // 2)
        )

    first = history_start(lengths_ref, users, i * blk) // blk
    zero = jnp.zeros((blk, PAIR), F32)
    acc = lax.fori_loop(first, i + 1, column, (zero,) * (heads // 2))
    qg[at_i, :] = jnp.concatenate(acc, axis=1)

    @pl.when(i == blocks - 1)
    def _():
        factor = 0.5 * scale / maxlen
        grads = [jnp.transpose(vg_t[...]) * (1.0 / maxlen), qg[...] * factor, jnp.transpose(kg_t[...]) * factor]
        pieces = [grads[kind][:, h * DH : (h + 1) * DH] for h in range(heads) for kind in range(3)]
        for n in range(3 * heads // 2):
            lanes = slice(n * PAIR, (n + 1) * PAIR)
            grad = jnp.concatenate(pieces[2 * n : 2 * n + 2], axis=1).astype(BF).astype(F32)
            grad_ref[:, lanes] = (grad * slopes_ref[:, lanes].astype(F32)).astype(BF)


def backward_attention(lengths, stats, mg, gate, head_outs, acts, slopes, weights, score_slope, blk, maxlen):
    positions, cols = mg.shape
    heads = cols // DH
    shards = len(stats)
    users = lengths.shape[1]
    elements = heads * positions * positions // 2
    whole = lambda i: (0, 0)
    return pl.pallas_call(
        functools.partial(backward_kernel, blk=blk, users=users, maxlen=maxlen, shards=shards),
        grid=(positions // blk,),
        in_specs=[pl.BlockSpec(memory_space=pltpu.SMEM)]
        + [pl.BlockSpec((8, positions), whole)] * shards
        + [
            pl.BlockSpec((positions, cols), whole),
            pl.BlockSpec((positions, cols), whole),
            pl.BlockSpec((positions, cols), whole),
            pl.BlockSpec((positions, 4 * cols), whole),
            pl.BlockSpec((positions, 4 * cols), whole),
            pl.BlockSpec((heads, blk, positions), lambda i: (0, i, 0)),
            pl.BlockSpec((heads, blk, positions), lambda i: (0, i, 0)),
        ],
        out_specs=[pl.BlockSpec((positions, 4 * cols), whole), pl.BlockSpec((positions, cols), whole)],
        out_shape=[
            jax.ShapeDtypeStruct((positions, 4 * cols), BF),
            jax.ShapeDtypeStruct((positions, cols), BF),
        ],
        scratch_shapes=[
            pltpu.VMEM((positions, cols), BF),
            pltpu.VMEM((cols, positions), BF),
            pltpu.VMEM((cols, positions), BF),
            pltpu.VMEM((cols, positions), BF),
            pltpu.VMEM((cols // PAIR, 2 * positions, PAIR), BF),
            pltpu.VMEM((cols, positions), F32),
            pltpu.VMEM((cols, positions), F32),
            pltpu.VMEM((positions, cols), F32),
        ],
        compiler_params=pltpu.CompilerParams(vmem_limit_bytes=VMEM_LIMIT),
        cost_estimate=pl.CostEstimate(
            flops=8 * elements * 256, bytes_accessed=4 * elements + 26 * positions * cols, transcendentals=0
        ),
        name="attention_backward",
    )(lengths, *stats, mg, gate, head_outs, acts, slopes, weights, score_slope)


def update_kernel(rows_ref, table_ref, accum_ref, new_table_ref, new_accum_ref, ids):
    i = pl.program_id(0)
    blk = table_ref.shape[0]
    slots = rows_ref.shape[0]

    @pl.when(i == 0)
    def _():
        numbers = jnp.transpose(rows_ref[:, D:].astype(F32))
        ids[...] = (numbers[0:1, :] * 256.0 + numbers[1:2, :]).astype(jnp.int32)

    row = i * blk + lax.broadcasted_iota(jnp.int32, (blk, slots), 0)
    hits = jnp.where(row == ids[...], 1.0, 0.0).astype(BF)
    grad = dot_nn(hits, rows_ref[:, :D])
    accum = jnp.transpose(jnp.broadcast_to(accum_ref[...], (128, blk)))[:, :1] + jnp.mean(grad * grad, axis=1, keepdims=True)
    new_accum_ref[...] = jnp.transpose(jnp.broadcast_to(accum, (blk, 128)))[:1, :]
    new_table_ref[...] = table_ref[...] - LEARN_RATE * grad * lax.rsqrt(accum)


def update_rows(got_rows, emb_table, row_accum):
    rows_own = emb_table.shape[0]
    slots = got_rows.shape[0]
    blk = min(256, rows_own)
    new_table, new_accum = pl.pallas_call(
        update_kernel,
        grid=(rows_own // blk,),
        in_specs=[
            pl.BlockSpec((slots, D + 128), lambda i: (0, 0)),
            pl.BlockSpec((blk, D), lambda i: (i, 0)),
            pl.BlockSpec((1, blk), lambda i: (0, i)),
        ],
        out_specs=[
            pl.BlockSpec((blk, D), lambda i: (i, 0)),
            pl.BlockSpec((1, blk), lambda i: (0, i)),
        ],
        out_shape=[
            jax.ShapeDtypeStruct((rows_own, D), F32),
            jax.ShapeDtypeStruct((1, rows_own), F32),
        ],
        scratch_shapes=[pltpu.VMEM((1, slots), jnp.int32)],
        compiler_params=pltpu.CompilerParams(vmem_limit_bytes=VMEM_LIMIT),
        cost_estimate=pl.CostEstimate(
            flops=2 * rows_own * slots * D, bytes_accessed=8 * rows_own * D + 2 * slots * D, transcendentals=rows_own
        ),
        name="update_rows",
    )(got_rows, emb_table, row_accum.reshape(1, rows_own))
    return new_table, new_accum.reshape(rows_own)


def own_weights(w_attn, w_gate, part, cols):
    attn = lax.dynamic_slice_in_dim(w_attn, part * 3 * cols, 3 * cols, 1)
    gate = lax.dynamic_slice_in_dim(w_gate, part * cols, cols, 1)
    return jnp.concatenate([attn, gate], axis=1)


def row_slots(owners, rows, devices, capacity):
    events = owners.shape[0]
    owner_hits = (owners[:, None] == jnp.arange(devices, dtype=jnp.int32)[None, :]).astype(BF)
    place = jnp.arange(events, dtype=jnp.int32)
    before = (place[:, None] > place[None, :]).astype(BF)
    earlier = jnp.dot(before, owner_hits, preferred_element_type=F32)
    slots = jnp.sum(earlier * owner_hits.astype(F32), axis=1).astype(jnp.int32)
    flat_slot = owners * capacity + slots
    slot_hits = jnp.arange(devices * capacity, dtype=jnp.int32)[:, None] == flat_slot[None, :]
    lane = jnp.arange(128, dtype=jnp.int32)[None, :]
    numbers = jnp.where(lane == 0, rows[:, None] // 256, jnp.where(lane == 1, rows[:, None] % 256, 0))
    return slot_hits.astype(BF), numbers.astype(BF)


def to_owners(rows, devices, capacity):
    shape = (devices, capacity) + rows.shape[1:]
    got = lax.all_to_all(rows.reshape(shape), ("seq", "dp"), split_axis=0, concat_axis=0, tiled=True)
    return got.reshape(rows.shape)


TN = (((0,), (0,)), ((), ()))


def dot_tn(a, b):
    return lax.dot_general(a, b, TN, preferred_element_type=F32)


def body_whole(
    layer_input, out_grad, lengths, item_owner, item_row, w_attn, w_gate, w_out, emb_table, row_accum
):
    seq_count = lax.axis_size("seq")
    dp_count = lax.axis_size("dp")
    devices = seq_count * dp_count
    seq_id = lax.axis_index("seq")
    tokens_dev = layer_input.shape[0]
    positions = tokens_dev * seq_count
    maxlen = 2 * positions // 3
    blk = min(256, positions)
    cols = D // seq_count
    capacity = max(2, 2 * tokens_dev // devices)

    w_own = own_weights(w_attn, w_gate, seq_id, cols)
    w_out_own = lax.dynamic_slice_in_dim(w_out, seq_id * cols, cols, 0)
    slot_matrix, numbers = row_slots(item_owner[:, 0], item_row, devices, capacity)

    x_full = lax.all_gather(layer_input, "seq", axis=0, tiled=True)
    og_full = lax.all_gather(out_grad, "seq", axis=0, tiled=True)
    order = jnp.arange(positions // blk, dtype=jnp.int32)
    acts, slopes, gate, weights, score_slope, heads = forward_attention(
        lengths, order, [x_full], w_own, blk, maxlen
    )
    mg, stats_own = event_stats(order, [og_full], w_out_own, gate, heads, blk)
    stats = lax.all_gather(stats_own, "seq", axis=0, tiled=False)
    grads, mixed = backward_attention(
        lengths, [stats[s] for s in range(seq_count)], mg, gate, heads, acts, slopes, weights, score_slope, blk, maxlen
    )

    input_part = dot_nt(grads, w_own).astype(BF)
    got = lax.all_to_all(
        input_part.reshape(seq_count, tokens_dev, D), "seq", split_axis=0, concat_axis=0, tiled=True
    )
    input_grad = jnp.sum(got.astype(F32), axis=0) + out_grad.astype(F32)
    rows = jnp.concatenate([input_grad.astype(BF), numbers], axis=1)
    rows = jnp.dot(slot_matrix, rows, preferred_element_type=F32).astype(BF)
    got_rows = to_owners(rows, devices, capacity)
    new_table, new_accum = update_rows(got_rows, emb_table, row_accum)

    out_part = dot_tn(mixed, og_full).astype(BF)
    share = dp_count // seq_count
    out_part = out_part.reshape(share, D // dp_count, seq_count, cols).transpose(0, 2, 1, 3).reshape(D, cols)
    merged = jnp.concatenate([dot_tn(x_full, grads).astype(BF), out_part], axis=1)
    merged = lax.psum_scatter(merged, "dp", scatter_dimension=0, tiled=True)
    steps = []
    for s in range(seq_count):
        for piece in range(dp_count):
            part, target = divmod(piece, seq_count)
            steps.append((s * dp_count + piece, target * dp_count + s * share + part))
    grad_out = lax.ppermute(merged[:, 4 * cols :], ("seq", "dp"), steps).astype(F32)
    grad_attn = merged[:, : 3 * cols].astype(F32)
    grad_gate = merged[:, 3 * cols : 4 * cols].astype(F32)
    return (grad_attn, grad_gate, grad_out, new_table, new_accum)


SEQ = 4
PLANE = 4


def send(array, target):
    steps = []
    for s in range(SEQ):
        for e in range(PLANE):
            for c in range(2):
                to = target(s, e, c)
                if to is not None:
                    steps.append((s * 2 * PLANE + 2 * e + c, to[0] * 2 * PLANE + 2 * to[1] + to[2]))
    return lax.ppermute(array, ("seq", "dp"), steps)


def home(s, c):
    return c == s // 2


def swap_far(array):
    return send(array, lambda s, e, c: None if home(s, c) else (3 - s, e, 1 - c))


def fetch_near(array):
    return send(array, lambda s, e, c: (s ^ 1, e, c) if home(s, c) else ((3 - s) ^ 1, e, 1 - c))


def swap_near(array):
    return send(array, lambda s, e, c: (s ^ 1, e, c))


def swap_core(array):
    return send(array, lambda s, e, c: (s, e, 1 - c))


def swap_x(array):
    return send(array, lambda s, e, c: (s, e ^ 1, c))


def swap_y(array):
    return send(array, lambda s, e, c: (s, e ^ 2, c))


def tie(*arrays):
    return lax.optimization_barrier(arrays)


def merge_kernel(yx_ref, a_kept, a_got, b_kept, b_got, a_next, a_sent, b_next, b_sent):
    for bit, kept, got, following, sent in (
        (yx_ref[0], a_kept, a_got, a_next, a_sent),
        (yx_ref[1], b_kept, b_got, b_next, b_sent),
    ):
        following[...] = (kept[bit].astype(F32) + got[bit].astype(F32)).astype(BF)
        sent[...] = (kept[1 - bit].astype(F32) + got[1 - bit].astype(F32)).astype(BF)


def merge_halves(yx, a_kept, a_got, b_kept, b_got):
    out = jax.ShapeDtypeStruct(a_kept.shape[1:], BF)
    return pl.pallas_call(
        merge_kernel,
        in_specs=[pl.BlockSpec(memory_space=pltpu.SMEM)] + [pl.BlockSpec(memory_space=pltpu.VMEM)] * 4,
        out_specs=[pl.BlockSpec(memory_space=pltpu.VMEM)] * 4,
        out_shape=[out] * 4,
        compiler_params=pltpu.CompilerParams(vmem_limit_bytes=VMEM_LIMIT),
        cost_estimate=pl.CostEstimate(flops=0, bytes_accessed=12_000_000, transcendentals=0),
        name="merge_halves",
    )(yx, a_kept, a_got, b_kept, b_got)


def sums_kernel(proj_one, proj_two, out_one, out_two, attn_ref, gate_ref, out_ref):
    cut = attn_ref.shape[1]
    attn_ref[...] = proj_one[:, :cut].astype(F32) + proj_two[:, :cut].astype(F32)
    gate_ref[...] = proj_one[:, cut:].astype(F32) + proj_two[:, cut:].astype(F32)
    out_ref[...] = out_one[...].astype(F32) + out_two[...].astype(F32)


def last_sums(proj, out):
    rows, cols = out[0].shape
    widths = (proj[0].shape[1] - cols, cols, cols)
    return pl.pallas_call(
        sums_kernel,
        in_specs=[pl.BlockSpec(memory_space=pltpu.VMEM)] * 4,
        out_specs=[pl.BlockSpec(memory_space=pltpu.VMEM)] * 3,
        out_shape=[jax.ShapeDtypeStruct((rows, width), F32) for width in widths],
        compiler_params=pltpu.CompilerParams(vmem_limit_bytes=VMEM_LIMIT),
        cost_estimate=pl.CostEstimate(flops=0, bytes_accessed=12 * rows * cols * 5, transcendentals=0),
        name="last_sums",
    )(*proj, *out)


def halves(array, bit, axis):
    kept = lax.dynamic_index_in_dim(array, bit, axis, keepdims=False)
    sent = lax.dynamic_index_in_dim(array, 1 - bit, axis, keepdims=False)
    return kept, sent


def body_pairs(
    layer_input, out_grad, lengths, item_owner, item_row, w_attn, w_gate, w_out, emb_table, row_accum
):
    devices = 2 * PLANE * SEQ
    s = lax.axis_index("seq")
    d = lax.axis_index("dp")
    e, c = d // 2, d % 2
    y, x = e // 2, e % 2
    tokens_dev = layer_input.shape[0]
    positions = tokens_dev * SEQ
    maxlen = 2 * positions // 3
    blk = min(256, positions)
    cols = D // SEQ
    rows_own = emb_table.shape[0]
    capacity = max(2, 2 * tokens_dev // devices)
    at_home = c == s // 2
    part = 2 * (s % 2) + c

    def block_of(seq, core):
        return jnp.where(core == seq // 2, seq, 3 - seq)

    mine_at, near_at = block_of(s, c), block_of(s ^ 1, c)
    core_at, diag_at = block_of(s, 1 - c), block_of(s ^ 1, 1 - c)
    order = jnp.stack([mine_at, near_at, core_at, diag_at]).astype(jnp.int32)

    x_far = swap_far(layer_input)
    x_near = fetch_near(layer_input)
    users = lengths.shape[1]
    keys = (item_owner[:, 0] * rows_own + item_row).reshape(1, tokens_dev)
    small = jnp.concatenate([keys, jnp.pad(lengths, ((0, 0), (0, 128 - users)))], axis=1)
    small = jnp.where(at_home, small, swap_far(small))
    keys, lengths = small[0, :tokens_dev], small[:, tokens_dev : tokens_dev + users]
    w_own = own_weights(w_attn, w_gate, part, cols)
    w_out_own = lax.dynamic_slice_in_dim(w_out, part * cols, cols, 0)
    slot_matrix, numbers = row_slots(keys // rows_own, keys % rows_own, devices, capacity)
    x_far, x_near, w_own, w_out_own, slot_matrix, numbers, lengths = tie(
        x_far, x_near, w_own, w_out_own, slot_matrix, numbers, lengths
    )
    x_here = jnp.concatenate([jnp.where(at_home, layer_input, x_far), x_near], axis=0)
    x_there = swap_core(x_here)
    x_here, og_own = tie(x_here, out_grad)
    og_near = fetch_near(og_own)
    og_far = swap_far(og_own)

    x_full, acts, slopes, gate, weights, score_slope, heads = forward_attention(
        lengths, order, [x_here, x_there], w_own, blk, maxlen
    )
    og_far, og_near, heads = tie(og_far, og_near, heads)
    og_mine = jnp.where(at_home, og_own, og_far)
    og_here = jnp.concatenate([og_mine, og_near], axis=0)
    og_there = swap_core(og_here)
    og_full, mg, stats_own = event_stats(order, [og_here, og_there], w_out_own, gate, heads, blk)
    stats = [
        stats_own,
        swap_core(stats_own),
        swap_near(stats_own),
        send(stats_own, lambda s, e, c: (s ^ 1, e, 1 - c)),
    ]
    grads, mixed = backward_attention(
        lengths, stats, mg, gate, heads, acts, slopes, weights, score_slope, blk, maxlen
    )

    def input_part(grads, block):
        return dot_nt(lax.dynamic_slice_in_dim(grads, block * tokens_dev, tokens_dev, 0), w_own)

    from_diag = swap_core(input_part(grads, diag_at).astype(BF))
    near_sum = (input_part(grads, near_at) + from_diag.astype(F32)).astype(BF)
    near_sum, grads = tie(near_sum, grads)
    from_near = swap_near(near_sum)
    core_part = input_part(grads, core_at).astype(BF)
    from_core = swap_core(core_part)
    input_grad = input_part(grads, mine_at) + og_mine.astype(F32)

    core_part, grads, mixed = tie(core_part, grads, mixed)
    half = 5 * cols // 2
    proj = dot_tn(x_full, grads).astype(BF).reshape(2, 2, D // PLANE, 4 * cols)
    out_part = dot_tn(mixed, og_full).astype(BF).reshape(cols, 2, 2, cols)
    a_kept, a_sent = halves(proj[..., :half], x, 1)
    b_kept, b_sent = halves(proj[..., half:], y, 0)
    out_kept, out_sent = (piece.transpose(1, 0, 2) for piece in halves(out_part, y, 1))
    b_kept = jnp.concatenate([b_kept, out_kept], axis=-1)
    b_sent = jnp.concatenate([b_sent, out_sent], axis=-1)
    a_got = swap_x(a_sent)
    b_got = swap_y(b_sent)

    input_grad = input_grad + from_core.astype(F32) + from_near.astype(F32)
    rows = jnp.concatenate([input_grad.astype(BF), numbers], axis=1)
    rows = jnp.dot(slot_matrix, rows, preferred_element_type=F32).astype(BF)
    got_rows = to_owners(rows, devices, capacity)

    yx = jnp.stack([y, x]).astype(jnp.int32)
    a_kept, a_sent, b_kept, b_sent = merge_halves(yx, a_kept, a_got, b_kept, b_got)
    a = (a_kept.astype(F32) + swap_y(a_sent).astype(F32)).astype(BF)
    b = (b_kept.astype(F32) + swap_x(b_sent).astype(F32)).astype(BF)

    def last(array, target):
        pieces = array.reshape(2, D // (2 * PLANE), array.shape[1])
        one, other = halves(pieces, s // 2, 0)
        one = send(one, lambda s, e, c: target(s, e, c, s // 2))
        return one, send(other, lambda s, e, c: target(s, e, c, 1 - s // 2))

    proj = jnp.concatenate([a, b[:, : 4 * cols - half]], axis=1)
    proj = last(proj, lambda s, e, c, piece: (2 * (s % 2) + c, e, piece))
    out = last(b[:, 4 * cols - half :], lambda s, e, c, piece: (e, 2 * (s % 2) + c, piece))
    new_table, new_accum = update_rows(got_rows, emb_table, row_accum)
    *proj, new_accum = tie(*proj, new_accum)
    attn, gate, grad_out = last_sums(proj, out)
    return (attn, gate, grad_out, new_table, new_accum)


def solution(mesh):
    placed = (
        P(("dp", "seq"), None),
        P(("dp", "seq"), None),
        P("dp", None),
        P(("dp", "seq"), None),
        P(("dp", "seq")),
        P(),
        P(),
        P(),
        P(("seq", "dp"), None),
        P(("seq", "dp")),
    )
    paired = mesh.shape["seq"] == SEQ and mesh.shape["dp"] == 2 * PLANE
    return jax.shard_map(
        body_pairs if paired else body_whole,
        mesh=mesh,
        in_specs=placed,
        out_specs=(
            P("dp", "seq"),
            P("dp", "seq"),
            P("dp", "seq"),
            P(("seq", "dp"), None),
            P(("seq", "dp")),
        ),
        check_vma=False,
    )
```

```python
import functools

import jax
import jax.numpy as jnp
from jax import lax
from jax.experimental import pallas as pl
from jax.experimental.pallas import tpu as pltpu
from jax.sharding import PartitionSpec as P

D = 1024
H = 16
DH = 64
PAIR = 2 * DH

NORM_EPS = 1e-05
LEARN_RATE = 0.1
VMEM_LIMIT = 56 * 1024 * 1024
BF = jnp.bfloat16
F32 = jnp.float32


def dot_nn(a, b):
    return lax.dot_general(a, b, (((1,), (0,)), ((), ())), preferred_element_type=F32)


def dot_nt(a, b):
    return lax.dot_general(a, b, (((1,), (1,)), ((), ())), preferred_element_type=F32)


def history_start(lengths_ref, users, place):
    start = jnp.zeros_like(place)
    end = jnp.int32(0)
    for user in range(users - 1):
        end = end + lengths_ref[0, user]
        start = jnp.where(place >= end, end, start)
    return start


def head_columns(kind, head):
    first = head // 2 * 4 * PAIR + head % 2 * 3 * DH + kind * DH
    return slice(first, first + DH)


def gate_columns(pair):
    return slice(pair * 4 * PAIR + 3 * PAIR, (pair + 1) * 4 * PAIR)


def split_pairs(acts_ref, split_ref, kind, block, blk):
    at = pl.ds(pl.multiple_of(block * blk, blk), blk)
    zero = jnp.zeros((blk, DH), BF)
    for p in range(split_ref.shape[0]):
        one, two = (acts_ref[at, head_columns(kind, 2 * p + h)] for h in range(2))
        below = pl.multiple_of(block * 2 * blk + blk, blk)
        split_ref[p, pl.ds(pl.multiple_of(block * 2 * blk, blk), blk), :] = jnp.concatenate([one, zero], axis=1)
        split_ref[p, pl.ds(below, blk), :] = jnp.concatenate([zero, two], axis=1)


def forward_kernel(*refs, blk, users, maxlen, count):
    lengths_ref, order_ref = refs[:2]
    x_refs = refs[2 : 2 + count]
    w_ref = refs[2 + count]
    outs = refs[3 + count :]
    if count > 1:
        x_out_ref, outs = outs[0], outs[1:]
    acts_ref, slopes_ref, gate_ref, weights_ref, score_slope_ref, heads_ref, k_t, v_split = outs
    i = pl.program_id(0)
    heads = weights_ref.shape[0]
    chunks = x_refs[0].shape[0] // blk

    @pl.when(i == 0)
    def _():
        for b in range(count):
            for r in range(chunks):
                at = pl.ds(pl.multiple_of(order_ref[b * chunks + r] * blk, blk), blk)
                x = x_refs[b][r * blk : (r + 1) * blk, :]
                if count > 1:
                    x_out_ref[at, :] = x
                for p in range(heads // 2):
                    lanes = slice(p * 4 * PAIR, (p + 1) * 4 * PAIR)
                    half = 0.5 * dot_nn(x, w_ref[:, lanes])
                    t = jnp.tanh(half)
                    prod = half * t
                    silu = half + prod
                    acts_ref[at, lanes] = silu.astype(BF)
                    gate_ref[at, p * PAIR : (p + 1) * PAIR] = silu[:, 3 * PAIR :]
                    slopes_ref[at, lanes] = (0.5 * (1.0 + t) * (1.0 + half - prod)).astype(BF)
                for h in range(heads):
                    k_t[h * DH : (h + 1) * DH, at] = jnp.transpose(acts_ref[at, head_columns(2, h)])
                split_pairs(acts_ref, v_split, 0, order_ref[b * chunks + r], blk)

    at_i = pl.ds(pl.multiple_of(i * blk, blk), blk)
    q_half = [acts_ref[at_i, head_columns(1, h)] * jnp.asarray(0.5 * DH**-0.5, BF) for h in range(heads)]
    row = i * blk + lax.broadcasted_iota(jnp.int32, (blk, blk), 0)
    col0 = lax.broadcasted_iota(jnp.int32, (blk, blk), 1)
    start = history_start(lengths_ref, users, row)

    def column(j, acc):
        at_j = pl.ds(pl.multiple_of(j * blk, blk), blk)
        both_j = pl.ds(pl.multiple_of(j * 2 * blk, 2 * blk), 2 * blk)
        col = col0 + j * blk
        allowed = (col <= row) & (col >= start)
        per_head = []
        for h in range(heads):
            half = dot_nn(q_half[h], k_t[h * DH : (h + 1) * DH, at_j])
            half = jnp.where(allowed, half, -64.0)
            t = jnp.tanh(half)
            p = half * t
            weights = (half + p).astype(BF)
            weights_ref[h, :, at_j] = weights
            score_slope_ref[h, :, at_j] = ((1.0 + t) * (1.0 + half - p)).astype(BF)
            per_head.append(weights)
        return tuple(
            acc[p] + dot_nn(jnp.concatenate(per_head[2 * p : 2 * p + 2], axis=1), v_split[p, both_j, :])
            for p in range(heads // 2)
        )

    first = history_start(lengths_ref, users, i * blk) // blk
    zero = jnp.zeros((blk, PAIR), F32)
    acc = lax.fori_loop(first, i + 1, column, (zero,) * (heads // 2))
    heads_ref[...] = (jnp.concatenate(acc, axis=1) * (1.0 / maxlen)).astype(BF)


def forward_attention(lengths, order, x_blocks, w_own, blk, maxlen):
    count = len(x_blocks)
    block_rows = x_blocks[0].shape[0]
    positions = count * block_rows
    cols = w_own.shape[1] // 4
    heads = cols // DH
    users = lengths.shape[1]
    elements = heads * positions * positions // 2
    whole = lambda i: (0, 0)
    out_specs = [
        pl.BlockSpec((positions, 4 * cols), whole),
        pl.BlockSpec((positions, 4 * cols), whole),
        pl.BlockSpec((positions, cols), whole),
        pl.BlockSpec((heads, blk, positions), lambda i: (0, i, 0)),
        pl.BlockSpec((heads, blk, positions), lambda i: (0, i, 0)),
        pl.BlockSpec((blk, cols), lambda i: (i, 0)),
    ]
    out_shape = [
        jax.ShapeDtypeStruct((positions, 4 * cols), BF),
        jax.ShapeDtypeStruct((positions, 4 * cols), BF),
        jax.ShapeDtypeStruct((positions, cols), F32),
        jax.ShapeDtypeStruct((heads, positions, positions), BF),
        jax.ShapeDtypeStruct((heads, positions, positions), BF),
        jax.ShapeDtypeStruct((positions, cols), BF),
    ]
    if count > 1:
        out_specs = [pl.BlockSpec((positions, D), whole)] + out_specs
        out_shape = [jax.ShapeDtypeStruct((positions, D), BF)] + out_shape
    return pl.pallas_call(
        functools.partial(forward_kernel, blk=blk, users=users, maxlen=maxlen, count=count),
        grid=(positions // blk,),
        in_specs=[pl.BlockSpec(memory_space=pltpu.SMEM), pl.BlockSpec(memory_space=pltpu.SMEM)]
        + [pl.BlockSpec((block_rows, D), whole)] * count
        + [pl.BlockSpec((D, 4 * cols), whole)],
        out_specs=out_specs,
        out_shape=out_shape,
        scratch_shapes=[pltpu.VMEM((cols, positions), BF), pltpu.VMEM((cols // PAIR, 2 * positions, PAIR), BF)],
        compiler_params=pltpu.CompilerParams(vmem_limit_bytes=VMEM_LIMIT),
        cost_estimate=pl.CostEstimate(
            flops=8 * positions * D * cols + 4 * elements * 256,
            bytes_accessed=4 * positions * D + 4 * elements,
            transcendentals=elements,
        ),
        name="attention_forward",
    )(lengths, order, *x_blocks, w_own)


def stats_kernel(*refs, blk, count):
    order_ref = refs[0]
    og_refs = refs[1 : 1 + count]
    w_ref, gate_ref, heads_ref = refs[1 + count : 4 + count]
    outs = refs[4 + count :]
    if count > 1:
        og_out_ref, outs = outs[0], outs[1:]
    mg_ref, stats_ref = outs
    chunks = og_refs[0].shape[0] // blk
    for b in range(count):
        for r in range(chunks):
            at = pl.ds(pl.multiple_of(order_ref[b * chunks + r] * blk, blk), blk)
            og = og_refs[b][r * blk : (r + 1) * blk, :]
            if count > 1:
                og_out_ref[at, :] = og
            mg = dot_nt(og, w_ref[...])
            mg_ref[at, :] = mg
            ng = mg * gate_ref[at, :]
            heads = heads_ref[at, :].astype(F32)
            mean = jnp.mean(heads, axis=1, keepdims=True)
            centred = heads - mean
            square = jnp.sum(centred * centred, axis=1, keepdims=True)
            total = jnp.sum(ng, axis=1, keepdims=True)
            cross = jnp.sum(ng * centred, axis=1, keepdims=True)
            lane = lax.broadcasted_iota(jnp.int32, (blk, 128), 1)
            packed = jnp.where(lane == 0, mean, jnp.where(lane == 1, square, jnp.where(lane == 2, total, cross)))
            stats_ref[:, at] = jnp.transpose(packed)[:8, :]


def event_stats(order, og_blocks, w_out_own, gate, heads, blk):
    positions, cols = heads.shape
    count = len(og_blocks)
    vmem = pl.BlockSpec(memory_space=pltpu.VMEM)
    out_shape = [
        jax.ShapeDtypeStruct((positions, cols), F32),
        jax.ShapeDtypeStruct((8, positions), F32),
    ]
    if count > 1:
        out_shape = [jax.ShapeDtypeStruct((positions, D), BF)] + out_shape
    return pl.pallas_call(
        functools.partial(stats_kernel, blk=blk, count=count),
        in_specs=[pl.BlockSpec(memory_space=pltpu.SMEM)] + [vmem] * (count + 3),
        out_specs=[vmem] * len(out_shape),
        out_shape=out_shape,
        compiler_params=pltpu.CompilerParams(vmem_limit_bytes=VMEM_LIMIT),
        cost_estimate=pl.CostEstimate(
            flops=2 * positions * cols * D, bytes_accessed=4 * positions * D + 10 * positions * cols, transcendentals=0
        ),
        name="event_stats",
    )(order, *og_blocks, w_out_own, gate, heads)


def combined_stats(stats_refs, cols):
    shards = len(stats_refs)
    positions = stats_refs[0].shape[1]
    means = [ref[0:1, :] for ref in stats_refs]
    mean = sum(means) * (1.0 / shards)
    square = jnp.zeros_like(mean)
    total = jnp.zeros_like(mean)
    cross = jnp.zeros_like(mean)
    for s, ref in enumerate(stats_refs):
        shift = means[s] - mean
        part = ref[2:3, :]
        square = square + ref[1:2, :] + cols * shift * shift
        total = total + part
        cross = cross + ref[3:4, :] + shift * part
    inv_dev = lax.rsqrt(square * (1.0 / D) + NORM_EPS)
    kind = lax.broadcasted_iota(jnp.int32, (128, positions), 0)
    rest = jnp.where(kind == 2, total * (1.0 / D), cross * inv_dev * (1.0 / D))
    packed = jnp.where(kind == 0, mean, jnp.where(kind == 1, inv_dev, rest))
    per_event = jnp.transpose(packed)
    return [per_event[:, k : k + 1] for k in range(4)]


def backward_kernel(*refs, blk, users, maxlen, shards):
    lengths_ref = refs[0]
    stats_refs = refs[1 : 1 + shards]
    mg_ref, gate_ref, heads_ref, acts_ref, slopes_ref, weights_ref, score_slope_ref = refs[1 + shards : 8 + shards]
    grad_ref, mixed_ref, o_ref, o_t, q_t, v_t, k_split, vg_t, kg_t, qg = refs[8 + shards :]
    i = pl.program_id(0)
    positions, cols = o_ref.shape
    heads = cols // DH
    blocks = positions // blk
    scale = DH ** (-0.5)

    @pl.when(i == 0)
    def _():
        mean, inv_dev, total, cross = combined_stats(stats_refs, cols)
        for p in range(heads // 2):
            lanes = slice(p * PAIR, (p + 1) * PAIR)
            normed = (heads_ref[:, lanes].astype(F32) - mean) * inv_dev
            gate = gate_ref[:, lanes]
            mg = mg_ref[:, lanes]
            mixed_ref[:, lanes] = (normed * gate).astype(BF)
            gate_slope = slopes_ref[:, gate_columns(p)].astype(F32)
            grad_ref[:, gate_columns(p)] = (mg * normed * gate_slope).astype(BF)
            o_ref[:, lanes] = (inv_dev * (mg * gate - total - normed * cross)).astype(BF)
        o_t[...] = jnp.transpose(o_ref[...])
        for scratch, kind in ((v_t, 0), (q_t, 1)):
            scratch[...] = jnp.transpose(jnp.concatenate([acts_ref[:, head_columns(kind, h)] for h in range(heads)], axis=1))
        for block in range(blocks):
            split_pairs(acts_ref, k_split, 2, block, blk)
        vg_t[...] = jnp.zeros_like(vg_t)
        kg_t[...] = jnp.zeros_like(kg_t)

    at_i = pl.ds(pl.multiple_of(i * blk, blk), blk)
    o_i = [o_ref[at_i, h * DH : (h + 1) * DH] for h in range(heads)]

    def column(j, acc):
        at_j = pl.ds(pl.multiple_of(j * blk, blk), blk)
        both_j = pl.ds(pl.multiple_of(j * 2 * blk, 2 * blk), 2 * blk)
        per_head = []
        for h in range(heads):
            lanes = slice(h * DH, (h + 1) * DH)
            weight_grad = dot_nn(o_i[h], v_t[lanes, at_j])
            score_grad = (weight_grad * score_slope_ref[h, :, at_j].astype(F32)).astype(BF)
            vg_t[lanes, at_j] += dot_nn(o_t[lanes, at_i], weights_ref[h, :, at_j])
            kg_t[lanes, at_j] += dot_nn(q_t[lanes, at_i], score_grad)
            per_head.append(score_grad)
        return tuple(
            acc[p] + dot_nn(jnp.concatenate(per_head[2 * p : 2 * p + 2], axis=1), k_split[p, both_j, :])
            for p in range(heads // 2)
        )

    first = history_start(lengths_ref, users, i * blk) // blk
    zero = jnp.zeros((blk, PAIR), F32)
    acc = lax.fori_loop(first, i + 1, column, (zero,) * (heads // 2))
    qg[at_i, :] = jnp.concatenate(acc, axis=1)

    @pl.when(i == blocks - 1)
    def _():
        factor = 0.5 * scale / maxlen
        grads = [jnp.transpose(vg_t[...]) * (1.0 / maxlen), qg[...] * factor, jnp.transpose(kg_t[...]) * factor]
        pieces = [grads[kind][:, h * DH : (h + 1) * DH] for h in range(heads) for kind in range(3)]
        for n in range(3 * heads // 2):
            first_lane = n // 3 * 4 * PAIR + n % 3 * PAIR
            lanes = slice(first_lane, first_lane + PAIR)
            grad = jnp.concatenate(pieces[2 * n : 2 * n + 2], axis=1).astype(BF).astype(F32)
            grad_ref[:, lanes] = (grad * slopes_ref[:, lanes].astype(F32)).astype(BF)


def backward_attention(lengths, stats, mg, gate, head_outs, acts, slopes, weights, score_slope, blk, maxlen):
    positions, cols = mg.shape
    heads = cols // DH
    shards = len(stats)
    users = lengths.shape[1]
    elements = heads * positions * positions // 2
    whole = lambda i: (0, 0)
    return pl.pallas_call(
        functools.partial(backward_kernel, blk=blk, users=users, maxlen=maxlen, shards=shards),
        grid=(positions // blk,),
        in_specs=[pl.BlockSpec(memory_space=pltpu.SMEM)]
        + [pl.BlockSpec((8, positions), whole)] * shards
        + [
            pl.BlockSpec((positions, cols), whole),
            pl.BlockSpec((positions, cols), whole),
            pl.BlockSpec((positions, cols), whole),
            pl.BlockSpec((positions, 4 * cols), whole),
            pl.BlockSpec((positions, 4 * cols), whole),
            pl.BlockSpec((heads, blk, positions), lambda i: (0, i, 0)),
            pl.BlockSpec((heads, blk, positions), lambda i: (0, i, 0)),
        ],
        out_specs=[pl.BlockSpec((positions, 4 * cols), whole), pl.BlockSpec((positions, cols), whole)],
        out_shape=[
            jax.ShapeDtypeStruct((positions, 4 * cols), BF),
            jax.ShapeDtypeStruct((positions, cols), BF),
        ],
        scratch_shapes=[
            pltpu.VMEM((positions, cols), BF),
            pltpu.VMEM((cols, positions), BF),
            pltpu.VMEM((cols, positions), BF),
            pltpu.VMEM((cols, positions), BF),
            pltpu.VMEM((cols // PAIR, 2 * positions, PAIR), BF),
            pltpu.VMEM((cols, positions), F32),
            pltpu.VMEM((cols, positions), F32),
            pltpu.VMEM((positions, cols), F32),
        ],
        compiler_params=pltpu.CompilerParams(vmem_limit_bytes=VMEM_LIMIT),
        cost_estimate=pl.CostEstimate(
            flops=8 * elements * 256, bytes_accessed=4 * elements + 26 * positions * cols, transcendentals=0
        ),
        name="attention_backward",
    )(lengths, *stats, mg, gate, head_outs, acts, slopes, weights, score_slope)


def update_kernel(rows_ref, table_ref, accum_ref, new_table_ref, new_accum_ref, ids):
    i = pl.program_id(0)
    blk = table_ref.shape[0]
    slots = rows_ref.shape[0]

    @pl.when(i == 0)
    def _():
        numbers = jnp.transpose(rows_ref[:, D:].astype(F32))
        ids[...] = (numbers[0:1, :] * 256.0 + numbers[1:2, :]).astype(jnp.int32)

    row = i * blk + lax.broadcasted_iota(jnp.int32, (blk, slots), 0)
    hits = jnp.where(row == ids[...], 1.0, 0.0).astype(BF)
    grad = dot_nn(hits, rows_ref[:, :D])
    accum = jnp.transpose(jnp.broadcast_to(accum_ref[...], (128, blk)))[:, :1] + jnp.mean(grad * grad, axis=1, keepdims=True)
    new_accum_ref[...] = jnp.transpose(jnp.broadcast_to(accum, (blk, 128)))[:1, :]
    new_table_ref[...] = table_ref[...] - LEARN_RATE * grad * lax.rsqrt(accum)


def update_rows(got_rows, emb_table, row_accum):
    rows_own = emb_table.shape[0]
    slots = got_rows.shape[0]
    blk = min(256, rows_own)
    new_table, new_accum = pl.pallas_call(
        update_kernel,
        grid=(rows_own // blk,),
        in_specs=[
            pl.BlockSpec((slots, D + 128), lambda i: (0, 0)),
            pl.BlockSpec((blk, D), lambda i: (i, 0)),
            pl.BlockSpec((1, blk), lambda i: (0, i)),
        ],
        out_specs=[
            pl.BlockSpec((blk, D), lambda i: (i, 0)),
            pl.BlockSpec((1, blk), lambda i: (0, i)),
        ],
        out_shape=[
            jax.ShapeDtypeStruct((rows_own, D), F32),
            jax.ShapeDtypeStruct((1, rows_own), F32),
        ],
        scratch_shapes=[pltpu.VMEM((1, slots), jnp.int32)],
        compiler_params=pltpu.CompilerParams(vmem_limit_bytes=VMEM_LIMIT),
        cost_estimate=pl.CostEstimate(
            flops=2 * rows_own * slots * D, bytes_accessed=8 * rows_own * D + 2 * slots * D, transcendentals=rows_own
        ),
        name="update_rows",
    )(got_rows, emb_table, row_accum.reshape(1, rows_own))
    return new_table, new_accum.reshape(rows_own)


def own_weights(w_attn, w_gate, part, pairs):
    slices = []
    for p in range(pairs):
        at = part * pairs + p
        slices.append(lax.dynamic_slice_in_dim(w_attn, at * 3 * PAIR, 3 * PAIR, 1))
        slices.append(lax.dynamic_slice_in_dim(w_gate, at * PAIR, PAIR, 1))
    return jnp.concatenate(slices, axis=1)


def attn_and_gate(proj, pairs):
    pieces = [proj[:, p * 4 * PAIR : (p + 1) * 4 * PAIR] for p in range(pairs)]
    attn = jnp.concatenate([piece[:, : 3 * PAIR] for piece in pieces], axis=1)
    return attn, jnp.concatenate([piece[:, 3 * PAIR :] for piece in pieces], axis=1)


def row_slots(owners, rows, devices, capacity):
    events = owners.shape[0]
    owner_hits = (owners[:, None] == jnp.arange(devices, dtype=jnp.int32)[None, :]).astype(BF)
    place = jnp.arange(events, dtype=jnp.int32)
    before = (place[:, None] > place[None, :]).astype(BF)
    earlier = jnp.dot(before, owner_hits, preferred_element_type=F32)
    slots = jnp.sum(earlier * owner_hits.astype(F32), axis=1).astype(jnp.int32)
    flat_slot = owners * capacity + slots
    slot_hits = jnp.arange(devices * capacity, dtype=jnp.int32)[:, None] == flat_slot[None, :]
    lane = jnp.arange(128, dtype=jnp.int32)[None, :]
    numbers = jnp.where(lane == 0, rows[:, None] // 256, jnp.where(lane == 1, rows[:, None] % 256, 0))
    return slot_hits.astype(BF), numbers.astype(BF)


def rows_to_owners(slot_matrix, input_grad, numbers, devices, capacity):
    rows = jnp.concatenate([input_grad.astype(BF), numbers], axis=1)
    rows = jnp.dot(slot_matrix, rows, preferred_element_type=F32).astype(BF)
    got = lax.all_to_all(
        rows.reshape(devices, capacity, D + 128), ("seq", "dp"), split_axis=0, concat_axis=0, tiled=True
    )
    return got.reshape(devices * capacity, D + 128)


TN = (((0,), (0,)), ((), ()))


def dot_tn(a, b):
    return lax.dot_general(a, b, TN, preferred_element_type=F32)


def body_whole(
    layer_input, out_grad, lengths, item_owner, item_row, w_attn, w_gate, w_out, emb_table, row_accum
):
    seq_count = lax.axis_size("seq")
    dp_count = lax.axis_size("dp")
    devices = seq_count * dp_count
    seq_id = lax.axis_index("seq")
    tokens_dev = layer_input.shape[0]
    positions = tokens_dev * seq_count
    maxlen = 2 * positions // 3
    blk = min(256, positions)
    cols = D // seq_count
    pairs = cols // PAIR
    capacity = max(2, 2 * tokens_dev // devices)

    w_own = own_weights(w_attn, w_gate, seq_id, pairs)
    w_out_own = lax.dynamic_slice_in_dim(w_out, seq_id * cols, cols, 0)
    slot_matrix, numbers = row_slots(item_owner[:, 0], item_row, devices, capacity)

    x_full = lax.all_gather(layer_input, "seq", axis=0, tiled=True)
    og_full = lax.all_gather(out_grad, "seq", axis=0, tiled=True)
    order = jnp.arange(positions // blk, dtype=jnp.int32)
    acts, slopes, gate, weights, score_slope, heads = forward_attention(
        lengths, order, [x_full], w_own, blk, maxlen
    )
    mg, stats_own = event_stats(order, [og_full], w_out_own, gate, heads, blk)
    stats = lax.all_gather(stats_own, "seq", axis=0, tiled=False)
    grads, mixed = backward_attention(
        lengths, [stats[s] for s in range(seq_count)], mg, gate, heads, acts, slopes, weights, score_slope, blk, maxlen
    )

    input_part = dot_nt(grads, w_own).astype(BF)
    got = lax.all_to_all(
        input_part.reshape(seq_count, tokens_dev, D), "seq", split_axis=0, concat_axis=0, tiled=True
    )
    input_grad = jnp.sum(got.astype(F32), axis=0) + out_grad.astype(F32)
    got_rows = rows_to_owners(slot_matrix, input_grad, numbers, devices, capacity)
    new_table, new_accum = update_rows(got_rows, emb_table, row_accum)

    out_part = dot_tn(mixed, og_full).astype(BF)
    share = dp_count // seq_count
    out_part = out_part.reshape(share, D // dp_count, seq_count, cols).transpose(0, 2, 1, 3).reshape(D, cols)
    merged = jnp.concatenate([dot_tn(x_full, grads).astype(BF), out_part], axis=1)
    merged = lax.psum_scatter(merged, "dp", scatter_dimension=0, tiled=True)
    steps = []
    for s in range(seq_count):
        for piece in range(dp_count):
            part, target = divmod(piece, seq_count)
            steps.append((s * dp_count + piece, target * dp_count + s * share + part))
    grad_out = lax.ppermute(merged[:, 4 * cols :], ("seq", "dp"), steps).astype(F32)
    grad_attn, grad_gate = attn_and_gate(merged[:, : 4 * cols].astype(F32), pairs)
    return (grad_attn, grad_gate, grad_out, new_table, new_accum)


SEQ = 4
PLANE = 4


def send(array, target):
    steps = []
    for s in range(SEQ):
        for e in range(PLANE):
            for c in range(2):
                to = target(s, e, c)
                if to is not None:
                    steps.append((s * 2 * PLANE + 2 * e + c, to[0] * 2 * PLANE + 2 * to[1] + to[2]))
    return lax.ppermute(array, ("seq", "dp"), steps)


def home(s, c):
    return c == s // 2


def swap_far(array):
    return send(array, lambda s, e, c: None if home(s, c) else (3 - s, e, 1 - c))


def fetch_near(array):
    return send(array, lambda s, e, c: (s ^ 1, e, c) if home(s, c) else ((3 - s) ^ 1, e, 1 - c))


def swap_near(array):
    return send(array, lambda s, e, c: (s ^ 1, e, c))


def swap_core(array):
    return send(array, lambda s, e, c: (s, e, 1 - c))


def swap_x(array):
    return send(array, lambda s, e, c: (s, e ^ 1, c))


def swap_y(array):
    return send(array, lambda s, e, c: (s, e ^ 2, c))


def tie(*arrays):
    return lax.optimization_barrier(arrays)


def halves(array, bit, axis):
    kept = lax.dynamic_index_in_dim(array, bit, axis, keepdims=False)
    sent = lax.dynamic_index_in_dim(array, 1 - bit, axis, keepdims=False)
    return kept, sent


def body_pairs(
    layer_input, out_grad, lengths, item_owner, item_row, w_attn, w_gate, w_out, emb_table, row_accum
):
    devices = 2 * PLANE * SEQ
    s = lax.axis_index("seq")
    d = lax.axis_index("dp")
    e, c = d // 2, d % 2
    y, x = e // 2, e % 2
    tokens_dev = layer_input.shape[0]
    positions = tokens_dev * SEQ
    maxlen = 2 * positions // 3
    blk = min(256, positions)
    cols = D // SEQ
    pairs = cols // PAIR
    rows_own = emb_table.shape[0]
    capacity = max(2, 2 * tokens_dev // devices)
    at_home = c == s // 2
    part = 2 * (s % 2) + c

    def block_of(seq, core):
        return jnp.where(core == seq // 2, seq, 3 - seq)

    mine_at, near_at = block_of(s, c), block_of(s ^ 1, c)
    core_at, diag_at = block_of(s, 1 - c), block_of(s ^ 1, 1 - c)
    order = jnp.stack([mine_at, near_at, core_at, diag_at]).astype(jnp.int32)

    x_far = swap_far(layer_input)
    x_near = fetch_near(layer_input)
    users = lengths.shape[1]
    keys = (item_owner[:, 0] * rows_own + item_row).reshape(1, tokens_dev)
    small = jnp.concatenate([keys, jnp.pad(lengths, ((0, 0), (0, 128 - users)))], axis=1)
    small = jnp.where(at_home, small, swap_far(small))
    keys, lengths = small[0, :tokens_dev], small[:, tokens_dev : tokens_dev + users]
    w_own = own_weights(w_attn, w_gate, part, pairs)
    w_out_own = lax.dynamic_slice_in_dim(w_out, part * cols, cols, 0)
    slot_matrix, numbers = row_slots(keys // rows_own, keys % rows_own, devices, capacity)
    x_far, x_near, w_own, w_out_own, slot_matrix, numbers, lengths = tie(
        x_far, x_near, w_own, w_out_own, slot_matrix, numbers, lengths
    )
    x_here = jnp.concatenate([jnp.where(at_home, layer_input, x_far), x_near], axis=0)
    x_there = swap_core(x_here)
    x_here, og_own = tie(x_here, out_grad)
    og_far = swap_far(og_own)
    og_near = fetch_near(og_own)

    x_full, acts, slopes, gate, weights, score_slope, heads = forward_attention(
        lengths, order, [x_here, x_there], w_own, blk, maxlen
    )
    og_far, og_near, heads = tie(og_far, og_near, heads)
    og_mine = jnp.where(at_home, og_own, og_far)
    og_here = jnp.concatenate([og_mine, og_near], axis=0)
    og_there = swap_core(og_here)
    og_full, mg, stats_own = event_stats(order, [og_here, og_there], w_out_own, gate, heads, blk)
    stats = [
        stats_own,
        swap_core(stats_own),
        swap_near(stats_own),
        send(stats_own, lambda s, e, c: (s ^ 1, e, 1 - c)),
    ]
    grads, mixed = backward_attention(
        lengths, stats, mg, gate, heads, acts, slopes, weights, score_slope, blk, maxlen
    )

    def input_part(grads, block):
        return dot_nt(lax.dynamic_slice_in_dim(grads, block * tokens_dev, tokens_dev, 0), w_own)

    from_diag = swap_core(input_part(grads, diag_at).astype(BF))
    near_sum = (input_part(grads, near_at) + from_diag.astype(F32)).astype(BF)
    near_sum, grads = tie(near_sum, grads)
    from_near = swap_near(near_sum)
    core_part = input_part(grads, core_at).astype(BF)
    from_core = swap_core(core_part)
    input_grad = input_part(grads, mine_at) + og_mine.astype(F32)

    core_part, grads, mixed = tie(core_part, grads, mixed)
    half = 5 * cols // 2
    proj = dot_tn(x_full, grads).astype(BF).reshape(2, 2, D // PLANE, 4 * cols)
    out_part = dot_tn(mixed, og_full).astype(BF).reshape(cols, 2, 2, cols)
    a_kept, a_sent = halves(proj[..., :half], x, 1)
    b_kept, b_sent = halves(proj[..., half:], y, 0)
    out_kept, out_sent = (piece.transpose(1, 0, 2) for piece in halves(out_part, y, 1))
    b_kept = jnp.concatenate([b_kept, out_kept], axis=-1)
    b_sent = jnp.concatenate([b_sent, out_sent], axis=-1)
    a_got = swap_x(a_sent)
    b_got = swap_y(b_sent)

    input_grad = input_grad + from_core.astype(F32) + from_near.astype(F32)
    got_rows = rows_to_owners(slot_matrix, input_grad, numbers, devices, capacity)

    a = (a_kept.astype(F32) + a_got.astype(F32)).astype(BF)
    b = (b_kept.astype(F32) + b_got.astype(F32)).astype(BF)
    a_kept, a_sent = halves(a, y, 0)
    b_kept, b_sent = halves(b, x, 0)
    a = (a_kept.astype(F32) + swap_y(a_sent).astype(F32)).astype(BF)
    b = (b_kept.astype(F32) + swap_x(b_sent).astype(F32)).astype(BF)

    def last(array, target):
        pieces = array.reshape(2, D // (2 * PLANE), array.shape[1])
        one, other = halves(pieces, s // 2, 0)
        one = send(one, lambda s, e, c: target(s, e, c, s // 2)).astype(F32)
        return one + send(other, lambda s, e, c: target(s, e, c, 1 - s // 2)).astype(F32)

    proj = jnp.concatenate([a, b[:, : 4 * cols - half]], axis=1)
    proj = last(proj, lambda s, e, c, piece: (2 * (s % 2) + c, e, piece))
    grad_out = last(b[:, 4 * cols - half :], lambda s, e, c, piece: (e, 2 * (s % 2) + c, piece))
    grad_attn, grad_gate = attn_and_gate(proj, pairs)
    new_table, new_accum = update_rows(got_rows, emb_table, row_accum)
    return (grad_attn, grad_gate, grad_out, new_table, new_accum)


def solution(mesh):
    placed = (
        P(("dp", "seq"), None),
        P(("dp", "seq"), None),
        P("dp", None),
        P(("dp", "seq"), None),
        P(("dp", "seq")),
        P(),
        P(),
        P(),
        P(("seq", "dp"), None),
        P(("seq", "dp")),
    )
    paired = mesh.shape["seq"] == SEQ and mesh.shape["dp"] == 2 * PLANE
    return jax.shard_map(
        body_pairs if paired else body_whole,
        mesh=mesh,
        in_specs=placed,
        out_specs=(
            P("dp", "seq"),
            P("dp", "seq"),
            P("dp", "seq"),
            P(("seq", "dp"), None),
            P(("seq", "dp")),
        ),
        check_vma=False,
    )
```

```python
import functools

import jax
import jax.numpy as jnp
from jax import lax
from jax.experimental import pallas as pl
from jax.experimental.pallas import tpu as pltpu
from jax.sharding import PartitionSpec as P

D = 1024
H = 16
DH = 64
PAIR = 2 * DH

NORM_EPS = 1e-05
LEARN_RATE = 0.1
VMEM_LIMIT = 56 * 1024 * 1024
BF = jnp.bfloat16
F32 = jnp.float32


def dot_nn(a, b):
    return lax.dot_general(a, b, (((1,), (0,)), ((), ())), preferred_element_type=F32)


def dot_nt(a, b):
    return lax.dot_general(a, b, (((1,), (1,)), ((), ())), preferred_element_type=F32)


def history_start(lengths_ref, users, place):
    start = jnp.zeros_like(place)
    end = jnp.int32(0)
    for user in range(users - 1):
        end = end + lengths_ref[0, user]
        start = jnp.where(place >= end, end, start)
    return start


def head_columns(kind, head):
    first = head // 2 * 4 * PAIR + head % 2 * 3 * DH + kind * DH
    return slice(first, first + DH)


def gate_columns(pair):
    return slice(pair * 4 * PAIR + 3 * PAIR, (pair + 1) * 4 * PAIR)


def split_pairs(acts_ref, split_ref, kind, block, blk):
    at = pl.ds(pl.multiple_of(block * blk, blk), blk)
    zero = jnp.zeros((blk, DH), BF)
    for p in range(split_ref.shape[0]):
        one, two = (acts_ref[at, head_columns(kind, 2 * p + h)] for h in range(2))
        below = pl.multiple_of(block * 2 * blk + blk, blk)
        split_ref[p, pl.ds(pl.multiple_of(block * 2 * blk, blk), blk), :] = jnp.concatenate([one, zero], axis=1)
        split_ref[p, pl.ds(below, blk), :] = jnp.concatenate([zero, two], axis=1)


def forward_kernel(*refs, blk, users, maxlen, count):
    lengths_ref, order_ref = refs[:2]
    x_refs = refs[2 : 2 + count]
    w_ref = refs[2 + count]
    outs = refs[3 + count :]
    if count > 1:
        x_out_ref, outs = outs[0], outs[1:]
    acts_ref, slopes_ref, gate_ref, weights_ref, score_slope_ref, heads_ref, k_t, v_split = outs
    i = pl.program_id(0)
    heads = weights_ref.shape[0]
    chunks = x_refs[0].shape[0] // blk

    @pl.when(i == 0)
    def _():
        for b in range(count):
            for r in range(chunks):
                at = pl.ds(pl.multiple_of(order_ref[b * chunks + r] * blk, blk), blk)
                x = x_refs[b][r * blk : (r + 1) * blk, :]
                if count > 1:
                    x_out_ref[at, :] = x
                for p in range(heads // 2):
                    lanes = slice(p * 4 * PAIR, (p + 1) * 4 * PAIR)
                    half = 0.5 * dot_nn(x, w_ref[:, lanes])
                    t = jnp.tanh(half)
                    prod = half * t
                    silu = half + prod
                    acts_ref[at, lanes] = silu.astype(BF)
                    gate_ref[at, p * PAIR : (p + 1) * PAIR] = silu[:, 3 * PAIR :]
                    slopes_ref[at, lanes] = (0.5 * (1.0 + t) * (1.0 + half - prod)).astype(BF)
                for h in range(heads):
                    k_t[h * DH : (h + 1) * DH, at] = jnp.transpose(acts_ref[at, head_columns(2, h)])
                split_pairs(acts_ref, v_split, 0, order_ref[b * chunks + r], blk)

    at_i = pl.ds(pl.multiple_of(i * blk, blk), blk)
    q_half = [acts_ref[at_i, head_columns(1, h)] * jnp.asarray(0.5 * DH**-0.5, BF) for h in range(heads)]
    row = i * blk + lax.broadcasted_iota(jnp.int32, (blk, blk), 0)
    col0 = lax.broadcasted_iota(jnp.int32, (blk, blk), 1)
    start = history_start(lengths_ref, users, row)

    def column(j, acc):
        at_j = pl.ds(pl.multiple_of(j * blk, blk), blk)
        both_j = pl.ds(pl.multiple_of(j * 2 * blk, 2 * blk), 2 * blk)
        col = col0 + j * blk
        allowed = (col <= row) & (col >= start)
        per_head = []
        for h in range(heads):
            half = dot_nn(q_half[h], k_t[h * DH : (h + 1) * DH, at_j])
            half = jnp.where(allowed, half, -64.0)
            t = jnp.tanh(half)
            p = half * t
            weights = (half + p).astype(BF)
            weights_ref[h, :, at_j] = weights
            score_slope_ref[h, :, at_j] = ((1.0 + t) * (1.0 + half - p)).astype(BF)
            per_head.append(weights)
        return tuple(
            acc[p] + dot_nn(jnp.concatenate(per_head[2 * p : 2 * p + 2], axis=1), v_split[p, both_j, :])
            for p in range(heads // 2)
        )

    first = history_start(lengths_ref, users, i * blk) // blk
    zero = jnp.zeros((blk, PAIR), F32)
    acc = lax.fori_loop(first, i + 1, column, (zero,) * (heads // 2))
    heads_ref[...] = (jnp.concatenate(acc, axis=1) * (1.0 / maxlen)).astype(BF)


def forward_attention(lengths, order, x_blocks, w_own, blk, maxlen):
    count = len(x_blocks)
    block_rows = x_blocks[0].shape[0]
    positions = count * block_rows
    cols = w_own.shape[1] // 4
    heads = cols // DH
    users = lengths.shape[1]
    elements = heads * positions * positions // 2
    whole = lambda i: (0, 0)
    out_specs = [
        pl.BlockSpec((positions, 4 * cols), whole),
        pl.BlockSpec((positions, 4 * cols), whole),
        pl.BlockSpec((positions, cols), whole),
        pl.BlockSpec((heads, blk, positions), lambda i: (0, i, 0)),
        pl.BlockSpec((heads, blk, positions), lambda i: (0, i, 0)),
        pl.BlockSpec((blk, cols), lambda i: (i, 0)),
    ]
    out_shape = [
        jax.ShapeDtypeStruct((positions, 4 * cols), BF),
        jax.ShapeDtypeStruct((positions, 4 * cols), BF),
        jax.ShapeDtypeStruct((positions, cols), F32),
        jax.ShapeDtypeStruct((heads, positions, positions), BF),
        jax.ShapeDtypeStruct((heads, positions, positions), BF),
        jax.ShapeDtypeStruct((positions, cols), BF),
    ]
    if count > 1:
        out_specs = [pl.BlockSpec((positions, D), whole)] + out_specs
        out_shape = [jax.ShapeDtypeStruct((positions, D), BF)] + out_shape
    return pl.pallas_call(
        functools.partial(forward_kernel, blk=blk, users=users, maxlen=maxlen, count=count),
        grid=(positions // blk,),
        in_specs=[pl.BlockSpec(memory_space=pltpu.SMEM), pl.BlockSpec(memory_space=pltpu.SMEM)]
        + [pl.BlockSpec((block_rows, D), whole)] * count
        + [pl.BlockSpec((D, 4 * cols), whole)],
        out_specs=out_specs,
        out_shape=out_shape,
        scratch_shapes=[pltpu.VMEM((cols, positions), BF), pltpu.VMEM((cols // PAIR, 2 * positions, PAIR), BF)],
        compiler_params=pltpu.CompilerParams(vmem_limit_bytes=VMEM_LIMIT),
        cost_estimate=pl.CostEstimate(
            flops=8 * positions * D * cols + 4 * elements * 256,
            bytes_accessed=4 * positions * D + 4 * elements,
            transcendentals=elements,
        ),
        name="attention_forward",
    )(lengths, order, *x_blocks, w_own)


def stats_kernel(*refs, blk, count):
    order_ref = refs[0]
    og_refs = refs[1 : 1 + count]
    w_ref, gate_ref, heads_ref = refs[1 + count : 4 + count]
    outs = refs[4 + count :]
    if count > 1:
        og_out_ref, outs = outs[0], outs[1:]
    mg_ref, stats_ref = outs
    chunks = og_refs[0].shape[0] // blk
    for b in range(count):
        for r in range(chunks):
            at = pl.ds(pl.multiple_of(order_ref[b * chunks + r] * blk, blk), blk)
            og = og_refs[b][r * blk : (r + 1) * blk, :]
            if count > 1:
                og_out_ref[at, :] = og
            mg = dot_nt(og, w_ref[...])
            mg_ref[at, :] = mg
            ng = mg * gate_ref[at, :]
            heads = heads_ref[at, :].astype(F32)
            mean = jnp.mean(heads, axis=1, keepdims=True)
            centred = heads - mean
            square = jnp.sum(centred * centred, axis=1, keepdims=True)
            total = jnp.sum(ng, axis=1, keepdims=True)
            cross = jnp.sum(ng * centred, axis=1, keepdims=True)
            lane = lax.broadcasted_iota(jnp.int32, (blk, 128), 1)
            packed = jnp.where(lane == 0, mean, jnp.where(lane == 1, square, jnp.where(lane == 2, total, cross)))
            stats_ref[:, at] = jnp.transpose(packed)[:8, :]


def event_stats(order, og_blocks, w_out_own, gate, heads, blk):
    positions, cols = heads.shape
    count = len(og_blocks)
    vmem = pl.BlockSpec(memory_space=pltpu.VMEM)
    out_shape = [
        jax.ShapeDtypeStruct((positions, cols), F32),
        jax.ShapeDtypeStruct((8, positions), F32),
    ]
    if count > 1:
        out_shape = [jax.ShapeDtypeStruct((positions, D), BF)] + out_shape
    return pl.pallas_call(
        functools.partial(stats_kernel, blk=blk, count=count),
        in_specs=[pl.BlockSpec(memory_space=pltpu.SMEM)] + [vmem] * (count + 3),
        out_specs=[vmem] * len(out_shape),
        out_shape=out_shape,
        compiler_params=pltpu.CompilerParams(vmem_limit_bytes=VMEM_LIMIT),
        cost_estimate=pl.CostEstimate(
            flops=2 * positions * cols * D, bytes_accessed=4 * positions * D + 10 * positions * cols, transcendentals=0
        ),
        name="event_stats",
    )(order, *og_blocks, w_out_own, gate, heads)


def combined_stats(stats_refs, cols):
    shards = len(stats_refs)
    positions = stats_refs[0].shape[1]
    means = [ref[0:1, :] for ref in stats_refs]
    mean = sum(means) * (1.0 / shards)
    square = jnp.zeros_like(mean)
    total = jnp.zeros_like(mean)
    cross = jnp.zeros_like(mean)
    for s, ref in enumerate(stats_refs):
        shift = means[s] - mean
        part = ref[2:3, :]
        square = square + ref[1:2, :] + cols * shift * shift
        total = total + part
        cross = cross + ref[3:4, :] + shift * part
    inv_dev = lax.rsqrt(square * (1.0 / D) + NORM_EPS)
    kind = lax.broadcasted_iota(jnp.int32, (128, positions), 0)
    rest = jnp.where(kind == 2, total * (1.0 / D), cross * inv_dev * (1.0 / D))
    packed = jnp.where(kind == 0, mean, jnp.where(kind == 1, inv_dev, rest))
    per_event = jnp.transpose(packed)
    return [per_event[:, k : k + 1] for k in range(4)]


def backward_kernel(*refs, blk, users, maxlen, shards):
    lengths_ref = refs[0]
    stats_refs = refs[1 : 1 + shards]
    mg_ref, gate_ref, heads_ref, acts_ref, slopes_ref, weights_ref, score_slope_ref = refs[1 + shards : 8 + shards]
    grad_ref, mixed_ref, o_ref, o_t, q_t, v_t, k_split, vg_t, kg_t, qg = refs[8 + shards :]
    i = pl.program_id(0)
    positions, cols = o_ref.shape
    heads = cols // DH
    blocks = positions // blk
    scale = DH ** (-0.5)

    @pl.when(i == 0)
    def _():
        mean, inv_dev, total, cross = combined_stats(stats_refs, cols)
        for p in range(heads // 2):
            lanes = slice(p * PAIR, (p + 1) * PAIR)
            normed = (heads_ref[:, lanes].astype(F32) - mean) * inv_dev
            gate = gate_ref[:, lanes]
            mg = mg_ref[:, lanes]
            mixed_ref[:, lanes] = (normed * gate).astype(BF)
            gate_slope = slopes_ref[:, gate_columns(p)].astype(F32)
            grad_ref[:, gate_columns(p)] = (mg * normed * gate_slope).astype(BF)
            o_ref[:, lanes] = (inv_dev * (mg * gate - total - normed * cross)).astype(BF)
        o_t[...] = jnp.transpose(o_ref[...])
        for scratch, kind in ((v_t, 0), (q_t, 1)):
            scratch[...] = jnp.transpose(jnp.concatenate([acts_ref[:, head_columns(kind, h)] for h in range(heads)], axis=1))
        for block in range(blocks):
            split_pairs(acts_ref, k_split, 2, block, blk)
        vg_t[...] = jnp.zeros_like(vg_t)
        kg_t[...] = jnp.zeros_like(kg_t)

    at_i = pl.ds(pl.multiple_of(i * blk, blk), blk)
    o_i = [o_ref[at_i, h * DH : (h + 1) * DH] for h in range(heads)]

    def column(j, acc):
        at_j = pl.ds(pl.multiple_of(j * blk, blk), blk)
        both_j = pl.ds(pl.multiple_of(j * 2 * blk, 2 * blk), 2 * blk)
        per_head = []
        for h in range(heads):
            lanes = slice(h * DH, (h + 1) * DH)
            weight_grad = dot_nn(o_i[h], v_t[lanes, at_j])
            score_grad = (weight_grad * score_slope_ref[h, :, at_j].astype(F32)).astype(BF)
            vg_t[lanes, at_j] += dot_nn(o_t[lanes, at_i], weights_ref[h, :, at_j])
            kg_t[lanes, at_j] += dot_nn(q_t[lanes, at_i], score_grad)
            per_head.append(score_grad)
        return tuple(
            acc[p] + dot_nn(jnp.concatenate(per_head[2 * p : 2 * p + 2], axis=1), k_split[p, both_j, :])
            for p in range(heads // 2)
        )

    first = history_start(lengths_ref, users, i * blk) // blk
    zero = jnp.zeros((blk, PAIR), F32)
    acc = lax.fori_loop(first, i + 1, column, (zero,) * (heads // 2))
    qg[at_i, :] = jnp.concatenate(acc, axis=1)

    @pl.when(i == blocks - 1)
    def _():
        factor = 0.5 * scale / maxlen
        grads = [jnp.transpose(vg_t[...]) * (1.0 / maxlen), qg[...] * factor, jnp.transpose(kg_t[...]) * factor]
        pieces = [grads[kind][:, h * DH : (h + 1) * DH] for h in range(heads) for kind in range(3)]
        for n in range(3 * heads // 2):
            first_lane = n // 3 * 4 * PAIR + n % 3 * PAIR
            lanes = slice(first_lane, first_lane + PAIR)
            grad = jnp.concatenate(pieces[2 * n : 2 * n + 2], axis=1).astype(BF).astype(F32)
            grad_ref[:, lanes] = (grad * slopes_ref[:, lanes].astype(F32)).astype(BF)


def backward_attention(lengths, stats, mg, gate, head_outs, acts, slopes, weights, score_slope, blk, maxlen):
    positions, cols = mg.shape
    heads = cols // DH
    shards = len(stats)
    users = lengths.shape[1]
    elements = heads * positions * positions // 2
    whole = lambda i: (0, 0)
    return pl.pallas_call(
        functools.partial(backward_kernel, blk=blk, users=users, maxlen=maxlen, shards=shards),
        grid=(positions // blk,),
        in_specs=[pl.BlockSpec(memory_space=pltpu.SMEM)]
        + [pl.BlockSpec((8, positions), whole)] * shards
        + [
            pl.BlockSpec((positions, cols), whole),
            pl.BlockSpec((positions, cols), whole),
            pl.BlockSpec((positions, cols), whole),
            pl.BlockSpec((positions, 4 * cols), whole),
            pl.BlockSpec((positions, 4 * cols), whole),
            pl.BlockSpec((heads, blk, positions), lambda i: (0, i, 0)),
            pl.BlockSpec((heads, blk, positions), lambda i: (0, i, 0)),
        ],
        out_specs=[pl.BlockSpec((positions, 4 * cols), whole), pl.BlockSpec((positions, cols), whole)],
        out_shape=[
            jax.ShapeDtypeStruct((positions, 4 * cols), BF),
            jax.ShapeDtypeStruct((positions, cols), BF),
        ],
        scratch_shapes=[
            pltpu.VMEM((positions, cols), BF),
            pltpu.VMEM((cols, positions), BF),
            pltpu.VMEM((cols, positions), BF),
            pltpu.VMEM((cols, positions), BF),
            pltpu.VMEM((cols // PAIR, 2 * positions, PAIR), BF),
            pltpu.VMEM((cols, positions), F32),
            pltpu.VMEM((cols, positions), F32),
            pltpu.VMEM((positions, cols), F32),
        ],
        compiler_params=pltpu.CompilerParams(vmem_limit_bytes=VMEM_LIMIT),
        cost_estimate=pl.CostEstimate(
            flops=8 * elements * 256, bytes_accessed=4 * elements + 26 * positions * cols, transcendentals=0
        ),
        name="attention_backward",
    )(lengths, *stats, mg, gate, head_outs, acts, slopes, weights, score_slope)


def update_kernel(rows_ref, table_ref, accum_ref, new_table_ref, new_accum_ref, ids):
    i = pl.program_id(0)
    blk = table_ref.shape[0]
    slots = rows_ref.shape[0]

    @pl.when(i == 0)
    def _():
        numbers = jnp.transpose(rows_ref[:, D:].astype(F32))
        ids[...] = (numbers[0:1, :] * 256.0 + numbers[1:2, :]).astype(jnp.int32)

    row = i * blk + lax.broadcasted_iota(jnp.int32, (blk, slots), 0)
    hits = jnp.where(row == ids[...], 1.0, 0.0).astype(BF)
    grad = dot_nn(hits, rows_ref[:, :D])
    accum = jnp.transpose(jnp.broadcast_to(accum_ref[...], (128, blk)))[:, :1] + jnp.mean(grad * grad, axis=1, keepdims=True)
    new_accum_ref[...] = jnp.transpose(jnp.broadcast_to(accum, (blk, 128)))[:1, :]
    new_table_ref[...] = table_ref[...] - LEARN_RATE * grad * lax.rsqrt(accum)


def update_rows(got_rows, emb_table, row_accum):
    rows_own = emb_table.shape[0]
    slots = got_rows.shape[0]
    blk = min(256, rows_own)
    new_table, new_accum = pl.pallas_call(
        update_kernel,
        grid=(rows_own // blk,),
        in_specs=[
            pl.BlockSpec((slots, D + 128), lambda i: (0, 0)),
            pl.BlockSpec((blk, D), lambda i: (i, 0)),
            pl.BlockSpec((1, blk), lambda i: (0, i)),
        ],
        out_specs=[
            pl.BlockSpec((blk, D), lambda i: (i, 0)),
            pl.BlockSpec((1, blk), lambda i: (0, i)),
        ],
        out_shape=[
            jax.ShapeDtypeStruct((rows_own, D), F32),
            jax.ShapeDtypeStruct((1, rows_own), F32),
        ],
        scratch_shapes=[pltpu.VMEM((1, slots), jnp.int32)],
        compiler_params=pltpu.CompilerParams(vmem_limit_bytes=VMEM_LIMIT),
        cost_estimate=pl.CostEstimate(
            flops=2 * rows_own * slots * D, bytes_accessed=8 * rows_own * D + 2 * slots * D, transcendentals=rows_own
        ),
        name="update_rows",
    )(got_rows, emb_table, row_accum.reshape(1, rows_own))
    return new_table, new_accum.reshape(rows_own)


def own_weights(w_attn, w_gate, part, pairs):
    slices = []
    for p in range(pairs):
        at = part * pairs + p
        slices.append(lax.dynamic_slice_in_dim(w_attn, at * 3 * PAIR, 3 * PAIR, 1))
        slices.append(lax.dynamic_slice_in_dim(w_gate, at * PAIR, PAIR, 1))
    return jnp.concatenate(slices, axis=1)


def attn_and_gate(proj, pairs):
    pieces = [proj[:, p * 4 * PAIR : (p + 1) * 4 * PAIR] for p in range(pairs)]
    attn = jnp.concatenate([piece[:, : 3 * PAIR] for piece in pieces], axis=1)
    return attn, jnp.concatenate([piece[:, 3 * PAIR :] for piece in pieces], axis=1)


def row_slots(owners, rows, devices, capacity):
    events = owners.shape[0]
    owner_hits = (owners[:, None] == jnp.arange(devices, dtype=jnp.int32)[None, :]).astype(BF)
    place = jnp.arange(events, dtype=jnp.int32)
    before = (place[:, None] > place[None, :]).astype(BF)
    earlier = jnp.dot(before, owner_hits, preferred_element_type=F32)
    slots = jnp.sum(earlier * owner_hits.astype(F32), axis=1).astype(jnp.int32)
    flat_slot = owners * capacity + slots
    slot_hits = jnp.arange(devices * capacity, dtype=jnp.int32)[:, None] == flat_slot[None, :]
    lane = jnp.arange(128, dtype=jnp.int32)[None, :]
    numbers = jnp.where(lane == 0, rows[:, None] // 256, jnp.where(lane == 1, rows[:, None] % 256, 0))
    return slot_hits.astype(BF), numbers.astype(BF)


def rows_to_owners(slot_matrix, input_grad, numbers, devices, capacity):
    rows = jnp.concatenate([input_grad.astype(BF), numbers], axis=1)
    rows = jnp.dot(slot_matrix, rows, preferred_element_type=F32).astype(BF)
    got = lax.all_to_all(
        rows.reshape(devices, capacity, D + 128), ("seq", "dp"), split_axis=0, concat_axis=0, tiled=True
    )
    return got.reshape(devices * capacity, D + 128)


TN = (((0,), (0,)), ((), ()))


def dot_tn(a, b):
    return lax.dot_general(a, b, TN, preferred_element_type=F32)


def body_whole(
    layer_input, out_grad, lengths, item_owner, item_row, w_attn, w_gate, w_out, emb_table, row_accum
):
    seq_count = lax.axis_size("seq")
    dp_count = lax.axis_size("dp")
    devices = seq_count * dp_count
    seq_id = lax.axis_index("seq")
    tokens_dev = layer_input.shape[0]
    positions = tokens_dev * seq_count
    maxlen = 2 * positions // 3
    blk = min(256, positions)
    cols = D // seq_count
    pairs = cols // PAIR
    capacity = max(2, 2 * tokens_dev // devices)

    w_own = own_weights(w_attn, w_gate, seq_id, pairs)
    w_out_own = lax.dynamic_slice_in_dim(w_out, seq_id * cols, cols, 0)
    slot_matrix, numbers = row_slots(item_owner[:, 0], item_row, devices, capacity)

    x_full = lax.all_gather(layer_input, "seq", axis=0, tiled=True)
    og_full = lax.all_gather(out_grad, "seq", axis=0, tiled=True)
    order = jnp.arange(positions // blk, dtype=jnp.int32)
    acts, slopes, gate, weights, score_slope, heads = forward_attention(
        lengths, order, [x_full], w_own, blk, maxlen
    )
    mg, stats_own = event_stats(order, [og_full], w_out_own, gate, heads, blk)
    stats = lax.all_gather(stats_own, "seq", axis=0, tiled=False)
    grads, mixed = backward_attention(
        lengths, [stats[s] for s in range(seq_count)], mg, gate, heads, acts, slopes, weights, score_slope, blk, maxlen
    )

    input_part = dot_nt(grads, w_own).astype(BF)
    got = lax.all_to_all(
        input_part.reshape(seq_count, tokens_dev, D), "seq", split_axis=0, concat_axis=0, tiled=True
    )
    input_grad = jnp.sum(got.astype(F32), axis=0) + out_grad.astype(F32)
    got_rows = rows_to_owners(slot_matrix, input_grad, numbers, devices, capacity)
    new_table, new_accum = update_rows(got_rows, emb_table, row_accum)

    out_part = dot_tn(mixed, og_full).astype(BF)
    share = dp_count // seq_count
    out_part = out_part.reshape(share, D // dp_count, seq_count, cols).transpose(0, 2, 1, 3).reshape(D, cols)
    merged = jnp.concatenate([dot_tn(x_full, grads).astype(BF), out_part], axis=1)
    merged = lax.psum_scatter(merged, "dp", scatter_dimension=0, tiled=True)
    steps = []
    for s in range(seq_count):
        for piece in range(dp_count):
            part, target = divmod(piece, seq_count)
            steps.append((s * dp_count + piece, target * dp_count + s * share + part))
    grad_out = lax.ppermute(merged[:, 4 * cols :], ("seq", "dp"), steps).astype(F32)
    grad_attn, grad_gate = attn_and_gate(merged[:, : 4 * cols].astype(F32), pairs)
    return (grad_attn, grad_gate, grad_out, new_table, new_accum)


SEQ = 4
PLANE = 4


def send(array, target):
    steps = []
    for s in range(SEQ):
        for e in range(PLANE):
            for c in range(2):
                to = target(s, e, c)
                if to is not None:
                    steps.append((s * 2 * PLANE + 2 * e + c, to[0] * 2 * PLANE + 2 * to[1] + to[2]))
    return lax.ppermute(array, ("seq", "dp"), steps)


def home(s, c):
    return c == s // 2


def swap_far(array):
    return send(array, lambda s, e, c: None if home(s, c) else (3 - s, e, 1 - c))


def fetch_near(array):
    return send(array, lambda s, e, c: (s ^ 1, e, c) if home(s, c) else ((3 - s) ^ 1, e, 1 - c))


def swap_near(array):
    return send(array, lambda s, e, c: (s ^ 1, e, c))


def swap_core(array):
    return send(array, lambda s, e, c: (s, e, 1 - c))


def swap_x(array):
    return send(array, lambda s, e, c: (s, e ^ 1, c))


def swap_y(array):
    return send(array, lambda s, e, c: (s, e ^ 2, c))


def tie(*arrays):
    return lax.optimization_barrier(arrays)


def halves(array, bit, axis):
    kept = lax.dynamic_index_in_dim(array, bit, axis, keepdims=False)
    sent = lax.dynamic_index_in_dim(array, 1 - bit, axis, keepdims=False)
    return kept, sent


def body_pairs(
    layer_input, out_grad, lengths, item_owner, item_row, w_attn, w_gate, w_out, emb_table, row_accum
):
    devices = 2 * PLANE * SEQ
    s = lax.axis_index("seq")
    d = lax.axis_index("dp")
    e, c = d // 2, d % 2
    y, x = e // 2, e % 2
    tokens_dev = layer_input.shape[0]
    positions = tokens_dev * SEQ
    maxlen = 2 * positions // 3
    blk = min(256, positions)
    cols = D // SEQ
    pairs = cols // PAIR
    rows_own = emb_table.shape[0]
    capacity = max(2, 2 * tokens_dev // devices)
    at_home = c == s // 2
    part = 2 * (s % 2) + c

    def block_of(seq, core):
        return jnp.where(core == seq // 2, seq, 3 - seq)

    mine_at, near_at = block_of(s, c), block_of(s ^ 1, c)
    core_at, diag_at = block_of(s, 1 - c), block_of(s ^ 1, 1 - c)
    order = jnp.stack([mine_at, near_at, core_at, diag_at]).astype(jnp.int32)

    x_far = swap_far(layer_input)
    x_near = fetch_near(layer_input)
    users = lengths.shape[1]
    keys = (item_owner[:, 0] * rows_own + item_row).reshape(1, tokens_dev)
    small = jnp.concatenate([keys, jnp.pad(lengths, ((0, 0), (0, 128 - users)))], axis=1)
    small = jnp.where(at_home, small, swap_far(small))
    keys, lengths = small[0, :tokens_dev], small[:, tokens_dev : tokens_dev + users]
    w_own = own_weights(w_attn, w_gate, part, pairs)
    w_out_own = lax.dynamic_slice_in_dim(w_out, part * cols, cols, 0)
    slot_matrix, numbers = row_slots(keys // rows_own, keys % rows_own, devices, capacity)
    x_far, x_near, w_own, w_out_own, slot_matrix, numbers, lengths = tie(
        x_far, x_near, w_own, w_out_own, slot_matrix, numbers, lengths
    )
    x_here = jnp.concatenate([jnp.where(at_home, layer_input, x_far), x_near], axis=0)
    x_there = swap_core(x_here)
    x_here, og_own = tie(x_here, out_grad)
    og_far = swap_far(og_own)
    og_near = fetch_near(og_own)

    x_full, acts, slopes, gate, weights, score_slope, heads = forward_attention(
        lengths, order, [x_here, x_there], w_own, blk, maxlen
    )
    og_far, og_near, heads = tie(og_far, og_near, heads)
    og_mine = jnp.where(at_home, og_own, og_far)
    og_here = jnp.concatenate([og_mine, og_near], axis=0)
    og_there = swap_core(og_here)
    og_full, mg, stats_own = event_stats(order, [og_here, og_there], w_out_own, gate, heads, blk)
    stats = [
        stats_own,
        swap_core(stats_own),
        swap_near(stats_own),
        send(stats_own, lambda s, e, c: (s ^ 1, e, 1 - c)),
    ]
    grads, mixed = backward_attention(
        lengths, stats, mg, gate, heads, acts, slopes, weights, score_slope, blk, maxlen
    )

    def input_part(grads, block):
        return dot_nt(lax.dynamic_slice_in_dim(grads, block * tokens_dev, tokens_dev, 0), w_own)

    from_diag = swap_core(input_part(grads, diag_at).astype(BF))
    near_sum = (input_part(grads, near_at) + from_diag.astype(F32)).astype(BF)
    near_sum, grads = tie(near_sum, grads)
    from_near = swap_near(near_sum)
    core_part = input_part(grads, core_at).astype(BF)
    from_core = swap_core(core_part)
    input_grad = input_part(grads, mine_at) + og_mine.astype(F32)

    core_part, grads, mixed = tie(core_part, grads, mixed)
    half = 5 * cols // 2
    proj = dot_tn(x_full, grads).astype(BF).reshape(2, 2, D // PLANE, 4 * cols)
    out_part = dot_tn(mixed, og_full).astype(BF).reshape(cols, 2, 2, cols)
    a_kept, a_sent = halves(proj[..., :half], x, 1)
    b_kept, b_sent = halves(proj[..., half:], y, 0)
    out_kept, out_sent = (piece.transpose(1, 0, 2) for piece in halves(out_part, y, 1))
    b_kept = jnp.concatenate([b_kept, out_kept], axis=-1)
    b_sent = jnp.concatenate([b_sent, out_sent], axis=-1)
    a_got = swap_x(a_sent)
    b_got = swap_y(b_sent)

    input_grad = input_grad + from_core.astype(F32) + from_near.astype(F32)
    got_rows = rows_to_owners(slot_matrix, input_grad, numbers, devices, capacity)

    a = (a_kept.astype(F32) + a_got.astype(F32)).astype(BF)
    b = (b_kept.astype(F32) + b_got.astype(F32)).astype(BF)
    a_kept, a_sent = halves(a, y, 0)
    b_kept, b_sent = halves(b, x, 0)
    a = (a_kept.astype(F32) + swap_y(a_sent).astype(F32)).astype(BF)
    b = (b_kept.astype(F32) + swap_x(b_sent).astype(F32)).astype(BF)

    def last(array, target):
        pieces = array.reshape(2, D // (2 * PLANE), array.shape[1])
        one, other = halves(pieces, s // 2, 0)
        one = send(one, lambda s, e, c: target(s, e, c, s // 2))
        return one, send(other, lambda s, e, c: target(s, e, c, 1 - s // 2))

    proj = jnp.concatenate([a, b[:, : 4 * cols - half]], axis=1)
    proj = last(proj, lambda s, e, c, piece: (2 * (s % 2) + c, e, piece))
    out = last(b[:, 4 * cols - half :], lambda s, e, c, piece: (e, 2 * (s % 2) + c, piece))
    grad_attn, grad_gate = attn_and_gate(proj[0].astype(F32) + proj[1].astype(F32), pairs)
    grad_gate, *out = tie(grad_gate, *out)
    grad_out = out[0].astype(F32) + out[1].astype(F32)
    new_table, new_accum = update_rows(got_rows, emb_table, row_accum)
    return (grad_attn, grad_gate, grad_out, new_table, new_accum)


def solution(mesh):
    placed = (
        P(("dp", "seq"), None),
        P(("dp", "seq"), None),
        P("dp", None),
        P(("dp", "seq"), None),
        P(("dp", "seq")),
        P(),
        P(),
        P(),
        P(("seq", "dp"), None),
        P(("seq", "dp")),
    )
    paired = mesh.shape["seq"] == SEQ and mesh.shape["dp"] == 2 * PLANE
    return jax.shard_map(
        body_pairs if paired else body_whole,
        mesh=mesh,
        in_specs=placed,
        out_specs=(
            P("dp", "seq"),
            P("dp", "seq"),
            P("dp", "seq"),
            P(("seq", "dp"), None),
            P(("seq", "dp")),
        ),
        check_vma=False,
    )
```

```python
import functools

import jax
import jax.numpy as jnp
from jax import lax
from jax.experimental import pallas as pl
from jax.experimental.pallas import tpu as pltpu
from jax.sharding import PartitionSpec as P

D = 1024
H = 16
DH = 64
PAIR = 2 * DH

NORM_EPS = 1e-05
LEARN_RATE = 0.1
VMEM_LIMIT = 56 * 1024 * 1024
BF = jnp.bfloat16
F32 = jnp.float32


def dot_nn(a, b):
    return lax.dot_general(a, b, (((1,), (0,)), ((), ())), preferred_element_type=F32)


def dot_nt(a, b):
    return lax.dot_general(a, b, (((1,), (1,)), ((), ())), preferred_element_type=F32)


def history_start(lengths_ref, users, place):
    start = jnp.zeros_like(place)
    end = jnp.int32(0)
    for user in range(users - 1):
        end = end + lengths_ref[0, user]
        start = jnp.where(place >= end, end, start)
    return start


def head_columns(kind, head):
    first = head * 3 * DH + kind * DH
    return slice(first, first + DH)


def split_pairs(acts_ref, split_ref, kind, block, blk):
    at = pl.ds(pl.multiple_of(block * blk, blk), blk)
    zero = jnp.zeros((blk, DH), BF)
    for p in range(split_ref.shape[0]):
        one, two = (acts_ref[at, head_columns(kind, 2 * p + h)] for h in range(2))
        below = pl.multiple_of(block * 2 * blk + blk, blk)
        split_ref[p, pl.ds(pl.multiple_of(block * 2 * blk, blk), blk), :] = jnp.concatenate([one, zero], axis=1)
        split_ref[p, pl.ds(below, blk), :] = jnp.concatenate([zero, two], axis=1)


def forward_kernel(*refs, blk, users, maxlen, count):
    lengths_ref, order_ref = refs[:2]
    x_refs = refs[2 : 2 + count]
    w_ref = refs[2 + count]
    outs = refs[3 + count :]
    if count > 1:
        x_out_ref, outs = outs[0], outs[1:]
    acts_ref, slopes_ref, gate_ref, weights_ref, score_slope_ref, heads_ref, k_t, v_split = outs
    i = pl.program_id(0)
    heads = weights_ref.shape[0]
    attn = 3 * heads * DH
    chunks = x_refs[0].shape[0] // blk

    @pl.when(i == 0)
    def _():
        for b in range(count):
            for r in range(chunks):
                at = pl.ds(pl.multiple_of(order_ref[b * chunks + r] * blk, blk), blk)
                x = x_refs[b][r * blk : (r + 1) * blk, :]
                if count > 1:
                    x_out_ref[at, :] = x
                for lane in range(0, w_ref.shape[1], 512):
                    lanes = slice(lane, lane + 512)
                    half = 0.5 * dot_nn(x, w_ref[:, lanes])
                    t = jnp.tanh(half)
                    prod = half * t
                    silu = half + prod
                    acts_ref[at, lanes] = silu.astype(BF)
                    slopes_ref[at, lanes] = (0.5 * (1.0 + t) * (1.0 + half - prod)).astype(BF)
                    skip = max(0, attn - lane)
                    if skip < 512:
                        gate_ref[at, lane + skip - attn : lane + 512 - attn] = silu[:, skip:]
                for h in range(heads):
                    k_t[h * DH : (h + 1) * DH, at] = jnp.transpose(acts_ref[at, head_columns(2, h)])
                split_pairs(acts_ref, v_split, 0, order_ref[b * chunks + r], blk)

    at_i = pl.ds(pl.multiple_of(i * blk, blk), blk)
    q_half = [acts_ref[at_i, head_columns(1, h)] * jnp.asarray(0.5 * DH**-0.5, BF) for h in range(heads)]
    row = i * blk + lax.broadcasted_iota(jnp.int32, (blk, blk), 0)
    col0 = lax.broadcasted_iota(jnp.int32, (blk, blk), 1)
    start = history_start(lengths_ref, users, row)

    def column(j, acc):
        at_j = pl.ds(pl.multiple_of(j * blk, blk), blk)
        both_j = pl.ds(pl.multiple_of(j * 2 * blk, 2 * blk), 2 * blk)
        col = col0 + j * blk
        allowed = (col <= row) & (col >= start)
        per_head = []
        for h in range(heads):
            half = dot_nn(q_half[h], k_t[h * DH : (h + 1) * DH, at_j])
            half = jnp.where(allowed, half, -64.0)
            t = jnp.tanh(half)
            p = half * t
            weights = (half + p).astype(BF)
            weights_ref[h, :, at_j] = weights
            score_slope_ref[h, :, at_j] = ((1.0 + t) * (1.0 + half - p)).astype(BF)
            per_head.append(weights)
        return tuple(
            acc[p] + dot_nn(jnp.concatenate(per_head[2 * p : 2 * p + 2], axis=1), v_split[p, both_j, :])
            for p in range(heads // 2)
        )

    first = history_start(lengths_ref, users, i * blk) // blk
    zero = jnp.zeros((blk, PAIR), F32)
    acc = lax.fori_loop(first, i + 1, column, (zero,) * (heads // 2))
    heads_ref[...] = (jnp.concatenate(acc, axis=1) * (1.0 / maxlen)).astype(BF)


def forward_attention(lengths, order, x_blocks, w_own, blk, maxlen):
    count = len(x_blocks)
    block_rows = x_blocks[0].shape[0]
    positions = count * block_rows
    cols = w_own.shape[1] // 4
    heads = cols // DH
    users = lengths.shape[1]
    elements = heads * positions * positions // 2
    whole = lambda i: (0, 0)
    out_specs = [
        pl.BlockSpec((positions, 4 * cols), whole),
        pl.BlockSpec((positions, 4 * cols), whole),
        pl.BlockSpec((positions, cols), whole),
        pl.BlockSpec((heads, blk, positions), lambda i: (0, i, 0)),
        pl.BlockSpec((heads, blk, positions), lambda i: (0, i, 0)),
        pl.BlockSpec((blk, cols), lambda i: (i, 0)),
    ]
    out_shape = [
        jax.ShapeDtypeStruct((positions, 4 * cols), BF),
        jax.ShapeDtypeStruct((positions, 4 * cols), BF),
        jax.ShapeDtypeStruct((positions, cols), F32),
        jax.ShapeDtypeStruct((heads, positions, positions), BF),
        jax.ShapeDtypeStruct((heads, positions, positions), BF),
        jax.ShapeDtypeStruct((positions, cols), BF),
    ]
    if count > 1:
        out_specs = [pl.BlockSpec((positions, D), whole)] + out_specs
        out_shape = [jax.ShapeDtypeStruct((positions, D), BF)] + out_shape
    return pl.pallas_call(
        functools.partial(forward_kernel, blk=blk, users=users, maxlen=maxlen, count=count),
        grid=(positions // blk,),
        in_specs=[pl.BlockSpec(memory_space=pltpu.SMEM), pl.BlockSpec(memory_space=pltpu.SMEM)]
        + [pl.BlockSpec((block_rows, D), whole)] * count
        + [pl.BlockSpec((D, 4 * cols), whole)],
        out_specs=out_specs,
        out_shape=out_shape,
        scratch_shapes=[pltpu.VMEM((cols, positions), BF), pltpu.VMEM((cols // PAIR, 2 * positions, PAIR), BF)],
        compiler_params=pltpu.CompilerParams(vmem_limit_bytes=VMEM_LIMIT),
        cost_estimate=pl.CostEstimate(
            flops=8 * positions * D * cols + 4 * elements * 256,
            bytes_accessed=4 * positions * D + 4 * elements,
            transcendentals=elements,
        ),
        name="attention_forward",
    )(lengths, order, *x_blocks, w_own)


def stats_kernel(*refs, blk, count):
    order_ref = refs[0]
    og_refs = refs[1 : 1 + count]
    w_ref, gate_ref, heads_ref = refs[1 + count : 4 + count]
    outs = refs[4 + count :]
    if count > 1:
        og_out_ref, outs = outs[0], outs[1:]
    mg_ref, stats_ref = outs
    chunks = og_refs[0].shape[0] // blk
    for b in range(count):
        for r in range(chunks):
            at = pl.ds(pl.multiple_of(order_ref[b * chunks + r] * blk, blk), blk)
            og = og_refs[b][r * blk : (r + 1) * blk, :]
            if count > 1:
                og_out_ref[at, :] = og
            mg = dot_nt(og, w_ref[...])
            mg_ref[at, :] = mg
            ng = mg * gate_ref[at, :]
            heads = heads_ref[at, :].astype(F32)
            mean = jnp.mean(heads, axis=1, keepdims=True)
            centred = heads - mean
            square = jnp.sum(centred * centred, axis=1, keepdims=True)
            total = jnp.sum(ng, axis=1, keepdims=True)
            cross = jnp.sum(ng * centred, axis=1, keepdims=True)
            lane = lax.broadcasted_iota(jnp.int32, (blk, 128), 1)
            packed = jnp.where(lane == 0, mean, jnp.where(lane == 1, square, jnp.where(lane == 2, total, cross)))
            stats_ref[:, at] = jnp.transpose(packed)[:8, :]


def event_stats(order, og_blocks, w_out_own, gate, heads, blk):
    positions, cols = heads.shape
    count = len(og_blocks)
    vmem = pl.BlockSpec(memory_space=pltpu.VMEM)
    out_shape = [
        jax.ShapeDtypeStruct((positions, cols), F32),
        jax.ShapeDtypeStruct((8, positions), F32),
    ]
    if count > 1:
        out_shape = [jax.ShapeDtypeStruct((positions, D), BF)] + out_shape
    return pl.pallas_call(
        functools.partial(stats_kernel, blk=blk, count=count),
        in_specs=[pl.BlockSpec(memory_space=pltpu.SMEM)] + [vmem] * (count + 3),
        out_specs=[vmem] * len(out_shape),
        out_shape=out_shape,
        compiler_params=pltpu.CompilerParams(vmem_limit_bytes=VMEM_LIMIT),
        cost_estimate=pl.CostEstimate(
            flops=2 * positions * cols * D, bytes_accessed=4 * positions * D + 10 * positions * cols, transcendentals=0
        ),
        name="event_stats",
    )(order, *og_blocks, w_out_own, gate, heads)


def combined_stats(stats_refs, cols):
    shards = len(stats_refs)
    positions = stats_refs[0].shape[1]
    means = [ref[0:1, :] for ref in stats_refs]
    mean = sum(means) * (1.0 / shards)
    square = jnp.zeros_like(mean)
    total = jnp.zeros_like(mean)
    cross = jnp.zeros_like(mean)
    for s, ref in enumerate(stats_refs):
        shift = means[s] - mean
        part = ref[2:3, :]
        square = square + ref[1:2, :] + cols * shift * shift
        total = total + part
        cross = cross + ref[3:4, :] + shift * part
    inv_dev = lax.rsqrt(square * (1.0 / D) + NORM_EPS)
    kind = lax.broadcasted_iota(jnp.int32, (128, positions), 0)
    rest = jnp.where(kind == 2, total * (1.0 / D), cross * inv_dev * (1.0 / D))
    packed = jnp.where(kind == 0, mean, jnp.where(kind == 1, inv_dev, rest))
    per_event = jnp.transpose(packed)
    return [per_event[:, k : k + 1] for k in range(4)]


def backward_kernel(*refs, blk, users, maxlen, shards):
    lengths_ref = refs[0]
    stats_refs = refs[1 : 1 + shards]
    mg_ref, gate_ref, heads_ref, acts_ref, slopes_ref, weights_ref, score_slope_ref = refs[1 + shards : 8 + shards]
    grad_ref, mixed_ref, o_ref, o_t, q_t, v_t, k_split, vg_t, kg_t, qg = refs[8 + shards :]
    i = pl.program_id(0)
    positions, cols = o_ref.shape
    heads = cols // DH
    blocks = positions // blk
    scale = DH ** (-0.5)

    @pl.when(i == 0)
    def _():
        mean, inv_dev, total, cross = combined_stats(stats_refs, cols)
        for p in range(heads // 2):
            lanes = slice(p * PAIR, (p + 1) * PAIR)
            normed = (heads_ref[:, lanes].astype(F32) - mean) * inv_dev
            gate = gate_ref[:, lanes]
            mg = mg_ref[:, lanes]
            mixed_ref[:, lanes] = (normed * gate).astype(BF)
            gate_lanes = slice(3 * cols + p * PAIR, 3 * cols + (p + 1) * PAIR)
            gate_slope = slopes_ref[:, gate_lanes].astype(F32)
            grad_ref[:, gate_lanes] = (mg * normed * gate_slope).astype(BF)
            o_ref[:, lanes] = (inv_dev * (mg * gate - total - normed * cross)).astype(BF)
        o_t[...] = jnp.transpose(o_ref[...])
        for scratch, kind in ((v_t, 0), (q_t, 1)):
            scratch[...] = jnp.transpose(jnp.concatenate([acts_ref[:, head_columns(kind, h)] for h in range(heads)], axis=1))
        for block in range(blocks):
            split_pairs(acts_ref, k_split, 2, block, blk)
        vg_t[...] = jnp.zeros_like(vg_t)
        kg_t[...] = jnp.zeros_like(kg_t)

    at_i = pl.ds(pl.multiple_of(i * blk, blk), blk)
    o_i = [o_ref[at_i, h * DH : (h + 1) * DH] for h in range(heads)]

    def column(j, acc):
        at_j = pl.ds(pl.multiple_of(j * blk, blk), blk)
        both_j = pl.ds(pl.multiple_of(j * 2 * blk, 2 * blk), 2 * blk)
        per_head = []
        for h in range(heads):
            lanes = slice(h * DH, (h + 1) * DH)
            weight_grad = dot_nn(o_i[h], v_t[lanes, at_j])
            score_grad = (weight_grad * score_slope_ref[h, :, at_j].astype(F32)).astype(BF)
            vg_t[lanes, at_j] += dot_nn(o_t[lanes, at_i], weights_ref[h, :, at_j])
            kg_t[lanes, at_j] += dot_nn(q_t[lanes, at_i], score_grad)
            per_head.append(score_grad)
        return tuple(
            acc[p] + dot_nn(jnp.concatenate(per_head[2 * p : 2 * p + 2], axis=1), k_split[p, both_j, :])
            for p in range(heads // 2)
        )

    first = history_start(lengths_ref, users, i * blk) // blk
    zero = jnp.zeros((blk, PAIR), F32)
    acc = lax.fori_loop(first, i + 1, column, (zero,) * (heads // 2))
    qg[at_i, :] = jnp.concatenate(acc, axis=1)

    @pl.when(i == blocks - 1)
    def _():
        factor = 0.5 * scale / maxlen
        grads = [jnp.transpose(vg_t[...]) * (1.0 / maxlen), qg[...] * factor, jnp.transpose(kg_t[...]) * factor]
        pieces = [grads[kind][:, h * DH : (h + 1) * DH] for h in range(heads) for kind in range(3)]
        for n in range(3 * heads // 2):
            lanes = slice(n * PAIR, (n + 1) * PAIR)
            grad = jnp.concatenate(pieces[2 * n : 2 * n + 2], axis=1).astype(BF).astype(F32)
            grad_ref[:, lanes] = (grad * slopes_ref[:, lanes].astype(F32)).astype(BF)


def backward_attention(lengths, stats, mg, gate, head_outs, acts, slopes, weights, score_slope, blk, maxlen):
    positions, cols = mg.shape
    heads = cols // DH
    shards = len(stats)
    users = lengths.shape[1]
    elements = heads * positions * positions // 2
    whole = lambda i: (0, 0)
    return pl.pallas_call(
        functools.partial(backward_kernel, blk=blk, users=users, maxlen=maxlen, shards=shards),
        grid=(positions // blk,),
        in_specs=[pl.BlockSpec(memory_space=pltpu.SMEM)]
        + [pl.BlockSpec((8, positions), whole)] * shards
        + [
            pl.BlockSpec((positions, cols), whole),
            pl.BlockSpec((positions, cols), whole),
            pl.BlockSpec((positions, cols), whole),
            pl.BlockSpec((positions, 4 * cols), whole),
            pl.BlockSpec((positions, 4 * cols), whole),
            pl.BlockSpec((heads, blk, positions), lambda i: (0, i, 0)),
            pl.BlockSpec((heads, blk, positions), lambda i: (0, i, 0)),
        ],
        out_specs=[pl.BlockSpec((positions, 4 * cols), whole), pl.BlockSpec((positions, cols), whole)],
        out_shape=[
            jax.ShapeDtypeStruct((positions, 4 * cols), BF),
            jax.ShapeDtypeStruct((positions, cols), BF),
        ],
        scratch_shapes=[
            pltpu.VMEM((positions, cols), BF),
            pltpu.VMEM((cols, positions), BF),
            pltpu.VMEM((cols, positions), BF),
            pltpu.VMEM((cols, positions), BF),
            pltpu.VMEM((cols // PAIR, 2 * positions, PAIR), BF),
            pltpu.VMEM((cols, positions), F32),
            pltpu.VMEM((cols, positions), F32),
            pltpu.VMEM((positions, cols), F32),
        ],
        compiler_params=pltpu.CompilerParams(vmem_limit_bytes=VMEM_LIMIT),
        cost_estimate=pl.CostEstimate(
            flops=8 * elements * 256, bytes_accessed=4 * elements + 26 * positions * cols, transcendentals=0
        ),
        name="attention_backward",
    )(lengths, *stats, mg, gate, head_outs, acts, slopes, weights, score_slope)


def update_kernel(rows_ref, table_ref, accum_ref, new_table_ref, new_accum_ref, ids):
    i = pl.program_id(0)
    blk = table_ref.shape[0]
    slots = rows_ref.shape[0]

    @pl.when(i == 0)
    def _():
        numbers = jnp.transpose(rows_ref[:, D:].astype(F32))
        ids[...] = (numbers[0:1, :] * 256.0 + numbers[1:2, :]).astype(jnp.int32)

    row = i * blk + lax.broadcasted_iota(jnp.int32, (blk, slots), 0)
    hits = jnp.where(row == ids[...], 1.0, 0.0).astype(BF)
    grad = dot_nn(hits, rows_ref[:, :D])
    accum = jnp.transpose(jnp.broadcast_to(accum_ref[...], (128, blk)))[:, :1] + jnp.mean(grad * grad, axis=1, keepdims=True)
    new_accum_ref[...] = jnp.transpose(jnp.broadcast_to(accum, (blk, 128)))[:1, :]
    new_table_ref[...] = table_ref[...] - LEARN_RATE * grad * lax.rsqrt(accum)


def update_rows(got_rows, emb_table, row_accum):
    rows_own = emb_table.shape[0]
    slots = got_rows.shape[0]
    blk = min(256, rows_own)
    new_table, new_accum = pl.pallas_call(
        update_kernel,
        grid=(rows_own // blk,),
        in_specs=[
            pl.BlockSpec((slots, D + 128), lambda i: (0, 0)),
            pl.BlockSpec((blk, D), lambda i: (i, 0)),
            pl.BlockSpec((1, blk), lambda i: (0, i)),
        ],
        out_specs=[
            pl.BlockSpec((blk, D), lambda i: (i, 0)),
            pl.BlockSpec((1, blk), lambda i: (0, i)),
        ],
        out_shape=[
            jax.ShapeDtypeStruct((rows_own, D), F32),
            jax.ShapeDtypeStruct((1, rows_own), F32),
        ],
        scratch_shapes=[pltpu.VMEM((1, slots), jnp.int32)],
        compiler_params=pltpu.CompilerParams(vmem_limit_bytes=VMEM_LIMIT),
        cost_estimate=pl.CostEstimate(
            flops=2 * rows_own * slots * D, bytes_accessed=8 * rows_own * D + 2 * slots * D, transcendentals=rows_own
        ),
        name="update_rows",
    )(got_rows, emb_table, row_accum.reshape(1, rows_own))
    return new_table, new_accum.reshape(rows_own)


def own_weights(w_attn, w_gate, part, cols):
    attn = lax.dynamic_slice_in_dim(w_attn, part * 3 * cols, 3 * cols, 1)
    gate = lax.dynamic_slice_in_dim(w_gate, part * cols, cols, 1)
    return jnp.concatenate([attn, gate], axis=1)


def row_slots(owners, rows, devices, capacity):
    events = owners.shape[0]
    owner_hits = (owners[:, None] == jnp.arange(devices, dtype=jnp.int32)[None, :]).astype(BF)
    place = jnp.arange(events, dtype=jnp.int32)
    before = (place[:, None] > place[None, :]).astype(BF)
    earlier = jnp.dot(before, owner_hits, preferred_element_type=F32)
    slots = jnp.sum(earlier * owner_hits.astype(F32), axis=1).astype(jnp.int32)
    flat_slot = owners * capacity + slots
    slot_hits = jnp.arange(devices * capacity, dtype=jnp.int32)[:, None] == flat_slot[None, :]
    lane = jnp.arange(128, dtype=jnp.int32)[None, :]
    numbers = jnp.where(lane == 0, rows[:, None] // 256, jnp.where(lane == 1, rows[:, None] % 256, 0))
    return slot_hits.astype(BF), numbers.astype(BF)


def to_owners(rows, devices, capacity):
    shape = (devices, capacity) + rows.shape[1:]
    got = lax.all_to_all(rows.reshape(shape), ("seq", "dp"), split_axis=0, concat_axis=0, tiled=True)
    return got.reshape(rows.shape)


TN = (((0,), (0,)), ((), ()))


def dot_tn(a, b):
    return lax.dot_general(a, b, TN, preferred_element_type=F32)


def body_whole(
    layer_input, out_grad, lengths, item_owner, item_row, w_attn, w_gate, w_out, emb_table, row_accum
):
    seq_count = lax.axis_size("seq")
    dp_count = lax.axis_size("dp")
    devices = seq_count * dp_count
    seq_id = lax.axis_index("seq")
    tokens_dev = layer_input.shape[0]
    positions = tokens_dev * seq_count
    maxlen = 2 * positions // 3
    blk = min(256, positions)
    cols = D // seq_count
    capacity = max(2, 2 * tokens_dev // devices)

    w_own = own_weights(w_attn, w_gate, seq_id, cols)
    w_out_own = lax.dynamic_slice_in_dim(w_out, seq_id * cols, cols, 0)
    slot_matrix, numbers = row_slots(item_owner[:, 0], item_row, devices, capacity)

    x_full = lax.all_gather(layer_input, "seq", axis=0, tiled=True)
    og_full = lax.all_gather(out_grad, "seq", axis=0, tiled=True)
    order = jnp.arange(positions // blk, dtype=jnp.int32)
    acts, slopes, gate, weights, score_slope, heads = forward_attention(
        lengths, order, [x_full], w_own, blk, maxlen
    )
    mg, stats_own = event_stats(order, [og_full], w_out_own, gate, heads, blk)
    stats = lax.all_gather(stats_own, "seq", axis=0, tiled=False)
    grads, mixed = backward_attention(
        lengths, [stats[s] for s in range(seq_count)], mg, gate, heads, acts, slopes, weights, score_slope, blk, maxlen
    )

    input_part = dot_nt(grads, w_own).astype(BF)
    got = lax.all_to_all(
        input_part.reshape(seq_count, tokens_dev, D), "seq", split_axis=0, concat_axis=0, tiled=True
    )
    input_grad = jnp.sum(got.astype(F32), axis=0) + out_grad.astype(F32)
    rows = jnp.concatenate([input_grad.astype(BF), numbers], axis=1)
    rows = jnp.dot(slot_matrix, rows, preferred_element_type=F32).astype(BF)
    got_rows = to_owners(rows, devices, capacity)
    new_table, new_accum = update_rows(got_rows, emb_table, row_accum)

    out_part = dot_tn(mixed, og_full).astype(BF)
    share = dp_count // seq_count
    out_part = out_part.reshape(share, D // dp_count, seq_count, cols).transpose(0, 2, 1, 3).reshape(D, cols)
    merged = jnp.concatenate([dot_tn(x_full, grads).astype(BF), out_part], axis=1)
    merged = lax.psum_scatter(merged, "dp", scatter_dimension=0, tiled=True)
    steps = []
    for s in range(seq_count):
        for piece in range(dp_count):
            part, target = divmod(piece, seq_count)
            steps.append((s * dp_count + piece, target * dp_count + s * share + part))
    grad_out = lax.ppermute(merged[:, 4 * cols :], ("seq", "dp"), steps).astype(F32)
    grad_attn = merged[:, : 3 * cols].astype(F32)
    grad_gate = merged[:, 3 * cols : 4 * cols].astype(F32)
    return (grad_attn, grad_gate, grad_out, new_table, new_accum)


SEQ = 4
PLANE = 4


def send(array, target):
    steps = []
    for s in range(SEQ):
        for e in range(PLANE):
            for c in range(2):
                to = target(s, e, c)
                if to is not None:
                    steps.append((s * 2 * PLANE + 2 * e + c, to[0] * 2 * PLANE + 2 * to[1] + to[2]))
    return lax.ppermute(array, ("seq", "dp"), steps)


def home(s, c):
    return c == s // 2


def swap_far(array):
    return send(array, lambda s, e, c: None if home(s, c) else (3 - s, e, 1 - c))


def fetch_near(array):
    return send(array, lambda s, e, c: (s ^ 1, e, c) if home(s, c) else ((3 - s) ^ 1, e, 1 - c))


def swap_near(array):
    return send(array, lambda s, e, c: (s ^ 1, e, c))


def swap_core(array):
    return send(array, lambda s, e, c: (s, e, 1 - c))


def swap_x(array):
    return send(array, lambda s, e, c: (s, e ^ 1, c))


def swap_y(array):
    return send(array, lambda s, e, c: (s, e ^ 2, c))


def tie(*arrays):
    return lax.optimization_barrier(arrays)


def halves(array, bit, axis):
    kept = lax.dynamic_index_in_dim(array, bit, axis, keepdims=False)
    sent = lax.dynamic_index_in_dim(array, 1 - bit, axis, keepdims=False)
    return kept, sent


def body_pairs(
    layer_input, out_grad, lengths, item_owner, item_row, w_attn, w_gate, w_out, emb_table, row_accum
):
    devices = 2 * PLANE * SEQ
    s = lax.axis_index("seq")
    d = lax.axis_index("dp")
    e, c = d // 2, d % 2
    y, x = e // 2, e % 2
    tokens_dev = layer_input.shape[0]
    positions = tokens_dev * SEQ
    maxlen = 2 * positions // 3
    blk = min(256, positions)
    cols = D // SEQ
    rows_own = emb_table.shape[0]
    capacity = max(2, 2 * tokens_dev // devices)
    at_home = c == s // 2
    part = 2 * (s % 2) + c

    def block_of(seq, core):
        return jnp.where(core == seq // 2, seq, 3 - seq)

    mine_at, near_at = block_of(s, c), block_of(s ^ 1, c)
    core_at, diag_at = block_of(s, 1 - c), block_of(s ^ 1, 1 - c)
    order = jnp.stack([mine_at, near_at, core_at, diag_at]).astype(jnp.int32)

    x_far = swap_far(layer_input)
    x_near = fetch_near(layer_input)
    users = lengths.shape[1]
    keys = (item_owner[:, 0] * rows_own + item_row).reshape(1, tokens_dev)
    small = jnp.concatenate([keys, jnp.pad(lengths, ((0, 0), (0, 128 - users)))], axis=1)
    small = jnp.where(at_home, small, swap_far(small))
    keys, lengths = small[0, :tokens_dev], small[:, tokens_dev : tokens_dev + users]
    w_own = own_weights(w_attn, w_gate, part, cols)
    w_out_own = lax.dynamic_slice_in_dim(w_out, part * cols, cols, 0)
    slot_matrix, numbers = row_slots(keys // rows_own, keys % rows_own, devices, capacity)
    x_far, x_near, w_own, w_out_own, slot_matrix, numbers, lengths = tie(
        x_far, x_near, w_own, w_out_own, slot_matrix, numbers, lengths
    )
    x_here = jnp.concatenate([jnp.where(at_home, layer_input, x_far), x_near], axis=0)
    x_there = swap_core(x_here)
    x_here, og_own = tie(x_here, out_grad)
    og_far = swap_far(og_own)
    og_near = fetch_near(og_own)

    x_full, acts, slopes, gate, weights, score_slope, heads = forward_attention(
        lengths, order, [x_here, x_there], w_own, blk, maxlen
    )
    og_far, og_near, heads = tie(og_far, og_near, heads)
    og_mine = jnp.where(at_home, og_own, og_far)
    og_here = jnp.concatenate([og_mine, og_near], axis=0)
    og_there = swap_core(og_here)
    og_full, mg, stats_own = event_stats(order, [og_here, og_there], w_out_own, gate, heads, blk)
    stats = [
        stats_own,
        swap_core(stats_own),
        swap_near(stats_own),
        send(stats_own, lambda s, e, c: (s ^ 1, e, 1 - c)),
    ]
    grads, mixed = backward_attention(
        lengths, stats, mg, gate, heads, acts, slopes, weights, score_slope, blk, maxlen
    )

    def input_part(grads, block):
        return dot_nt(lax.dynamic_slice_in_dim(grads, block * tokens_dev, tokens_dev, 0), w_own)

    from_diag = swap_core(input_part(grads, diag_at).astype(BF))
    near_sum = (input_part(grads, near_at) + from_diag.astype(F32)).astype(BF)
    near_sum, grads = tie(near_sum, grads)
    from_near = swap_near(near_sum)
    core_part = input_part(grads, core_at).astype(BF)
    from_core = swap_core(core_part)
    input_grad = input_part(grads, mine_at) + og_mine.astype(F32)

    core_part, grads, mixed = tie(core_part, grads, mixed)
    half = 5 * cols // 2
    proj = dot_tn(x_full, grads).astype(BF).reshape(2, 2, D // PLANE, 4 * cols)
    out_part = dot_tn(mixed, og_full).astype(BF).reshape(cols, 2, 2, cols)
    a_kept, a_sent = halves(proj[..., :half], x, 1)
    b_kept, b_sent = halves(proj[..., half:], y, 0)
    out_kept, out_sent = (piece.transpose(1, 0, 2) for piece in halves(out_part, y, 1))
    b_kept = jnp.concatenate([b_kept, out_kept], axis=-1)
    b_sent = jnp.concatenate([b_sent, out_sent], axis=-1)
    a_got = swap_x(a_sent)
    b_got = swap_y(b_sent)

    input_grad = input_grad + from_core.astype(F32) + from_near.astype(F32)
    rows = jnp.concatenate([input_grad.astype(BF), numbers], axis=1)
    rows = jnp.dot(slot_matrix, rows, preferred_element_type=F32).astype(BF)
    got_rows = to_owners(rows, devices, capacity)

    a = (a_kept.astype(F32) + a_got.astype(F32)).astype(BF)
    b = (b_kept.astype(F32) + b_got.astype(F32)).astype(BF)
    a_kept, a_sent = halves(a, y, 0)
    b_kept, b_sent = halves(b, x, 0)
    a = (a_kept.astype(F32) + swap_y(a_sent).astype(F32)).astype(BF)
    b = (b_kept.astype(F32) + swap_x(b_sent).astype(F32)).astype(BF)

    def last(array, target):
        pieces = array.reshape(2, D // (2 * PLANE), array.shape[1])
        one, other = halves(pieces, s // 2, 0)
        one = send(one, lambda s, e, c: target(s, e, c, s // 2))
        return one, send(other, lambda s, e, c: target(s, e, c, 1 - s // 2))

    proj = jnp.concatenate([a, b[:, : 4 * cols - half]], axis=1)
    proj = last(proj, lambda s, e, c, piece: (2 * (s % 2) + c, e, piece))
    out = last(b[:, 4 * cols - half :], lambda s, e, c, piece: (e, 2 * (s % 2) + c, piece))
    new_table, new_accum = update_rows(got_rows, emb_table, row_accum)
    attn = proj[0][:, : 3 * cols].astype(F32) + proj[1][:, : 3 * cols].astype(F32)
    gate = proj[0][:, 3 * cols :].astype(F32) + proj[1][:, 3 * cols :].astype(F32)
    return (attn, gate, out[0].astype(F32) + out[1].astype(F32), new_table, new_accum)


def solution(mesh):
    placed = (
        P(("dp", "seq"), None),
        P(("dp", "seq"), None),
        P("dp", None),
        P(("dp", "seq"), None),
        P(("dp", "seq")),
        P(),
        P(),
        P(),
        P(("seq", "dp"), None),
        P(("seq", "dp")),
    )
    paired = mesh.shape["seq"] == SEQ and mesh.shape["dp"] == 2 * PLANE
    return jax.shard_map(
        body_pairs if paired else body_whole,
        mesh=mesh,
        in_specs=placed,
        out_specs=(
            P("dp", "seq"),
            P("dp", "seq"),
            P("dp", "seq"),
            P(("seq", "dp"), None),
            P(("seq", "dp")),
        ),
        check_vma=False,
    )
```

```python
import functools

import jax
import jax.numpy as jnp
from jax import lax
from jax.experimental import pallas as pl
from jax.experimental.pallas import tpu as pltpu
from jax.sharding import PartitionSpec as P

D = 1024
H = 16
DH = 64
PAIR = 2 * DH

NORM_EPS = 1e-05
LEARN_RATE = 0.1
VMEM_LIMIT = 56 * 1024 * 1024
BF = jnp.bfloat16
F32 = jnp.float32


def dot_nn(a, b):
    return lax.dot_general(a, b, (((1,), (0,)), ((), ())), preferred_element_type=F32)


def dot_nt(a, b):
    return lax.dot_general(a, b, (((1,), (1,)), ((), ())), preferred_element_type=F32)


def history_start(lengths_ref, users, place):
    start = jnp.zeros_like(place)
    end = jnp.int32(0)
    for user in range(users - 1):
        end = end + lengths_ref[0, user]
        start = jnp.where(place >= end, end, start)
    return start


def head_columns(kind, head):
    first = head // 2 * 4 * PAIR + head % 2 * 3 * DH + kind * DH
    return slice(first, first + DH)


def gate_columns(pair):
    return slice(pair * 4 * PAIR + 3 * PAIR, (pair + 1) * 4 * PAIR)


def split_pairs(acts_ref, split_ref, kind, block, blk):
    at = pl.ds(pl.multiple_of(block * blk, blk), blk)
    zero = jnp.zeros((blk, DH), BF)
    for p in range(split_ref.shape[0]):
        one, two = (acts_ref[at, head_columns(kind, 2 * p + h)] for h in range(2))
        below = pl.multiple_of(block * 2 * blk + blk, blk)
        split_ref[p, pl.ds(pl.multiple_of(block * 2 * blk, blk), blk), :] = jnp.concatenate([one, zero], axis=1)
        split_ref[p, pl.ds(below, blk), :] = jnp.concatenate([zero, two], axis=1)


def forward_kernel(*refs, blk, users, maxlen, count):
    lengths_ref, order_ref = refs[:2]
    x_refs = refs[2 : 2 + count]
    w_ref = refs[2 + count]
    outs = refs[3 + count :]
    if count > 1:
        x_out_ref, outs = outs[0], outs[1:]
    acts_out, slopes_out, gate_out, weights_ref, score_slope_ref, heads_ref = outs[:6]
    k_t, v_split, acts_ref, slopes_ref, gate_ref, sems = outs[6:]
    i = pl.program_id(0)
    heads = weights_ref.shape[0]
    chunks = x_refs[0].shape[0] // blk

    def copies():
        pairs = [(acts_ref, acts_out), (slopes_ref, slopes_out), (gate_ref, gate_out)]
        if count > 1:
            for b in range(count):
                for r in range(chunks):
                    at = pl.ds(pl.multiple_of(order_ref[b * chunks + r] * blk, blk), blk)
                    pairs.append((x_refs[b].at[pl.ds(r * blk, blk), :], x_out_ref.at[at, :]))
        return [pltpu.make_async_copy(source, target, sems.at[n]) for n, (source, target) in enumerate(pairs)]

    @pl.when(i == 0)
    def _():
        for b in range(count):
            for r in range(chunks):
                at = pl.ds(pl.multiple_of(order_ref[b * chunks + r] * blk, blk), blk)
                x = x_refs[b][r * blk : (r + 1) * blk, :]
                for p in range(heads // 2):
                    lanes = slice(p * 4 * PAIR, (p + 1) * 4 * PAIR)
                    half = 0.5 * dot_nn(x, w_ref[:, lanes])
                    t = jnp.tanh(half)
                    prod = half * t
                    silu = half + prod
                    acts_ref[at, lanes] = silu.astype(BF)
                    gate_ref[at, p * PAIR : (p + 1) * PAIR] = silu[:, 3 * PAIR :]
                    slopes_ref[at, lanes] = (0.5 * (1.0 + t) * (1.0 + half - prod)).astype(BF)
                for h in range(heads):
                    k_t[h * DH : (h + 1) * DH, at] = jnp.transpose(acts_ref[at, head_columns(2, h)])
                split_pairs(acts_ref, v_split, 0, order_ref[b * chunks + r], blk)
        for copy in copies():
            copy.start()

    at_i = pl.ds(pl.multiple_of(i * blk, blk), blk)
    q_half = [acts_ref[at_i, head_columns(1, h)] * jnp.asarray(0.5 * DH**-0.5, BF) for h in range(heads)]
    row = i * blk + lax.broadcasted_iota(jnp.int32, (blk, blk), 0)
    col0 = lax.broadcasted_iota(jnp.int32, (blk, blk), 1)
    start = history_start(lengths_ref, users, row)

    def column(j, acc):
        at_j = pl.ds(pl.multiple_of(j * blk, blk), blk)
        both_j = pl.ds(pl.multiple_of(j * 2 * blk, 2 * blk), 2 * blk)
        col = col0 + j * blk
        allowed = (col <= row) & (col >= start)
        per_head = []
        for h in range(heads):
            half = dot_nn(q_half[h], k_t[h * DH : (h + 1) * DH, at_j])
            half = jnp.where(allowed, half, -64.0)
            t = jnp.tanh(half)
            p = half * t
            weights = (half + p).astype(BF)
            weights_ref[h, :, at_j] = weights
            score_slope_ref[h, :, at_j] = ((1.0 + t) * (1.0 + half - p)).astype(BF)
            per_head.append(weights)
        return tuple(
            acc[p] + dot_nn(jnp.concatenate(per_head[2 * p : 2 * p + 2], axis=1), v_split[p, both_j, :])
            for p in range(heads // 2)
        )

    first = history_start(lengths_ref, users, i * blk) // blk
    zero = jnp.zeros((blk, PAIR), F32)
    acc = lax.fori_loop(first, i + 1, column, (zero,) * (heads // 2))
    heads_ref[...] = (jnp.concatenate(acc, axis=1) * (1.0 / maxlen)).astype(BF)

    @pl.when(i == pl.num_programs(0) - 1)
    def _():
        for copy in copies():
            copy.wait()


def forward_attention(lengths, order, x_blocks, w_own, blk, maxlen):
    count = len(x_blocks)
    block_rows = x_blocks[0].shape[0]
    positions = count * block_rows
    cols = w_own.shape[1] // 4
    heads = cols // DH
    users = lengths.shape[1]
    elements = heads * positions * positions // 2
    whole = lambda i: (0, 0)
    out_specs = [
        pl.BlockSpec(memory_space=pl.ANY),
        pl.BlockSpec(memory_space=pl.ANY),
        pl.BlockSpec(memory_space=pl.ANY),
        pl.BlockSpec((heads, blk, positions), lambda i: (0, i, 0)),
        pl.BlockSpec((heads, blk, positions), lambda i: (0, i, 0)),
        pl.BlockSpec((blk, cols), lambda i: (i, 0)),
    ]
    out_shape = [
        jax.ShapeDtypeStruct((positions, 4 * cols), BF),
        jax.ShapeDtypeStruct((positions, 4 * cols), BF),
        jax.ShapeDtypeStruct((positions, cols), F32),
        jax.ShapeDtypeStruct((heads, positions, positions), BF),
        jax.ShapeDtypeStruct((heads, positions, positions), BF),
        jax.ShapeDtypeStruct((positions, cols), BF),
    ]
    if count > 1:
        out_specs = [pl.BlockSpec(memory_space=pl.ANY)] + out_specs
        out_shape = [jax.ShapeDtypeStruct((positions, D), BF)] + out_shape
    return pl.pallas_call(
        functools.partial(forward_kernel, blk=blk, users=users, maxlen=maxlen, count=count),
        grid=(positions // blk,),
        in_specs=[pl.BlockSpec(memory_space=pltpu.SMEM), pl.BlockSpec(memory_space=pltpu.SMEM)]
        + [pl.BlockSpec((block_rows, D), whole)] * count
        + [pl.BlockSpec((D, 4 * cols), whole)],
        out_specs=out_specs,
        out_shape=out_shape,
        scratch_shapes=[
            pltpu.VMEM((cols, positions), BF),
            pltpu.VMEM((cols // PAIR, 2 * positions, PAIR), BF),
            pltpu.VMEM((positions, 4 * cols), BF),
            pltpu.VMEM((positions, 4 * cols), BF),
            pltpu.VMEM((positions, cols), F32),
            pltpu.SemaphoreType.DMA((3 + positions // blk,)),
        ],
        compiler_params=pltpu.CompilerParams(vmem_limit_bytes=VMEM_LIMIT),
        cost_estimate=pl.CostEstimate(
            flops=8 * positions * D * cols + 4 * elements * 256,
            bytes_accessed=4 * positions * D + 4 * elements,
            transcendentals=elements,
        ),
        name="attention_forward",
    )(lengths, order, *x_blocks, w_own)


def stats_kernel(*refs, count):
    og_refs = refs[1 : 1 + count]
    w_ref, gate_ref, heads_ref = refs[1 + count : 4 + count]
    outs = refs[4 + count :]
    og = og_refs[0][...]
    if count > 1:
        og_out_ref, outs = outs[0], outs[1:]
        chunks = pl.num_programs(0) // count
        for b in range(1, count):
            og = jnp.where(pl.program_id(0) >= b * chunks, og_refs[b][...], og)
        og_out_ref[...] = og
    mg_ref, stats_ref = outs
    mg = dot_nt(og, w_ref[...])
    mg_ref[...] = mg
    ng = mg * gate_ref[...]
    heads = heads_ref[...].astype(F32)
    mean = jnp.mean(heads, axis=1, keepdims=True)
    centred = heads - mean
    square = jnp.sum(centred * centred, axis=1, keepdims=True)
    total = jnp.sum(ng, axis=1, keepdims=True)
    cross = jnp.sum(ng * centred, axis=1, keepdims=True)
    lane = lax.broadcasted_iota(jnp.int32, (heads.shape[0], 128), 1)
    packed = jnp.where(lane == 0, mean, jnp.where(lane == 1, square, jnp.where(lane == 2, total, cross)))
    stats_ref[...] = jnp.transpose(packed)[:8, :]


def event_stats(order, og_blocks, w_out_own, gate, heads, blk):
    positions, cols = heads.shape
    count = len(og_blocks)
    steps = positions // blk
    chunks = steps // count
    placed = lambda i, order: (order[i], 0)
    og_specs = [
        pl.BlockSpec((blk, D), lambda i, order, b=b: (jnp.clip(i - b * chunks, 0, chunks - 1), 0)) for b in range(count)
    ]
    out_specs = [pl.BlockSpec((blk, cols), placed), pl.BlockSpec((8, blk), lambda i, order: (0, order[i]))]
    out_shape = [
        jax.ShapeDtypeStruct((positions, cols), F32),
        jax.ShapeDtypeStruct((8, positions), F32),
    ]
    if count > 1:
        out_specs = [pl.BlockSpec((blk, D), placed)] + out_specs
        out_shape = [jax.ShapeDtypeStruct((positions, D), BF)] + out_shape
    return pl.pallas_call(
        functools.partial(stats_kernel, count=count),
        grid_spec=pltpu.PrefetchScalarGridSpec(
            num_scalar_prefetch=1,
            grid=(steps,),
            in_specs=og_specs
            + [
                pl.BlockSpec((cols, D), lambda i, order: (0, 0)),
                pl.BlockSpec((blk, cols), placed),
                pl.BlockSpec((blk, cols), placed),
            ],
            out_specs=out_specs,
        ),
        out_shape=out_shape,
        compiler_params=pltpu.CompilerParams(vmem_limit_bytes=VMEM_LIMIT),
        cost_estimate=pl.CostEstimate(
            flops=2 * positions * cols * D, bytes_accessed=4 * positions * D + 10 * positions * cols, transcendentals=0
        ),
        name="event_stats",
    )(order, *og_blocks, w_out_own, gate, heads)


def combined_stats(stats_refs, cols):
    shards = len(stats_refs)
    positions = stats_refs[0].shape[1]
    means = [ref[0:1, :] for ref in stats_refs]
    mean = sum(means) * (1.0 / shards)
    square = jnp.zeros_like(mean)
    total = jnp.zeros_like(mean)
    cross = jnp.zeros_like(mean)
    for s, ref in enumerate(stats_refs):
        shift = means[s] - mean
        part = ref[2:3, :]
        square = square + ref[1:2, :] + cols * shift * shift
        total = total + part
        cross = cross + ref[3:4, :] + shift * part
    inv_dev = lax.rsqrt(square * (1.0 / D) + NORM_EPS)
    kind = lax.broadcasted_iota(jnp.int32, (128, positions), 0)
    rest = jnp.where(kind == 2, total * (1.0 / D), cross * inv_dev * (1.0 / D))
    packed = jnp.where(kind == 0, mean, jnp.where(kind == 1, inv_dev, rest))
    per_event = jnp.transpose(packed)
    return [per_event[:, k : k + 1] for k in range(4)]


def backward_kernel(*refs, blk, users, maxlen, shards):
    lengths_ref = refs[0]
    stats_refs = refs[1 : 1 + shards]
    mg_ref, gate_ref, heads_ref, acts_ref, slopes_ref, weights_ref, score_slope_ref = refs[1 + shards : 8 + shards]
    grad_ref, mixed_ref, o_ref, o_t, q_t, v_t, k_split, vg_t, kg_t, qg = refs[8 + shards :]
    i = pl.program_id(0)
    positions, cols = o_ref.shape
    heads = cols // DH
    blocks = positions // blk
    scale = DH ** (-0.5)

    @pl.when(i == 0)
    def _():
        mean, inv_dev, total, cross = combined_stats(stats_refs, cols)
        for p in range(heads // 2):
            lanes = slice(p * PAIR, (p + 1) * PAIR)
            normed = (heads_ref[:, lanes].astype(F32) - mean) * inv_dev
            gate = gate_ref[:, lanes]
            mg = mg_ref[:, lanes]
            mixed_ref[:, lanes] = (normed * gate).astype(BF)
            gate_slope = slopes_ref[:, gate_columns(p)].astype(F32)
            grad_ref[:, gate_columns(p)] = (mg * normed * gate_slope).astype(BF)
            o_ref[:, lanes] = (inv_dev * (mg * gate - total - normed * cross)).astype(BF)
        o_t[...] = jnp.transpose(o_ref[...])
        for scratch, kind in ((v_t, 0), (q_t, 1)):
            scratch[...] = jnp.transpose(jnp.concatenate([acts_ref[:, head_columns(kind, h)] for h in range(heads)], axis=1))
        for block in range(blocks):
            split_pairs(acts_ref, k_split, 2, block, blk)
        vg_t[...] = jnp.zeros_like(vg_t)
        kg_t[...] = jnp.zeros_like(kg_t)

    at_i = pl.ds(pl.multiple_of(i * blk, blk), blk)
    o_i = [o_ref[at_i, h * DH : (h + 1) * DH] for h in range(heads)]

    def column(j, acc):
        at_j = pl.ds(pl.multiple_of(j * blk, blk), blk)
        both_j = pl.ds(pl.multiple_of(j * 2 * blk, 2 * blk), 2 * blk)
        per_head = []
        for h in range(heads):
            lanes = slice(h * DH, (h + 1) * DH)
            weight_grad = dot_nn(o_i[h], v_t[lanes, at_j])
            score_grad = (weight_grad * score_slope_ref[h, :, at_j].astype(F32)).astype(BF)
            vg_t[lanes, at_j] += dot_nn(o_t[lanes, at_i], weights_ref[h, :, at_j])
            kg_t[lanes, at_j] += dot_nn(q_t[lanes, at_i], score_grad)
            per_head.append(score_grad)
        return tuple(
            acc[p] + dot_nn(jnp.concatenate(per_head[2 * p : 2 * p + 2], axis=1), k_split[p, both_j, :])
            for p in range(heads // 2)
        )

    first = history_start(lengths_ref, users, i * blk) // blk
    zero = jnp.zeros((blk, PAIR), F32)
    acc = lax.fori_loop(first, i + 1, column, (zero,) * (heads // 2))
    qg[at_i, :] = jnp.concatenate(acc, axis=1)

    @pl.when(i == blocks - 1)
    def _():
        factor = 0.5 * scale / maxlen
        grads = [jnp.transpose(vg_t[...]) * (1.0 / maxlen), qg[...] * factor, jnp.transpose(kg_t[...]) * factor]
        pieces = [grads[kind][:, h * DH : (h + 1) * DH] for h in range(heads) for kind in range(3)]
        for n in range(3 * heads // 2):
            first_lane = n // 3 * 4 * PAIR + n % 3 * PAIR
            lanes = slice(first_lane, first_lane + PAIR)
            grad = jnp.concatenate(pieces[2 * n : 2 * n + 2], axis=1).astype(BF).astype(F32)
            grad_ref[:, lanes] = (grad * slopes_ref[:, lanes].astype(F32)).astype(BF)


def backward_attention(lengths, stats, mg, gate, head_outs, acts, slopes, weights, score_slope, blk, maxlen):
    positions, cols = mg.shape
    heads = cols // DH
    shards = len(stats)
    users = lengths.shape[1]
    elements = heads * positions * positions // 2
    whole = lambda i: (0, 0)
    return pl.pallas_call(
        functools.partial(backward_kernel, blk=blk, users=users, maxlen=maxlen, shards=shards),
        grid=(positions // blk,),
        in_specs=[pl.BlockSpec(memory_space=pltpu.SMEM)]
        + [pl.BlockSpec((8, positions), whole)] * shards
        + [
            pl.BlockSpec((positions, cols), whole),
            pl.BlockSpec((positions, cols), whole),
            pl.BlockSpec((positions, cols), whole),
            pl.BlockSpec((positions, 4 * cols), whole),
            pl.BlockSpec((positions, 4 * cols), whole),
            pl.BlockSpec((heads, blk, positions), lambda i: (0, i, 0)),
            pl.BlockSpec((heads, blk, positions), lambda i: (0, i, 0)),
        ],
        out_specs=[pl.BlockSpec((positions, 4 * cols), whole), pl.BlockSpec((positions, cols), whole)],
        out_shape=[
            jax.ShapeDtypeStruct((positions, 4 * cols), BF),
            jax.ShapeDtypeStruct((positions, cols), BF),
        ],
        scratch_shapes=[
            pltpu.VMEM((positions, cols), BF),
            pltpu.VMEM((cols, positions), BF),
            pltpu.VMEM((cols, positions), BF),
            pltpu.VMEM((cols, positions), BF),
            pltpu.VMEM((cols // PAIR, 2 * positions, PAIR), BF),
            pltpu.VMEM((cols, positions), F32),
            pltpu.VMEM((cols, positions), F32),
            pltpu.VMEM((positions, cols), F32),
        ],
        compiler_params=pltpu.CompilerParams(vmem_limit_bytes=VMEM_LIMIT),
        cost_estimate=pl.CostEstimate(
            flops=8 * elements * 256, bytes_accessed=4 * elements + 26 * positions * cols, transcendentals=0
        ),
        name="attention_backward",
    )(lengths, *stats, mg, gate, head_outs, acts, slopes, weights, score_slope)


def update_kernel(rows_ref, table_ref, accum_ref, new_table_ref, new_accum_ref, ids):
    i = pl.program_id(0)
    blk = table_ref.shape[0]
    slots = rows_ref.shape[0]

    @pl.when(i == 0)
    def _():
        numbers = jnp.transpose(rows_ref[:, D:].astype(F32))
        ids[...] = (numbers[0:1, :] * 256.0 + numbers[1:2, :]).astype(jnp.int32)

    row = i * blk + lax.broadcasted_iota(jnp.int32, (blk, slots), 0)
    hits = jnp.where(row == ids[...], 1.0, 0.0).astype(BF)
    grad = dot_nn(hits, rows_ref[:, :D])
    accum = jnp.transpose(jnp.broadcast_to(accum_ref[...], (128, blk)))[:, :1] + jnp.mean(grad * grad, axis=1, keepdims=True)
    new_accum_ref[...] = jnp.transpose(jnp.broadcast_to(accum, (blk, 128)))[:1, :]
    new_table_ref[...] = table_ref[...] - LEARN_RATE * grad * lax.rsqrt(accum)


def update_rows(got_rows, emb_table, row_accum):
    rows_own = emb_table.shape[0]
    slots = got_rows.shape[0]
    blk = min(256, rows_own)
    new_table, new_accum = pl.pallas_call(
        update_kernel,
        grid=(rows_own // blk,),
        in_specs=[
            pl.BlockSpec((slots, D + 128), lambda i: (0, 0)),
            pl.BlockSpec((blk, D), lambda i: (i, 0)),
            pl.BlockSpec((1, blk), lambda i: (0, i)),
        ],
        out_specs=[
            pl.BlockSpec((blk, D), lambda i: (i, 0)),
            pl.BlockSpec((1, blk), lambda i: (0, i)),
        ],
        out_shape=[
            jax.ShapeDtypeStruct((rows_own, D), F32),
            jax.ShapeDtypeStruct((1, rows_own), F32),
        ],
        scratch_shapes=[pltpu.VMEM((1, slots), jnp.int32)],
        compiler_params=pltpu.CompilerParams(vmem_limit_bytes=VMEM_LIMIT),
        cost_estimate=pl.CostEstimate(
            flops=2 * rows_own * slots * D, bytes_accessed=8 * rows_own * D + 2 * slots * D, transcendentals=rows_own
        ),
        name="update_rows",
    )(got_rows, emb_table, row_accum.reshape(1, rows_own))
    return new_table, new_accum.reshape(rows_own)


def own_weights(w_attn, w_gate, part, pairs):
    slices = []
    for p in range(pairs):
        at = part * pairs + p
        slices.append(lax.dynamic_slice_in_dim(w_attn, at * 3 * PAIR, 3 * PAIR, 1))
        slices.append(lax.dynamic_slice_in_dim(w_gate, at * PAIR, PAIR, 1))
    return jnp.concatenate(slices, axis=1)


def attn_and_gate(proj, pairs):
    pieces = [proj[:, p * 4 * PAIR : (p + 1) * 4 * PAIR] for p in range(pairs)]
    attn = jnp.concatenate([piece[:, : 3 * PAIR] for piece in pieces], axis=1)
    return attn, jnp.concatenate([piece[:, 3 * PAIR :] for piece in pieces], axis=1)


def row_slots(owners, rows, devices, capacity):
    events = owners.shape[0]
    owner_hits = (owners[:, None] == jnp.arange(devices, dtype=jnp.int32)[None, :]).astype(BF)
    place = jnp.arange(events, dtype=jnp.int32)
    before = (place[:, None] > place[None, :]).astype(BF)
    earlier = jnp.dot(before, owner_hits, preferred_element_type=F32)
    slots = jnp.sum(earlier * owner_hits.astype(F32), axis=1).astype(jnp.int32)
    flat_slot = owners * capacity + slots
    slot_hits = jnp.arange(devices * capacity, dtype=jnp.int32)[:, None] == flat_slot[None, :]
    lane = jnp.arange(128, dtype=jnp.int32)[None, :]
    numbers = jnp.where(lane == 0, rows[:, None] // 256, jnp.where(lane == 1, rows[:, None] % 256, 0))
    return slot_hits.astype(BF), numbers.astype(BF)


def rows_to_owners(slot_matrix, input_grad, numbers, devices, capacity):
    rows = jnp.concatenate([input_grad.astype(BF), numbers], axis=1)
    rows = jnp.dot(slot_matrix, rows, preferred_element_type=F32).astype(BF)
    got = lax.all_to_all(
        rows.reshape(devices, capacity, D + 128), ("seq", "dp"), split_axis=0, concat_axis=0, tiled=True
    )
    return got.reshape(devices * capacity, D + 128)


TN = (((0,), (0,)), ((), ()))


def dot_tn(a, b):
    return lax.dot_general(a, b, TN, preferred_element_type=F32)


def body_whole(
    layer_input, out_grad, lengths, item_owner, item_row, w_attn, w_gate, w_out, emb_table, row_accum
):
    seq_count = lax.axis_size("seq")
    dp_count = lax.axis_size("dp")
    devices = seq_count * dp_count
    seq_id = lax.axis_index("seq")
    tokens_dev = layer_input.shape[0]
    positions = tokens_dev * seq_count
    maxlen = 2 * positions // 3
    blk = min(256, positions)
    cols = D // seq_count
    pairs = cols // PAIR
    capacity = max(2, 2 * tokens_dev // devices)

    w_own = own_weights(w_attn, w_gate, seq_id, pairs)
    w_out_own = lax.dynamic_slice_in_dim(w_out, seq_id * cols, cols, 0)
    slot_matrix, numbers = row_slots(item_owner[:, 0], item_row, devices, capacity)

    x_full = lax.all_gather(layer_input, "seq", axis=0, tiled=True)
    og_full = lax.all_gather(out_grad, "seq", axis=0, tiled=True)
    order = jnp.arange(positions // blk, dtype=jnp.int32)
    acts, slopes, gate, weights, score_slope, heads = forward_attention(
        lengths, order, [x_full], w_own, blk, maxlen
    )
    mg, stats_own = event_stats(order, [og_full], w_out_own, gate, heads, blk)
    stats = lax.all_gather(stats_own, "seq", axis=0, tiled=False)
    grads, mixed = backward_attention(
        lengths, [stats[s] for s in range(seq_count)], mg, gate, heads, acts, slopes, weights, score_slope, blk, maxlen
    )

    input_part = dot_nt(grads, w_own).astype(BF)
    got = lax.all_to_all(
        input_part.reshape(seq_count, tokens_dev, D), "seq", split_axis=0, concat_axis=0, tiled=True
    )
    input_grad = jnp.sum(got.astype(F32), axis=0) + out_grad.astype(F32)
    got_rows = rows_to_owners(slot_matrix, input_grad, numbers, devices, capacity)
    new_table, new_accum = update_rows(got_rows, emb_table, row_accum)

    out_part = dot_tn(mixed, og_full).astype(BF)
    share = dp_count // seq_count
    out_part = out_part.reshape(share, D // dp_count, seq_count, cols).transpose(0, 2, 1, 3).reshape(D, cols)
    merged = jnp.concatenate([dot_tn(x_full, grads).astype(BF), out_part], axis=1)
    merged = lax.psum_scatter(merged, "dp", scatter_dimension=0, tiled=True)
    steps = []
    for s in range(seq_count):
        for piece in range(dp_count):
            part, target = divmod(piece, seq_count)
            steps.append((s * dp_count + piece, target * dp_count + s * share + part))
    grad_out = lax.ppermute(merged[:, 4 * cols :], ("seq", "dp"), steps).astype(F32)
    grad_attn, grad_gate = attn_and_gate(merged[:, : 4 * cols].astype(F32), pairs)
    return (grad_attn, grad_gate, grad_out, new_table, new_accum)


SEQ = 4
PLANE = 4


def send(array, target):
    steps = []
    for s in range(SEQ):
        for e in range(PLANE):
            for c in range(2):
                to = target(s, e, c)
                if to is not None:
                    steps.append((s * 2 * PLANE + 2 * e + c, to[0] * 2 * PLANE + 2 * to[1] + to[2]))
    return lax.ppermute(array, ("seq", "dp"), steps)


def home(s, c):
    return c == s // 2


def swap_far(array):
    return send(array, lambda s, e, c: None if home(s, c) else (3 - s, e, 1 - c))


def fetch_near(array):
    return send(array, lambda s, e, c: (s ^ 1, e, c) if home(s, c) else ((3 - s) ^ 1, e, 1 - c))


def swap_near(array):
    return send(array, lambda s, e, c: (s ^ 1, e, c))


def swap_core(array):
    return send(array, lambda s, e, c: (s, e, 1 - c))


def swap_x(array):
    return send(array, lambda s, e, c: (s, e ^ 1, c))


def swap_y(array):
    return send(array, lambda s, e, c: (s, e ^ 2, c))


def tie(*arrays):
    return lax.optimization_barrier(arrays)


def halves(array, bit, axis):
    kept = lax.dynamic_index_in_dim(array, bit, axis, keepdims=False)
    sent = lax.dynamic_index_in_dim(array, 1 - bit, axis, keepdims=False)
    return kept, sent


def body_pairs(
    layer_input, out_grad, lengths, item_owner, item_row, w_attn, w_gate, w_out, emb_table, row_accum
):
    devices = 2 * PLANE * SEQ
    s = lax.axis_index("seq")
    d = lax.axis_index("dp")
    e, c = d // 2, d % 2
    y, x = e // 2, e % 2
    tokens_dev = layer_input.shape[0]
    positions = tokens_dev * SEQ
    maxlen = 2 * positions // 3
    blk = min(256, positions)
    cols = D // SEQ
    pairs = cols // PAIR
    rows_own = emb_table.shape[0]
    capacity = max(2, 2 * tokens_dev // devices)
    at_home = c == s // 2
    part = 2 * (s % 2) + c

    def block_of(seq, core):
        return jnp.where(core == seq // 2, seq, 3 - seq)

    mine_at, near_at = block_of(s, c), block_of(s ^ 1, c)
    core_at, diag_at = block_of(s, 1 - c), block_of(s ^ 1, 1 - c)
    order = jnp.stack([mine_at, near_at, core_at, diag_at]).astype(jnp.int32)

    x_far = swap_far(layer_input)
    x_near = fetch_near(layer_input)
    users = lengths.shape[1]
    keys = (item_owner[:, 0] * rows_own + item_row).reshape(1, tokens_dev)
    small = jnp.concatenate([keys, jnp.pad(lengths, ((0, 0), (0, 128 - users)))], axis=1)
    small = jnp.where(at_home, small, swap_far(small))
    keys, lengths = small[0, :tokens_dev], small[:, tokens_dev : tokens_dev + users]
    w_own = own_weights(w_attn, w_gate, part, pairs)
    w_out_own = lax.dynamic_slice_in_dim(w_out, part * cols, cols, 0)
    slot_matrix, numbers = row_slots(keys // rows_own, keys % rows_own, devices, capacity)
    x_far, x_near, w_own, w_out_own, slot_matrix, numbers, lengths = tie(
        x_far, x_near, w_own, w_out_own, slot_matrix, numbers, lengths
    )
    x_here = jnp.concatenate([jnp.where(at_home, layer_input, x_far), x_near], axis=0)
    x_there = swap_core(x_here)
    x_here, og_own = tie(x_here, out_grad)
    og_far = swap_far(og_own)
    og_near = fetch_near(og_own)

    x_full, acts, slopes, gate, weights, score_slope, heads = forward_attention(
        lengths, order, [x_here, x_there], w_own, blk, maxlen
    )
    og_far, og_near, heads = tie(og_far, og_near, heads)
    og_mine = jnp.where(at_home, og_own, og_far)
    og_here = jnp.concatenate([og_mine, og_near], axis=0)
    og_there = swap_core(og_here)
    og_full, mg, stats_own = event_stats(order, [og_here, og_there], w_out_own, gate, heads, blk)
    stats = [
        stats_own,
        swap_core(stats_own),
        swap_near(stats_own),
        send(stats_own, lambda s, e, c: (s ^ 1, e, 1 - c)),
    ]
    grads, mixed = backward_attention(
        lengths, stats, mg, gate, heads, acts, slopes, weights, score_slope, blk, maxlen
    )

    def input_part(grads, block):
        return dot_nt(lax.dynamic_slice_in_dim(grads, block * tokens_dev, tokens_dev, 0), w_own)

    from_diag = swap_core(input_part(grads, diag_at).astype(BF))
    near_sum = (input_part(grads, near_at) + from_diag.astype(F32)).astype(BF)
    near_sum, grads = tie(near_sum, grads)
    from_near = swap_near(near_sum)
    core_part = input_part(grads, core_at).astype(BF)
    from_core = swap_core(core_part)
    input_grad = input_part(grads, mine_at) + og_mine.astype(F32)

    core_part, grads, mixed = tie(core_part, grads, mixed)
    half = 5 * cols // 2
    proj = dot_tn(x_full, grads).astype(BF).reshape(2, 2, D // PLANE, 4 * cols)
    out_part = dot_tn(mixed, og_full).astype(BF).reshape(cols, 2, 2, cols)
    a_kept, a_sent = halves(proj[..., :half], x, 1)
    b_kept, b_sent = halves(proj[..., half:], y, 0)
    out_kept, out_sent = (piece.transpose(1, 0, 2) for piece in halves(out_part, y, 1))
    b_kept = jnp.concatenate([b_kept, out_kept], axis=-1)
    b_sent = jnp.concatenate([b_sent, out_sent], axis=-1)
    a_got = swap_x(a_sent)
    b_got = swap_y(b_sent)

    input_grad = input_grad + from_core.astype(F32) + from_near.astype(F32)
    got_rows = rows_to_owners(slot_matrix, input_grad, numbers, devices, capacity)

    a = (a_kept.astype(F32) + a_got.astype(F32)).astype(BF)
    b = (b_kept.astype(F32) + b_got.astype(F32)).astype(BF)
    a_kept, a_sent = halves(a, y, 0)
    b_kept, b_sent = halves(b, x, 0)
    a = (a_kept.astype(F32) + swap_y(a_sent).astype(F32)).astype(BF)
    b = (b_kept.astype(F32) + swap_x(b_sent).astype(F32)).astype(BF)

    def last(array, target):
        pieces = array.reshape(2, D // (2 * PLANE), array.shape[1])
        one, other = halves(pieces, s // 2, 0)
        one = send(one, lambda s, e, c: target(s, e, c, s // 2)).astype(F32)
        return one + send(other, lambda s, e, c: target(s, e, c, 1 - s // 2)).astype(F32)

    proj = jnp.concatenate([a, b[:, : 4 * cols - half]], axis=1)
    proj = last(proj, lambda s, e, c, piece: (2 * (s % 2) + c, e, piece))
    grad_out = last(b[:, 4 * cols - half :], lambda s, e, c, piece: (e, 2 * (s % 2) + c, piece))
    grad_attn, grad_gate = attn_and_gate(proj, pairs)
    new_table, new_accum = update_rows(got_rows, emb_table, row_accum)
    return (grad_attn, grad_gate, grad_out, new_table, new_accum)


def solution(mesh):
    placed = (
        P(("dp", "seq"), None),
        P(("dp", "seq"), None),
        P("dp", None),
        P(("dp", "seq"), None),
        P(("dp", "seq")),
        P(),
        P(),
        P(),
        P(("seq", "dp"), None),
        P(("seq", "dp")),
    )
    paired = mesh.shape["seq"] == SEQ and mesh.shape["dp"] == 2 * PLANE
    return jax.shard_map(
        body_pairs if paired else body_whole,
        mesh=mesh,
        in_specs=placed,
        out_specs=(
            P("dp", "seq"),
            P("dp", "seq"),
            P("dp", "seq"),
            P(("seq", "dp"), None),
            P(("seq", "dp")),
        ),
        check_vma=False,
    )
```

```python
import functools

import jax
import jax.numpy as jnp
from jax import lax
from jax.experimental import pallas as pl
from jax.experimental.pallas import tpu as pltpu
from jax.sharding import PartitionSpec as P

D = 1024
H = 16
DH = 64
PAIR = 2 * DH

NORM_EPS = 1e-05
LEARN_RATE = 0.1
VMEM_LIMIT = 56 * 1024 * 1024
BF = jnp.bfloat16
F32 = jnp.float32


def dot_nn(a, b):
    return lax.dot_general(a, b, (((1,), (0,)), ((), ())), preferred_element_type=F32)


def dot_nt(a, b):
    return lax.dot_general(a, b, (((1,), (1,)), ((), ())), preferred_element_type=F32)


def history_start(lengths_ref, users, place):
    start = jnp.zeros_like(place)
    end = jnp.int32(0)
    for user in range(users - 1):
        end = end + lengths_ref[0, user]
        start = jnp.where(place >= end, end, start)
    return start


def head_columns(kind, head):
    first = head // 2 * 4 * PAIR + head % 2 * 3 * DH + kind * DH
    return slice(first, first + DH)


def gate_columns(pair):
    return slice(pair * 4 * PAIR + 3 * PAIR, (pair + 1) * 4 * PAIR)


def split_pairs(acts_ref, split_ref, kind, block, blk):
    at = pl.ds(pl.multiple_of(block * blk, blk), blk)
    zero = jnp.zeros((blk, DH), BF)
    for p in range(split_ref.shape[0]):
        one, two = (acts_ref[at, head_columns(kind, 2 * p + h)] for h in range(2))
        below = pl.multiple_of(block * 2 * blk + blk, blk)
        split_ref[p, pl.ds(pl.multiple_of(block * 2 * blk, blk), blk), :] = jnp.concatenate([one, zero], axis=1)
        split_ref[p, pl.ds(below, blk), :] = jnp.concatenate([zero, two], axis=1)


def forward_kernel(*refs, blk, users, maxlen, count):
    lengths_ref, order_ref = refs[:2]
    x_refs = refs[2 : 2 + count]
    w_ref = refs[2 + count]
    outs = refs[3 + count :]
    if count > 1:
        x_out_ref, outs = outs[0], outs[1:]
    acts_ref, slopes_ref, gate_ref, weights_ref, score_slope_ref, heads_ref, k_t, v_split = outs
    i = pl.program_id(0)
    heads = weights_ref.shape[0]
    chunks = x_refs[0].shape[0] // blk

    @pl.when(i == 0)
    def _():
        for b in range(count):
            for r in range(chunks):
                at = pl.ds(pl.multiple_of(order_ref[b * chunks + r] * blk, blk), blk)
                x = x_refs[b][r * blk : (r + 1) * blk, :]
                if count > 1:
                    x_out_ref[at, :] = x
                for p in range(heads // 2):
                    lanes = slice(p * 4 * PAIR, (p + 1) * 4 * PAIR)
                    half = 0.5 * dot_nn(x, w_ref[:, lanes])
                    t = jnp.tanh(half)
                    prod = half * t
                    silu = half + prod
                    acts_ref[at, lanes] = silu.astype(BF)
                    gate_ref[at, p * PAIR : (p + 1) * PAIR] = silu[:, 3 * PAIR :]
                    slopes_ref[at, lanes] = (0.5 * (1.0 + t) * (1.0 + half - prod)).astype(BF)
                for h in range(heads):
                    k_t[h * DH : (h + 1) * DH, at] = jnp.transpose(acts_ref[at, head_columns(2, h)])
                split_pairs(acts_ref, v_split, 0, order_ref[b * chunks + r], blk)

    at_i = pl.ds(pl.multiple_of(i * blk, blk), blk)
    q_half = [acts_ref[at_i, head_columns(1, h)] * jnp.asarray(0.5 * DH**-0.5, BF) for h in range(heads)]
    row = i * blk + lax.broadcasted_iota(jnp.int32, (blk, blk), 0)
    col0 = lax.broadcasted_iota(jnp.int32, (blk, blk), 1)
    start = history_start(lengths_ref, users, row)

    def column(j, acc):
        at_j = pl.ds(pl.multiple_of(j * blk, blk), blk)
        both_j = pl.ds(pl.multiple_of(j * 2 * blk, 2 * blk), 2 * blk)
        col = col0 + j * blk
        allowed = (col <= row) & (col >= start)
        per_head = []
        for h in range(heads):
            half = dot_nn(q_half[h], k_t[h * DH : (h + 1) * DH, at_j])
            half = jnp.where(allowed, half, -64.0)
            t = jnp.tanh(half)
            p = half * t
            weights = (half + p).astype(BF)
            weights_ref[h, :, at_j] = weights
            score_slope_ref[h, :, at_j] = ((1.0 + t) * (1.0 + half - p)).astype(BF)
            per_head.append(weights)
        return tuple(
            acc[p] + dot_nn(jnp.concatenate(per_head[2 * p : 2 * p + 2], axis=1), v_split[p, both_j, :])
            for p in range(heads // 2)
        )

    first = history_start(lengths_ref, users, i * blk) // blk
    zero = jnp.zeros((blk, PAIR), F32)
    acc = lax.fori_loop(first, i + 1, column, (zero,) * (heads // 2))
    heads_ref[...] = (jnp.concatenate(acc, axis=1) * (1.0 / maxlen)).astype(BF)


def forward_attention(lengths, order, x_blocks, w_own, blk, maxlen):
    count = len(x_blocks)
    block_rows = x_blocks[0].shape[0]
    positions = count * block_rows
    cols = w_own.shape[1] // 4
    heads = cols // DH
    users = lengths.shape[1]
    elements = heads * positions * positions // 2
    whole = lambda i: (0, 0)
    out_specs = [
        pl.BlockSpec((positions, 4 * cols), whole),
        pl.BlockSpec((positions, 4 * cols), whole),
        pl.BlockSpec((positions, cols), whole),
        pl.BlockSpec((heads, blk, positions), lambda i: (0, i, 0)),
        pl.BlockSpec((heads, blk, positions), lambda i: (0, i, 0)),
        pl.BlockSpec((blk, cols), lambda i: (i, 0)),
    ]
    out_shape = [
        jax.ShapeDtypeStruct((positions, 4 * cols), BF),
        jax.ShapeDtypeStruct((positions, 4 * cols), BF),
        jax.ShapeDtypeStruct((positions, cols), F32),
        jax.ShapeDtypeStruct((heads, positions, positions), BF),
        jax.ShapeDtypeStruct((heads, positions, positions), BF),
        jax.ShapeDtypeStruct((positions, cols), BF),
    ]
    if count > 1:
        out_specs = [pl.BlockSpec((positions, D), whole)] + out_specs
        out_shape = [jax.ShapeDtypeStruct((positions, D), BF)] + out_shape
    return pl.pallas_call(
        functools.partial(forward_kernel, blk=blk, users=users, maxlen=maxlen, count=count),
        grid=(positions // blk,),
        in_specs=[pl.BlockSpec(memory_space=pltpu.SMEM), pl.BlockSpec(memory_space=pltpu.SMEM)]
        + [pl.BlockSpec((block_rows, D), whole)] * count
        + [pl.BlockSpec((D, 4 * cols), whole)],
        out_specs=out_specs,
        out_shape=out_shape,
        scratch_shapes=[pltpu.VMEM((cols, positions), BF), pltpu.VMEM((cols // PAIR, 2 * positions, PAIR), BF)],
        compiler_params=pltpu.CompilerParams(vmem_limit_bytes=VMEM_LIMIT),
        cost_estimate=pl.CostEstimate(
            flops=8 * positions * D * cols + 4 * elements * 256,
            bytes_accessed=4 * positions * D + 4 * elements,
            transcendentals=elements,
        ),
        name="attention_forward",
    )(lengths, order, *x_blocks, w_own)


def stats_kernel(*refs, blk, count):
    order_ref = refs[0]
    og_refs = refs[1 : 1 + count]
    w_ref, gate_ref, heads_ref = refs[1 + count : 4 + count]
    outs = refs[4 + count :]
    if count > 1:
        og_out_ref, outs = outs[0], outs[1:]
    mg_ref, stats_ref = outs
    chunks = og_refs[0].shape[0] // blk
    for b in range(count):
        for r in range(chunks):
            at = pl.ds(pl.multiple_of(order_ref[b * chunks + r] * blk, blk), blk)
            og = og_refs[b][r * blk : (r + 1) * blk, :]
            if count > 1:
                og_out_ref[at, :] = og
            mg = dot_nt(og, w_ref[...])
            mg_ref[at, :] = mg
            ng = mg * gate_ref[at, :]
            heads = heads_ref[at, :].astype(F32)
            mean = jnp.mean(heads, axis=1, keepdims=True)
            centred = heads - mean
            square = jnp.sum(centred * centred, axis=1, keepdims=True)
            total = jnp.sum(ng, axis=1, keepdims=True)
            cross = jnp.sum(ng * centred, axis=1, keepdims=True)
            lane = lax.broadcasted_iota(jnp.int32, (blk, 128), 1)
            packed = jnp.where(lane == 0, mean, jnp.where(lane == 1, square, jnp.where(lane == 2, total, cross)))
            stats_ref[:, at] = jnp.transpose(packed)[:8, :]


def event_stats(order, og_blocks, w_out_own, gate, heads, blk):
    positions, cols = heads.shape
    count = len(og_blocks)
    vmem = pl.BlockSpec(memory_space=pltpu.VMEM)
    out_shape = [
        jax.ShapeDtypeStruct((positions, cols), F32),
        jax.ShapeDtypeStruct((8, positions), F32),
    ]
    if count > 1:
        out_shape = [jax.ShapeDtypeStruct((positions, D), BF)] + out_shape
    return pl.pallas_call(
        functools.partial(stats_kernel, blk=blk, count=count),
        in_specs=[pl.BlockSpec(memory_space=pltpu.SMEM)] + [vmem] * (count + 3),
        out_specs=[vmem] * len(out_shape),
        out_shape=out_shape,
        compiler_params=pltpu.CompilerParams(vmem_limit_bytes=VMEM_LIMIT),
        cost_estimate=pl.CostEstimate(
            flops=2 * positions * cols * D, bytes_accessed=4 * positions * D + 10 * positions * cols, transcendentals=0
        ),
        name="event_stats",
    )(order, *og_blocks, w_out_own, gate, heads)


def combined_stats(stats_refs, cols):
    shards = len(stats_refs)
    positions = stats_refs[0].shape[1]
    means = [ref[0:1, :] for ref in stats_refs]
    mean = sum(means) * (1.0 / shards)
    square = jnp.zeros_like(mean)
    total = jnp.zeros_like(mean)
    cross = jnp.zeros_like(mean)
    for s, ref in enumerate(stats_refs):
        shift = means[s] - mean
        part = ref[2:3, :]
        square = square + ref[1:2, :] + cols * shift * shift
        total = total + part
        cross = cross + ref[3:4, :] + shift * part
    inv_dev = lax.rsqrt(square * (1.0 / D) + NORM_EPS)
    kind = lax.broadcasted_iota(jnp.int32, (128, positions), 0)
    rest = jnp.where(kind == 2, total * (1.0 / D), cross * inv_dev * (1.0 / D))
    packed = jnp.where(kind == 0, mean, jnp.where(kind == 1, inv_dev, rest))
    per_event = jnp.transpose(packed)
    return [per_event[:, k : k + 1] for k in range(4)]


def backward_kernel(*refs, blk, users, maxlen, shards):
    lengths_ref = refs[0]
    stats_refs = refs[1 : 1 + shards]
    mg_ref, gate_ref, heads_ref, acts_ref, slopes_ref, weights_ref, score_slope_ref = refs[1 + shards : 8 + shards]
    grad_ref, mixed_ref, o_ref, o_t, q_t, v_t, k_split, vg_t, kg_t, qg = refs[8 + shards :]
    i = pl.program_id(0)
    positions, cols = o_ref.shape
    heads = cols // DH
    blocks = positions // blk
    scale = DH ** (-0.5)

    @pl.when(i == 0)
    def _():
        mean, inv_dev, total, cross = combined_stats(stats_refs, cols)
        for p in range(heads // 2):
            lanes = slice(p * PAIR, (p + 1) * PAIR)
            normed = (heads_ref[:, lanes].astype(F32) - mean) * inv_dev
            gate = gate_ref[:, lanes]
            mg = mg_ref[:, lanes]
            mixed_ref[:, lanes] = (normed * gate).astype(BF)
            gate_slope = slopes_ref[:, gate_columns(p)].astype(F32)
            grad_ref[:, gate_columns(p)] = (mg * normed * gate_slope).astype(BF)
            o_ref[:, lanes] = (inv_dev * (mg * gate - total - normed * cross)).astype(BF)
        o_t[...] = jnp.transpose(o_ref[...])
        for scratch, kind in ((v_t, 0), (q_t, 1)):
            scratch[...] = jnp.transpose(jnp.concatenate([acts_ref[:, head_columns(kind, h)] for h in range(heads)], axis=1))
        for block in range(blocks):
            split_pairs(acts_ref, k_split, 2, block, blk)
        vg_t[...] = jnp.zeros_like(vg_t)
        kg_t[...] = jnp.zeros_like(kg_t)

    at_i = pl.ds(pl.multiple_of(i * blk, blk), blk)
    o_i = [o_ref[at_i, h * DH : (h + 1) * DH] for h in range(heads)]

    def column(j, acc):
        at_j = pl.ds(pl.multiple_of(j * blk, blk), blk)
        both_j = pl.ds(pl.multiple_of(j * 2 * blk, 2 * blk), 2 * blk)
        per_head = []
        for h in range(heads):
            lanes = slice(h * DH, (h + 1) * DH)
            weight_grad = dot_nn(o_i[h], v_t[lanes, at_j])
            score_grad = (weight_grad * score_slope_ref[h, :, at_j].astype(F32)).astype(BF)
            vg_t[lanes, at_j] += dot_nn(o_t[lanes, at_i], weights_ref[h, :, at_j])
            kg_t[lanes, at_j] += dot_nn(q_t[lanes, at_i], score_grad)
            per_head.append(score_grad)
        return tuple(
            acc[p] + dot_nn(jnp.concatenate(per_head[2 * p : 2 * p + 2], axis=1), k_split[p, both_j, :])
            for p in range(heads // 2)
        )

    first = history_start(lengths_ref, users, i * blk) // blk
    zero = jnp.zeros((blk, PAIR), F32)
    acc = lax.fori_loop(first, i + 1, column, (zero,) * (heads // 2))
    qg[at_i, :] = jnp.concatenate(acc, axis=1)

    @pl.when(i == blocks - 1)
    def _():
        factor = 0.5 * scale / maxlen
        grads = [jnp.transpose(vg_t[...]) * (1.0 / maxlen), qg[...] * factor, jnp.transpose(kg_t[...]) * factor]
        pieces = [grads[kind][:, h * DH : (h + 1) * DH] for h in range(heads) for kind in range(3)]
        for n in range(3 * heads // 2):
            first_lane = n // 3 * 4 * PAIR + n % 3 * PAIR
            lanes = slice(first_lane, first_lane + PAIR)
            grad = jnp.concatenate(pieces[2 * n : 2 * n + 2], axis=1).astype(BF).astype(F32)
            grad_ref[:, lanes] = (grad * slopes_ref[:, lanes].astype(F32)).astype(BF)


def backward_attention(lengths, stats, mg, gate, head_outs, acts, slopes, weights, score_slope, blk, maxlen):
    positions, cols = mg.shape
    heads = cols // DH
    shards = len(stats)
    users = lengths.shape[1]
    elements = heads * positions * positions // 2
    whole = lambda i: (0, 0)
    return pl.pallas_call(
        functools.partial(backward_kernel, blk=blk, users=users, maxlen=maxlen, shards=shards),
        grid=(positions // blk,),
        in_specs=[pl.BlockSpec(memory_space=pltpu.SMEM)]
        + [pl.BlockSpec((8, positions), whole)] * shards
        + [
            pl.BlockSpec((positions, cols), whole),
            pl.BlockSpec((positions, cols), whole),
            pl.BlockSpec((positions, cols), whole),
            pl.BlockSpec((positions, 4 * cols), whole),
            pl.BlockSpec((positions, 4 * cols), whole),
            pl.BlockSpec((heads, blk, positions), lambda i: (0, i, 0)),
            pl.BlockSpec((heads, blk, positions), lambda i: (0, i, 0)),
        ],
        out_specs=[pl.BlockSpec((positions, 4 * cols), whole), pl.BlockSpec((positions, cols), whole)],
        out_shape=[
            jax.ShapeDtypeStruct((positions, 4 * cols), BF),
            jax.ShapeDtypeStruct((positions, cols), BF),
        ],
        scratch_shapes=[
            pltpu.VMEM((positions, cols), BF),
            pltpu.VMEM((cols, positions), BF),
            pltpu.VMEM((cols, positions), BF),
            pltpu.VMEM((cols, positions), BF),
            pltpu.VMEM((cols // PAIR, 2 * positions, PAIR), BF),
            pltpu.VMEM((cols, positions), F32),
            pltpu.VMEM((cols, positions), F32),
            pltpu.VMEM((positions, cols), F32),
        ],
        compiler_params=pltpu.CompilerParams(vmem_limit_bytes=VMEM_LIMIT),
        cost_estimate=pl.CostEstimate(
            flops=8 * elements * 256, bytes_accessed=4 * elements + 26 * positions * cols, transcendentals=0
        ),
        name="attention_backward",
    )(lengths, *stats, mg, gate, head_outs, acts, slopes, weights, score_slope)


def update_kernel(rows_hbm, table_hbm, accum_ref, new_table_hbm, new_accum_ref, rows_ref, table_ref, new_ref, sems):
    slots = rows_ref.shape[0]
    rows_own = table_ref.shape[0]
    blk = min(256, rows_own)
    blocks = [pl.ds(b * blk, blk) for b in range(rows_own // blk)]
    fetch_rows = pltpu.make_async_copy(rows_hbm, rows_ref, sems.at[0])
    fetch_rows.start()
    fetches, stores = [], []
    for b, at in enumerate(blocks):
        fetches.append(pltpu.make_async_copy(table_hbm.at[at, :], table_ref.at[at, :], sems.at[1 + 2 * b]))
        stores.append(pltpu.make_async_copy(new_ref.at[at, :], new_table_hbm.at[at, :], sems.at[2 + 2 * b]))
        fetches[-1].start()
    fetch_rows.wait()
    numbers = jnp.transpose(rows_ref[:, D:].astype(F32))
    ids = (numbers[0:1, :] * 256.0 + numbers[1:2, :]).astype(jnp.int32)
    for b, at in enumerate(blocks):
        row = b * blk + lax.broadcasted_iota(jnp.int32, (blk, slots), 0)
        hits = jnp.where(row == ids, 1.0, 0.0).astype(BF)
        grad = dot_nn(hits, rows_ref[:, :D])
        old = jnp.transpose(jnp.broadcast_to(accum_ref[:, at], (128, blk)))[:, :1]
        accum = old + jnp.mean(grad * grad, axis=1, keepdims=True)
        new_accum_ref[:, at] = jnp.transpose(jnp.broadcast_to(accum, (blk, 128)))[:1, :]
        fetches[b].wait()
        new_ref[at, :] = table_ref[at, :] - LEARN_RATE * grad * lax.rsqrt(accum)
        stores[b].start()
    for store in stores:
        store.wait()


def update_rows(got_rows, emb_table, row_accum):
    rows_own = emb_table.shape[0]
    slots = got_rows.shape[0]
    hbm = pl.BlockSpec(memory_space=pltpu.HBM)
    vmem = pl.BlockSpec(memory_space=pltpu.VMEM)
    new_table, new_accum = pl.pallas_call(
        update_kernel,
        in_specs=[hbm, hbm, vmem],
        out_specs=[hbm, vmem],
        out_shape=[
            jax.ShapeDtypeStruct((rows_own, D), F32),
            jax.ShapeDtypeStruct((1, rows_own), F32),
        ],
        scratch_shapes=[
            pltpu.VMEM(got_rows.shape, BF),
            pltpu.VMEM((rows_own, D), F32),
            pltpu.VMEM((rows_own, D), F32),
            pltpu.SemaphoreType.DMA((1 + 2 * (rows_own // min(256, rows_own)),)),
        ],
        compiler_params=pltpu.CompilerParams(vmem_limit_bytes=VMEM_LIMIT),
        cost_estimate=pl.CostEstimate(
            flops=2 * rows_own * slots * D, bytes_accessed=8 * rows_own * D + 2 * slots * D, transcendentals=rows_own
        ),
        name="update_rows",
    )(got_rows, emb_table, row_accum.reshape(1, rows_own))
    return new_table, new_accum.reshape(rows_own)


def own_weights(w_attn, w_gate, part, pairs):
    slices = []
    for p in range(pairs):
        at = part * pairs + p
        slices.append(lax.dynamic_slice_in_dim(w_attn, at * 3 * PAIR, 3 * PAIR, 1))
        slices.append(lax.dynamic_slice_in_dim(w_gate, at * PAIR, PAIR, 1))
    return jnp.concatenate(slices, axis=1)


def attn_and_gate(proj, pairs):
    pieces = [proj[:, p * 4 * PAIR : (p + 1) * 4 * PAIR] for p in range(pairs)]
    attn = jnp.concatenate([piece[:, : 3 * PAIR] for piece in pieces], axis=1)
    return attn, jnp.concatenate([piece[:, 3 * PAIR :] for piece in pieces], axis=1)


def row_slots(owners, rows, devices, capacity):
    events = owners.shape[0]
    owner_hits = (owners[:, None] == jnp.arange(devices, dtype=jnp.int32)[None, :]).astype(BF)
    place = jnp.arange(events, dtype=jnp.int32)
    before = (place[:, None] > place[None, :]).astype(BF)
    earlier = jnp.dot(before, owner_hits, preferred_element_type=F32)
    slots = jnp.sum(earlier * owner_hits.astype(F32), axis=1).astype(jnp.int32)
    flat_slot = owners * capacity + slots
    slot_hits = jnp.arange(devices * capacity, dtype=jnp.int32)[:, None] == flat_slot[None, :]
    lane = jnp.arange(128, dtype=jnp.int32)[None, :]
    numbers = jnp.where(lane == 0, rows[:, None] // 256, jnp.where(lane == 1, rows[:, None] % 256, 0))
    return slot_hits.astype(BF), numbers.astype(BF)


def rows_to_owners(slot_matrix, input_grad, numbers, devices, capacity):
    rows = jnp.concatenate([input_grad.astype(BF), numbers], axis=1)
    rows = jnp.dot(slot_matrix, rows, preferred_element_type=F32).astype(BF)
    got = lax.all_to_all(
        rows.reshape(devices, capacity, D + 128), ("seq", "dp"), split_axis=0, concat_axis=0, tiled=True
    )
    return got.reshape(devices * capacity, D + 128)


TN = (((0,), (0,)), ((), ()))


def dot_tn(a, b):
    return lax.dot_general(a, b, TN, preferred_element_type=F32)


def body_whole(
    layer_input, out_grad, lengths, item_owner, item_row, w_attn, w_gate, w_out, emb_table, row_accum
):
    seq_count = lax.axis_size("seq")
    dp_count = lax.axis_size("dp")
    devices = seq_count * dp_count
    seq_id = lax.axis_index("seq")
    tokens_dev = layer_input.shape[0]
    positions = tokens_dev * seq_count
    maxlen = 2 * positions // 3
    blk = min(256, positions)
    cols = D // seq_count
    pairs = cols // PAIR
    capacity = max(2, 2 * tokens_dev // devices)

    w_own = own_weights(w_attn, w_gate, seq_id, pairs)
    w_out_own = lax.dynamic_slice_in_dim(w_out, seq_id * cols, cols, 0)
    slot_matrix, numbers = row_slots(item_owner[:, 0], item_row, devices, capacity)

    x_full = lax.all_gather(layer_input, "seq", axis=0, tiled=True)
    og_full = lax.all_gather(out_grad, "seq", axis=0, tiled=True)
    order = jnp.arange(positions // blk, dtype=jnp.int32)
    acts, slopes, gate, weights, score_slope, heads = forward_attention(
        lengths, order, [x_full], w_own, blk, maxlen
    )
    mg, stats_own = event_stats(order, [og_full], w_out_own, gate, heads, blk)
    stats = lax.all_gather(stats_own, "seq", axis=0, tiled=False)
    grads, mixed = backward_attention(
        lengths, [stats[s] for s in range(seq_count)], mg, gate, heads, acts, slopes, weights, score_slope, blk, maxlen
    )

    input_part = dot_nt(grads, w_own).astype(BF)
    got = lax.all_to_all(
        input_part.reshape(seq_count, tokens_dev, D), "seq", split_axis=0, concat_axis=0, tiled=True
    )
    input_grad = jnp.sum(got.astype(F32), axis=0) + out_grad.astype(F32)
    got_rows = rows_to_owners(slot_matrix, input_grad, numbers, devices, capacity)
    new_table, new_accum = update_rows(got_rows, emb_table, row_accum)

    out_part = dot_tn(mixed, og_full).astype(BF)
    share = dp_count // seq_count
    out_part = out_part.reshape(share, D // dp_count, seq_count, cols).transpose(0, 2, 1, 3).reshape(D, cols)
    merged = jnp.concatenate([dot_tn(x_full, grads).astype(BF), out_part], axis=1)
    merged = lax.psum_scatter(merged, "dp", scatter_dimension=0, tiled=True)
    steps = []
    for s in range(seq_count):
        for piece in range(dp_count):
            part, target = divmod(piece, seq_count)
            steps.append((s * dp_count + piece, target * dp_count + s * share + part))
    grad_out = lax.ppermute(merged[:, 4 * cols :], ("seq", "dp"), steps).astype(F32)
    grad_attn, grad_gate = attn_and_gate(merged[:, : 4 * cols].astype(F32), pairs)
    return (grad_attn, grad_gate, grad_out, new_table, new_accum)


SEQ = 4
PLANE = 4


def send(array, target):
    steps = []
    for s in range(SEQ):
        for e in range(PLANE):
            for c in range(2):
                to = target(s, e, c)
                if to is not None:
                    steps.append((s * 2 * PLANE + 2 * e + c, to[0] * 2 * PLANE + 2 * to[1] + to[2]))
    return lax.ppermute(array, ("seq", "dp"), steps)


def home(s, c):
    return c == s // 2


def swap_far(array):
    return send(array, lambda s, e, c: None if home(s, c) else (3 - s, e, 1 - c))


def fetch_near(array):
    return send(array, lambda s, e, c: (s ^ 1, e, c) if home(s, c) else ((3 - s) ^ 1, e, 1 - c))


def swap_near(array):
    return send(array, lambda s, e, c: (s ^ 1, e, c))


def swap_core(array):
    return send(array, lambda s, e, c: (s, e, 1 - c))


def swap_x(array):
    return send(array, lambda s, e, c: (s, e ^ 1, c))


def swap_y(array):
    return send(array, lambda s, e, c: (s, e ^ 2, c))


def tie(*arrays):
    return lax.optimization_barrier(arrays)


def halves(array, bit, axis):
    kept = lax.dynamic_index_in_dim(array, bit, axis, keepdims=False)
    sent = lax.dynamic_index_in_dim(array, 1 - bit, axis, keepdims=False)
    return kept, sent


def body_pairs(
    layer_input, out_grad, lengths, item_owner, item_row, w_attn, w_gate, w_out, emb_table, row_accum
):
    devices = 2 * PLANE * SEQ
    s = lax.axis_index("seq")
    d = lax.axis_index("dp")
    e, c = d // 2, d % 2
    y, x = e // 2, e % 2
    tokens_dev = layer_input.shape[0]
    positions = tokens_dev * SEQ
    maxlen = 2 * positions // 3
    blk = min(256, positions)
    cols = D // SEQ
    pairs = cols // PAIR
    rows_own = emb_table.shape[0]
    capacity = max(2, 2 * tokens_dev // devices)
    at_home = c == s // 2
    part = 2 * (s % 2) + c

    def block_of(seq, core):
        return jnp.where(core == seq // 2, seq, 3 - seq)

    mine_at, near_at = block_of(s, c), block_of(s ^ 1, c)
    core_at, diag_at = block_of(s, 1 - c), block_of(s ^ 1, 1 - c)
    order = jnp.stack([mine_at, near_at, core_at, diag_at]).astype(jnp.int32)

    x_far = swap_far(layer_input)
    x_near = fetch_near(layer_input)
    users = lengths.shape[1]
    keys = (item_owner[:, 0] * rows_own + item_row).reshape(1, tokens_dev)
    small = jnp.concatenate([keys, jnp.pad(lengths, ((0, 0), (0, 128 - users)))], axis=1)
    small = jnp.where(at_home, small, swap_far(small))
    keys, lengths = small[0, :tokens_dev], small[:, tokens_dev : tokens_dev + users]
    w_own = own_weights(w_attn, w_gate, part, pairs)
    w_out_own = lax.dynamic_slice_in_dim(w_out, part * cols, cols, 0)
    slot_matrix, numbers = row_slots(keys // rows_own, keys % rows_own, devices, capacity)
    x_far, x_near, w_own, w_out_own, slot_matrix, numbers, lengths = tie(
        x_far, x_near, w_own, w_out_own, slot_matrix, numbers, lengths
    )
    x_here = jnp.concatenate([jnp.where(at_home, layer_input, x_far), x_near], axis=0)
    x_there = swap_core(x_here)
    x_here, og_own = tie(x_here, out_grad)
    og_far = swap_far(og_own)
    og_near = fetch_near(og_own)

    x_full, acts, slopes, gate, weights, score_slope, heads = forward_attention(
        lengths, order, [x_here, x_there], w_own, blk, maxlen
    )
    og_far, og_near, heads = tie(og_far, og_near, heads)
    og_mine = jnp.where(at_home, og_own, og_far)
    og_here = jnp.concatenate([og_mine, og_near], axis=0)
    og_there = swap_core(og_here)
    og_full, mg, stats_own = event_stats(order, [og_here, og_there], w_out_own, gate, heads, blk)
    stats = [
        stats_own,
        swap_core(stats_own),
        swap_near(stats_own),
        send(stats_own, lambda s, e, c: (s ^ 1, e, 1 - c)),
    ]
    grads, mixed = backward_attention(
        lengths, stats, mg, gate, heads, acts, slopes, weights, score_slope, blk, maxlen
    )

    def input_part(grads, block):
        return dot_nt(lax.dynamic_slice_in_dim(grads, block * tokens_dev, tokens_dev, 0), w_own)

    from_diag = swap_core(input_part(grads, diag_at).astype(BF))
    near_sum = (input_part(grads, near_at) + from_diag.astype(F32)).astype(BF)
    near_sum, grads = tie(near_sum, grads)
    from_near = swap_near(near_sum)
    core_part = input_part(grads, core_at).astype(BF)
    from_core = swap_core(core_part)
    input_grad = input_part(grads, mine_at) + og_mine.astype(F32)

    core_part, grads, mixed = tie(core_part, grads, mixed)
    half = 5 * cols // 2
    proj = dot_tn(x_full, grads).astype(BF).reshape(2, 2, D // PLANE, 4 * cols)
    out_part = dot_tn(mixed, og_full).astype(BF).reshape(cols, 2, 2, cols)
    a_kept, a_sent = halves(proj[..., :half], x, 1)
    b_kept, b_sent = halves(proj[..., half:], y, 0)
    out_kept, out_sent = (piece.transpose(1, 0, 2) for piece in halves(out_part, y, 1))
    b_kept = jnp.concatenate([b_kept, out_kept], axis=-1)
    b_sent = jnp.concatenate([b_sent, out_sent], axis=-1)
    a_got = swap_x(a_sent)
    b_got = swap_y(b_sent)

    input_grad = input_grad + from_core.astype(F32) + from_near.astype(F32)
    got_rows = rows_to_owners(slot_matrix, input_grad, numbers, devices, capacity)

    a = (a_kept.astype(F32) + a_got.astype(F32)).astype(BF)
    b = (b_kept.astype(F32) + b_got.astype(F32)).astype(BF)
    a_kept, a_sent = halves(a, y, 0)
    b_kept, b_sent = halves(b, x, 0)
    a = (a_kept.astype(F32) + swap_y(a_sent).astype(F32)).astype(BF)
    b = (b_kept.astype(F32) + swap_x(b_sent).astype(F32)).astype(BF)

    def last(array, target):
        pieces = array.reshape(2, D // (2 * PLANE), array.shape[1])
        one, other = halves(pieces, s // 2, 0)
        one = send(one, lambda s, e, c: target(s, e, c, s // 2)).astype(F32)
        return one + send(other, lambda s, e, c: target(s, e, c, 1 - s // 2)).astype(F32)

    proj = jnp.concatenate([a, b[:, : 4 * cols - half]], axis=1)
    proj = last(proj, lambda s, e, c, piece: (2 * (s % 2) + c, e, piece))
    grad_out = last(b[:, 4 * cols - half :], lambda s, e, c, piece: (e, 2 * (s % 2) + c, piece))
    grad_attn, grad_gate = attn_and_gate(proj, pairs)
    new_table, new_accum = update_rows(got_rows, emb_table, row_accum)
    return (grad_attn, grad_gate, grad_out, new_table, new_accum)


def solution(mesh):
    placed = (
        P(("dp", "seq"), None),
        P(("dp", "seq"), None),
        P("dp", None),
        P(("dp", "seq"), None),
        P(("dp", "seq")),
        P(),
        P(),
        P(),
        P(("seq", "dp"), None),
        P(("seq", "dp")),
    )
    paired = mesh.shape["seq"] == SEQ and mesh.shape["dp"] == 2 * PLANE
    return jax.shard_map(
        body_pairs if paired else body_whole,
        mesh=mesh,
        in_specs=placed,
        out_specs=(
            P("dp", "seq"),
            P("dp", "seq"),
            P("dp", "seq"),
            P(("seq", "dp"), None),
            P(("seq", "dp")),
        ),
        check_vma=False,
    )
```

```python
import functools

import jax
import jax.numpy as jnp
from jax import lax
from jax.experimental import pallas as pl
from jax.experimental.pallas import tpu as pltpu
from jax.sharding import PartitionSpec as P

D = 1024
H = 16
DH = 64
PAIR = 2 * DH

NORM_EPS = 1e-05
LEARN_RATE = 0.1
VMEM_LIMIT = 56 * 1024 * 1024
BF = jnp.bfloat16
F32 = jnp.float32


def dot_nn(a, b):
    return lax.dot_general(a, b, (((1,), (0,)), ((), ())), preferred_element_type=F32)


def dot_nt(a, b):
    return lax.dot_general(a, b, (((1,), (1,)), ((), ())), preferred_element_type=F32)


def history_start(lengths_ref, users, place):
    start = jnp.zeros_like(place)
    end = jnp.int32(0)
    for user in range(users - 1):
        end = end + lengths_ref[0, user]
        start = jnp.where(place >= end, end, start)
    return start


def head_columns(kind, head):
    first = head // 2 * 4 * PAIR + head % 2 * 3 * DH + kind * DH
    return slice(first, first + DH)


def gate_columns(pair):
    return slice(pair * 4 * PAIR + 3 * PAIR, (pair + 1) * 4 * PAIR)


def split_pairs(acts_ref, split_ref, kind, block, blk):
    at = pl.ds(pl.multiple_of(block * blk, blk), blk)
    zero = jnp.zeros((blk, DH), BF)
    for p in range(split_ref.shape[0]):
        one, two = (acts_ref[at, head_columns(kind, 2 * p + h)] for h in range(2))
        below = pl.multiple_of(block * 2 * blk + blk, blk)
        split_ref[p, pl.ds(pl.multiple_of(block * 2 * blk, blk), blk), :] = jnp.concatenate([one, zero], axis=1)
        split_ref[p, pl.ds(below, blk), :] = jnp.concatenate([zero, two], axis=1)


def forward_kernel(*refs, blk, users, maxlen, count):
    lengths_ref, order_ref = refs[:2]
    x_refs = refs[2 : 2 + count]
    w_ref = refs[2 + count]
    outs = refs[3 + count :]
    if count > 1:
        x_out_ref, outs = outs[0], outs[1:]
    acts_ref, slopes_ref, gate_ref, weights_ref, score_slope_ref, heads_ref, k_t, v_split = outs
    i = pl.program_id(0)
    heads = weights_ref.shape[0]
    chunks = x_refs[0].shape[0] // blk

    @pl.when(i == 0)
    def _():
        for b in range(count):
            for r in range(chunks):
                at = pl.ds(pl.multiple_of(order_ref[b * chunks + r] * blk, blk), blk)
                x = x_refs[b][r * blk : (r + 1) * blk, :]
                if count > 1:
                    x_out_ref[at, :] = x
                for p in range(heads // 2):
                    lanes = slice(p * 4 * PAIR, (p + 1) * 4 * PAIR)
                    half = 0.5 * dot_nn(x, w_ref[:, lanes])
                    t = jnp.tanh(half)
                    prod = half * t
                    silu = half + prod
                    acts_ref[at, lanes] = silu.astype(BF)
                    gate_ref[at, p * PAIR : (p + 1) * PAIR] = silu[:, 3 * PAIR :]
                    slopes_ref[at, lanes] = (0.5 * (1.0 + t) * (1.0 + half - prod)).astype(BF)
                for h in range(heads):
                    k_t[h * DH : (h + 1) * DH, at] = jnp.transpose(acts_ref[at, head_columns(2, h)])
                split_pairs(acts_ref, v_split, 0, order_ref[b * chunks + r], blk)

    at_i = pl.ds(pl.multiple_of(i * blk, blk), blk)
    q_half = [acts_ref[at_i, head_columns(1, h)] * jnp.asarray(0.5 * DH**-0.5, BF) for h in range(heads)]
    row = i * blk + lax.broadcasted_iota(jnp.int32, (blk, blk), 0)
    col0 = lax.broadcasted_iota(jnp.int32, (blk, blk), 1)
    start = history_start(lengths_ref, users, row)

    def column(j, acc):
        at_j = pl.ds(pl.multiple_of(j * blk, blk), blk)
        both_j = pl.ds(pl.multiple_of(j * 2 * blk, 2 * blk), 2 * blk)
        col = col0 + j * blk
        allowed = (col <= row) & (col >= start)
        per_head = []
        for h in range(heads):
            half = dot_nn(q_half[h], k_t[h * DH : (h + 1) * DH, at_j])
            half = jnp.where(allowed, half, -64.0)
            t = jnp.tanh(half)
            p = half * t
            weights = (half + p).astype(BF)
            weights_ref[h, :, at_j] = weights
            score_slope_ref[h, :, at_j] = ((1.0 + t) * (1.0 + half - p)).astype(BF)
            per_head.append(weights)
        return tuple(
            acc[p] + dot_nn(jnp.concatenate(per_head[2 * p : 2 * p + 2], axis=1), v_split[p, both_j, :])
            for p in range(heads // 2)
        )

    first = history_start(lengths_ref, users, i * blk) // blk
    zero = jnp.zeros((blk, PAIR), F32)
    acc = lax.fori_loop(first, i + 1, column, (zero,) * (heads // 2))
    heads_ref[...] = (jnp.concatenate(acc, axis=1) * (1.0 / maxlen)).astype(BF)


def forward_attention(lengths, order, x_blocks, w_own, blk, maxlen):
    count = len(x_blocks)
    block_rows = x_blocks[0].shape[0]
    positions = count * block_rows
    cols = w_own.shape[1] // 4
    heads = cols // DH
    users = lengths.shape[1]
    elements = heads * positions * positions // 2
    whole = lambda i: (0, 0)
    out_specs = [
        pl.BlockSpec((positions, 4 * cols), whole),
        pl.BlockSpec((positions, 4 * cols), whole),
        pl.BlockSpec((positions, cols), whole),
        pl.BlockSpec((heads, blk, positions), lambda i: (0, i, 0)),
        pl.BlockSpec((heads, blk, positions), lambda i: (0, i, 0)),
        pl.BlockSpec((blk, cols), lambda i: (i, 0)),
    ]
    out_shape = [
        jax.ShapeDtypeStruct((positions, 4 * cols), BF),
        jax.ShapeDtypeStruct((positions, 4 * cols), BF),
        jax.ShapeDtypeStruct((positions, cols), F32),
        jax.ShapeDtypeStruct((heads, positions, positions), BF),
        jax.ShapeDtypeStruct((heads, positions, positions), BF),
        jax.ShapeDtypeStruct((positions, cols), BF),
    ]
    if count > 1:
        out_specs = [pl.BlockSpec((positions, D), whole)] + out_specs
        out_shape = [jax.ShapeDtypeStruct((positions, D), BF)] + out_shape
    return pl.pallas_call(
        functools.partial(forward_kernel, blk=blk, users=users, maxlen=maxlen, count=count),
        grid=(positions // blk,),
        in_specs=[pl.BlockSpec(memory_space=pltpu.SMEM), pl.BlockSpec(memory_space=pltpu.SMEM)]
        + [pl.BlockSpec((block_rows, D), whole)] * count
        + [pl.BlockSpec((D, 4 * cols), whole)],
        out_specs=out_specs,
        out_shape=out_shape,
        scratch_shapes=[pltpu.VMEM((cols, positions), BF), pltpu.VMEM((cols // PAIR, 2 * positions, PAIR), BF)],
        compiler_params=pltpu.CompilerParams(vmem_limit_bytes=VMEM_LIMIT),
        cost_estimate=pl.CostEstimate(
            flops=8 * positions * D * cols + 4 * elements * 256,
            bytes_accessed=4 * positions * D + 4 * elements,
            transcendentals=elements,
        ),
        name="attention_forward",
    )(lengths, order, *x_blocks, w_own)


def stats_kernel(*refs, blk, count):
    order_ref = refs[0]
    og_refs = refs[1 : 1 + count]
    w_ref, gate_ref, heads_ref = refs[1 + count : 4 + count]
    outs = refs[4 + count :]
    if count > 1:
        og_out_ref, outs = outs[0], outs[1:]
    mg_ref, stats_ref = outs
    chunks = og_refs[0].shape[0] // blk
    for b in range(count):
        for r in range(chunks):
            at = pl.ds(pl.multiple_of(order_ref[b * chunks + r] * blk, blk), blk)
            og = og_refs[b][r * blk : (r + 1) * blk, :]
            if count > 1:
                og_out_ref[at, :] = og
            mg = dot_nt(og, w_ref[...])
            mg_ref[at, :] = mg
            ng = mg * gate_ref[at, :]
            heads = heads_ref[at, :].astype(F32)
            mean = jnp.mean(heads, axis=1, keepdims=True)
            centred = heads - mean
            square = jnp.sum(centred * centred, axis=1, keepdims=True)
            total = jnp.sum(ng, axis=1, keepdims=True)
            cross = jnp.sum(ng * centred, axis=1, keepdims=True)
            lane = lax.broadcasted_iota(jnp.int32, (blk, 128), 1)
            packed = jnp.where(lane == 0, mean, jnp.where(lane == 1, square, jnp.where(lane == 2, total, cross)))
            stats_ref[:, at] = jnp.transpose(packed)[:8, :]


def event_stats(order, og_blocks, w_out_own, gate, heads, blk):
    positions, cols = heads.shape
    count = len(og_blocks)
    vmem = pl.BlockSpec(memory_space=pltpu.VMEM)
    out_shape = [
        jax.ShapeDtypeStruct((positions, cols), F32),
        jax.ShapeDtypeStruct((8, positions), F32),
    ]
    if count > 1:
        out_shape = [jax.ShapeDtypeStruct((positions, D), BF)] + out_shape
    return pl.pallas_call(
        functools.partial(stats_kernel, blk=blk, count=count),
        in_specs=[pl.BlockSpec(memory_space=pltpu.SMEM)] + [vmem] * (count + 3),
        out_specs=[vmem] * len(out_shape),
        out_shape=out_shape,
        compiler_params=pltpu.CompilerParams(vmem_limit_bytes=VMEM_LIMIT),
        cost_estimate=pl.CostEstimate(
            flops=2 * positions * cols * D, bytes_accessed=4 * positions * D + 10 * positions * cols, transcendentals=0
        ),
        name="event_stats",
    )(order, *og_blocks, w_out_own, gate, heads)


def combined_stats(stats_refs, cols):
    shards = len(stats_refs)
    positions = stats_refs[0].shape[1]
    means = [ref[0:1, :] for ref in stats_refs]
    mean = sum(means) * (1.0 / shards)
    square = jnp.zeros_like(mean)
    total = jnp.zeros_like(mean)
    cross = jnp.zeros_like(mean)
    for s, ref in enumerate(stats_refs):
        shift = means[s] - mean
        part = ref[2:3, :]
        square = square + ref[1:2, :] + cols * shift * shift
        total = total + part
        cross = cross + ref[3:4, :] + shift * part
    inv_dev = lax.rsqrt(square * (1.0 / D) + NORM_EPS)
    kind = lax.broadcasted_iota(jnp.int32, (128, positions), 0)
    rest = jnp.where(kind == 2, total * (1.0 / D), cross * inv_dev * (1.0 / D))
    packed = jnp.where(kind == 0, mean, jnp.where(kind == 1, inv_dev, rest))
    per_event = jnp.transpose(packed)
    return [per_event[:, k : k + 1] for k in range(4)]


def backward_kernel(*refs, blk, users, maxlen, shards):
    lengths_ref = refs[0]
    stats_refs = refs[1 : 1 + shards]
    mg_ref, gate_ref, heads_ref, acts_ref, slopes_ref, weights_ref, score_slope_ref = refs[1 + shards : 8 + shards]
    grad_ref, mixed_ref, o_ref, o_t, q_t, v_t, k_split, vg_t, kg_t, qg = refs[8 + shards :]
    i = pl.program_id(0)
    positions, cols = o_ref.shape
    heads = cols // DH
    blocks = positions // blk
    scale = DH ** (-0.5)

    @pl.when(i == 0)
    def _():
        mean, inv_dev, total, cross = combined_stats(stats_refs, cols)
        for p in range(heads // 2):
            lanes = slice(p * PAIR, (p + 1) * PAIR)
            normed = (heads_ref[:, lanes].astype(F32) - mean) * inv_dev
            gate = gate_ref[:, lanes]
            mg = mg_ref[:, lanes]
            mixed_ref[:, lanes] = (normed * gate).astype(BF)
            gate_slope = slopes_ref[:, gate_columns(p)].astype(F32)
            grad_ref[:, gate_columns(p)] = (mg * normed * gate_slope).astype(BF)
            o_ref[:, lanes] = (inv_dev * (mg * gate - total - normed * cross)).astype(BF)
        o_t[...] = jnp.transpose(o_ref[...])
        for scratch, kind in ((v_t, 0), (q_t, 1)):
            scratch[...] = jnp.transpose(jnp.concatenate([acts_ref[:, head_columns(kind, h)] for h in range(heads)], axis=1))
        for block in range(blocks):
            split_pairs(acts_ref, k_split, 2, block, blk)
        vg_t[...] = jnp.zeros_like(vg_t)
        kg_t[...] = jnp.zeros_like(kg_t)

    at_i = pl.ds(pl.multiple_of(i * blk, blk), blk)
    o_i = [o_ref[at_i, h * DH : (h + 1) * DH] for h in range(heads)]

    def column(j, acc):
        at_j = pl.ds(pl.multiple_of(j * blk, blk), blk)
        both_j = pl.ds(pl.multiple_of(j * 2 * blk, 2 * blk), 2 * blk)
        per_head = []
        for h in range(heads):
            lanes = slice(h * DH, (h + 1) * DH)
            weight_grad = dot_nn(o_i[h], v_t[lanes, at_j])
            score_grad = (weight_grad * score_slope_ref[h, :, at_j].astype(F32)).astype(BF)
            vg_t[lanes, at_j] += dot_nn(o_t[lanes, at_i], weights_ref[h, :, at_j])
            kg_t[lanes, at_j] += dot_nn(q_t[lanes, at_i], score_grad)
            per_head.append(score_grad)
        return tuple(
            acc[p] + dot_nn(jnp.concatenate(per_head[2 * p : 2 * p + 2], axis=1), k_split[p, both_j, :])
            for p in range(heads // 2)
        )

    first = history_start(lengths_ref, users, i * blk) // blk
    zero = jnp.zeros((blk, PAIR), F32)
    acc = lax.fori_loop(first, i + 1, column, (zero,) * (heads // 2))
    qg[at_i, :] = jnp.concatenate(acc, axis=1)

    @pl.when(i == blocks - 1)
    def _():
        factor = 0.5 * scale / maxlen
        grads = [jnp.transpose(vg_t[...]) * (1.0 / maxlen), qg[...] * factor, jnp.transpose(kg_t[...]) * factor]
        pieces = [grads[kind][:, h * DH : (h + 1) * DH] for h in range(heads) for kind in range(3)]
        for n in range(3 * heads // 2):
            first_lane = n // 3 * 4 * PAIR + n % 3 * PAIR
            lanes = slice(first_lane, first_lane + PAIR)
            grad = jnp.concatenate(pieces[2 * n : 2 * n + 2], axis=1).astype(BF).astype(F32)
            grad_ref[:, lanes] = (grad * slopes_ref[:, lanes].astype(F32)).astype(BF)


def backward_attention(lengths, stats, mg, gate, head_outs, acts, slopes, weights, score_slope, blk, maxlen):
    positions, cols = mg.shape
    heads = cols // DH
    shards = len(stats)
    users = lengths.shape[1]
    elements = heads * positions * positions // 2
    whole = lambda i: (0, 0)
    return pl.pallas_call(
        functools.partial(backward_kernel, blk=blk, users=users, maxlen=maxlen, shards=shards),
        grid=(positions // blk,),
        in_specs=[pl.BlockSpec(memory_space=pltpu.SMEM)]
        + [pl.BlockSpec((8, positions), whole)] * shards
        + [
            pl.BlockSpec((positions, cols), whole),
            pl.BlockSpec((positions, cols), whole),
            pl.BlockSpec((positions, cols), whole),
            pl.BlockSpec((positions, 4 * cols), whole),
            pl.BlockSpec((positions, 4 * cols), whole),
            pl.BlockSpec((heads, blk, positions), lambda i: (0, i, 0)),
            pl.BlockSpec((heads, blk, positions), lambda i: (0, i, 0)),
        ],
        out_specs=[pl.BlockSpec((positions, 4 * cols), whole), pl.BlockSpec((positions, cols), whole)],
        out_shape=[
            jax.ShapeDtypeStruct((positions, 4 * cols), BF),
            jax.ShapeDtypeStruct((positions, cols), BF),
        ],
        scratch_shapes=[
            pltpu.VMEM((positions, cols), BF),
            pltpu.VMEM((cols, positions), BF),
            pltpu.VMEM((cols, positions), BF),
            pltpu.VMEM((cols, positions), BF),
            pltpu.VMEM((cols // PAIR, 2 * positions, PAIR), BF),
            pltpu.VMEM((cols, positions), F32),
            pltpu.VMEM((cols, positions), F32),
            pltpu.VMEM((positions, cols), F32),
        ],
        compiler_params=pltpu.CompilerParams(vmem_limit_bytes=VMEM_LIMIT),
        cost_estimate=pl.CostEstimate(
            flops=8 * elements * 256, bytes_accessed=4 * elements + 26 * positions * cols, transcendentals=0
        ),
        name="attention_backward",
    )(lengths, *stats, mg, gate, head_outs, acts, slopes, weights, score_slope)


def update_kernel(rows_ref, table_ref, accum_ref, new_table_ref, new_accum_ref, ids):
    i = pl.program_id(0)
    blk = table_ref.shape[0]
    slots = rows_ref.shape[0]

    @pl.when(i == 0)
    def _():
        numbers = jnp.transpose(rows_ref[:, D:].astype(F32))
        ids[...] = (numbers[0:1, :] * 256.0 + numbers[1:2, :]).astype(jnp.int32)

    row = i * blk + lax.broadcasted_iota(jnp.int32, (blk, slots), 0)
    hits = jnp.where(row == ids[...], 1.0, 0.0).astype(BF)
    grad = dot_nn(hits, rows_ref[:, :D])
    accum = jnp.transpose(jnp.broadcast_to(accum_ref[...], (128, blk)))[:, :1] + jnp.mean(grad * grad, axis=1, keepdims=True)
    new_accum_ref[...] = jnp.transpose(jnp.broadcast_to(accum, (blk, 128)))[:1, :]
    new_table_ref[...] = table_ref[...] - LEARN_RATE * grad * lax.rsqrt(accum)


def update_rows(got_rows, emb_table, row_accum):
    rows_own = emb_table.shape[0]
    slots = got_rows.shape[0]
    blk = min(512, rows_own)
    new_table, new_accum = pl.pallas_call(
        update_kernel,
        grid=(rows_own // blk,),
        in_specs=[
            pl.BlockSpec((slots, D + 128), lambda i: (0, 0)),
            pl.BlockSpec((blk, D), lambda i: (i, 0)),
            pl.BlockSpec((1, blk), lambda i: (0, i)),
        ],
        out_specs=[
            pl.BlockSpec((blk, D), lambda i: (i, 0)),
            pl.BlockSpec((1, blk), lambda i: (0, i)),
        ],
        out_shape=[
            jax.ShapeDtypeStruct((rows_own, D), F32),
            jax.ShapeDtypeStruct((1, rows_own), F32),
        ],
        scratch_shapes=[pltpu.VMEM((1, slots), jnp.int32)],
        compiler_params=pltpu.CompilerParams(vmem_limit_bytes=VMEM_LIMIT),
        cost_estimate=pl.CostEstimate(
            flops=2 * rows_own * slots * D, bytes_accessed=8 * rows_own * D + 2 * slots * D, transcendentals=rows_own
        ),
        name="update_rows",
    )(got_rows, emb_table, row_accum.reshape(1, rows_own))
    return new_table, new_accum.reshape(rows_own)


def own_weights(w_attn, w_gate, part, pairs):
    slices = []
    for p in range(pairs):
        at = part * pairs + p
        slices.append(lax.dynamic_slice_in_dim(w_attn, at * 3 * PAIR, 3 * PAIR, 1))
        slices.append(lax.dynamic_slice_in_dim(w_gate, at * PAIR, PAIR, 1))
    return jnp.concatenate(slices, axis=1)


def attn_and_gate(proj, pairs):
    pieces = [proj[:, p * 4 * PAIR : (p + 1) * 4 * PAIR] for p in range(pairs)]
    attn = jnp.concatenate([piece[:, : 3 * PAIR] for piece in pieces], axis=1)
    return attn, jnp.concatenate([piece[:, 3 * PAIR :] for piece in pieces], axis=1)


def row_slots(owners, rows, devices, capacity):
    events = owners.shape[0]
    owner_hits = (owners[:, None] == jnp.arange(devices, dtype=jnp.int32)[None, :]).astype(BF)
    place = jnp.arange(events, dtype=jnp.int32)
    before = (place[:, None] > place[None, :]).astype(BF)
    earlier = jnp.dot(before, owner_hits, preferred_element_type=F32)
    slots = jnp.sum(earlier * owner_hits.astype(F32), axis=1).astype(jnp.int32)
    flat_slot = owners * capacity + slots
    slot_hits = jnp.arange(devices * capacity, dtype=jnp.int32)[:, None] == flat_slot[None, :]
    lane = jnp.arange(128, dtype=jnp.int32)[None, :]
    numbers = jnp.where(lane == 0, rows[:, None] // 256, jnp.where(lane == 1, rows[:, None] % 256, 0))
    return slot_hits.astype(BF), numbers.astype(BF)


def rows_to_owners(slot_matrix, input_grad, numbers, devices, capacity):
    rows = jnp.concatenate([input_grad.astype(BF), numbers], axis=1)
    rows = jnp.dot(slot_matrix, rows, preferred_element_type=F32).astype(BF)
    got = lax.all_to_all(
        rows.reshape(devices, capacity, D + 128), ("seq", "dp"), split_axis=0, concat_axis=0, tiled=True
    )
    return got.reshape(devices * capacity, D + 128)


TN = (((0,), (0,)), ((), ()))


def dot_tn(a, b):
    return lax.dot_general(a, b, TN, preferred_element_type=F32)


def body_whole(
    layer_input, out_grad, lengths, item_owner, item_row, w_attn, w_gate, w_out, emb_table, row_accum
):
    seq_count = lax.axis_size("seq")
    dp_count = lax.axis_size("dp")
    devices = seq_count * dp_count
    seq_id = lax.axis_index("seq")
    tokens_dev = layer_input.shape[0]
    positions = tokens_dev * seq_count
    maxlen = 2 * positions // 3
    blk = min(256, positions)
    cols = D // seq_count
    pairs = cols // PAIR
    capacity = max(2, 2 * tokens_dev // devices)

    w_own = own_weights(w_attn, w_gate, seq_id, pairs)
    w_out_own = lax.dynamic_slice_in_dim(w_out, seq_id * cols, cols, 0)
    slot_matrix, numbers = row_slots(item_owner[:, 0], item_row, devices, capacity)

    x_full = lax.all_gather(layer_input, "seq", axis=0, tiled=True)
    og_full = lax.all_gather(out_grad, "seq", axis=0, tiled=True)
    order = jnp.arange(positions // blk, dtype=jnp.int32)
    acts, slopes, gate, weights, score_slope, heads = forward_attention(
        lengths, order, [x_full], w_own, blk, maxlen
    )
    mg, stats_own = event_stats(order, [og_full], w_out_own, gate, heads, blk)
    stats = lax.all_gather(stats_own, "seq", axis=0, tiled=False)
    grads, mixed = backward_attention(
        lengths, [stats[s] for s in range(seq_count)], mg, gate, heads, acts, slopes, weights, score_slope, blk, maxlen
    )

    input_part = dot_nt(grads, w_own).astype(BF)
    got = lax.all_to_all(
        input_part.reshape(seq_count, tokens_dev, D), "seq", split_axis=0, concat_axis=0, tiled=True
    )
    input_grad = jnp.sum(got.astype(F32), axis=0) + out_grad.astype(F32)
    got_rows = rows_to_owners(slot_matrix, input_grad, numbers, devices, capacity)
    new_table, new_accum = update_rows(got_rows, emb_table, row_accum)

    out_part = dot_tn(mixed, og_full).astype(BF)
    share = dp_count // seq_count
    out_part = out_part.reshape(share, D // dp_count, seq_count, cols).transpose(0, 2, 1, 3).reshape(D, cols)
    merged = jnp.concatenate([dot_tn(x_full, grads).astype(BF), out_part], axis=1)
    merged = lax.psum_scatter(merged, "dp", scatter_dimension=0, tiled=True)
    steps = []
    for s in range(seq_count):
        for piece in range(dp_count):
            part, target = divmod(piece, seq_count)
            steps.append((s * dp_count + piece, target * dp_count + s * share + part))
    grad_out = lax.ppermute(merged[:, 4 * cols :], ("seq", "dp"), steps).astype(F32)
    grad_attn, grad_gate = attn_and_gate(merged[:, : 4 * cols].astype(F32), pairs)
    return (grad_attn, grad_gate, grad_out, new_table, new_accum)


SEQ = 4
PLANE = 4


def send(array, target):
    steps = []
    for s in range(SEQ):
        for e in range(PLANE):
            for c in range(2):
                to = target(s, e, c)
                if to is not None:
                    steps.append((s * 2 * PLANE + 2 * e + c, to[0] * 2 * PLANE + 2 * to[1] + to[2]))
    return lax.ppermute(array, ("seq", "dp"), steps)


def home(s, c):
    return c == s // 2


def swap_far(array):
    return send(array, lambda s, e, c: None if home(s, c) else (3 - s, e, 1 - c))


def fetch_near(array):
    return send(array, lambda s, e, c: (s ^ 1, e, c) if home(s, c) else ((3 - s) ^ 1, e, 1 - c))


def swap_near(array):
    return send(array, lambda s, e, c: (s ^ 1, e, c))


def swap_core(array):
    return send(array, lambda s, e, c: (s, e, 1 - c))


def swap_x(array):
    return send(array, lambda s, e, c: (s, e ^ 1, c))


def swap_y(array):
    return send(array, lambda s, e, c: (s, e ^ 2, c))


def tie(*arrays):
    return lax.optimization_barrier(arrays)


def halves(array, bit, axis):
    kept = lax.dynamic_index_in_dim(array, bit, axis, keepdims=False)
    sent = lax.dynamic_index_in_dim(array, 1 - bit, axis, keepdims=False)
    return kept, sent


def body_pairs(
    layer_input, out_grad, lengths, item_owner, item_row, w_attn, w_gate, w_out, emb_table, row_accum
):
    devices = 2 * PLANE * SEQ
    s = lax.axis_index("seq")
    d = lax.axis_index("dp")
    e, c = d // 2, d % 2
    y, x = e // 2, e % 2
    tokens_dev = layer_input.shape[0]
    positions = tokens_dev * SEQ
    maxlen = 2 * positions // 3
    blk = min(256, positions)
    cols = D // SEQ
    pairs = cols // PAIR
    rows_own = emb_table.shape[0]
    capacity = max(2, 2 * tokens_dev // devices)
    at_home = c == s // 2
    part = 2 * (s % 2) + c

    def block_of(seq, core):
        return jnp.where(core == seq // 2, seq, 3 - seq)

    mine_at, near_at = block_of(s, c), block_of(s ^ 1, c)
    core_at, diag_at = block_of(s, 1 - c), block_of(s ^ 1, 1 - c)
    order = jnp.stack([mine_at, near_at, core_at, diag_at]).astype(jnp.int32)

    x_far = swap_far(layer_input)
    x_near = fetch_near(layer_input)
    users = lengths.shape[1]
    keys = (item_owner[:, 0] * rows_own + item_row).reshape(1, tokens_dev)
    small = jnp.concatenate([keys, jnp.pad(lengths, ((0, 0), (0, 128 - users)))], axis=1)
    small = jnp.where(at_home, small, swap_far(small))
    keys, lengths = small[0, :tokens_dev], small[:, tokens_dev : tokens_dev + users]
    w_own = own_weights(w_attn, w_gate, part, pairs)
    w_out_own = lax.dynamic_slice_in_dim(w_out, part * cols, cols, 0)
    slot_matrix, numbers = row_slots(keys // rows_own, keys % rows_own, devices, capacity)
    x_far, x_near, w_own, w_out_own, slot_matrix, numbers, lengths = tie(
        x_far, x_near, w_own, w_out_own, slot_matrix, numbers, lengths
    )
    x_here = jnp.concatenate([jnp.where(at_home, layer_input, x_far), x_near], axis=0)
    x_there = swap_core(x_here)
    x_here, og_own = tie(x_here, out_grad)
    og_far = swap_far(og_own)
    og_near = fetch_near(og_own)

    x_full, acts, slopes, gate, weights, score_slope, heads = forward_attention(
        lengths, order, [x_here, x_there], w_own, blk, maxlen
    )
    og_far, og_near, heads = tie(og_far, og_near, heads)
    og_mine = jnp.where(at_home, og_own, og_far)
    og_here = jnp.concatenate([og_mine, og_near], axis=0)
    og_there = swap_core(og_here)
    og_full, mg, stats_own = event_stats(order, [og_here, og_there], w_out_own, gate, heads, blk)
    stats = [
        stats_own,
        swap_core(stats_own),
        swap_near(stats_own),
        send(stats_own, lambda s, e, c: (s ^ 1, e, 1 - c)),
    ]
    grads, mixed = backward_attention(
        lengths, stats, mg, gate, heads, acts, slopes, weights, score_slope, blk, maxlen
    )

    def input_part(grads, block):
        return dot_nt(lax.dynamic_slice_in_dim(grads, block * tokens_dev, tokens_dev, 0), w_own)

    from_diag = swap_core(input_part(grads, diag_at).astype(BF))
    near_sum = (input_part(grads, near_at) + from_diag.astype(F32)).astype(BF)
    near_sum, grads = tie(near_sum, grads)
    from_near = swap_near(near_sum)
    core_part = input_part(grads, core_at).astype(BF)
    from_core = swap_core(core_part)
    input_grad = input_part(grads, mine_at) + og_mine.astype(F32)

    core_part, grads, mixed = tie(core_part, grads, mixed)
    half = 5 * cols // 2
    proj = dot_tn(x_full, grads).astype(BF).reshape(2, 2, D // PLANE, 4 * cols)
    out_part = dot_tn(mixed, og_full).astype(BF).reshape(cols, 2, 2, cols)
    a_kept, a_sent = halves(proj[..., :half], x, 1)
    b_kept, b_sent = halves(proj[..., half:], y, 0)
    out_kept, out_sent = (piece.transpose(1, 0, 2) for piece in halves(out_part, y, 1))
    b_kept = jnp.concatenate([b_kept, out_kept], axis=-1)
    b_sent = jnp.concatenate([b_sent, out_sent], axis=-1)
    a_got = swap_x(a_sent)
    b_got = swap_y(b_sent)

    input_grad = input_grad + from_core.astype(F32) + from_near.astype(F32)
    got_rows = rows_to_owners(slot_matrix, input_grad, numbers, devices, capacity)

    a = (a_kept.astype(F32) + a_got.astype(F32)).astype(BF)
    b = (b_kept.astype(F32) + b_got.astype(F32)).astype(BF)
    a_kept, a_sent = halves(a, y, 0)
    b_kept, b_sent = halves(b, x, 0)
    a = (a_kept.astype(F32) + swap_y(a_sent).astype(F32)).astype(BF)
    b = (b_kept.astype(F32) + swap_x(b_sent).astype(F32)).astype(BF)

    def last(array, target):
        pieces = array.reshape(2, D // (2 * PLANE), array.shape[1])
        one, other = halves(pieces, s // 2, 0)
        one = send(one, lambda s, e, c: target(s, e, c, s // 2)).astype(F32)
        return one + send(other, lambda s, e, c: target(s, e, c, 1 - s // 2)).astype(F32)

    proj = jnp.concatenate([a, b[:, : 4 * cols - half]], axis=1)
    proj = last(proj, lambda s, e, c, piece: (2 * (s % 2) + c, e, piece))
    grad_out = last(b[:, 4 * cols - half :], lambda s, e, c, piece: (e, 2 * (s % 2) + c, piece))
    grad_attn, grad_gate = attn_and_gate(proj, pairs)
    new_table, new_accum = update_rows(got_rows, emb_table, row_accum)
    return (grad_attn, grad_gate, grad_out, new_table, new_accum)


def solution(mesh):
    placed = (
        P(("dp", "seq"), None),
        P(("dp", "seq"), None),
        P("dp", None),
        P(("dp", "seq"), None),
        P(("dp", "seq")),
        P(),
        P(),
        P(),
        P(("seq", "dp"), None),
        P(("seq", "dp")),
    )
    paired = mesh.shape["seq"] == SEQ and mesh.shape["dp"] == 2 * PLANE
    return jax.shard_map(
        body_pairs if paired else body_whole,
        mesh=mesh,
        in_specs=placed,
        out_specs=(
            P("dp", "seq"),
            P("dp", "seq"),
            P("dp", "seq"),
            P(("seq", "dp"), None),
            P(("seq", "dp")),
        ),
        check_vma=False,
    )
```
